32 devices in a mesh: prot: 2 (over core), res: 4 (over z), mp: 4 (over y, x).
Axes of the slice: x: 2, y: 2, z: 4, core: 2. Of those that a mesh axis runs over, the one named last changes fastest.
Arguments:
- node_states: bfloat16 [8, 1024, 512], P('prot', 'res'), may hold values from -6 to 6
- edge_states: bfloat16 [8, 1024, 60, 192], P('prot', 'res', 'mp'), may hold values from -6 to 6
- neighbour_slots: int32 [8, 1024, 60], P('prot', 'res'), may hold values from 0 to 319, as said below
- send_rows: int32 [8, 4, 4, 16], P('prot', 'res'), may hold values from 0 to 255, as said below
- live_counts: int32 [8, 1024], P('prot', 'res'), may hold values from 0 to 60
- message_nodes: bfloat16 [2, 512, 512], P(None, None, 'mp'), may hold values from -0.15625 to 0.15625
- message_edges: bfloat16 [192, 512], replicated, may hold values from -0.15625 to 0.15625
- message_bias: bfloat16 [512], P('mp'), may hold values from -3 to 3
- message_output: bfloat16 [512, 512], P('mp'), may hold values from -0.75 to 0.75
- feedforward_weight: bfloat16 [512, 2048], P(None, 'mp'), may hold values from -0.25 to 0.25
- feedforward_bias: bfloat16 [2048], P('mp'), may hold values from -3 to 3
- feedforward_output: bfloat16 [2048, 512], P('mp'), may hold values from -0.1875 to 0.1875
- output_biases: bfloat16 [2, 512], replicated, may hold values from -2 to 2
- norm_gains: bfloat16 [2, 512], replicated, may hold values from 0.5 to 1.5
- norm_shifts: bfloat16 [2, 512], replicated, may hold values from -2 to 2
- update_weight: bfloat16 [1216, 192], replicated, may hold values from -0.15625 to 0.15625
- update_bias: bfloat16 [192], replicated, may hold values from -3 to 3
- update_output: bfloat16 [192, 192], replicated, may hold values from -0.625 to 0.625
- branch_bias: bfloat16 [192], replicated, may hold values from -2 to 2
- edge_gain: bfloat16 [192], replicated, may hold values from 0.5 to 1.5
- edge_shift: bfloat16 [192], replicated, may hold values from -2 to 2
- node_cotangent: bfloat16 [8, 1024, 512], P('prot', 'res'), may hold values from -6 to 6
- edge_cotangent: bfloat16 [8, 1024, 60, 192], P('prot', 'res', 'mp'), may hold values from -6 to 6
Outputs:
- node_result: bfloat16 [8, 1024, 512], P('prot', 'res')
- edge_result: bfloat16 [8, 1024, 60, 192], P('prot', 'res', 'mp')
- node_grad: bfloat16 [8, 1024, 512], P('prot', 'res')
- edge_grad: bfloat16 [8, 1024, 60, 192], P('prot', 'res', 'mp')
- message_nodes_grad: float32 [2, 512, 512], P(None, None, 'mp')
- message_edges_grad: float32 [192, 512], replicated
- message_bias_grad: float32 [512], P('mp')
- message_output_grad: float32 [512, 512], P('mp')
- feedforward_weight_grad: float32 [512, 2048], P(None, 'mp')
- feedforward_bias_grad: float32 [2048], P('mp')
- feedforward_output_grad: float32 [2048, 512], P('mp')
- output_biases_grad: float32 [2, 512], replicated
- norm_gains_grad: float32 [2, 512], replicated
- norm_shifts_grad: float32 [2, 512], replicated
- update_weight_grad: float32 [1216, 192], replicated
- update_bias_grad: float32 [192], replicated
- update_output_grad: float32 [192, 192], replicated
- branch_bias_grad: float32 [192], replicated
- edge_gain_grad: float32 [192], replicated
- edge_shift_grad: float32 [192], replicated
The draws below stay inside these ranges and needn't reach their ends.
Inputs may be any that keep to these rules, and one draw needn't show every extreme that they name: send_rows[b,p,d,c] is a row of block p; for each pair of blocks the first entries (none when p = d, all 16 for at least one sender to each block) are distinct rows that block d may name, and the remaining entries are 0 and named by no slot. `neighbour_slots`: A slot below 256 names a row of the residue's own block; a larger slot s names entry (s - 256) % 16 of what block (s - 256) // 16 sends to the residue's block, and only entries that the promise on send_rows calls used; every used entry is named by some residue of the receiving block; the 60 slots of a residue are distinct.
All inputs are finite; a program needn't handle non-finite values.
Results may differ from the reference program's by a relative error of at most 0.025.
Values may be sent and summed in bfloat16 or wider, within the bound.
No kernel may reach another device: no remote copies, remote signals or barrier semaphores. Data moves between devices by JAX's collectives and lax.ppermute only.
A program may use at most 320 MiB of HBM per device.

```python
import jax
import jax.numpy as jnp
from jax import lax

D = 512
CE = 192
KNB = 60
HM = 512
FF = 2048
HE = 192
CAP = 16
PROTS = 8
RES_DEV = 256
LENGTH = 1024
POOL = 320


def graph_tables(key):
    res_peers = LENGTH // RES_DEV
    count_key = jax.random.fold_in(jax.random.fold_in(key, 7), 0)
    row_key = jax.random.fold_in(jax.random.fold_in(key, 7), 2)
    pick_key = jax.random.fold_in(jax.random.fold_in(key, 7), 3)
    peer_ids = jnp.arange(res_peers, dtype=jnp.int32)
    counts = jax.random.randint(count_key, (PROTS, res_peers, res_peers), 0, CAP + 1, dtype=jnp.int32)
    forced_source = (peer_ids[None, None, :] + res_peers // 2) % res_peers
    forced = peer_ids[None, :, None] == forced_source
    corner = (peer_ids[:, None] == res_peers - 1) & (peer_ids[None, :] == 0)
    counts = jnp.where(forced | corner[None], CAP, counts)
    counts = jnp.where((peer_ids[:, None] == peer_ids[None, :])[None], 0, counts)
    row_scores = jax.random.randint(row_key, (PROTS, res_peers, res_peers, RES_DEV), 0, 65536, dtype=jnp.int32) * RES_DEV + jnp.arange(RES_DEV, dtype=jnp.int32)
    chosen = jnp.argsort(row_scores, axis=-1)[..., :CAP].astype(jnp.int32)
    filled = jnp.arange(CAP, dtype=jnp.int32)[None, None, None, :] < counts[..., None]
    send_table = jnp.where(filled, chosen, 0).astype(jnp.int32)
    slot_ids = jnp.arange(POOL, dtype=jnp.int32)
    remote = jnp.maximum(slot_ids - RES_DEV, 0)
    peer_of_slot = jnp.minimum(remote // CAP, res_peers - 1)
    received = jnp.transpose(counts, (0, 2, 1))
    slot_count = jnp.take(received, peer_of_slot, axis=2)
    usable = (slot_ids < RES_DEV)[None, None, :] | ((remote % CAP)[None, None, :] < slot_count)
    home_block = jnp.arange(LENGTH, dtype=jnp.int32) // RES_DEV
    usable_rows = usable[:, home_block, :]
    raw_scores = jax.random.randint(pick_key, (PROTS, LENGTH, POOL), 0, 1024, dtype=jnp.int32)
    raw_scores = raw_scores + jnp.where(slot_ids < RES_DEV, 1024, 0)[None, None, :]
    scores = jnp.where(usable_rows, raw_scores * POOL + slot_ids, -1 - slot_ids)
    local_index = jnp.arange(LENGTH, dtype=jnp.int32) % RES_DEV
    owner_match = (slot_ids[None, :] >= RES_DEV) & (remote[None, :] % RES_DEV == local_index[:, None])
    scores = jnp.where(usable_rows & owner_match[None], 2 ** 29 + slot_ids[None, None, :], scores)
    marked = (jnp.arange(LENGTH, dtype=jnp.int32)[:, None] == 0) & (slot_ids[None, :] == POOL - 1)
    scores = jnp.where(marked[None], 2 ** 30, scores)
    slot_choice = lax.top_k(scores, KNB)[1].astype(jnp.int32)
    return (send_table, slot_choice)


def draw_send_rows(key, part):
    return graph_tables(key)[0]


def draw_neighbour_slots(key, part):
    return graph_tables(key)[1]


def set_ends(array, own_key, least, top_value):
    spot = [jax.random.randint(jax.random.fold_in(own_key, axis), (), 0, length) for axis, length in enumerate(array.shape)]
    longest = array.shape.index(max(array.shape))
    beside = spot[:longest] + [(spot[longest] + 1) % array.shape[longest]] + spot[longest + 1:]
    return array.at[tuple(spot)].set(least).at[tuple(beside)].set(top_value)


def level_of(rng, dims, shards, least, high):
    def one(dim, shards_of):
        draws = jax.random.uniform(jax.random.fold_in(jax.random.fold_in(rng, 6), dim), (shards_of,), jnp.float32, least / len(shards), high / len(shards))
        return jnp.repeat(jnp.exp(draws), dims[dim] // shards_of).reshape((-1,) + (1,) * (len(dims) - dim - 1))

    level = one(*shards[0])
    for cut in shards[1:]:
        level = level * one(*cut)
    return level


def bell_draw(own_key, dims, deviation, bound, pieces=(), held_as=jnp.bfloat16):
    entries = jax.random.normal(own_key, dims, jnp.float32) * deviation
    if len(pieces) > 0:
        entries = level_of(own_key, dims, pieces, -0.22, 0.18) * entries
    return jnp.clip(entries, min=-bound, max=bound).astype(held_as)


def setup_inputs(seed: int = 0) -> dict:
    keys = jax.random.split(jax.random.key(seed), 24)
    node_states = bell_draw(keys[0], (PROTS, LENGTH, D), 1.0, 6.0, ((0, 2), (1, 4)))
    edge_states = bell_draw(keys[1], (PROTS, LENGTH, KNB, CE), 1.0, 6.0, ((0, 2), (1, 4), (2, 4)))
    neighbour_slots = draw_neighbour_slots(jax.random.fold_in(keys[23], 71), 0)
    send_rows = draw_send_rows(jax.random.fold_in(keys[23], 71), 0)
    live_counts = set_ends(jax.random.randint(keys[4], (PROTS, LENGTH), 0, KNB + 1), jax.random.fold_in(keys[4], 1), 0, KNB).astype(jnp.int32)
    message_nodes = bell_draw(keys[5], (2, D, HM), (2 * D + CE) ** -0.5, 0.15625, ((2, 4),))
    message_edges = bell_draw(keys[6], (CE, HM), (2 * D + CE) ** -0.5, 0.15625)
    message_bias = bell_draw(keys[7], (HM,), 0.5, 3.0, ((0, 4),))
    message_output = bell_draw(keys[8], (HM, D), (HM // 8) ** -0.5, 0.75, ((0, 4),))
    feedforward_weight = bell_draw(keys[9], (D, FF), D ** -0.5, 0.25, ((1, 4),))
    feedforward_bias = bell_draw(keys[10], (FF,), 0.5, 3.0, ((0, 4),))
    feedforward_output = bell_draw(keys[11], (FF, D), (FF // 2) ** -0.5, 0.1875, ((0, 4),))
    output_biases = bell_draw(keys[12], (2, D), 0.3, 2.0)
    norm_gains = jnp.clip(1.0 + 0.1 * jax.random.normal(keys[13], (2, D), jnp.float32), 0.5, 1.5).astype(jnp.bfloat16)
    norm_shifts = bell_draw(keys[14], (2, D), 0.3, 2.0)
    update_weight = bell_draw(keys[15], (2 * D + CE, HE), (2 * D + CE) ** -0.5, 0.15625)
    update_bias = bell_draw(keys[16], (HE,), 0.5, 3.0)
    update_output = bell_draw(keys[17], (HE, CE), (HE // 2) ** -0.5, 0.625)
    branch_bias = bell_draw(keys[18], (CE,), 0.3, 2.0)
    edge_gain = jnp.clip(1.0 + 0.1 * jax.random.normal(keys[19], (CE,), jnp.float32), 0.5, 1.5).astype(jnp.bfloat16)
    edge_shift = bell_draw(keys[20], (CE,), 0.3, 2.0)
    node_cotangent = bell_draw(keys[21], (PROTS, LENGTH, D), 1.0, 6.0, ((0, 2), (1, 4)))
    edge_cotangent = bell_draw(keys[22], (PROTS, LENGTH, KNB, CE), 1.0, 6.0, ((0, 2), (1, 4), (2, 4)))
    return {"node_states": node_states, "edge_states": edge_states, "neighbour_slots": neighbour_slots, "send_rows": send_rows, "live_counts": live_counts, "message_nodes": message_nodes, "message_edges": message_edges, "message_bias": message_bias, "message_output": message_output, "feedforward_weight": feedforward_weight, "feedforward_bias": feedforward_bias, "feedforward_output": feedforward_output, "output_biases": output_biases, "norm_gains": norm_gains, "norm_shifts": norm_shifts, "update_weight": update_weight, "update_bias": update_bias, "update_output": update_output, "branch_bias": branch_bias, "edge_gain": edge_gain, "edge_shift": edge_shift, "node_cotangent": node_cotangent, "edge_cotangent": edge_cotangent}


EPSILON = 1e-05
HIGHEST = lax.Precision.HIGHEST

@jax.custom_vjp
def low(v):
    return lax.optimization_barrier(v.astype(jnp.bfloat16)).astype(jnp.float32)

@jax.custom_vjp
def low_back(v):
    return v

def low_keep(v):
    return (low(v), None)

def low_pass(kept, grad):
    return (grad,)

def back_keep(v):
    return (v, None)

def back_low(kept, grad):
    return (low(grad),)
low.defvjp(low_keep, low_pass)
low_back.defvjp(back_keep, back_low)

def activation(value):
    return jax.nn.gelu(value, approximate=True)

def layer_norm(value, gain, shift):
    centred = value - lax.optimization_barrier(jnp.mean(value, axis=-1, keepdims=True))
    return centred * lax.rsqrt(lax.optimization_barrier(jnp.mean(centred * centred, axis=-1, keepdims=True)) + EPSILON) * gain + shift

def neighbour_index(neighbour_slots, send_rows):
    res_peers = LENGTH // RES_DEV
    peer_ids = jnp.arange(res_peers, dtype=jnp.int32)
    own_rows = peer_ids[:, None] * RES_DEV + jnp.arange(RES_DEV, dtype=jnp.int32)[None, :]
    shifted = send_rows.astype(jnp.int32) + (peer_ids * RES_DEV)[None, :, None, None]
    remote = jnp.transpose(shifted, (0, 2, 1, 3)).reshape(PROTS, res_peers, res_peers * CAP)
    table = jnp.concatenate([jnp.broadcast_to(own_rows[None], (PROTS, res_peers, RES_DEV)), remote], axis=2)
    home_block = jnp.arange(LENGTH, dtype=jnp.int32) // RES_DEV
    return jnp.take_along_axis(table[:, home_block, :], neighbour_slots.astype(jnp.int32), axis=2).astype(jnp.int32)

def protein_layer(weights, protein_item):
    message_nodes, message_edges, message_bias, message_output, feedforward_weight, feedforward_bias, feedforward_output, output_biases, norm_gains, norm_shifts, update_weight, update_bias, update_output, branch_bias, edge_gain, edge_shift = weights
    node_states, edge_states, neighbours, live_counts = protein_item
    live_edge = (jnp.arange(KNB, dtype=jnp.int32)[None, :] < live_counts[:, None]).astype(jnp.float32)
    live_total = lax.optimization_barrier(jnp.sum(live_edge, axis=1))
    mean_scale = 1.0 / jnp.maximum(live_total, 1.0)
    self_term = jnp.dot(node_states, message_nodes[0], precision=HIGHEST)
    other_term = jnp.dot(node_states, message_nodes[1], precision=HIGHEST)[neighbours]
    edge_term = jnp.einsum('lkc,ch->lkh', edge_states, message_edges, precision=HIGHEST)
    pre_message = low_back(self_term[:, None, :] + other_term + edge_term + message_bias)
    hidden_message = low(activation(pre_message))
    mean_hidden = jnp.einsum('lk,lkh->lh', live_edge * mean_scale[:, None], hidden_message, precision=HIGHEST)
    aggregate = low_back(jnp.dot(mean_hidden, message_output, precision=HIGHEST) + (live_total * mean_scale)[:, None] * output_biases[0])
    first_norm = layer_norm(node_states + aggregate, norm_gains[0], norm_shifts[0])
    first_low = low(first_norm)
    pre_forward = low_back(jnp.dot(first_low, feedforward_weight, precision=HIGHEST) + feedforward_bias)
    hidden_forward = low(activation(pre_forward))
    forward_out = low_back(jnp.dot(hidden_forward, feedforward_output, precision=HIGHEST) + output_biases[1])
    second_norm = low(layer_norm(first_norm + forward_out, norm_gains[1], norm_shifts[1]))
    self_update = jnp.dot(second_norm, update_weight[:D], precision=HIGHEST)
    other_update = jnp.dot(second_norm, update_weight[D:2 * D], precision=HIGHEST)[neighbours]
    edge_update = jnp.einsum('lkc,ch->lkh', edge_states, update_weight[2 * D:], precision=HIGHEST)
    pre_update = low_back(self_update[:, None, :] + other_update + edge_update + update_bias)
    hidden_update = low(activation(pre_update))
    branch = low_back(jnp.einsum('lkh,hc->lkc', hidden_update, update_output, precision=HIGHEST) + branch_bias)
    edge_result = layer_norm(edge_states + live_edge[:, :, None] * branch, edge_gain, edge_shift)
    return (second_norm, edge_result)

def reference(node_states, edge_states, neighbour_slots, send_rows, live_counts, message_nodes, message_edges, message_bias, message_output, feedforward_weight, feedforward_bias, feedforward_output, output_biases, norm_gains, norm_shifts, update_weight, update_bias, update_output, branch_bias, edge_gain, edge_shift, node_cotangent, edge_cotangent):
    neighbours = neighbour_index(neighbour_slots, send_rows)
    weights = tuple((weight.astype(jnp.float32) for weight in (message_nodes, message_edges, message_bias, message_output, feedforward_weight, feedforward_bias, feedforward_output, output_biases, norm_gains, norm_shifts, update_weight, update_bias, update_output, branch_bias, edge_gain, edge_shift)))
    checked_layer = jax.checkpoint(protein_layer)

    def forward(nodes_float, edges_float, weight_list):
        return lax.map(lambda protein_item: checked_layer(weight_list, protein_item), (nodes_float, edges_float, neighbours, live_counts))
    outputs, pullback = jax.vjp(forward, node_states.astype(jnp.float32), edge_states.astype(jnp.float32), weights)
    node_grad, edge_grad, weight_grads = pullback((node_cotangent.astype(jnp.float32), edge_cotangent.astype(jnp.float32)))
    return (outputs[0].astype(jnp.bfloat16), outputs[1].astype(jnp.bfloat16), node_grad.astype(jnp.bfloat16), edge_grad.astype(jnp.bfloat16), weight_grads[0], weight_grads[1], weight_grads[2], weight_grads[3], weight_grads[4], weight_grads[5], weight_grads[6], weight_grads[7], weight_grads[8], weight_grads[9], weight_grads[10], weight_grads[11], weight_grads[12], weight_grads[13], weight_grads[14], weight_grads[15])
```

```python
import functools

import jax
import jax.numpy as jnp
from jax import lax
from jax.experimental import pallas as pl
from jax.experimental.pallas import tpu as pltpu
from jax.sharding import PartitionSpec as P

EPSILON = 1e-05
F32 = jnp.float32
BF16 = jnp.bfloat16
DEAD = -30000.0
CUBIC = 0.044715
ROOT = 0.7978845608028654
VMEM_LIMIT = 56 * 1024 * 1024


def dot(left, right):
    return jnp.dot(left, right, preferred_element_type=F32)


def dot_nt(left, right):
    return lax.dot_general(left, right, (((1,), (1,)), ((), ())), preferred_element_type=F32)


def gelu_pair(value):
    square = value * value
    gate = 0.5 + 0.5 * jnp.tanh(value * (ROOT + (ROOT * CUBIC) * square))
    out = value * gate
    slope = gate + (out - out * gate) * (2.0 * ROOT + (6.0 * ROOT * CUBIC) * square)
    return out, slope


def activation(value):
    return jax.nn.gelu(value, approximate=True)


def activation_grad(value, upstream):
    return jax.vjp(activation, value)[1](upstream)[0]


def norm_forward(value, gain, shift):
    centred = value - jnp.mean(value, axis=-1, keepdims=True)
    inverse = lax.rsqrt(jnp.mean(centred * centred, axis=-1, keepdims=True) + EPSILON)
    normed = centred * inverse
    return (normed * gain + shift, normed, inverse)


def norm_backward(upstream, normed, inverse, gain):
    scaled = upstream * gain
    inner = (
        scaled
        - jnp.mean(scaled, axis=-1, keepdims=True)
        - normed * jnp.mean(scaled * normed, axis=-1, keepdims=True)
    )
    return inverse * inner


def selector(slot_row, rows):
    positions = lax.broadcasted_iota(jnp.int32, (rows, slot_row.shape[1]), 0)
    return jnp.where(positions == slot_row, 1.0, 0.0).astype(BF16)


def message_forward_body(perm_ref, edge_ref, slot_ref, table_ref, self_ref, slope_ref, sum_ref):
    steps = edge_ref.shape[1]
    rows = table_ref.shape[2] - edge_ref.shape[2]

    @pl.when(pl.program_id(1) == 0)
    def _():
        sum_ref[...] = jnp.zeros_like(sum_ref)

    for step in range(steps):
        picked = selector(slot_ref[0, 0, step : step + 1, :], rows)
        operand = jnp.concatenate([edge_ref[0, step], picked], axis=0)
        value = dot(table_ref[0], operand) + self_ref[0]
        out, slope = gelu_pair(value)
        slope_ref[0, step] = slope.astype(BF16)
        sum_ref[0] += out.astype(BF16).astype(F32)


def message_backward_body(
    perm_ref, edge_ref, slot_ref, slope_ref, up_ref, weight_ref, part_ref, grad_ref, table_ref, self_ref
):
    steps = edge_ref.shape[1]
    rows = table_ref.shape[2] - edge_ref.shape[2]

    @pl.when(pl.program_id(1) == 0)
    def _():
        table_ref[...] = jnp.zeros_like(table_ref)
        self_ref[...] = jnp.zeros_like(self_ref)

    for step in range(steps):
        picked = selector(slot_ref[0, 0, step : step + 1, :], rows)
        operand = jnp.concatenate([edge_ref[0, step], picked], axis=0)
        grad = slope_ref[0, step] * up_ref[0]
        table_ref[0] += dot_nt(grad, operand)
        self_ref[0] += grad.astype(F32)
        edge = dot(weight_ref[...], grad)
        grad_ref[0, step] = (part_ref[0, step].astype(F32) + edge).astype(BF16)


def update_body(
    perm_ref,
    edge_ref,
    slot_ref,
    up_ref,
    table_ref,
    self_ref,
    out_t_ref,
    out_ref,
    weight_ref,
    gain_ref,
    shift_ref,
    result_ref,
    part_ref,
    table_grad_ref,
    self_grad_ref,
    out_grad_ref,
    gain_grad_ref,
    shift_grad_ref,
    *,
    dead_base,
):
    steps, width, lanes = edge_ref.shape[1:]
    hidden = self_ref.shape[1]
    rows = table_ref.shape[2] - width
    extra = out_t_ref.shape[1] - hidden

    @pl.when(pl.program_id(1) == 0)
    def _():
        table_grad_ref[...] = jnp.zeros_like(table_grad_ref)
        self_grad_ref[...] = jnp.zeros_like(self_grad_ref)

    @pl.when((pl.program_id(0) == 0) & (pl.program_id(1) == 0))
    def _():
        out_grad_ref[...] = jnp.zeros_like(out_grad_ref)
        gain_grad_ref[...] = jnp.zeros_like(gain_grad_ref)
        shift_grad_ref[...] = jnp.zeros_like(shift_grad_ref)

    dead = perm_ref[perm_ref.shape[0] - 1]
    for step in range(steps):
        slot_row = slot_ref[0, 0, step : step + 1, :]
        picked = selector(slot_row, rows)
        edge = edge_ref[0, step]
        operand = jnp.concatenate([edge, picked], axis=0)
        out, slope = gelu_pair(dot(table_ref[0], operand) + self_ref[0])
        first = lax.broadcasted_iota(jnp.int32, (extra, lanes), 0) == 0
        live = jnp.where(first & (slot_row != dead), 1.0, 0.0).astype(BF16)
        out = jnp.concatenate([out.astype(BF16), live], axis=0)
        value = edge.astype(F32) + dot(out_t_ref[...], out)
        centred = value - jnp.mean(value, axis=0, keepdims=True)
        inverse = lax.rsqrt(jnp.mean(centred * centred, axis=0, keepdims=True) + EPSILON)
        normed = centred * inverse
        gain = gain_ref[...]
        result_ref[0, step] = (normed * gain + shift_ref[...]).astype(BF16)
        upstream = up_ref[0, step].astype(F32)
        gain_grad_ref[...] += upstream * normed
        shift_grad_ref[...] += upstream
        scaled = upstream * gain
        mixed = inverse * (
            scaled
            - jnp.mean(scaled, axis=0, keepdims=True)
            - normed * jnp.mean(scaled * normed, axis=0, keepdims=True)
        )
        low = mixed.astype(BF16)
        out_grad_ref[...] += dot_nt(low, out)
        grad = slope * dot(out_ref[...], low)
        self_grad_ref[0] += grad
        grad = grad.astype(BF16)
        table_grad_ref[0] += dot_nt(grad, operand)
        part_ref[0, step] = (mixed + dot(weight_ref[...], grad)).astype(BF16)


def group_of(total):
    for size in (5, 4, 3, 2, 1):
        if total % size == 0:
            return size


def edge_call(body, perm, grid, ins, outs, flops, moved, name):
    spec = pltpu.PrefetchScalarGridSpec(
        num_scalar_prefetch=1,
        grid=grid,
        in_specs=[pl.BlockSpec(block, index) for _, block, index in ins],
        out_specs=[pl.BlockSpec(block, index) for _, _, block, index in outs],
    )
    return pl.pallas_call(
        body,
        grid_spec=spec,
        out_shape=[jax.ShapeDtypeStruct(shape, dtype) for shape, dtype, _, _ in outs],
        compiler_params=pltpu.CompilerParams(
            dimension_semantics=("arbitrary", "arbitrary"), vmem_limit_bytes=VMEM_LIMIT
        ),
        cost_estimate=pl.CostEstimate(flops=flops, bytes_accessed=moved, transcendentals=0),
        name=name,
    )(perm, *[array for array, _, _ in ins])


def build(prot_size, res_size, mp_size):
    def across(value, offset):
        pairs = [(spot, spot ^ offset) for spot in range(mp_size)]
        return lax.ppermute(value, "mp", pairs)

    def gather(value, axis):
        parts = [value] + [across(value, offset) for offset in range(1, mp_size)]
        return jnp.concatenate(parts, axis=axis)

    def scatter_sum(parts):
        total = parts[0]
        for offset in range(1, mp_size):
            total = total + across(parts[offset].astype(BF16), offset).astype(F32)
        return total

    def exchange(value):
        return lax.all_to_all(value, "res", split_axis=0, concat_axis=0, tiled=True)

    def sum_groups(value):
        rows, lanes = value.shape
        unit = prot_size * res_size * 16
        padded = -(-rows // unit) * unit
        value = jnp.pad(value, ((0, padded - rows), (0, 0)))
        core = lax.axis_index("prot")
        place = lax.axis_index("res")
        if prot_size == 2:
            half = padded // 2
            other = lax.dynamic_slice_in_dim(value, (1 - core) * half, half, 0).astype(BF16)
            mine = lax.dynamic_slice_in_dim(value, core * half, half, 0)
            value = mine + lax.ppermute(other, "prot", [(0, 1), (1, 0)]).astype(F32)
        piece = value.shape[0] // res_size
        total = lax.dynamic_slice_in_dim(value, place * piece, piece, 0)
        for hop in range(1, res_size):
            target = lax.rem(place + hop, res_size)
            part = lax.dynamic_slice_in_dim(value, target * piece, piece, 0).astype(BF16)
            pairs = [(spot, (spot + hop) % res_size) for spot in range(res_size)]
            total = total + lax.ppermute(part, "res", pairs).astype(F32)
        total = total.astype(BF16)
        value = jnp.zeros(value.shape, BF16)
        value = lax.dynamic_update_slice_in_dim(value, total, place * piece, 0)
        for hop in range(1, res_size):
            source = lax.rem(place - hop + res_size, res_size)
            pairs = [(spot, (spot + hop) % res_size) for spot in range(res_size)]
            value = lax.dynamic_update_slice_in_dim(
                value, lax.ppermute(total, "res", pairs), source * piece, 0
            )
        if prot_size == 2:
            other = lax.ppermute(value, "prot", [(0, 1), (1, 0)])
            first = jnp.where(core == 0, value, other)
            second = jnp.where(core == 0, other, value)
            value = jnp.concatenate([first, second], axis=0)
        return value[:rows].astype(F32)

    def columns(value):
        return jnp.concatenate(
            [value[:, spot : spot + 128] for spot in range(0, value.shape[1], 128)], axis=0
        )

    def uncolumns(value, rows):
        return jnp.concatenate(
            [value[spot : spot + rows] for spot in range(0, value.shape[0], rows)], axis=1
        )

    def per_device(
        node_states,
        edge_states,
        neighbour_slots,
        send_rows,
        live_counts,
        message_nodes,
        message_edges,
        message_bias,
        message_output,
        feedforward_weight,
        feedforward_bias,
        feedforward_output,
        output_biases,
        norm_gains,
        norm_shifts,
        update_weight,
        update_bias,
        update_output,
        branch_bias,
        edge_gain,
        edge_shift,
        node_cotangent,
        edge_cotangent,
    ):
        proteins, lanes, width = node_states.shape
        own_k, channels = edge_states.shape[2:]
        slots = send_rows.shape[3]
        pool = lanes + res_size * slots
        part = message_nodes.shape[2]
        hidden = part * mp_size
        update_hidden = update_output.shape[0]
        assert proteins == mp_size
        me = lax.axis_index("mp")
        place = lax.axis_index("res")
        dead = lanes + place * slots
        order = [me ^ offset for offset in range(mp_size)]
        perm = jnp.stack(order + [dead]).astype(jnp.int32)

        def reorder(value, axis=0):
            size = value.shape[axis] // mp_size
            return jnp.concatenate(
                [lax.dynamic_slice_in_dim(value, spot * size, size, axis) for spot in order], axis=axis
            )

        own_slots = lax.dynamic_slice_in_dim(neighbour_slots, me * own_k, own_k, 2)
        alive = lax.broadcasted_iota(jnp.int32, own_slots.shape, 2) + me * own_k < live_counts[..., None]
        own_slots = jnp.transpose(jnp.where(alive, own_slots, dead), (0, 2, 1))
        group = group_of(own_k)
        groups = own_k // group
        own_slots = own_slots.reshape(proteins, groups, group, lanes)
        counts = reorder(live_counts).astype(F32)
        scale = 1.0 / jnp.maximum(counts, 1.0)
        share = (counts * scale)[0][:, None]
        edges = jnp.transpose(edge_states, (0, 2, 3, 1))
        edge_up = jnp.transpose(edge_cotangent, (0, 2, 3, 1))
        nodes = reorder(node_states)
        send = reorder(send_rows[:, 0])
        send_table = (
            send.reshape(proteins, -1)[..., None]
            == lax.broadcasted_iota(jnp.int32, (1, 1, lanes), 2)
        ).astype(BF16)
        own_table = send_table[0]

        node_weights = gather(message_nodes, 2)
        bias = gather(message_bias, 0).astype(F32)
        output_weight = gather(message_output, 0)
        wide_in = gather(feedforward_weight, 1)
        wide_bias = gather(feedforward_bias, 0).astype(F32)
        wide_out = gather(feedforward_output, 0)
        edge_weight = reorder(message_edges, 1)
        gains = norm_gains.astype(F32)
        shifts = norm_shifts.astype(F32)
        biases = output_biases.astype(F32)

        leaving = jnp.einsum("bsr,brd->sbd", send_table, nodes, preferred_element_type=F32)
        leaving = leaving.astype(BF16).reshape(res_size, slots, proteins, width)
        arriving = exchange(leaving).reshape(res_size * slots, proteins, width)
        pool_nodes = jnp.concatenate([nodes, jnp.transpose(arriving, (1, 0, 2))], axis=1)
        pool_is_dead = lax.broadcasted_iota(jnp.int32, (1, 1, pool), 2) == dead

        def table_of(weights, edge_part, rows):
            term = jnp.einsum("dh,bpd->bhp", weights, rows, preferred_element_type=F32)
            term = jnp.where(pool_is_dead, DEAD, term).astype(BF16)
            fixed = jnp.broadcast_to(edge_part.T[None], (proteins,) + edge_part.T.shape)
            return jnp.concatenate([fixed, term], axis=2)

        table = table_of(node_weights[1], edge_weight, pool_nodes)
        self_term = (
            jnp.einsum("dh,brd->bhr", node_weights[0], nodes, preferred_element_type=F32)
            + bias[None, :, None]
        )

        depth = channels + pool
        grid = (proteins, groups)
        edge_block = (1, group, channels, lanes)
        by_perm = lambda p, j, perm: (perm[p], j, 0, 0)
        by_step = lambda p, j, perm: (p, j, 0, 0)
        by_protein = lambda p, j, perm: (p, 0, 0)
        fixed = lambda p, j, perm: (0, 0)
        edge_in = (edges, edge_block, by_perm)
        slot_in = (own_slots, (1, 1, group, lanes), by_perm)
        count = proteins * own_k * lanes
        edge_shape = (proteins, own_k, channels, lanes)
        slope, hidden_sum = edge_call(
            message_forward_body,
            perm,
            grid,
            [
                edge_in,
                slot_in,
                (table, (1, hidden, depth), by_protein),
                (self_term, (1, hidden, lanes), by_protein),
            ],
            [
                ((proteins, own_k, hidden, lanes), BF16, (1, group, hidden, lanes), by_step),
                ((proteins, hidden, lanes), F32, (1, hidden, lanes), by_protein),
            ],
            2 * count * depth * hidden,
            count * (channels + hidden) * 2,
            "message_forward",
        )
        mean_hidden = hidden_sum * scale[:, None, :]
        upper = mean_hidden.astype(BF16)
        lower = (mean_hidden - upper.astype(F32)).astype(BF16)
        message_part = jnp.einsum(
            "bhr,hd->brd", upper, output_weight, preferred_element_type=F32
        ) + jnp.einsum("bhr,hd->brd", lower, output_weight, preferred_element_type=F32)
        aggregate = scatter_sum(message_part) + share * biases[0]
        first_norm, first_normed, first_inverse = norm_forward(
            nodes[0].astype(F32) + aggregate, gains[0], shifts[0]
        )
        first_low = first_norm.astype(BF16)
        pre_forward = dot(first_low, wide_in) + wide_bias
        forward_out = dot(activation(pre_forward).astype(BF16), wide_out) + biases[1]
        second_norm, second_normed, second_inverse = norm_forward(
            first_norm + forward_out, gains[1], shifts[1]
        )
        second_low = second_norm.astype(BF16)

        leaving = dot(own_table, second_low).astype(BF16).reshape(res_size, slots, width)
        arriving = exchange(leaving).reshape(res_size * slots, width)
        pool_own = jnp.concatenate([second_low, arriving], axis=0)
        pool_second = gather(pool_own[None], 0)
        update_self = update_weight[:width]
        update_other = update_weight[width : 2 * width]
        update_edge = update_weight[2 * width :]
        table = table_of(update_other, update_edge, pool_second)
        self_term = jnp.einsum(
            "dh,brd->bhr", update_self, pool_second[:, :lanes], preferred_element_type=F32
        ) + update_bias.astype(F32)[None, :, None]
        out_t = jnp.concatenate(
            [update_output.T, branch_bias[:, None], jnp.zeros((channels, 15), BF16)], axis=1
        )
        spread = lambda vector: jnp.broadcast_to(vector.astype(F32)[:, None], (channels, lanes))
        edge_result, edge_part, table_grad, self_grad, out_grad, gain_grad, shift_grad = edge_call(
            functools.partial(update_body, dead_base=lanes),
            perm,
            grid,
            [
                edge_in,
                slot_in,
                (edge_up, edge_block, by_perm),
                (table, (1, update_hidden, depth), by_protein),
                (self_term, (1, update_hidden, lanes), by_protein),
                (out_t, out_t.shape, fixed),
                (update_output, update_output.shape, fixed),
                (update_edge, update_edge.shape, fixed),
                (spread(edge_gain), (channels, lanes), fixed),
                (spread(edge_shift), (channels, lanes), fixed),
            ],
            [
                (edge_shape, BF16, edge_block, by_perm),
                (edge_shape, BF16, edge_block, by_perm),
                ((proteins, update_hidden, depth), F32, (1, update_hidden, depth), by_protein),
                ((proteins, update_hidden, lanes), F32, (1, update_hidden, lanes), by_protein),
                ((channels, update_hidden + 16), F32, (channels, update_hidden + 16), fixed),
                ((channels, lanes), F32, (channels, lanes), fixed),
                ((channels, lanes), F32, (channels, lanes), fixed),
            ],
            2 * count * (2 * depth + 4 * channels) * update_hidden,
            count * channels * 8,
            "edge_update",
        )
        sums = jnp.concatenate([self_grad, table_grad[:, :, channels:]], axis=2)
        sums = scatter_sum(sums)
        self_sum, pool_sum = sums[:, :lanes].astype(BF16), sums[:, lanes:].astype(BF16)
        self_rows = dot_nt(self_sum, second_low.T)
        other_rows = dot_nt(pool_sum, pool_own.T)
        edge_rows = jnp.sum(table_grad[:, :, :channels], axis=0)
        update_bias_grad = jnp.sum(self_grad, axis=(0, 2))
        pool_back = jnp.einsum("hp,dh->pd", pool_sum, update_other, preferred_element_type=F32)
        self_back = jnp.einsum("hr,dh->rd", self_sum, update_self, preferred_element_type=F32)

        def settle(rows, table):
            return jnp.einsum("sr,sd->rd", table, rows, preferred_element_type=F32)

        returned = exchange(pool_back[lanes:].astype(BF16).reshape(res_size, slots, width))
        second_grad = (
            node_cotangent_own(node_cotangent, order)
            + self_back
            + pool_back[:lanes]
            + settle(returned.reshape(-1, width), own_table)
        )
        second_gain_grad = jnp.sum(second_grad * second_normed, axis=0)
        second_shift_grad = jnp.sum(second_grad, axis=0)
        sum_two_grad = norm_backward(second_grad, second_normed, second_inverse, gains[1])
        forward_grad = sum_two_grad.astype(BF16)
        forward_bias_two = jnp.sum(forward_grad, axis=0, dtype=F32)
        hidden_grad = dot_nt(forward_grad, wide_out)
        pre_forward_grad = activation_grad(pre_forward, hidden_grad).astype(BF16)
        first_grad = sum_two_grad + dot_nt(pre_forward_grad, wide_in)
        first_gain_grad = jnp.sum(first_grad * first_normed, axis=0)
        first_shift_grad = jnp.sum(first_grad, axis=0)
        sum_one_grad = norm_backward(first_grad, first_normed, first_inverse, gains[0])
        aggregate_grad = sum_one_grad.astype(BF16)
        message_bias_one = jnp.sum(share * aggregate_grad.astype(F32), axis=0)

        all_aggregate = gather(aggregate_grad[None], 0)
        mean_grad = jnp.einsum(
            "hd,brd->bhr", output_weight, all_aggregate, preferred_element_type=F32
        )
        upstream = (mean_grad * scale[:, None, :]).astype(BF16)
        edge_grad, table_grad, self_grad = edge_call(
            message_backward_body,
            perm,
            grid,
            [
                edge_in,
                slot_in,
                (slope, (1, group, hidden, lanes), by_step),
                (upstream, (1, hidden, lanes), by_protein),
                (edge_weight, (channels, hidden), fixed),
                (edge_part, edge_block, by_perm),
            ],
            [
                (edge_shape, BF16, edge_block, by_perm),
                ((proteins, hidden, depth), F32, (1, hidden, depth), by_protein),
                ((proteins, hidden, lanes), F32, (1, hidden, lanes), by_protein),
            ],
            2 * count * (depth + channels) * hidden,
            count * (3 * channels + hidden) * 2,
            "message_backward",
        )
        pool_grad = table_grad[:, :, channels:]
        self_low = self_grad.astype(BF16)
        pool_low = pool_grad.astype(BF16)
        pool_back = jnp.einsum("bhp,dh->bpd", pool_low, node_weights[1], preferred_element_type=F32)
        self_back = jnp.einsum("bhr,dh->brd", self_low, node_weights[0], preferred_element_type=F32)
        back = jnp.concatenate([self_back + pool_back[:, :lanes], pool_back[:, lanes:]], axis=1)
        back = scatter_sum(back)
        returned = exchange(back[lanes:].astype(BF16).reshape(res_size, slots, width))
        node_grad = sum_one_grad + back[:lanes] + settle(returned.reshape(-1, width), own_table)
        node_grad = reorder(gather(node_grad.astype(BF16)[None], 0))
        node_result = reorder(pool_second[:, :lanes])

        self_nodes = jnp.einsum("brd,bhr->dh", nodes, self_low, preferred_element_type=F32)
        other_nodes = jnp.einsum("bpd,bhp->dh", pool_nodes, pool_low, preferred_element_type=F32)
        split = lambda value, axis: [
            lax.slice_in_dim(value, spot * part, (spot + 1) * part, axis=axis)
            for spot in range(mp_size)
        ]
        self_nodes = scatter_sum(split(self_nodes, 1))
        other_nodes = scatter_sum(split(other_nodes, 1))
        message_bias_grad = scatter_sum(split(jnp.sum(self_grad, axis=(0, 2))[None], 1))
        output_grad = jnp.einsum(
            "bhr,brd->hd", upper, all_aggregate, preferred_element_type=F32
        ) + jnp.einsum("bhr,brd->hd", lower, all_aggregate, preferred_element_type=F32)
        output_grad = scatter_sum(split(output_grad, 0))
        all_low = gather(first_low, 0)
        all_forward = gather(forward_grad, 0)
        pre_part = dot(all_low, feedforward_weight) + feedforward_bias.astype(F32)
        hidden_part = activation(pre_part).astype(BF16)
        wide_grad = activation_grad(pre_part, dot_nt(all_forward, feedforward_output)).astype(BF16)
        weight_in_grad = jnp.einsum("rd,rf->df", all_low, wide_grad, preferred_element_type=F32)
        weight_out_grad = jnp.einsum("rf,rd->fd", hidden_part, all_forward, preferred_element_type=F32)
        wide_bias_grad = jnp.sum(wide_grad, axis=0, dtype=F32)

        edge_columns = jnp.sum(table_grad[:, :, :channels], axis=0)
        back_order = [jnp.int32(spot) ^ me for spot in range(mp_size)]
        edge_columns = jnp.concatenate(
            [lax.dynamic_slice_in_dim(edge_columns, spot * part, part, 0) for spot in back_order],
            axis=0,
        ).T
        update_columns = jnp.concatenate(
            [self_rows, other_rows, edge_rows, out_grad[:, :update_hidden].T], axis=1
        )
        update_total = update_columns.shape[1]
        update_columns = jnp.pad(update_columns, ((0, 0), (0, -update_total % 128)))
        vectors = [
            update_bias_grad,
            out_grad[:, update_hidden],
            jnp.sum(gain_grad, axis=1),
            jnp.sum(shift_grad, axis=1),
            message_bias_one,
            forward_bias_two,
            first_gain_grad,
            second_gain_grad,
            first_shift_grad,
            second_shift_grad,
        ]
        lengths = [vector.shape[0] for vector in vectors]
        vectors = jnp.concatenate(
            [jnp.pad(vector, (0, -vector.shape[0] % 128)) for vector in vectors]
        ).reshape(-1, 128)
        whole = [columns(edge_columns), columns(update_columns), vectors]
        whole_rows = [value.shape[0] for value in whole]
        whole = jnp.concatenate(whole, axis=0)
        unit = 16 * mp_size
        whole = jnp.pad(whole, ((0, -whole.shape[0] % unit), (0, 0)))
        piece = whole.shape[0] // mp_size
        whole = scatter_sum(
            [lax.dynamic_slice_in_dim(whole, spot * piece, piece, 0) for spot in order]
        )
        pieces = [
            columns(weight_in_grad),
            columns(weight_out_grad),
            columns(output_grad),
            columns(self_nodes),
            columns(other_nodes),
            jnp.concatenate([message_bias_grad.reshape(-1), wide_bias_grad]).reshape(-1, 128),
            whole,
        ]
        piece_rows = [value.shape[0] for value in pieces]
        summed = sum_groups(jnp.concatenate(pieces, axis=0))
        pieces = []
        spot = 0
        for rows in piece_rows:
            pieces.append(summed[spot : spot + rows])
            spot += rows
        weight_in_grad = uncolumns(pieces[0], width)
        weight_out_grad = uncolumns(pieces[1], feedforward_output.shape[0])
        output_grad = uncolumns(pieces[2], part)
        node_weight_grad = jnp.stack([uncolumns(pieces[3], width), uncolumns(pieces[4], width)])
        small = pieces[5].reshape(-1)
        whole = reorder(gather(pieces[6].astype(BF16), 0)).astype(F32)
        spot = whole_rows[0]
        edge_columns = uncolumns(whole[:spot], channels)
        update_columns = uncolumns(whole[spot : spot + whole_rows[1]], update_hidden)
        spot += whole_rows[1]
        vectors = whole[spot : spot + whole_rows[2]].reshape(-1)
        found = []
        spot = 0
        for length in lengths:
            found.append(vectors[spot : spot + length])
            spot += length + (-length % 128)
        turn = lambda value: jnp.transpose(value, (0, 3, 1, 2))
        return (
            node_result,
            turn(edge_result),
            node_grad,
            turn(edge_grad),
            node_weight_grad,
            edge_columns,
            small[:part],
            output_grad,
            weight_in_grad,
            small[part:],
            weight_out_grad,
            jnp.stack([found[4], found[5]]),
            jnp.stack([found[6], found[7]]),
            jnp.stack([found[8], found[9]]),
            update_columns[:, : update_weight.shape[0]].T,
            found[0],
            update_columns[:, update_weight.shape[0] : update_total],
            found[1],
            found[2],
            found[3],
        )

    return per_device


def node_cotangent_own(node_cotangent, order):
    return lax.dynamic_index_in_dim(node_cotangent, order[0], 0, keepdims=False).astype(F32)


def solution(mesh):
    return jax.shard_map(
        build(mesh.shape["prot"], mesh.shape["res"], mesh.shape["mp"]),
        mesh=mesh,
        in_specs=(
            P("prot", "res", None),
            P("prot", "res", "mp", None),
            P("prot", "res", None),
            P("prot", "res", None, None),
            P("prot", "res"),
            P(None, None, "mp"),
            P(),
            P("mp"),
            P("mp", None),
            P(None, "mp"),
            P("mp"),
            P("mp", None),
            P(),
            P(),
            P(),
            P(),
            P(),
            P(),
            P(),
            P(),
            P(),
            P("prot", "res", None),
            P("prot", "res", "mp", None),
        ),
        out_specs=(
            P("prot", "res", None),
            P("prot", "res", "mp", None),
            P("prot", "res", None),
            P("prot", "res", "mp", None),
            P(None, None, "mp"),
            P(),
            P("mp"),
            P("mp", None),
            P(None, "mp"),
            P("mp"),
            P("mp", None),
            P(),
            P(),
            P(),
            P(),
            P(),
            P(),
            P(),
            P(),
            P(),
        ),
        check_vma=False,
    )
```

```python
import functools

import jax
import jax.numpy as jnp
from jax import lax
from jax.experimental import pallas as pl
from jax.experimental.pallas import tpu as pltpu
from jax.sharding import PartitionSpec as P

EPSILON = 1e-05
F32 = jnp.float32
BF16 = jnp.bfloat16
DEAD = -30000.0
CUBIC = 0.044715
ROOT = 0.7978845608028654
VMEM_LIMIT = 56 * 1024 * 1024


def dot(left, right):
    return jnp.dot(left, right, preferred_element_type=F32)


def dot_nt(left, right):
    return lax.dot_general(left, right, (((1,), (1,)), ((), ())), preferred_element_type=F32)


def gelu_pair(value):
    square = value * value
    gate = 0.5 + 0.5 * jnp.tanh(value * (ROOT + (ROOT * CUBIC) * square))
    out = value * gate
    slope = gate + (out - out * gate) * (2.0 * ROOT + (6.0 * ROOT * CUBIC) * square)
    return out, slope


def activation(value):
    return jax.nn.gelu(value, approximate=True)


def activation_grad(value, upstream):
    return jax.vjp(activation, value)[1](upstream)[0]


def norm_forward(value, gain, shift):
    centred = value - jnp.mean(value, axis=-1, keepdims=True)
    inverse = lax.rsqrt(jnp.mean(centred * centred, axis=-1, keepdims=True) + EPSILON)
    normed = centred * inverse
    return (normed * gain + shift, normed, inverse)


def norm_backward(upstream, normed, inverse, gain):
    scaled = upstream * gain
    inner = (
        scaled
        - jnp.mean(scaled, axis=-1, keepdims=True)
        - normed * jnp.mean(scaled * normed, axis=-1, keepdims=True)
    )
    return inverse * inner


def selector(slot_row, rows):
    positions = lax.broadcasted_iota(jnp.int32, (rows, slot_row.shape[1]), 0)
    return jnp.where(positions == slot_row, 1.0, 0.0).astype(BF16)


def dot_tn(left, right):
    return lax.dot_general(left, right, (((0,), (0,)), ((), ())), preferred_element_type=F32)


def pool_of(place_id, count, locals_, remotes, pool_ref):
    rows = locals_[0].shape[0]
    for spot in range(count):

        @pl.when(place_id == spot)
        def _(spot=spot):
            pool_ref[0:rows, :] = locals_[spot][...]
            pool_ref[rows:, :] = remotes[spot][...]


def masked_table(fixed, term, dead):
    positions = lax.broadcasted_iota(jnp.int32, term.shape, 1)
    term = jnp.where(positions == dead, DEAD, term).astype(BF16)
    return jnp.concatenate([fixed, term], axis=1)


def message_forward_body(perm_ref, *refs, count):
    edge_ref, slot_ref, node_ref, arrive_ref, fixed_ref, scale_ref = refs[:6]
    weights = refs[6 : 6 + count]
    refs = refs[6 + count :]
    slope_ref, mean_ref = refs[:2]
    parts = refs[2 : 2 + count]
    table_ref, self_ref, sum_ref = refs[2 + count :]
    number = pl.program_id(0)
    dead = perm_ref[count]
    steps, channels, lanes = edge_ref.shape[1:]
    width = node_ref.shape[2]
    part = weights[0].shape[0]
    nodes = node_ref[0]
    arrive = arrive_ref[...].reshape(-1, width)
    pool = lanes + arrive.shape[0]
    rows = jnp.concatenate([nodes, arrive], axis=0)
    for spot in range(count):
        span = slice(spot * part, (spot + 1) * part)
        weight = weights[spot]
        term = dot_nt(weight[:, width : 2 * width], rows)
        table_ref[span, :] = masked_table(fixed_ref[span, :], term, dead)
        bias = weight[:, 3 * width : 3 * width + 1].astype(F32)
        self_ref[span, :] = dot_nt(weight[:, 0:width], nodes) + bias
    sum_ref[...] = jnp.zeros_like(sum_ref)

    def one(step):
        picked = selector(slot_ref[0, pl.ds(step, 1), :], pool)
        operand = jnp.concatenate([edge_ref[0, step], picked], axis=0)
        value = dot(table_ref[...], operand) + self_ref[...]
        out, slope = gelu_pair(value)
        slope_ref[0, step] = slope.astype(BF16)
        sum_ref[...] += out.astype(BF16).astype(F32)

    unrolled(steps, one)
    mean = sum_ref[...] * scale_ref[0]
    upper = mean.astype(BF16)
    lower = (mean - upper.astype(F32)).astype(BF16)
    mean_ref[0] = upper
    total = None
    for spot in range(count):
        span = slice(spot * part, (spot + 1) * part)
        weight = weights[spot][:, 2 * width : 3 * width]
        term = dot_tn(upper[span], weight) + dot_tn(lower[span], weight)
        total = term if total is None else total + term
    for spot in range(count):

        @pl.when(number == spot)
        def _(spot=spot):
            parts[spot][...] = total.astype(BF16)


def unrolled(steps, one):
    group = group_of(steps)

    def some(index, carry):
        for step in range(group):
            one(index * group + step)
        return carry

    lax.fori_loop(0, steps // group, some, 0)


def forward_body(*refs, count):
    parts = refs[:count]
    node_ref, share_ref, vector_ref, send_ref = refs[count : count + 4]
    blocks = refs[count + 4 : 2 * count + 4]
    other_ref = refs[2 * count + 4]
    one_ref, two_ref, first_ref, second_ref, leave_ref = refs[2 * count + 5 :]
    total = parts[0][...].astype(F32)
    for spot in range(1, count):
        total = total + parts[spot][...].astype(F32)
    value = node_ref[0].astype(F32) + total + share_ref[:, 0:1] * vector_ref[0:1, :]
    one_ref[...] = value
    first_norm, _, _ = norm_forward(value, vector_ref[2:3, :], vector_ref[4:5, :])
    first_low = first_norm.astype(BF16)
    first_ref[...] = first_low
    value = first_norm + vector_ref[1:2, :]
    for spot in range(2 * count):
        block = blocks[spot] if spot < count else other_ref.at[spot - count]
        half = (block.shape[0] - 16) // 2
        pre = dot_nt(first_low, block[0:half, :]) + block[2 * half : 2 * half + 1, 0:half].astype(F32)
        value = value + dot(activation(pre).astype(BF16), block[half : 2 * half, :])
    two_ref[...] = value
    second_norm, _, _ = norm_forward(value, vector_ref[3:4, :], vector_ref[5:6, :])
    second = second_norm.astype(BF16)
    second_ref[...] = second
    leave_ref[...] = dot(send_ref[...], second).astype(BF16)


def update_body(perm_ref, *refs, count):
    edge_ref, slot_ref, up_ref = refs[:3]
    locals_ = refs[3 : 3 + count]
    remotes = refs[3 + count : 3 + 2 * count]
    turned_ref, column_ref, out_t_ref, out_ref, weight_ref = refs[3 + 2 * count : 8 + 2 * count]
    refs = refs[8 + 2 * count :]
    result_ref, part_ref, node_ref = refs[:3]
    sums = refs[3 : 3 + count]
    whole_ref = refs[3 + count]
    pool_ref, table_ref, self_ref, table_grad_ref, self_grad_ref = refs[4 + count : 9 + count]
    gain_grad_ref, shift_grad_ref, turned_grad_ref, out_grad_ref, bias_grad_ref = refs[
        9 + count : 14 + count
    ]
    gain_ref, shift_ref = refs[14 + count :]
    number = pl.program_id(0)
    dead = perm_ref[count]
    steps, channels, lanes = edge_ref.shape[1:]
    hidden = turned_ref.shape[0]
    pool, width = pool_ref.shape
    extra = out_t_ref.shape[1] - hidden

    @pl.when(number == 0)
    def _():
        turned_grad_ref[...] = jnp.zeros_like(turned_grad_ref)
        out_grad_ref[...] = jnp.zeros_like(out_grad_ref)
        bias_grad_ref[...] = jnp.zeros_like(bias_grad_ref)
        gain_grad_ref[...] = jnp.zeros_like(gain_grad_ref)
        shift_grad_ref[...] = jnp.zeros_like(shift_grad_ref)
        gain_ref[...] = jnp.broadcast_to(column_ref[:, 1:2], gain_ref.shape)
        shift_ref[...] = jnp.broadcast_to(column_ref[:, 2:3], shift_ref.shape)

    pool_of(number, count, locals_, remotes, pool_ref)
    node_ref[0] = pool_ref[0:lanes, :]
    term = dot_nt(turned_ref[:, width : 2 * width], pool_ref[...])
    table_ref[...] = masked_table(turned_ref[:, 2 * width :], term, dead)
    self_ref[...] = dot_nt(turned_ref[:, 0:width], pool_ref[0:lanes, :]) + column_ref[:, 0:1]
    table_grad_ref[...] = jnp.zeros_like(table_grad_ref)
    self_grad_ref[...] = jnp.zeros_like(self_grad_ref)

    def one(step):
        slot_row = slot_ref[0, pl.ds(step, 1), :]
        picked = selector(slot_row, pool)
        edge = edge_ref[0, step]
        operand = jnp.concatenate([edge, picked], axis=0)
        out, slope = gelu_pair(dot(table_ref[...], operand) + self_ref[...])
        first = lax.broadcasted_iota(jnp.int32, (extra, lanes), 0) == 0
        live = jnp.where(first & (slot_row != dead), 1.0, 0.0).astype(BF16)
        out = jnp.concatenate([out.astype(BF16), live], axis=0)
        value = edge.astype(F32) + dot(out_t_ref[...], out)
        centred = value - jnp.mean(value, axis=0, keepdims=True)
        inverse = lax.rsqrt(jnp.mean(centred * centred, axis=0, keepdims=True) + EPSILON)
        normed = centred * inverse
        gain = gain_ref[...]
        result_ref[0, step] = (normed * gain + shift_ref[...]).astype(BF16)
        upstream = up_ref[0, step].astype(F32)
        gain_grad_ref[...] += upstream * normed
        shift_grad_ref[...] += upstream
        scaled = upstream * gain
        mixed = inverse * (
            scaled
            - jnp.mean(scaled, axis=0, keepdims=True)
            - normed * jnp.mean(scaled * normed, axis=0, keepdims=True)
        )
        low = mixed.astype(BF16)
        out_grad_ref[...] += dot_nt(low, out)
        grad = slope * dot(out_ref[...], low)
        self_grad_ref[...] += grad
        grad = grad.astype(BF16)
        table_grad_ref[...] += dot_nt(grad, operand)
        part_ref[0, step] = (mixed + dot(weight_ref[...], grad)).astype(BF16)

    unrolled(steps, one)
    self_grad = self_grad_ref[...]
    pool_grad = table_grad_ref[:, channels:]
    self_low = self_grad.astype(BF16)
    pool_low = pool_grad.astype(BF16)
    for spot in range(count):

        @pl.when(number == spot)
        def _(spot=spot):
            sums[spot][:, 0:lanes] = self_low
            sums[spot][:, lanes:] = pool_low

    turned_grad_ref[:, 0:width] += dot(self_low, pool_ref[0:lanes, :])
    turned_grad_ref[:, width : 2 * width] += dot(pool_low, pool_ref[...])
    turned_grad_ref[:, 2 * width :] += table_grad_ref[:, 0:channels]
    bias_grad_ref[...] += self_grad

    @pl.when(number == count - 1)
    def _():
        flat = lambda ref: jnp.sum(ref[...], axis=1, keepdims=True)
        lane = lax.broadcasted_iota(jnp.int32, (channels, 128), 1)
        vectors = jnp.where(
            lane == 0,
            flat(bias_grad_ref),
            jnp.where(
                lane == 1,
                flat(gain_grad_ref),
                jnp.where(lane == 2, flat(shift_grad_ref), out_grad_ref[:, hidden : hidden + 1]),
            ),
        )
        end = turned_grad_ref.shape[1]
        whole_ref[...] = jnp.concatenate(
            [turned_grad_ref[...], out_grad_ref[:, 0:hidden], vectors], axis=1
        )


def return_body(*refs, count):
    sums = refs[:count]
    turned_ref, up_ref, second_ref, leave_ref = refs[count:]
    total = sums[0][...].astype(F32)
    for spot in range(1, count):
        total = total + sums[spot][...].astype(F32)
    low = total.astype(BF16)
    lanes, width = second_ref.shape
    back = dot_tn(low[:, lanes:], turned_ref[:, width : 2 * width])
    second_ref[...] = (
        up_ref[0].astype(F32) + dot_tn(low[:, 0:lanes], turned_ref[:, 0:width]) + back[0:lanes]
    )
    leave_ref[...] = back[lanes:].astype(BF16)


def backward_body(*refs, count):
    second_ref, return_ref, send_ref, one_ref, two_ref, share_ref, vector_ref = refs[:7]
    blocks = refs[7 : 7 + count]
    other_ref = refs[7 + count]
    aggregate_ref, forward_ref, sum_ref, grad_ref = refs[8 + count :]
    lanes = one_ref.shape[0]
    second_grad = second_ref[...] + dot_tn(send_ref[...], return_ref[...])
    first_norm, first_normed, first_inverse = norm_forward(
        one_ref[...], vector_ref[2:3, :], vector_ref[4:5, :]
    )
    _, second_normed, second_inverse = norm_forward(
        two_ref[...], vector_ref[3:4, :], vector_ref[5:6, :]
    )
    first_low = first_norm.astype(BF16)
    total = lambda value: jnp.sum(value, axis=0, keepdims=True)
    grad_ref[3:4, :] = total(second_grad * second_normed)
    grad_ref[5:6, :] = total(second_grad)
    sum_two = norm_backward(second_grad, second_normed, second_inverse, vector_ref[3:4, :])
    low = sum_two.astype(BF16)
    forward_ref[0:lanes, :] = low
    grad_ref[1:2, :] = total(low.astype(F32))
    first_grad = sum_two
    for spot in range(2 * count):
        block = blocks[spot] if spot < count else other_ref.at[spot - count]
        half = (block.shape[0] - 16) // 2
        pre = dot_nt(first_low, block[0:half, :]) + block[2 * half : 2 * half + 1, 0:half].astype(F32)
        slope = gelu_pair(pre)[1]
        grad = (slope * dot_nt(low, block[half : 2 * half, :])).astype(BF16)
        first_grad = first_grad + dot(grad, block[0:half, :])
    grad_ref[2:3, :] = total(first_grad * first_normed)
    grad_ref[4:5, :] = total(first_grad)
    sum_one = norm_backward(first_grad, first_normed, first_inverse, vector_ref[2:3, :])
    sum_ref[...] = sum_one
    aggregate = sum_one.astype(BF16)
    aggregate_ref[...] = aggregate
    grad_ref[0:1, :] = total(share_ref[:, 0:1] * aggregate.astype(F32))
    grad_ref[6:16, :] = jnp.zeros((10, grad_ref.shape[1]), F32)
    forward_ref[lanes:, :] = grad_ref[...].astype(BF16)


def message_backward_body(perm_ref, *refs, count):
    edge_ref, slot_ref, slope_ref, part_ref, node_ref, arrive_ref, weight_ref, scale_ref = refs[:8]
    mean_ref, whole_ref = refs[8:10]
    weights = refs[10 : 10 + count]
    ups = refs[10 + count : 10 + 2 * count]
    refs = refs[10 + 2 * count :]
    grad_ref = refs[0]
    backs = refs[1 : 1 + count]
    mine_ref, other_ref = refs[1 + count : 3 + count]
    up_ref, table_grad_ref, self_grad_ref, total_ref, edge_total_ref = refs[3 + count :]
    number = pl.program_id(0)
    steps, channels, lanes = edge_ref.shape[1:]
    width = node_ref.shape[2]
    part = weights[0].shape[0]
    nodes = node_ref[0]
    rows = jnp.concatenate([nodes, arrive_ref[...].reshape(-1, width)], axis=0)
    pool = rows.shape[0]
    start = 2 * width

    @pl.when(number == 0)
    def _():
        total_ref[...] = jnp.zeros_like(total_ref)
        edge_total_ref[...] = jnp.zeros_like(edge_total_ref)

    for own in range(count):

        @pl.when(number == own)
        def _(own=own):
            for spot in range(count):
                span = slice(spot * part, (spot + 1) * part)
                value = dot_nt(weights[spot][:, 2 * width : 3 * width], ups[own][...])
                up_ref[span, :] = (value * scale_ref[0]).astype(BF16)
            total_ref[:, start : start + width] += dot(mean_ref[0], ups[own][...])

    table_grad_ref[...] = jnp.zeros_like(table_grad_ref)
    self_grad_ref[...] = jnp.zeros_like(self_grad_ref)

    def one(step):
        picked = selector(slot_ref[0, pl.ds(step, 1), :], pool)
        operand = jnp.concatenate([edge_ref[0, step], picked], axis=0)
        grad = slope_ref[0, step] * up_ref[...]
        table_grad_ref[...] += dot_nt(grad, operand)
        self_grad_ref[...] += grad.astype(F32)
        edge = dot(weight_ref[...], grad)
        grad_ref[0, step] = (part_ref[0, step].astype(F32) + edge).astype(BF16)

    unrolled(steps, one)
    self_grad = self_grad_ref[...]
    self_low = self_grad.astype(BF16)
    pool_low = table_grad_ref[:, channels:].astype(BF16)
    self_back = None
    pool_back = None
    for spot in range(count):
        span = slice(spot * part, (spot + 1) * part)
        one_term = dot_tn(self_low[span], weights[spot][:, 0:width])
        two_term = dot_tn(pool_low[span], weights[spot][:, width : 2 * width])
        self_back = one_term if spot == 0 else self_back + one_term
        pool_back = two_term if spot == 0 else pool_back + two_term
    for spot in range(count):

        @pl.when(number == spot)
        def _(spot=spot):
            backs[spot][0:lanes, :] = (self_back + pool_back[0:lanes]).astype(BF16)
            backs[spot][lanes:, :] = pool_back[lanes:].astype(BF16)

    total_ref[:, 0:width] += dot(self_low, nodes)
    total_ref[:, width : 2 * width] += dot(pool_low, rows)
    edge_total_ref[...] += table_grad_ref[:, 0:channels]
    total_ref[:, 3 * width :] += jnp.broadcast_to(
        jnp.sum(self_grad, axis=1, keepdims=True), (total_ref.shape[0], 128)
    )

    @pl.when(number == count - 1)
    def _():
        core = perm_ref[count + 1]
        half = part // 2
        rows = whole_ref.shape[0] // count // 2
        for spot in range(count):
            for place, ref in ((core, mine_ref), (1 - core, other_ref)):
                first = pl.multiple_of(spot * part + place * half, half)
                ref[spot, 0:half, :] = total_ref[pl.ds(first, half), :].astype(ref.dtype)
                whole = pl.multiple_of(perm_ref[spot] * (2 * rows) + place * rows, 8)
                fold = jnp.concatenate(
                    [edge_total_ref[pl.ds(first + 8 * turn, 8), :] for turn in range(half // 8)],
                    axis=1,
                )
                both = jnp.concatenate([whole_ref[pl.ds(whole, rows), :], fold], axis=0)
                ref[spot, half:, 0 : fold.shape[1]] = both.astype(ref.dtype)
                ref[spot, half:, fold.shape[1] :] = jnp.zeros(
                    (both.shape[0], ref.shape[2] - fold.shape[1]), ref.dtype
                )


def wide_body(
    perm_ref, low_ref, forward_ref, weight_ref, bias_ref, output_ref, mine_ref, other_ref, all_ref, *, count
):
    width = low_ref.shape[1]
    wide = weight_ref.shape[1]
    step = forward_ref.shape[0] // count
    lanes = step - 16
    low = low_ref[...]
    forward = jnp.concatenate(
        [forward_ref[spot * step : spot * step + lanes, :] for spot in range(count)], axis=0
    )
    lines = None
    for spot in range(count):
        line = forward_ref[spot * step + lanes : (spot + 1) * step, :].astype(F32)
        lines = line if spot == 0 else lines + line
    pre = dot(low, weight_ref[...]) + bias_ref[0:1, :].astype(F32)
    out, slope = gelu_pair(pre)
    grad = slope * dot_nt(forward, output_ref[...])
    all_ref[0:width, :] = dot_tn(low, grad.astype(BF16))
    all_ref[width : width + wide, :] = dot_tn(out.astype(BF16), forward)
    at = width + wide
    total = jnp.broadcast_to(jnp.sum(grad, axis=0, keepdims=True), (8, wide))
    all_ref[at : at + 8, :] = total
    all_ref[at + 8 : at + 16, :] = lines[0:8]
    all_ref[at + 16 :, :] = jnp.zeros((all_ref.shape[0] - at - 16, width), F32)
    half = mine_ref.shape[0]
    core = perm_ref[count + 1]
    mine_ref[...] = all_ref[pl.ds(pl.multiple_of(core * half, 8), half), :]
    other_ref[...] = all_ref[pl.ds(pl.multiple_of((1 - core) * half, 8), half), :].astype(BF16)


def wide_finish_body(
    perm_ref, mine_ref, other_ref, in_ref, out_ref, bias_ref, one_ref, two_ref, three_ref, all_ref, *, count
):
    core = perm_ref[count + 1]
    half = mine_ref.shape[0]
    all_ref[pl.ds(pl.multiple_of(core * half, 8), half), :] = mine_ref[...].astype(F32)
    all_ref[pl.ds(pl.multiple_of((1 - core) * half, 8), half), :] = other_ref[...].astype(F32)
    width = in_ref.shape[0]
    wide = out_ref.shape[0]
    in_ref[...] = all_ref[0:width, :]
    out_ref[...] = all_ref[width : width + wide, :]
    at = width + wide
    bias_ref[...] = all_ref[at : at + 1, :]
    one_ref[...] = all_ref[at + 8 : at + 10, :]
    two_ref[...] = all_ref[at + 10 : at + 12, :]
    three_ref[...] = all_ref[at + 12 : at + 14, :]


def late_finish_body(
    perm_ref,
    mine_ref,
    other_ref,
    mine_parts_ref,
    other_parts_ref,
    nodes_ref,
    output_ref,
    bias_ref,
    turned_ref,
    update_ref,
    hidden_bias_ref,
    gain_ref,
    shift_ref,
    branch_ref,
    edge_ref,
    own_ref,
    whole_ref,
    edges_ref,
    *,
    count,
):
    core = perm_ref[count + 1]
    part = own_ref.shape[0]
    half = part // 2
    width = output_ref.shape[1]
    rows = whole_ref.shape[0] // count // 2
    channels = edges_ref.shape[1]
    for place, ref, parts in ((core, mine_ref, mine_parts_ref), (1 - core, other_ref, other_parts_ref)):
        own_ref[pl.ds(pl.multiple_of(place * half, 8), half), :] = ref[0:half, :].astype(F32)
        for spot in range(count):
            value = parts[spot].astype(F32)
            start = pl.multiple_of(perm_ref[spot] * (2 * rows) + place * rows, 8)
            whole_ref[pl.ds(start, rows), :] = value[0:rows, :]
            first = perm_ref[spot] * part + place * half
            for turn in range(half // 8):
                start = pl.multiple_of(first + 8 * turn, 8)
                edges_ref[pl.ds(start, 8), :] = value[rows:, turn * channels : (turn + 1) * channels]
    nodes_ref[0] = own_ref[:, 0:width].T
    nodes_ref[1] = own_ref[:, width : 2 * width].T
    output_ref[...] = own_ref[:, 2 * width : 3 * width]
    bias_ref[...] = own_ref[:, 3 * width : 3 * width + 128].T[0:1, :]
    end = turned_ref.shape[1]
    hidden = update_ref.shape[0]
    turned_ref[...] = whole_ref[:, 0:end]
    update_ref[...] = whole_ref[:, end : end + hidden].T
    vectors = whole_ref[:, end + hidden :].T
    hidden_bias_ref[...] = vectors[0:1, :]
    gain_ref[...] = vectors[1:2, :]
    shift_ref[...] = vectors[2:3, :]
    branch_ref[...] = vectors[3:4, :]
    edge_ref[...] = edges_ref[...].T


def place_body(perm_ref, *refs, count):
    for spot in range(count):

        @pl.when(pl.program_id(0) == spot)
        def _(spot=spot):
            refs[count][0] = refs[spot][...]


def group_of(total):
    for size in (5, 4, 3, 2, 1):
        if total % size == 0:
            return size


def call(body, grid, ins, outs, scratch, flops, moved, name, perm=None):
    whole = lambda block: (block, lambda *_: (0,) * len(block))
    in_specs = [
        pl.BlockSpec(*(entry[1:] if len(entry) == 3 else whole(entry[0].shape))) for entry in ins
    ]
    out_specs = [
        pl.BlockSpec(*(entry[2:] if len(entry) == 4 else whole(entry[0]))) for entry in outs
    ]
    spec = pltpu.PrefetchScalarGridSpec(
        num_scalar_prefetch=0 if perm is None else 1,
        grid=grid,
        in_specs=in_specs,
        out_specs=out_specs,
        scratch_shapes=scratch,
    )
    operands = [entry[0] for entry in ins]
    return pl.pallas_call(
        body,
        grid_spec=spec,
        out_shape=[jax.ShapeDtypeStruct(entry[0], entry[1]) for entry in outs],
        compiler_params=pltpu.CompilerParams(
            dimension_semantics=("arbitrary",) * len(grid), vmem_limit_bytes=VMEM_LIMIT
        ),
        cost_estimate=pl.CostEstimate(flops=flops, bytes_accessed=moved, transcendentals=0),
        name=name,
    )(*([] if perm is None else [perm]), *operands)


def build(prot_size, res_size, mp_size):
    def across(value, offset):
        pairs = [(spot, spot ^ offset) for spot in range(mp_size)]
        return lax.ppermute(value, "mp", pairs)

    def gather(value):
        return [value] + [across(value, offset) for offset in range(1, mp_size)]

    def scatter(parts):
        return [parts[0]] + [across(parts[offset], offset) for offset in range(1, mp_size)]

    def exchange(value):
        return lax.all_to_all(value, "res", split_axis=0, concat_axis=0, tiled=True)

    def block_parts(value):
        place = lax.axis_index("res")
        piece = value.shape[0] // res_size
        parts = [lax.dynamic_slice_in_dim(value, place * piece, piece, 0)]
        low = value.astype(BF16)
        for hop in range(1, res_size):
            target = lax.rem(place + hop, res_size)
            part = lax.dynamic_slice_in_dim(low, target * piece, piece, 0)
            pairs = [(spot, (spot + hop) % res_size) for spot in range(res_size)]
            parts.append(lax.ppermute(part, "res", pairs))
        return parts

    def block_gather(own):
        parts = [own]
        for hop in range(1, res_size):
            pairs = [(spot, (spot - hop) % res_size) for spot in range(res_size)]
            parts.append(lax.ppermute(own, "res", pairs))
        return parts

    def block_order(parts):
        place = lax.axis_index("res")
        piece = parts[0].shape[0]
        both = jnp.concatenate(parts + parts, axis=0)
        return lax.dynamic_slice_in_dim(both, (res_size - place) * piece, res_size * piece, 0)

    def swap(value):
        return lax.ppermute(value, "prot", [(0, 1), (1, 0)])

    def per_device(
        node_states,
        edge_states,
        neighbour_slots,
        send_rows,
        live_counts,
        message_nodes,
        message_edges,
        message_bias,
        message_output,
        feedforward_weight,
        feedforward_bias,
        feedforward_output,
        output_biases,
        norm_gains,
        norm_shifts,
        update_weight,
        update_bias,
        update_output,
        branch_bias,
        edge_gain,
        edge_shift,
        node_cotangent,
        edge_cotangent,
    ):
        proteins, lanes, width = node_states.shape
        own_k, channels = edge_states.shape[2:]
        slots = send_rows.shape[3]
        remote = res_size * slots
        pool = lanes + remote
        part = message_nodes.shape[2]
        hidden = part * mp_size
        update_hidden = update_output.shape[0]
        wide = feedforward_weight.shape[1]
        assert proteins == mp_size and prot_size == 2
        me = lax.axis_index("mp")
        core = lax.axis_index("prot")
        place = lax.axis_index("res")
        dead = lanes + place * slots
        order = [me ^ offset for offset in range(mp_size)]
        perm = jnp.stack(order + [dead, core]).astype(jnp.int32)

        def reorder(value, axis=0):
            size = value.shape[axis] // mp_size
            return jnp.concatenate(
                [lax.dynamic_slice_in_dim(value, spot * size, size, axis) for spot in order], axis=axis
            )

        send_table = (
            send_rows[:, 0].reshape(proteins, -1)[..., None]
            == lax.broadcasted_iota(jnp.int32, (1, 1, lanes), 2)
        ).astype(BF16)
        message_pack = jnp.concatenate(
            [
                message_nodes[0].T,
                message_nodes[1].T,
                message_output,
                jnp.broadcast_to(message_bias[:, None], (part, 128)),
            ],
            axis=1,
        )
        leaving = jnp.einsum("bsr,brd->bsd", send_table, node_states, preferred_element_type=F32)
        leaving = leaving.astype(BF16).reshape(proteins, res_size, slots, width)
        leaving = jnp.transpose(leaving, (1, 0, 2, 3))
        leaving, message_pack = lax.optimization_barrier((leaving, message_pack))
        arriving = exchange(leaving)
        weights = gather(message_pack)
        half = wide // 2
        bias_row = lax.dynamic_slice_in_dim(feedforward_bias, core * half, half, 0)
        block = jnp.concatenate(
            [
                lax.dynamic_slice_in_dim(feedforward_weight, core * half, half, 1).T,
                lax.dynamic_slice_in_dim(feedforward_output, core * half, half, 0),
                jnp.pad(bias_row[None], ((0, 15), (0, width - half))),
            ],
            axis=0,
        )

        own_slots = lax.dynamic_slice_in_dim(neighbour_slots, me * own_k, own_k, 2)
        alive = lax.broadcasted_iota(jnp.int32, own_slots.shape, 2) + me * own_k < live_counts[..., None]
        own_slots = jnp.transpose(jnp.where(alive, own_slots, dead), (0, 2, 1))
        counts = live_counts.astype(F32)
        scale = 1.0 / jnp.maximum(counts, 1.0)
        own_share = lax.dynamic_index_in_dim(counts * scale, me, 0, keepdims=False)
        share = jnp.broadcast_to(own_share[:, None], (lanes, 128))
        scale = scale[:, None, :]
        edges = jnp.transpose(edge_states, (0, 2, 3, 1))
        edge_up = jnp.transpose(edge_cotangent, (0, 2, 3, 1))
        own_table = lax.dynamic_index_in_dim(send_table, me, 0, keepdims=False)
        edge_weight = reorder(message_edges, 1)
        vectors = jnp.concatenate(
            [output_biases, norm_gains, norm_shifts, jnp.zeros_like(norm_shifts)], axis=0
        ).astype(F32)

        turned = update_weight.T
        lane = lax.broadcasted_iota(jnp.int32, (1, 128), 1)
        columns = jnp.where(
            lane == 0,
            update_bias.astype(F32)[:, None],
            jnp.where(
                lane == 1, edge_gain.astype(F32)[:, None], edge_shift.astype(F32)[:, None]
            ),
        )
        out_t = jnp.concatenate(
            [update_output.T, branch_bias[:, None], jnp.zeros((channels, 15), BF16)], axis=1
        )
        turned_edge = update_weight[2 * width :]
        edge_weight_t = edge_weight.T
        own_node = lax.dynamic_index_in_dim(node_states, me, 0)
        own_up = lax.dynamic_index_in_dim(node_cotangent, me, 0)
        wide_bias = jnp.broadcast_to(feedforward_bias[None], (16, wide))
        small = (
            own_slots,
            scale,
            share,
            vectors,
            own_table,
            columns,
            out_t,
            turned_edge,
            edge_weight,
            edge_weight_t,
            own_node,
            own_up,
            wide_bias,
        )
        weights, arriving, block, small = lax.optimization_barrier((weights, arriving, block, small))
        (
            own_slots,
            scale,
            share,
            vectors,
            own_table,
            columns,
            out_t,
            turned_edge,
            edge_weight,
            edge_weight_t,
            own_node,
            own_up,
            wide_bias,
        ) = small
        blocks = gather(block)

        depth = channels + pool
        count = proteins * own_k * lanes
        by_perm4 = lambda p, perm: (perm[p], 0, 0, 0)
        by_perm3 = lambda p, perm: (perm[p], 0, 0)
        by_step4 = lambda p, perm: (p, 0, 0, 0)
        by_step3 = lambda p, perm: (p, 0, 0)
        edge_block = (1, own_k, channels, lanes)
        edge_shape = (proteins, own_k, channels, lanes)
        slope_shape = (proteins, own_k, hidden, lanes)
        slope_block = (1, own_k, hidden, lanes)
        edge_in = (edges, edge_block, by_perm4)
        slot_in = (own_slots, (1, own_k, lanes), by_perm3)
        node_in = (node_states, (1, lanes, width), by_perm3)
        arrive_in = (
            arriving,
            (res_size, 1, slots, width),
            lambda p, perm: (0, perm[p], 0, 0),
        )
        scale_in = (scale, (1, 1, lanes), by_perm3)
        found = call(
            functools.partial(message_forward_body, count=proteins),
            (proteins,),
            [edge_in, slot_in, node_in, arrive_in, (edge_weight_t,), scale_in]
            + [(value,) for value in weights],
            [
                (slope_shape, BF16, slope_block, by_step4),
                ((proteins, hidden, lanes), BF16, (1, hidden, lanes), by_step3),
            ]
            + [((lanes, width), BF16)] * proteins,
            [
                pltpu.VMEM((hidden, depth), BF16),
                pltpu.VMEM((hidden, lanes), F32),
                pltpu.VMEM((hidden, lanes), F32),
            ],
            2 * count * depth * hidden,
            count * (channels + hidden) * 2,
            "message_forward",
            perm,
        )
        slope, mean_hidden = found[:2]
        parts = scatter(found[2:])
        blocks, _ = lax.optimization_barrier((blocks, found[2]))
        others = swap(jnp.stack(blocks))
        one, two, first_low, second_low, leaving = call(
            functools.partial(forward_body, count=proteins),
            (),
            [(value,) for value in parts]
            + [(own_node,), (share,), (vectors,), (own_table,)]
            + [(value,) for value in blocks]
            + [(others,)],
            [
                ((lanes, width), F32),
                ((lanes, width), F32),
                ((lanes, width), BF16),
                ((lanes, width), BF16),
                ((remote, width), BF16),
            ],
            [],
            4 * lanes * width * wide * mp_size,
            4 * width * wide * mp_size,
            "feed_forward",
        )

        arrived = exchange(leaving.reshape(res_size, slots, width)).reshape(remote, width)
        pool_locals = gather(second_low)
        pool_remotes = gather(arrived)
        all_low = lax.all_gather(first_low, "mp", axis=0, tiled=True)
        turned_width = 2 * width + channels
        found = call(
            functools.partial(update_body, count=proteins),
            (proteins,),
            [edge_in, slot_in, (edge_up, edge_block, by_perm4)]
            + [(value,) for value in pool_locals + pool_remotes]
            + [
                (turned,),
                (columns,),
                (out_t,),
                (update_output,),
                (turned_edge,),
            ],
            [
                (edge_shape, BF16, edge_block, by_perm4),
                (edge_shape, BF16, edge_block, by_perm4),
                ((proteins, lanes, width), BF16, (1, lanes, width), by_perm3),
            ]
            + [((update_hidden, lanes + pool), BF16)] * proteins
            + [((update_hidden, turned_width + update_hidden + 128), F32)],
            [
                pltpu.VMEM((pool, width), BF16),
                pltpu.VMEM((update_hidden, depth), BF16),
                pltpu.VMEM((update_hidden, lanes), F32),
                pltpu.VMEM((update_hidden, depth), F32),
                pltpu.VMEM((update_hidden, lanes), F32),
                pltpu.VMEM((channels, lanes), F32),
                pltpu.VMEM((channels, lanes), F32),
                pltpu.VMEM((update_hidden, turned_width), F32),
                pltpu.VMEM((channels, update_hidden + 16), F32),
                pltpu.VMEM((update_hidden, lanes), F32),
                pltpu.VMEM((channels, lanes), F32),
                pltpu.VMEM((channels, lanes), F32),
            ],
            2 * count * (2 * depth + 4 * channels) * update_hidden,
            count * channels * 8,
            "edge_update",
            perm,
        )
        edge_result, edge_part, node_result = found[:3]
        own_sums, all_low = lax.optimization_barrier((found[3 : 3 + proteins], all_low))
        sums = scatter(own_sums)
        whole = found[3 + proteins]
        second_part, leaving = call(
            functools.partial(return_body, count=proteins),
            (),
            [(value,) for value in sums] + [(turned,), (own_up,)],
            [((lanes, width), F32), ((remote, width), BF16)],
            [],
            2 * (lanes + pool) * width * update_hidden,
            (lanes + pool) * width * 2,
            "update_return",
        )
        returned = exchange(leaving.reshape(res_size, slots, width)).reshape(remote, width)
        aggregate_grad, forward_grad, sum_one, _ = call(
            functools.partial(backward_body, count=proteins),
            (),
            [(second_part,), (returned,), (own_table,), (one,), (two,), (share,), (vectors,)]
            + [(value,) for value in blocks]
            + [(others,)],
            [
                ((lanes, width), BF16),
                ((lanes + 16, width), BF16),
                ((lanes, width), F32),
                ((16, width), F32),
            ],
            [],
            6 * lanes * width * wide * mp_size,
            4 * width * wide * mp_size,
            "feed_backward",
        )
        ups = gather(aggregate_grad)
        all_forward = lax.all_gather(forward_grad, "mp", axis=0, tiled=True)
        total_width = 3 * width + 128
        late_shape = (proteins, part // 2 + update_hidden // mp_size // 2 + 8, total_width)
        found = call(
            functools.partial(message_backward_body, count=proteins),
            (proteins,),
            [
                edge_in,
                slot_in,
                (slope, slope_block, by_step4),
                (edge_part, edge_block, by_perm4),
                node_in,
                arrive_in,
                (edge_weight,),
                scale_in,
                (mean_hidden, (1, hidden, lanes), by_step3),
                (whole,),
            ]
            + [(value,) for value in weights + ups],
            [(edge_shape, BF16, edge_block, by_perm4)]
            + [((pool, width), BF16)] * proteins
            + [(late_shape, F32), (late_shape, BF16)],
            [
                pltpu.VMEM((hidden, lanes), BF16),
                pltpu.VMEM((hidden, depth), F32),
                pltpu.VMEM((hidden, lanes), F32),
                pltpu.VMEM((hidden, total_width), F32),
                pltpu.VMEM((hidden, channels), F32),
            ],
            2 * count * (depth + channels) * hidden,
            count * (3 * channels + hidden) * 2,
            "message_backward",
            perm,
        )
        edge_grad = found[0]
        backs, late_mine, late_other, all_forward = lax.optimization_barrier(
            (found[1 : 1 + proteins], *found[1 + proteins :], all_forward)
        )
        late_swapped = swap(late_other)
        back = scatter(backs)
        unit = prot_size * res_size * 8
        wide_rows = -(-(width + wide + 16) // unit) * unit
        early_mine, early_other = call(
            functools.partial(wide_body, count=proteins),
            (1,),
            [
                (all_low,),
                (all_forward,),
                (feedforward_weight,),
                (wide_bias,),
                (feedforward_output,),
            ],
            [((wide_rows // 2, width), F32), ((wide_rows // 2, width), BF16)],
            [pltpu.VMEM((wide_rows, width), F32)],
            10 * proteins * lanes * width * wide,
            8 * proteins * lanes * width,
            "feed_weights",
            perm,
        )
        late_swapped, early_mine, early_other = lax.optimization_barrier(
            (late_swapped, early_mine, early_other)
        )
        early_swapped = swap(early_other)
        late = late_mine + late_swapped.astype(F32)
        late_own = late[0]
        late_low = [late[offset].astype(BF16) for offset in range(1, mp_size)]
        late_own, late_low, back = lax.optimization_barrier((late_own, late_low, back))
        late_parts = scatter([late_own] + late_low)
        total = sum(value.astype(F32) for value in back)
        leaving = total[lanes:].astype(BF16).reshape(res_size, slots, width)
        leaving, early_swapped = lax.optimization_barrier((leaving, early_swapped))
        returned = exchange(leaving)
        early = early_mine + early_swapped.astype(F32)
        early, returned = lax.optimization_barrier((early, returned))
        early_parts = block_parts(early)
        node_grad = (
            sum_one
            + total[:lanes]
            + jnp.einsum(
                "sr,sd->rd", own_table, returned.reshape(remote, width), preferred_element_type=F32
            )
        ).astype(BF16)
        node_grad, early_parts, late_parts = lax.optimization_barrier((node_grad, early_parts, late_parts))
        node_parts = gather(node_grad)
        late = sum(value.astype(F32) for value in late_parts)
        early = sum(value.astype(F32) for value in early_parts).astype(BF16)
        late, early = lax.optimization_barrier((late, early))
        late_parts = block_parts(late)
        early_parts = block_gather(early)
        late_parts, early_parts, node_parts = lax.optimization_barrier((late_parts, early_parts, node_parts))
        late_parts = block_gather(sum(value.astype(F32) for value in late_parts).astype(BF16))
        early = block_order(early_parts)
        early_swapped = swap(early)
        (node_grad,) = call(
            functools.partial(place_body, count=proteins),
            (proteins,),
            [(value,) for value in node_parts],
            [((proteins, lanes, width), BF16, (1, lanes, width), by_perm3)],
            [],
            0,
            4 * proteins * lanes * width,
            "place_rows",
            perm,
        )
        node_grad, late_parts, early_swapped = lax.optimization_barrier(
            (node_grad, late_parts, early_swapped)
        )
        late = block_order(late_parts)
        shared_parts = gather(late[part // 2 :, : turned_width + update_hidden + 128])
        late_swapped = swap(late)
        weight_in_grad, weight_out_grad, wide_bias_grad, biases_grad, gains_grad, shifts_grad = call(
            functools.partial(wide_finish_body, count=proteins),
            (1,),
            [(early,), (early_swapped,)],
            [
                ((width, wide), F32),
                ((wide, width), F32),
                ((1, wide), F32),
                ((2, width), F32),
                ((2, width), F32),
                ((2, width), F32),
            ],
            [pltpu.VMEM((wide_rows, width), F32)],
            0,
            8 * wide_rows * width,
            "feed_weights_out",
            perm,
        )
        weight_in_grad, shared_parts, late_swapped = lax.optimization_barrier(
            (weight_in_grad, shared_parts, late_swapped)
        )
        shared = jnp.stack(shared_parts)
        found = call(
            functools.partial(late_finish_body, count=proteins),
            (1,),
            [(late,), (late_swapped,), (shared,), (swap(shared),)],
            [
                ((2, width, part), F32),
                ((part, width), F32),
                ((1, part), F32),
                ((update_hidden, turned_width), F32),
                ((update_hidden, channels), F32),
                ((1, update_hidden), F32),
                ((1, channels), F32),
                ((1, channels), F32),
                ((1, channels), F32),
                ((channels, hidden), F32),
            ],
            [
                pltpu.VMEM((part, total_width), F32),
                pltpu.VMEM((update_hidden, turned_width + update_hidden + 128), F32),
                pltpu.VMEM((hidden, channels), F32),
            ],
            0,
            8 * hidden * total_width,
            "message_weights_out",
            perm,
        )
        turn = lambda value: jnp.transpose(value, (0, 3, 1, 2))
        return (
            node_result,
            turn(edge_result),
            node_grad,
            turn(edge_grad),
            found[0],
            found[9],
            found[2].reshape(part),
            found[1],
            weight_in_grad,
            wide_bias_grad.reshape(wide),
            weight_out_grad,
            biases_grad,
            gains_grad,
            shifts_grad,
            found[3].T,
            found[5].reshape(update_hidden),
            found[4],
            found[8].reshape(channels),
            found[6].reshape(channels),
            found[7].reshape(channels),
        )

    return per_device


def solution(mesh):
    return jax.shard_map(
        build(mesh.shape["prot"], mesh.shape["res"], mesh.shape["mp"]),
        mesh=mesh,
        in_specs=(
            P("prot", "res", None),
            P("prot", "res", "mp", None),
            P("prot", "res", None),
            P("prot", "res", None, None),
            P("prot", "res"),
            P(None, None, "mp"),
            P(),
            P("mp"),
            P("mp", None),
            P(None, "mp"),
            P("mp"),
            P("mp", None),
            P(),
            P(),
            P(),
            P(),
            P(),
            P(),
            P(),
            P(),
            P(),
            P("prot", "res", None),
            P("prot", "res", "mp", None),
        ),
        out_specs=(
            P("prot", "res", None),
            P("prot", "res", "mp", None),
            P("prot", "res", None),
            P("prot", "res", "mp", None),
            P(None, None, "mp"),
            P(),
            P("mp"),
            P("mp", None),
            P(None, "mp"),
            P("mp"),
            P("mp", None),
            P(),
            P(),
            P(),
            P(),
            P(),
            P(),
            P(),
            P(),
            P(),
        ),
        check_vma=False,
    )
```

```python
import functools

import jax
import jax.numpy as jnp
from jax import lax
from jax.experimental import pallas as pl
from jax.experimental.pallas import tpu as pltpu
from jax.sharding import PartitionSpec as P

EPSILON = 1e-05
F32 = jnp.float32
BF16 = jnp.bfloat16
DEAD = -30000.0
CUBIC = 0.044715
ROOT = 0.7978845608028654


def dot(left, right):
    return jnp.dot(left, right, preferred_element_type=F32)


def dot_nt(left, right):
    return lax.dot_general(left, right, (((1,), (1,)), ((), ())), preferred_element_type=F32)


def gelu_pair(value):
    square = value * value
    gate = 0.5 + 0.5 * jnp.tanh(value * (ROOT + (ROOT * CUBIC) * square))
    out = value * gate
    slope = gate + (out - out * gate) * (2.0 * ROOT + (6.0 * ROOT * CUBIC) * square)
    return out, slope


def low(value):
    return jnp.asarray(value, BF16)


def gelu_pair_low(value):
    value = value.astype(BF16)
    square = value * value
    inner = value * (low(-2.0 * ROOT) + low(-2.0 * ROOT * CUBIC) * square)
    power = jnp.exp(jnp.minimum(inner, low(80.0)))
    gate = pl.reciprocal(low(1.0) + power, approx=True)
    out = value * gate
    slope = gate + (out * (power * gate)) * (low(2.0 * ROOT) + low(6.0 * ROOT * CUBIC) * square)
    return out, slope


def activation(value):
    return jax.nn.gelu(value, approximate=True)


def activation_grad(value, upstream):
    return jax.vjp(activation, value)[1](upstream)[0]


def norm_forward(value, gain, shift):
    centred = value - jnp.mean(value, axis=-1, keepdims=True)
    inverse = lax.rsqrt(jnp.mean(centred * centred, axis=-1, keepdims=True) + EPSILON)
    normed = centred * inverse
    return (normed * gain + shift, normed, inverse)


def norm_backward(upstream, normed, inverse, gain):
    scaled = upstream * gain
    inner = (
        scaled
        - jnp.mean(scaled, axis=-1, keepdims=True)
        - normed * jnp.mean(scaled * normed, axis=-1, keepdims=True)
    )
    return inverse * inner


def selector(slot_row, rows):
    positions = lax.broadcasted_iota(jnp.int32, (rows, slot_row.shape[1]), 0)
    return jnp.where(positions == slot_row, 1.0, 0.0).astype(BF16)


def dot_tn(left, right):
    return lax.dot_general(left, right, (((0,), (0,)), ((), ())), preferred_element_type=F32)


def masked_table(fixed, term, dead):
    positions = lax.broadcasted_iota(jnp.int32, term.shape, 1)
    term = jnp.where(positions == dead, DEAD, term).astype(BF16)
    return jnp.concatenate([fixed, term], axis=1)


def message_forward_body(perm_ref, *refs, count, calls):
    edge_ref, slot_ref, node_ref, arrive_ref, fixed_ref, scale_ref = refs[:6]
    weights = refs[6 : 6 + count]
    refs = refs[6 + count :]
    slope_ref, mean_ref = refs[:2]
    parts = refs[2 : 2 + calls]
    weight_ref, table_ref, self_ref, sum_ref, operand_ref, value_ref = refs[2 + calls :]
    number = pl.program_id(0)
    group = operand_ref.shape[0]
    dead = perm_ref[count]
    steps, channels, lanes = edge_ref.shape[1:]
    width = node_ref.shape[2]
    part = weights[0].shape[0]

    @pl.when(number == 0)
    def _():
        for spot in range(count):
            weight_ref[spot * part : (spot + 1) * part, :] = weights[spot][...]

    nodes = node_ref[0]
    arrive = arrive_ref[...].reshape(-1, width)
    pool = lanes + arrive.shape[0]
    rows = jnp.concatenate([nodes, arrive], axis=0)
    term = dot_nt(weight_ref[:, width : 2 * width], rows)
    table_ref[...] = masked_table(fixed_ref[...], term, dead)
    bias = weight_ref[:, 3 * width : 3 * width + 1].astype(F32)
    self_ref[...] = dot_nt(weight_ref[:, 0:width], nodes) + bias
    sum_ref[...] = jnp.zeros_like(sum_ref)

    def some(index, carry):
        spots = [index * group + spot for spot in range(group)]
        for spot in range(group):
            operand_ref[spot, 0:channels] = edge_ref[0, spots[spot]]
            operand_ref[spot, channels:] = selector(slot_ref[0, pl.ds(spots[spot], 1), :], pool)
        for spot in range(group):
            value_ref[spot] = dot(table_ref[...], operand_ref[spot])
        total = sum_ref[...]
        for spot in range(group):
            out, slope = gelu_pair_low(value_ref[spot] + self_ref[...])
            slope_ref[0, spots[spot]] = slope
            total = total + out.astype(F32)
        sum_ref[...] = total
        return carry

    lax.fori_loop(0, steps // group, some, 0)
    mean = (sum_ref[...] * scale_ref[0]).astype(BF16)
    mean_ref[0] = mean
    total = dot_tn(mean, weight_ref[:, 2 * width : 3 * width]).astype(BF16)
    for spot in range(calls):

        @pl.when(number == spot)
        def _(spot=spot):
            parts[spot][...] = total


def forward_body(*refs, count):
    parts = refs[:count]
    node_ref, share_ref, vector_ref, send_ref, turned_ref = refs[count : count + 5]
    blocks = refs[count + 5 : 2 * count + 5]
    other_ref = refs[2 * count + 5]
    one_ref, two_ref, first_ref, second_ref, leave_ref, term_ref = refs[2 * count + 6 :]
    total = parts[0][...].astype(F32)
    for spot in range(1, count):
        total = total + parts[spot][...].astype(F32)
    value = node_ref[0].astype(F32) + total + share_ref[:, 0:1] * vector_ref[0:1, :]
    one_ref[...] = value
    first_norm, _, _ = norm_forward(value, vector_ref[2:3, :], vector_ref[4:5, :])
    first_low = first_norm.astype(BF16)
    first_ref[...] = first_low
    value = first_norm + vector_ref[1:2, :]
    for spot in range(2 * count):
        block = blocks[spot] if spot < count else other_ref.at[spot - count]
        half = (block.shape[0] - 16) // 2
        pre = dot_nt(first_low, block[0:half, :]) + block[2 * half : 2 * half + 1, 0:half].astype(F32)
        value = value + dot(activation(pre).astype(BF16), block[half : 2 * half, :])
    two_ref[...] = value
    second_norm, _, _ = norm_forward(value, vector_ref[3:4, :], vector_ref[5:6, :])
    second = second_norm.astype(BF16)
    second_ref[...] = second
    leave_ref[...] = dot(send_ref[...], second).astype(BF16)
    lanes, width = second.shape
    term_ref[:, 0:lanes] = dot_nt(turned_ref[:, 0:width], second).astype(BF16)
    term_ref[:, lanes:] = dot_nt(turned_ref[:, width : 2 * width], second).astype(BF16)


def update_body(perm_ref, *refs, count, calls, first_call):
    edge_ref, slot_ref, up_ref = refs[:3]
    terms = refs[3 : 3 + calls]
    remotes = refs[3 + calls : 3 + 2 * calls]
    turned_ref, column_ref, out_t_ref, out_ref, weight_ref = refs[3 + 2 * calls : 8 + 2 * calls]
    refs = refs[8 + 2 * calls :]
    if not first_call:
        start_ref = refs[0]
        refs = refs[2:]
    result_ref, part_ref = refs[:2]
    sums = refs[2 : 2 + calls]
    total_ref = refs[2 + calls]
    table_ref, self_ref, table_grad_ref, self_grad_ref = refs[3 + calls : 7 + calls]
    gain_grad_ref, shift_grad_ref, edge_grad_ref, out_grad_ref = refs[7 + calls : 11 + calls]
    gain_ref, shift_ref, operand_ref, out_low_ref, mixed_ref, grad_ref, product_ref, value_ref, slope_ref = refs[
        11 + calls :
    ]
    group = operand_ref.shape[1] // edge_ref.shape[3]
    number = pl.program_id(0)
    dead = perm_ref[count]
    steps, channels, lanes = edge_ref.shape[1:]
    hidden = turned_ref.shape[0]
    width = remotes[0].shape[1]
    pool = lanes + remotes[0].shape[0]
    extra = out_t_ref.shape[1] - hidden
    grads = (edge_grad_ref, out_grad_ref, gain_grad_ref, shift_grad_ref)
    bases = (0, 256, 512, 640)

    @pl.when(number == 0)
    def _():
        for ref, base in zip(grads, bases):
            if first_call:
                ref[...] = jnp.zeros_like(ref)
            else:
                ref[...] = start_ref[:, base : base + ref.shape[1]]
        gain_ref[...] = jnp.broadcast_to(column_ref[:, 1:2], gain_ref.shape)
        shift_ref[...] = jnp.broadcast_to(column_ref[:, 2:3], shift_ref.shape)

    for spot in range(calls):

        @pl.when(number == spot)
        def _(spot=spot):
            remote = dot_nt(turned_ref[:, width : 2 * width], remotes[spot][...])
            term = jnp.concatenate([terms[spot][:, lanes:].astype(F32), remote], axis=1)
            table_ref[...] = masked_table(turned_ref[:, 2 * width :], term, dead)
            self_ref[...] = terms[spot][:, 0:lanes].astype(F32) + column_ref[:, 0:1]

    table_grad_ref[...] = jnp.zeros_like(table_grad_ref)
    self_grad_ref[...] = jnp.zeros_like(self_grad_ref)
    share = 1.0 / channels
    first = lax.broadcasted_iota(jnp.int32, (extra, lanes), 0) == 0
    spans = [slice(spot * lanes, (spot + 1) * lanes) for spot in range(group)]
    total = lambda value: jnp.sum(value, axis=0, keepdims=True)

    def some(index, carry):
        spots = [index * group + spot for spot in range(group)]
        for spot, span in zip(spots, spans):
            slot_row = slot_ref[0, pl.ds(spot, 1), :]
            operand_ref[0:channels, span] = edge_ref[0, spot]
            operand_ref[channels:, span] = selector(slot_row, pool)
            live = jnp.where(first & (slot_row != dead), 1.0, 0.0)
            out_low_ref[hidden:, span] = live.astype(BF16)
        for span in spans:
            value_ref[:, span] = dot(table_ref[...], operand_ref[:, span])
        for span in spans:
            out, slope = gelu_pair_low(value_ref[:, span] + self_ref[...])
            out_low_ref[0:hidden, span] = out
            slope_ref[:, span] = slope
        for span in spans:
            value_ref[:, span] = dot(out_t_ref[...], out_low_ref[:, span])
        for spot, span in zip(spots, spans):
            value = edge_ref[0, spot].astype(F32) + value_ref[:, span]
            centred = value - total(value) * share
            inverse = lax.rsqrt(total(centred * centred) * share + EPSILON)
            normed = centred * inverse
            gain = gain_ref[...]
            result_ref[0, spot] = (normed * gain + shift_ref[...]).astype(BF16)
            scaled = up_ref[0, spot].astype(F32) * gain
            product = scaled * normed
            product_ref[:, span] = product.astype(BF16)
            mixed = inverse * (scaled - total(scaled) * share - normed * (total(product) * share))
            mixed_ref[:, span] = mixed.astype(BF16)
        for span in spans:
            value_ref[:, span] = dot(out_ref[...], mixed_ref[:, span])
        for span in spans:
            grad = slope_ref[:, span].astype(F32) * value_ref[:, span]
            self_grad_ref[...] += grad
            grad_ref[:, span] = grad.astype(BF16)
        out_grad_ref[...] += dot_nt(mixed_ref[...], out_low_ref[...])
        for spot, span in zip(spots, spans):
            edge = dot(weight_ref[...], grad_ref[:, span])
            part_ref[0, spot] = (mixed_ref[:, span].astype(F32) + edge).astype(BF16)
        table_grad_ref[...] += dot_nt(grad_ref[...], operand_ref[...])
        gain_grad_ref[...] += dot_nt(product_ref[...], jnp.ones((8, group * lanes), BF16))
        for spot in spots:
            shift_grad_ref[...] += dot_nt(up_ref[0, spot], jnp.ones((8, lanes), BF16))
        return carry

    lax.fori_loop(0, steps // group, some, 0)
    edge_grad_ref[...] += table_grad_ref[:, 0:channels]
    for spot in range(calls):

        @pl.when(number == spot)
        def _(spot=spot):
            sums[spot][:, 0:lanes] = self_grad_ref[...].astype(BF16)
            sums[spot][:, lanes:] = table_grad_ref[:, channels:].astype(BF16)

    @pl.when(number == calls - 1)
    def _():
        for ref, base in zip(grads, bases):
            total_ref[:, base : base + ref.shape[1]] = ref[...]


def return_body(*refs, count):
    sums = refs[:count]
    turned_ref, up_ref, low_ref, arrive_ref, grad_ref, column_ref = refs[count : count + 6]
    second_ref, leave_ref, whole_ref = refs[count + 6 :]
    total = sums[0][...].astype(F32)
    for spot in range(1, count):
        total = total + sums[spot][...].astype(F32)
    low = total.astype(BF16)
    lanes, width = second_ref.shape
    back = dot_tn(low[:, lanes:], turned_ref[:, width : 2 * width])
    leave_ref[...] = back[lanes:].astype(BF16)
    second_ref[...] = (
        up_ref[0].astype(F32) + dot_tn(low[:, 0:lanes], turned_ref[:, 0:width]) + back[0:lanes]
    )
    channels = grad_ref.shape[0]
    hidden = low.shape[0]
    rows = jnp.concatenate([low_ref[...], arrive_ref[...]], axis=0)
    lane = lax.broadcasted_iota(jnp.int32, (channels, 128), 1)
    vectors = jnp.where(
        lane == 0,
        jnp.sum(total[:, 0:lanes], axis=1, keepdims=True),
        jnp.where(
            lane == 1,
            grad_ref[:, 512:513] / column_ref[:, 1:2],
            jnp.where(lane == 2, grad_ref[:, 640:641], grad_ref[:, 256 + hidden : 257 + hidden]),
        ),
    )
    whole_ref[...] = jnp.concatenate(
        [
            dot(low[:, 0:lanes], low_ref[...]),
            dot(low[:, lanes:], rows),
            grad_ref[:, 0:channels],
            grad_ref[:, 256 : 256 + hidden],
            vectors,
        ],
        axis=1,
    )


def backward_body(*refs, count):
    second_ref, return_ref, send_ref, one_ref, two_ref, share_ref, vector_ref = refs[:7]
    blocks = refs[7 : 7 + count]
    other_ref = refs[7 + count]
    aggregate_ref, forward_ref, sum_ref, grad_ref = refs[8 + count :]
    lanes = one_ref.shape[0]
    second_grad = second_ref[...] + dot_tn(send_ref[...], return_ref[...])
    first_norm, first_normed, first_inverse = norm_forward(
        one_ref[...], vector_ref[2:3, :], vector_ref[4:5, :]
    )
    _, second_normed, second_inverse = norm_forward(
        two_ref[...], vector_ref[3:4, :], vector_ref[5:6, :]
    )
    first_low = first_norm.astype(BF16)
    total = lambda value: jnp.sum(value, axis=0, keepdims=True)
    grad_ref[3:4, :] = total(second_grad * second_normed)
    grad_ref[5:6, :] = total(second_grad)
    sum_two = norm_backward(second_grad, second_normed, second_inverse, vector_ref[3:4, :])
    low = sum_two.astype(BF16)
    forward_ref[0:lanes, :] = low
    grad_ref[1:2, :] = total(low.astype(F32))
    first_grad = sum_two
    for spot in range(2 * count):
        block = blocks[spot] if spot < count else other_ref.at[spot - count]
        half = (block.shape[0] - 16) // 2
        pre = dot_nt(first_low, block[0:half, :]) + block[2 * half : 2 * half + 1, 0:half].astype(F32)
        slope = gelu_pair(pre)[1]
        grad = (slope * dot_nt(low, block[half : 2 * half, :])).astype(BF16)
        first_grad = first_grad + dot(grad, block[0:half, :])
    grad_ref[2:3, :] = total(first_grad * first_normed)
    grad_ref[4:5, :] = total(first_grad)
    sum_one = norm_backward(first_grad, first_normed, first_inverse, vector_ref[2:3, :])
    sum_ref[...] = sum_one
    aggregate = sum_one.astype(BF16)
    aggregate_ref[...] = aggregate
    grad_ref[0:1, :] = total(share_ref[:, 0:1] * aggregate.astype(F32))
    grad_ref[6:16, :] = jnp.zeros((10, grad_ref.shape[1]), F32)
    forward_ref[lanes:, :] = grad_ref[...].astype(BF16)


def message_backward_body(perm_ref, *refs, count, calls, first_call):
    edge_ref, slot_ref, slope_ref, part_ref, edge_weight_ref, scale_ref = refs[:6]
    weights = refs[6 : 6 + count]
    ups = refs[6 + count : 6 + count + calls]
    refs = refs[6 + count + calls :]
    if not first_call:
        node_ref, arrive_ref, own_node_ref, own_arrive_ref, mean_ref, own_mean_ref = refs[:6]
        own_up_ref, own_low_ref, own_edge_ref, whole_ref = refs[6:10]
        refs = refs[11:]
    grad_ref = refs[0]
    backs = refs[1 : 1 + calls]
    low_out_ref, edge_out_ref = refs[1 + calls : 3 + calls]
    weight_ref, up_ref, table_grad_ref, self_grad_ref = refs[3 + calls : 7 + calls]
    operand_ref, grad_low_ref = refs[7 + calls : 9 + calls]
    if not first_call:
        mine_ref, other_ref = low_out_ref, edge_out_ref
        low_ref, row_ref, mean_all_ref, up_all_ref = refs[9 + calls : 13 + calls]
        edge_total_ref, bias_ref, total_ref, out_total_ref = refs[13 + calls :]
    group = operand_ref.shape[1] // edge_ref.shape[3]
    number = pl.program_id(0)
    steps, channels, lanes = edge_ref.shape[1:]
    part = weights[0].shape[0]
    hidden = part * count
    width = backs[0].shape[1]
    pool = backs[0].shape[0]

    @pl.when(number == 0)
    def _():
        for spot in range(count):
            weight_ref[spot * part : (spot + 1) * part, :] = weights[spot][...]
        if not first_call:
            low_ref[:, 0:pool] = own_low_ref[...]
            row_ref[0:lanes, :] = own_node_ref[0]
            row_ref[lanes:pool, :] = own_arrive_ref[...].reshape(-1, width)
            mean_all_ref[:, 0:lanes] = own_mean_ref[0]
            up_all_ref[0:lanes, :] = own_up_ref[...]
            edge_total_ref[...] = own_edge_ref[...]

    for spot in range(calls):

        @pl.when(number == spot)
        def _(spot=spot):
            value = dot_nt(weight_ref[:, 2 * width : 3 * width], ups[spot][...])
            up_ref[...] = (value * scale_ref[0]).astype(BF16)
            if not first_call:
                at = (spot + 1) * pool
                row_ref[at : at + lanes, :] = node_ref[0]
                row_ref[at + lanes : at + pool, :] = arrive_ref[...].reshape(-1, width)
                at = (spot + 1) * lanes
                mean_all_ref[:, at : at + lanes] = mean_ref[0]
                up_all_ref[at : at + lanes, :] = ups[spot][...]

    table_grad_ref[...] = jnp.zeros_like(table_grad_ref)
    self_grad_ref[...] = jnp.zeros_like(self_grad_ref)
    spans = [slice(spot * lanes, (spot + 1) * lanes) for spot in range(group)]

    def some(index, carry):
        spots = [index * group + spot for spot in range(group)]
        for spot, span in zip(spots, spans):
            operand_ref[0:channels, span] = edge_ref[0, spot]
            operand_ref[channels:, span] = selector(slot_ref[0, pl.ds(spot, 1), :], pool)
        total = self_grad_ref[...]
        for spot, span in zip(spots, spans):
            grad = slope_ref[0, spot] * up_ref[...]
            grad_low_ref[:, span] = grad
            total = total + grad.astype(F32)
        self_grad_ref[...] = total
        for spot, span in zip(spots, spans):
            edge = dot(edge_weight_ref[...], grad_low_ref[:, span])
            grad_ref[0, spot] = (part_ref[0, spot].astype(F32) + edge).astype(BF16)
        table_grad_ref[...] += dot_nt(grad_low_ref[...], operand_ref[...])
        return carry

    lax.fori_loop(0, steps // group, some, 0)
    self_low = self_grad_ref[...].astype(BF16)
    pool_low = table_grad_ref[:, channels:].astype(BF16)
    self_back = dot_tn(self_low, weight_ref[:, 0:width])
    pool_back = dot_tn(pool_low, weight_ref[:, width : 2 * width])
    low_both = jnp.concatenate(
        [
            jnp.concatenate([self_low, jnp.zeros((hidden, pool - lanes), BF16)], axis=1),
            pool_low,
        ],
        axis=0,
    )
    for spot in range(calls):

        @pl.when(number == spot)
        def _(spot=spot):
            backs[spot][0:lanes, :] = (self_back + pool_back[0:lanes]).astype(BF16)
            backs[spot][lanes:, :] = pool_back[lanes:].astype(BF16)
            if not first_call:
                low_ref[:, (spot + 1) * pool : (spot + 2) * pool] = low_both

    if first_call:
        low_out_ref[...] = low_both
        edge_out_ref[...] = table_grad_ref[:, 0:channels]
        return
    edge_total_ref[...] += table_grad_ref[:, 0:channels]

    @pl.when(number == calls - 1)
    def _():
        total_ref[...] = dot(low_ref[...], row_ref[...])
        out_total_ref[...] = dot(mean_all_ref[...], up_all_ref[...])
        ones = jnp.ones((row_ref.shape[0], 128), BF16)
        bias_ref[...] = dot(low_ref[0:hidden, :], ones)
        core = perm_ref[count + 1]
        half = part // 2
        rows = whole_ref.shape[0] // count // 2
        for spot in range(count):
            for place, ref in ((core, mine_ref), (1 - core, other_ref)):
                first = pl.multiple_of(spot * part + place * half, half)
                kind = ref.dtype
                ref[spot, 0:half, 0:width] = total_ref[pl.ds(first, half), :].astype(kind)
                ref[spot, 0:half, width : 2 * width] = total_ref[pl.ds(hidden + first, half), :].astype(kind)
                ref[spot, 0:half, 2 * width : 3 * width] = out_total_ref[pl.ds(first, half), :].astype(kind)
                ref[spot, 0:half, 3 * width :] = bias_ref[pl.ds(first, half), :].astype(kind)
                whole = pl.multiple_of(perm_ref[spot] * (2 * rows) + place * rows, 8)
                fold = jnp.concatenate(
                    [edge_total_ref[pl.ds(first + 8 * turn, 8), :] for turn in range(half // 8)],
                    axis=1,
                )
                both = jnp.concatenate([whole_ref[pl.ds(whole, rows), :], fold], axis=0)
                ref[spot, half:, 0 : fold.shape[1]] = both.astype(kind)
                ref[spot, half:, fold.shape[1] :] = jnp.zeros(
                    (both.shape[0], ref.shape[2] - fold.shape[1]), kind
                )


def wide_body(
    perm_ref, low_ref, forward_ref, weight_ref, bias_ref, output_ref, mine_ref, other_ref, all_ref, *, count
):
    width = low_ref.shape[1]
    wide = weight_ref.shape[1]
    step = forward_ref.shape[0] // count
    lanes = step - 16
    low = low_ref[...]
    forward = jnp.concatenate(
        [forward_ref[spot * step : spot * step + lanes, :] for spot in range(count)], axis=0
    )
    lines = None
    for spot in range(count):
        line = forward_ref[spot * step + lanes : (spot + 1) * step, :].astype(F32)
        lines = line if spot == 0 else lines + line
    pre = dot(low, weight_ref[...]) + bias_ref[0:1, :].astype(F32)
    out, slope = gelu_pair(pre)
    grad = slope * dot_nt(forward, output_ref[...])
    all_ref[0:width, :] = dot_tn(low, grad.astype(BF16))
    all_ref[width : width + wide, :] = dot_tn(out.astype(BF16), forward)
    at = width + wide
    total = jnp.broadcast_to(jnp.sum(grad, axis=0, keepdims=True), (8, wide))
    all_ref[at : at + 8, :] = total
    all_ref[at + 8 : at + 16, :] = lines[0:8]
    all_ref[at + 16 :, :] = jnp.zeros((all_ref.shape[0] - at - 16, width), F32)
    half = mine_ref.shape[0]
    core = perm_ref[count + 1]
    mine_ref[...] = all_ref[pl.ds(pl.multiple_of(core * half, 8), half), :]
    other_ref[...] = all_ref[pl.ds(pl.multiple_of((1 - core) * half, 8), half), :].astype(BF16)


def wide_finish_body(
    perm_ref, mine_ref, other_ref, in_ref, out_ref, bias_ref, one_ref, two_ref, three_ref, all_ref, *, count
):
    core = perm_ref[count + 1]
    half = mine_ref.shape[0]
    all_ref[pl.ds(pl.multiple_of(core * half, 8), half), :] = mine_ref[...].astype(F32)
    all_ref[pl.ds(pl.multiple_of((1 - core) * half, 8), half), :] = other_ref[...].astype(F32)
    width = in_ref.shape[0]
    wide = out_ref.shape[0]
    in_ref[...] = all_ref[0:width, :]
    out_ref[...] = all_ref[width : width + wide, :]
    at = width + wide
    bias_ref[...] = all_ref[at : at + 1, :]
    one_ref[...] = all_ref[at + 8 : at + 10, :]
    two_ref[...] = all_ref[at + 10 : at + 12, :]
    three_ref[...] = all_ref[at + 12 : at + 14, :]


def late_finish_body(
    perm_ref,
    mine_ref,
    other_ref,
    mine_parts_ref,
    other_parts_ref,
    nodes_ref,
    output_ref,
    bias_ref,
    turned_ref,
    update_ref,
    hidden_bias_ref,
    gain_ref,
    shift_ref,
    branch_ref,
    edge_ref,
    own_ref,
    whole_ref,
    edges_ref,
    *,
    count,
):
    core = perm_ref[count + 1]
    part = own_ref.shape[0]
    half = part // 2
    width = output_ref.shape[1]
    rows = whole_ref.shape[0] // count // 2
    channels = edges_ref.shape[1]
    for place, ref, parts in ((core, mine_ref, mine_parts_ref), (1 - core, other_ref, other_parts_ref)):
        own_ref[pl.ds(pl.multiple_of(place * half, 8), half), :] = ref[0:half, :].astype(F32)
        for spot in range(count):
            value = parts[spot].astype(F32)
            start = pl.multiple_of(perm_ref[spot] * (2 * rows) + place * rows, 8)
            whole_ref[pl.ds(start, rows), :] = value[0:rows, :]
            first = perm_ref[spot] * part + place * half
            for turn in range(half // 8):
                start = pl.multiple_of(first + 8 * turn, 8)
                edges_ref[pl.ds(start, 8), :] = value[rows:, turn * channels : (turn + 1) * channels]
    nodes_ref[0] = own_ref[:, 0:width].T
    nodes_ref[1] = own_ref[:, width : 2 * width].T
    output_ref[...] = own_ref[:, 2 * width : 3 * width]
    bias_ref[...] = own_ref[:, 3 * width : 3 * width + 128].T[0:1, :]
    end = turned_ref.shape[1]
    hidden = update_ref.shape[0]
    turned_ref[...] = whole_ref[:, 0:end]
    update_ref[...] = whole_ref[:, end : end + hidden].T
    vectors = whole_ref[:, end + hidden :].T
    hidden_bias_ref[...] = vectors[0:1, :]
    gain_ref[...] = vectors[1:2, :]
    shift_ref[...] = vectors[2:3, :]
    branch_ref[...] = vectors[3:4, :]
    edge_ref[...] = edges_ref[...].T


def place_body(perm_ref, *refs, count):
    for spot in range(count):

        @pl.when(pl.program_id(0) == spot)
        def _(spot=spot):
            refs[count][0] = refs[spot][...]


def group_of(total):
    for size in (5, 4, 3, 2, 1):
        if total % size == 0:
            return size


def call(body, grid, ins, outs, scratch, flops, moved, name, perm=None, limit=56, aliases=()):
    whole = lambda block: (block, lambda *_: (0,) * len(block))
    in_specs = [
        pl.BlockSpec(memory_space=pl.ANY)
        if len(entry) == 2
        else pl.BlockSpec(*(entry[1:] if len(entry) == 3 else whole(entry[0].shape)))
        for entry in ins
    ]
    out_specs = [
        pl.BlockSpec(*(entry[2:] if len(entry) == 4 else whole(entry[0]))) for entry in outs
    ]
    spec = pltpu.PrefetchScalarGridSpec(
        num_scalar_prefetch=0 if perm is None else 1,
        grid=grid,
        in_specs=in_specs,
        out_specs=out_specs,
        scratch_shapes=scratch,
    )
    operands = [entry[0] for entry in ins]
    return pl.pallas_call(
        body,
        grid_spec=spec,
        out_shape=[jax.ShapeDtypeStruct(entry[0], entry[1]) for entry in outs],
        input_output_aliases={source + 1: target for source, target in aliases},
        compiler_params=pltpu.CompilerParams(
            dimension_semantics=("arbitrary",) * len(grid), vmem_limit_bytes=limit * 2**20
        ),
        cost_estimate=pl.CostEstimate(flops=flops, bytes_accessed=moved, transcendentals=0),
        name=name,
    )(*([] if perm is None else [perm]), *operands)


def build(prot_size, res_size, mp_size):
    def across(value, offset):
        pairs = [(spot, spot ^ offset) for spot in range(mp_size)]
        return lax.ppermute(value, "mp", pairs)

    def gather(value):
        return [value] + [across(value, offset) for offset in range(1, mp_size)]

    def scatter(parts):
        return [parts[0]] + [across(parts[offset], offset) for offset in range(1, mp_size)]

    def exchange(value):
        return lax.all_to_all(value, "res", split_axis=0, concat_axis=0, tiled=True)

    def block_parts(value):
        place = lax.axis_index("res")
        piece = value.shape[0] // res_size
        parts = [lax.dynamic_slice_in_dim(value, place * piece, piece, 0)]
        low = value.astype(BF16)
        for hop in range(1, res_size):
            target = lax.rem(place + hop, res_size)
            part = lax.dynamic_slice_in_dim(low, target * piece, piece, 0)
            pairs = [(spot, (spot + hop) % res_size) for spot in range(res_size)]
            parts.append(lax.ppermute(part, "res", pairs))
        return parts

    def block_gather(own):
        parts = [own]
        for hop in range(1, res_size):
            pairs = [(spot, (spot - hop) % res_size) for spot in range(res_size)]
            parts.append(lax.ppermute(own, "res", pairs))
        return parts

    def block_order(parts):
        place = lax.axis_index("res")
        piece = parts[0].shape[0]
        both = jnp.concatenate(parts + parts, axis=0)
        return lax.dynamic_slice_in_dim(both, (res_size - place) * piece, res_size * piece, 0)

    def swap(value):
        return lax.ppermute(value, "prot", [(0, 1), (1, 0)])

    def per_device(
        node_states,
        edge_states,
        neighbour_slots,
        send_rows,
        live_counts,
        message_nodes,
        message_edges,
        message_bias,
        message_output,
        feedforward_weight,
        feedforward_bias,
        feedforward_output,
        output_biases,
        norm_gains,
        norm_shifts,
        update_weight,
        update_bias,
        update_output,
        branch_bias,
        edge_gain,
        edge_shift,
        node_cotangent,
        edge_cotangent,
    ):
        proteins, lanes, width = node_states.shape
        own_k, channels = edge_states.shape[2:]
        slots = send_rows.shape[3]
        remote = res_size * slots
        pool = lanes + remote
        part = message_nodes.shape[2]
        hidden = part * mp_size
        update_hidden = update_output.shape[0]
        wide = feedforward_weight.shape[1]
        assert proteins == mp_size and prot_size == 2
        me = lax.axis_index("mp")
        core = lax.axis_index("prot")
        place = lax.axis_index("res")
        dead = lanes + place * slots
        order = [me ^ offset for offset in range(mp_size)]
        perm = jnp.stack(order + [dead, core]).astype(jnp.int32)

        def reorder(value, axis=0):
            size = value.shape[axis] // mp_size
            return jnp.concatenate(
                [lax.dynamic_slice_in_dim(value, spot * size, size, axis) for spot in order], axis=axis
            )

        send_table = (
            send_rows[:, 0].reshape(proteins, -1)[..., None]
            == lax.broadcasted_iota(jnp.int32, (1, 1, lanes), 2)
        ).astype(BF16)
        message_pack = jnp.concatenate(
            [
                message_nodes[0].T,
                message_nodes[1].T,
                message_output,
                jnp.broadcast_to(message_bias[:, None], (part, 128)),
            ],
            axis=1,
        )
        leaving = jnp.einsum("bsr,brd->bsd", send_table, node_states, preferred_element_type=F32)
        leaving = leaving.astype(BF16).reshape(proteins, res_size, slots, width)
        leaving = jnp.transpose(leaving, (1, 0, 2, 3))
        leaving, message_pack = lax.optimization_barrier((leaving, message_pack))
        arriving = exchange(leaving)
        weights = gather(message_pack)
        half = wide // 2
        bias_row = lax.dynamic_slice_in_dim(feedforward_bias, core * half, half, 0)
        block = jnp.concatenate(
            [
                lax.dynamic_slice_in_dim(feedforward_weight, core * half, half, 1).T,
                lax.dynamic_slice_in_dim(feedforward_output, core * half, half, 0),
                jnp.pad(bias_row[None], ((0, 15), (0, width - half))),
            ],
            axis=0,
        )

        own_slots = lax.dynamic_slice_in_dim(neighbour_slots, me * own_k, own_k, 2)
        alive = lax.broadcasted_iota(jnp.int32, own_slots.shape, 2) + me * own_k < live_counts[..., None]
        own_slots = jnp.transpose(jnp.where(alive, own_slots, dead), (0, 2, 1))
        counts = live_counts.astype(F32)
        scale = 1.0 / jnp.maximum(counts, 1.0)
        own_share = lax.dynamic_index_in_dim(counts * scale, me, 0, keepdims=False)
        share = jnp.broadcast_to(own_share[:, None], (lanes, 128))
        scale = scale[:, None, :]
        edges = jnp.transpose(edge_states, (0, 2, 3, 1))
        edge_up = jnp.transpose(edge_cotangent, (0, 2, 3, 1))
        own_table = lax.dynamic_index_in_dim(send_table, me, 0, keepdims=False)
        edge_weight = reorder(message_edges, 1)
        vectors = jnp.concatenate(
            [output_biases, norm_gains, norm_shifts, jnp.zeros_like(norm_shifts)], axis=0
        ).astype(F32)

        turned = update_weight.T
        lane = lax.broadcasted_iota(jnp.int32, (1, 128), 1)
        columns = jnp.where(
            lane == 0,
            update_bias.astype(F32)[:, None],
            jnp.where(
                lane == 1, edge_gain.astype(F32)[:, None], edge_shift.astype(F32)[:, None]
            ),
        )
        out_t = jnp.concatenate(
            [update_output.T, branch_bias[:, None], jnp.zeros((channels, 15), BF16)], axis=1
        )
        turned_edge = update_weight[2 * width :]
        edge_weight_t = edge_weight.T
        own_node = lax.dynamic_index_in_dim(node_states, me, 0)
        own_up = lax.dynamic_index_in_dim(node_cotangent, me, 0)
        wide_bias = jnp.broadcast_to(feedforward_bias[None], (16, wide))
        small = (
            own_slots,
            scale,
            share,
            vectors,
            own_table,
            columns,
            out_t,
            turned_edge,
            edge_weight,
            edge_weight_t,
            own_node,
            own_up,
            wide_bias,
        )
        weights, arriving, block, small = lax.optimization_barrier((weights, arriving, block, small))
        (
            own_slots,
            scale,
            share,
            vectors,
            own_table,
            columns,
            out_t,
            turned_edge,
            edge_weight,
            edge_weight_t,
            own_node,
            own_up,
            wide_bias,
        ) = small
        blocks = gather(block)

        depth = channels + pool
        group = group_of(own_k)
        count = proteins * own_k * lanes
        by_step4 = lambda p, perm: (p, 0, 0, 0)
        by_step3 = lambda p, perm: (p, 0, 0)
        others = proteins - 1

        def shifted(start):
            return (
                lambda p, perm: (perm[p + start], 0, 0, 0),
                lambda p, perm: (perm[p + start], 0, 0),
                lambda p, perm: (0, perm[p + start], 0, 0),
            )

        edge_block = (1, own_k, channels, lanes)
        edge_shape = (proteins, own_k, channels, lanes)
        slope_shape = (proteins, own_k, hidden, lanes)
        slope_block = (1, own_k, hidden, lanes)

        def edge_ins(start):
            by_perm4, by_perm3, _ = shifted(start)
            return [(edges, edge_block, by_perm4), (own_slots, (1, own_k, lanes), by_perm3)]

        def row_ins(start):
            _, by_perm3, by_arrive = shifted(start)
            return [
                (node_states, (1, lanes, width), by_perm3),
                (arriving, (res_size, 1, slots, width), by_arrive),
            ]

        def scale_in(start):
            return (scale, (1, 1, lanes), shifted(start)[1])

        def message_forward(start, calls, after):
            slots_after, _ = lax.optimization_barrier((own_slots, after))
            found = call(
                functools.partial(message_forward_body, count=proteins, calls=calls),
                (calls,),
                [edge_ins(start)[0], (slots_after,) + edge_ins(start)[1][1:]]
                + row_ins(start)
                + [(edge_weight_t,), scale_in(start)]
                + [(value,) for value in weights],
                [
                    ((calls, own_k, hidden, lanes), BF16, slope_block, by_step4),
                    ((calls, hidden, lanes), BF16, (1, hidden, lanes), by_step3),
                ]
                + [((lanes, width), BF16)] * calls,
                [
                    pltpu.VMEM((hidden, weights[0].shape[1]), BF16),
                    pltpu.VMEM((hidden, depth), BF16),
                    pltpu.VMEM((hidden, lanes), F32),
                    pltpu.VMEM((hidden, lanes), F32),
                    pltpu.VMEM((group, depth, lanes), BF16),
                    pltpu.VMEM((group, hidden, lanes), F32),
                ],
                2 * calls * own_k * lanes * depth * hidden,
                calls * own_k * lanes * (channels + hidden) * 2,
                "message_forward",
                perm,
            )
            return found[0], found[1], list(found[2:])

        slope_others, mean_others, part_others = message_forward(1, others, own_slots)
        slope_own, mean_own, part_own = message_forward(0, 1, part_others[0])
        parts = scatter(part_own + part_others)
        blocks, _ = lax.optimization_barrier((blocks, part_others[0]))
        other_blocks = swap(jnp.stack(blocks))
        one, two, first_low, second_low, leaving, own_term = call(
            functools.partial(forward_body, count=proteins),
            (),
            [(value,) for value in parts]
            + [(own_node,), (share,), (vectors,), (own_table,), (turned,)]
            + [(value,) for value in blocks]
            + [(other_blocks,)],
            [
                ((lanes, width), F32),
                ((lanes, width), F32),
                ((lanes, width), BF16),
                ((lanes, width), BF16),
                ((remote, width), BF16),
                ((update_hidden, 2 * lanes), BF16),
            ],
            [],
            4 * lanes * width * wide * mp_size,
            4 * width * wide * mp_size,
            "feed_forward",
            limit=56,
        )

        arrived = exchange(leaving.reshape(res_size, slots, width)).reshape(remote, width)
        terms = gather(own_term)
        pool_remotes = gather(arrived)
        all_low = lax.all_gather(first_low, "mp", axis=0, tiled=True)
        node_result = lax.all_gather(second_low[None], "mp", axis=0, tiled=True)
        turned_width = 2 * width + channels

        def edge_update(start, calls, earlier):
            by_perm4 = shifted(start)[0]
            ins = (
                edge_ins(start)
                + [(edge_up, edge_block, by_perm4)]
                + [(value,) for value in terms[start : start + calls]]
                + [(value,) for value in pool_remotes[start : start + calls]]
                + [(turned,), (columns,), (out_t,), (update_output,), (turned_edge,)]
            )
            aliases = ()
            if earlier is not None:
                ins = ins + [(earlier[1],), (earlier[0], None)]
                aliases = ((len(ins) - 1, 0),)
            found = call(
                functools.partial(
                    update_body, count=proteins, calls=calls, first_call=earlier is None
                ),
                (calls,),
                ins,
                [
                    (edge_shape, BF16, edge_block, by_perm4),
                    ((calls, own_k, channels, lanes), BF16, edge_block, by_step4),
                ]
                + [((update_hidden, lanes + pool), BF16)] * calls
                + [((update_hidden, 768), F32)],
                [
                    pltpu.VMEM((update_hidden, depth), BF16),
                    pltpu.VMEM((update_hidden, lanes), F32),
                    pltpu.VMEM((update_hidden, depth), F32),
                    pltpu.VMEM((update_hidden, lanes), F32),
                    pltpu.VMEM((channels, 8), F32),
                    pltpu.VMEM((channels, 8), F32),
                    pltpu.VMEM((update_hidden, channels), F32),
                    pltpu.VMEM((channels, update_hidden + 16), F32),
                    pltpu.VMEM((channels, lanes), F32),
                    pltpu.VMEM((channels, lanes), F32),
                    pltpu.VMEM((depth, group * lanes), BF16),
                    pltpu.VMEM((update_hidden + 16, group * lanes), BF16),
                    pltpu.VMEM((channels, group * lanes), BF16),
                    pltpu.VMEM((update_hidden, group * lanes), BF16),
                    pltpu.VMEM((channels, group * lanes), BF16),
                    pltpu.VMEM((update_hidden, group * lanes), F32),
                    pltpu.VMEM((update_hidden, group * lanes), BF16),
                ],
                2 * calls * own_k * lanes * (2 * depth + 4 * channels) * update_hidden,
                calls * own_k * lanes * channels * 8,
                "edge_update",
                perm,
                aliases=aliases,
            )
            return found[0], found[-1], found[1], found[2:-1]

        edge_result, grads, edge_part_own, sums_own = edge_update(0, 1, None)
        edge_result, grads, edge_part_others, sums_others = edge_update(1, others, (edge_result, grads))
        sums_own, sums_others, all_low = lax.optimization_barrier((sums_own, sums_others, all_low))
        sums = scatter(list(sums_own) + list(sums_others))
        second_part, leaving, whole = call(
            functools.partial(return_body, count=proteins),
            (),
            [(value,) for value in sums]
            + [(turned,), (own_up,), (second_low,), (arrived,), (grads,), (columns,)],
            [
                ((lanes, width), F32),
                ((remote, width), BF16),
                ((update_hidden, turned_width + update_hidden + 128), F32),
            ],
            [],
            2 * (lanes + pool) * width * update_hidden,
            (lanes + pool) * width * 2,
            "update_return",
            limit=56,
        )
        returned = exchange(leaving.reshape(res_size, slots, width)).reshape(remote, width)
        aggregate_grad, forward_grad, sum_one, _ = call(
            functools.partial(backward_body, count=proteins),
            (),
            [(second_part,), (returned,), (own_table,), (one,), (two,), (share,), (vectors,)]
            + [(value,) for value in blocks]
            + [(other_blocks,)],
            [
                ((lanes, width), BF16),
                ((lanes + 16, width), BF16),
                ((lanes, width), F32),
                ((16, width), F32),
            ],
            [],
            6 * lanes * width * wide * mp_size,
            4 * width * wide * mp_size,
            "feed_backward",
            limit=56,
        )
        ups = gather(aggregate_grad)
        all_forward = lax.all_gather(forward_grad, "mp", axis=0, tiled=True)
        total_width = 3 * width + 128
        late_shape = (proteins, part // 2 + update_hidden // mp_size // 2 + 8, total_width)

        def message_backward(start, calls, earlier):
            by_perm4 = shifted(start)[0]
            ins = (
                edge_ins(start)
                + [
                    (slope_own if earlier is None else slope_others, slope_block, by_step4),
                    (edge_part_own if earlier is None else edge_part_others, edge_block, by_step4),
                    (edge_weight,),
                    scale_in(start),
                ]
                + [(value,) for value in weights + ups[start : start + calls]]
            )
            aliases = ()
            scratch = [
                pltpu.VMEM((hidden, weights[0].shape[1]), BF16),
                pltpu.VMEM((hidden, lanes), BF16),
                pltpu.VMEM((hidden, depth), F32),
                pltpu.VMEM((hidden, lanes), F32),
                pltpu.VMEM((depth, group * lanes), BF16),
                pltpu.VMEM((hidden, group * lanes), BF16),
            ]
            if earlier is None:
                last = [((2 * hidden, pool), BF16), ((hidden, channels), F32)]
            else:
                mean_block = (1, hidden, lanes)
                ins = ins + row_ins(start)
                ins = ins + [
                    (node_states, (1, lanes, width), lambda p, perm: (perm[0], 0, 0)),
                    (arriving, (res_size, 1, slots, width), lambda p, perm: (0, perm[0], 0, 0)),
                    (mean_others, mean_block, by_step3),
                    (mean_own,),
                    (ups[0],),
                    (earlier[1],),
                    (earlier[2],),
                    (whole,),
                    (earlier[0], None),
                ]
                aliases = ((len(ins) - 1, 0),)
                last = [(late_shape, F32), (late_shape, BF16)]
                scratch = scratch + [
                    pltpu.VMEM((2 * hidden, proteins * pool), BF16),
                    pltpu.VMEM((proteins * pool, width), BF16),
                    pltpu.VMEM((hidden, proteins * lanes), BF16),
                    pltpu.VMEM((proteins * lanes, width), BF16),
                    pltpu.VMEM((hidden, channels), F32),
                    pltpu.VMEM((hidden, 128), F32),
                    pltpu.VMEM((2 * hidden, width), F32),
                    pltpu.VMEM((hidden, width), F32),
                ]
            found = call(
                functools.partial(
                    message_backward_body, count=proteins, calls=calls, first_call=earlier is None
                ),
                (calls,),
                ins,
                [(edge_shape, BF16, edge_block, by_perm4)] + [((pool, width), BF16)] * calls + last,
                scratch,
                2 * calls * own_k * lanes * (depth + channels) * hidden,
                calls * own_k * lanes * (3 * channels + hidden) * 2,
                "message_backward",
                perm,
                aliases=aliases,
            )
            return found[0], found[-2], found[-1], found[1 : 1 + calls]

        edge_grad, own_low, own_edge, back_own = message_backward(0, 1, None)
        edge_grad, late_mine, late_other, back_others = message_backward(
            1, others, (edge_grad, own_low, own_edge)
        )
        found = list(back_own) + list(back_others)
        backs, late_mine, late_other, all_forward, node_result = lax.optimization_barrier(
            (found, late_mine, late_other, all_forward, node_result)
        )
        late_swapped = swap(late_other)
        back = scatter(backs)
        unit = prot_size * res_size * 8
        wide_rows = -(-(width + wide + 16) // unit) * unit
        early_mine, early_other = call(
            functools.partial(wide_body, count=proteins),
            (1,),
            [
                (all_low,),
                (all_forward,),
                (feedforward_weight,),
                (wide_bias,),
                (feedforward_output,),
            ],
            [((wide_rows // 2, width), F32), ((wide_rows // 2, width), BF16)],
            [pltpu.VMEM((wide_rows, width), F32)],
            10 * proteins * lanes * width * wide,
            8 * proteins * lanes * width,
            "feed_weights",
            perm,
            32,
        )
        late_swapped, early_mine, early_other = lax.optimization_barrier(
            (late_swapped, early_mine, early_other)
        )
        early_swapped = swap(early_other)
        late = late_mine + late_swapped.astype(F32)
        late_own = late[0]
        late_low = [late[offset].astype(BF16) for offset in range(1, mp_size)]
        late_own, late_low, back = lax.optimization_barrier((late_own, late_low, back))
        late_parts = scatter([late_own] + late_low)
        total = sum(value.astype(F32) for value in back)
        leaving = total[lanes:].astype(BF16).reshape(res_size, slots, width)
        leaving, early_swapped = lax.optimization_barrier((leaving, early_swapped))
        returned = exchange(leaving)
        early = early_mine + early_swapped.astype(F32)
        early, returned = lax.optimization_barrier((early, returned))
        early_parts = block_parts(early)
        node_grad = (
            sum_one
            + total[:lanes]
            + jnp.einsum(
                "sr,sd->rd", own_table, returned.reshape(remote, width), preferred_element_type=F32
            )
        ).astype(BF16)
        node_grad, early_parts, late_parts = lax.optimization_barrier((node_grad, early_parts, late_parts))
        node_parts = gather(node_grad)
        late = sum(value.astype(F32) for value in late_parts)
        early = sum(value.astype(F32) for value in early_parts).astype(BF16)
        late, early = lax.optimization_barrier((late, early))
        late_parts = block_parts(late)
        early_parts = block_gather(early)
        late_parts, early_parts, node_parts = lax.optimization_barrier((late_parts, early_parts, node_parts))
        late_parts = block_gather(sum(value.astype(F32) for value in late_parts).astype(BF16))
        early = block_order(early_parts)
        early_swapped = swap(early)
        (node_grad,) = call(
            functools.partial(place_body, count=proteins),
            (proteins,),
            [(value,) for value in node_parts],
            [((proteins, lanes, width), BF16, (1, lanes, width), shifted(0)[1])],
            [],
            0,
            4 * proteins * lanes * width,
            "place_rows",
            perm,
            16,
        )
        node_grad, late_parts, early_swapped = lax.optimization_barrier(
            (node_grad, late_parts, early_swapped)
        )
        late = block_order(late_parts)
        shared_parts = gather(late[part // 2 :, : turned_width + update_hidden + 128])
        late_swapped = swap(late)
        weight_in_grad, weight_out_grad, wide_bias_grad, biases_grad, gains_grad, shifts_grad = call(
            functools.partial(wide_finish_body, count=proteins),
            (1,),
            [(early,), (early_swapped,)],
            [
                ((width, wide), F32),
                ((wide, width), F32),
                ((1, wide), F32),
                ((2, width), F32),
                ((2, width), F32),
                ((2, width), F32),
            ],
            [pltpu.VMEM((wide_rows, width), F32)],
            0,
            8 * wide_rows * width,
            "feed_weights_out",
            perm,
            16,
        )
        weight_in_grad, shared_parts, late_swapped = lax.optimization_barrier(
            (weight_in_grad, shared_parts, late_swapped)
        )
        shared = jnp.stack(shared_parts)
        found = call(
            functools.partial(late_finish_body, count=proteins),
            (1,),
            [(late,), (late_swapped,), (shared,), (swap(shared),)],
            [
                ((2, width, part), F32),
                ((part, width), F32),
                ((1, part), F32),
                ((update_hidden, turned_width), F32),
                ((update_hidden, channels), F32),
                ((1, update_hidden), F32),
                ((1, channels), F32),
                ((1, channels), F32),
                ((1, channels), F32),
                ((channels, hidden), F32),
            ],
            [
                pltpu.VMEM((part, total_width), F32),
                pltpu.VMEM((update_hidden, turned_width + update_hidden + 128), F32),
                pltpu.VMEM((hidden, channels), F32),
            ],
            0,
            8 * hidden * total_width,
            "message_weights_out",
            perm,
            16,
        )
        turn = lambda value: jnp.transpose(value, (0, 3, 1, 2))
        return (
            node_result,
            turn(edge_result),
            node_grad,
            turn(edge_grad),
            found[0],
            found[9],
            found[2].reshape(part),
            found[1],
            weight_in_grad,
            wide_bias_grad.reshape(wide),
            weight_out_grad,
            biases_grad,
            gains_grad,
            shifts_grad,
            found[3].T,
            found[5].reshape(update_hidden),
            found[4],
            found[8].reshape(channels),
            found[6].reshape(channels),
            found[7].reshape(channels),
        )

    return per_device


def solution(mesh):
    return jax.shard_map(
        build(mesh.shape["prot"], mesh.shape["res"], mesh.shape["mp"]),
        mesh=mesh,
        in_specs=(
            P("prot", "res", None),
            P("prot", "res", "mp", None),
            P("prot", "res", None),
            P("prot", "res", None, None),
            P("prot", "res"),
            P(None, None, "mp"),
            P(),
            P("mp"),
            P("mp", None),
            P(None, "mp"),
            P("mp"),
            P("mp", None),
            P(),
            P(),
            P(),
            P(),
            P(),
            P(),
            P(),
            P(),
            P(),
            P("prot", "res", None),
            P("prot", "res", "mp", None),
        ),
        out_specs=(
            P("prot", "res", None),
            P("prot", "res", "mp", None),
            P("prot", "res", None),
            P("prot", "res", "mp", None),
            P(None, None, "mp"),
            P(),
            P("mp"),
            P("mp", None),
            P(None, "mp"),
            P("mp"),
            P("mp", None),
            P(),
            P(),
            P(),
            P(),
            P(),
            P(),
            P(),
            P(),
            P(),
        ),
        check_vma=False,
    )
```

```python
import functools

import jax
import jax.numpy as jnp
from jax import lax
from jax.experimental import pallas as pl
from jax.experimental.pallas import tpu as pltpu
from jax.sharding import PartitionSpec as P

EPSILON = 1e-05
F32 = jnp.float32
PINNED = ("prepare",)
BF16 = jnp.bfloat16
DEAD = -30000.0
CUBIC = 0.044715
ROOT = 0.7978845608028654


def dot(left, right):
    return jnp.dot(left, right, preferred_element_type=F32)


def dot_nt(left, right):
    return lax.dot_general(left, right, (((1,), (1,)), ((), ())), preferred_element_type=F32)


def gelu_pair(value):
    square = value * value
    gate = 0.5 + 0.5 * jnp.tanh(value * (ROOT + (ROOT * CUBIC) * square))
    out = value * gate
    slope = gate + (out - out * gate) * (2.0 * ROOT + (6.0 * ROOT * CUBIC) * square)
    return out, slope


def low(value):
    return jnp.asarray(value, BF16)


def gelu_pair_low(value):
    value = value.astype(BF16)
    square = value * value
    inner = value * (low(-2.0 * ROOT) + low(-2.0 * ROOT * CUBIC) * square)
    power = jnp.exp(jnp.minimum(inner, low(80.0)))
    gate = pl.reciprocal(low(1.0) + power, approx=True)
    out = value * gate
    slope = gate + (out * (power * gate)) * (low(2.0 * ROOT) + low(6.0 * ROOT * CUBIC) * square)
    return out, slope


def activation(value):
    return jax.nn.gelu(value, approximate=True)


def activation_grad(value, upstream):
    return jax.vjp(activation, value)[1](upstream)[0]


def norm_forward(value, gain, shift):
    centred = value - jnp.mean(value, axis=-1, keepdims=True)
    inverse = lax.rsqrt(jnp.mean(centred * centred, axis=-1, keepdims=True) + EPSILON)
    normed = centred * inverse
    return (normed * gain + shift, normed, inverse)


def norm_backward(upstream, normed, inverse, gain):
    scaled = upstream * gain
    inner = (
        scaled
        - jnp.mean(scaled, axis=-1, keepdims=True)
        - normed * jnp.mean(scaled * normed, axis=-1, keepdims=True)
    )
    return inverse * inner


def selector(slot_row, rows):
    positions = lax.broadcasted_iota(jnp.int16, (rows, slot_row.shape[1]), 0)
    return jnp.where(positions == slot_row.astype(jnp.int16), low(1.0), low(0.0))


def dot_tn(left, right):
    return lax.dot_general(left, right, (((0,), (0,)), ((), ())), preferred_element_type=F32)


def masked_table(fixed, term, dead):
    positions = lax.broadcasted_iota(jnp.int32, term.shape, 1)
    term = jnp.where(positions == dead, DEAD, term).astype(BF16)
    return jnp.concatenate([fixed, term], axis=1)


def message_forward_body(perm_ref, *refs, count, calls):
    edge_ref, slot_ref, node_ref, arrive_ref, fixed_ref, scale_ref = refs[:6]
    weights = refs[6 : 6 + count]
    others = refs[6 + count : 6 + 2 * count]
    refs = refs[6 + 2 * count :]
    slope_ref, mean_ref = refs[:2]
    parts = refs[2 : 2 + calls]
    weight_ref, table_ref, self_ref, sum_ref, operand_ref, value_ref = refs[2 + calls :]
    number = pl.program_id(0)
    group = operand_ref.shape[0]
    dead = perm_ref[count]
    steps, channels, lanes = edge_ref.shape[1:]
    width = node_ref.shape[2]

    @pl.when(number == 0)
    def _():
        fill_weights(perm_ref, weights, others, weight_ref, count)

    nodes = node_ref[0]
    arrive = arrive_ref[...].reshape(-1, width)
    pool = lanes + arrive.shape[0]
    rows = jnp.concatenate([nodes, arrive], axis=0)
    term = dot_nt(weight_ref[:, width : 2 * width], rows)
    table_ref[...] = masked_table(fixed_ref[...], term, dead)
    bias = weight_ref[:, 3 * width : 3 * width + 1].astype(F32)
    self_ref[...] = dot_nt(weight_ref[:, 0:width], nodes) + bias
    sum_ref[...] = jnp.zeros_like(sum_ref)

    def some(index, carry):
        spots = [index * group + spot for spot in range(group)]
        for spot in range(group):
            operand_ref[spot, 0:channels] = edge_ref[0, spots[spot]]
            operand_ref[spot, channels:] = selector(slot_ref[0, pl.ds(spots[spot], 1), :], pool)
        for spot in range(group):
            value_ref[spot] = dot(table_ref[...], operand_ref[spot])
        total = sum_ref[...]
        for spot in range(group):
            out, slope = gelu_pair_low(value_ref[spot] + self_ref[...])
            slope_ref[0, spots[spot]] = slope
            total = total + out.astype(F32)
        sum_ref[...] = total
        return carry

    lax.fori_loop(0, steps // group, some, 0)
    mean = (sum_ref[...] * scale_ref[0]).astype(BF16)
    mean_ref[0] = mean
    total = dot_tn(mean, weight_ref[:, 2 * width : 3 * width]).astype(BF16)
    for spot in range(calls):

        @pl.when(number == spot)
        def _(spot=spot):
            parts[spot][...] = total


def pack_body(perm_ref, nodes_ref, output_ref, bias_ref, send_ref, node_ref, pack_ref, leave_ref, all_ref, *, count):
    width = output_ref.shape[1]
    part = output_ref.shape[0]
    all_ref[:, 0:width] = nodes_ref[0].T
    all_ref[:, width : 2 * width] = nodes_ref[1].T
    all_ref[:, 2 * width : 3 * width] = output_ref[...]
    tall = lambda row: jnp.broadcast_to(row, (8, row.shape[1])).T[:, 0:1]
    bias = tall(bias_ref[...].astype(F32).reshape(1, -1)).astype(BF16)
    all_ref[:, 3 * width :] = jnp.broadcast_to(bias, (part, all_ref.shape[1] - 3 * width))
    half = part // 2
    start = pl.multiple_of(perm_ref[count + 1] * half, half)
    pack_ref[...] = all_ref[pl.ds(start, half), :]
    proteins, lanes, _ = node_ref.shape
    for spot in range(proteins):
        rows = tall(send_ref[spot : spot + 1, :].astype(F32))
        lane = lax.broadcasted_iota(jnp.int32, (rows.shape[0], lanes), 1).astype(F32)
        table = jnp.where(lane == rows, 1.0, 0.0).astype(BF16)
        leave_ref[:, spot] = dot(table, node_ref[spot]).astype(BF16).reshape(leave_ref[:, spot].shape)


def prepare_body(
    perm_ref,
    edge_ref,
    turned_ref,
    out_ref,
    hidden_bias_ref,
    gain_ref,
    shift_ref,
    branch_ref,
    wide_ref,
    biases_ref,
    gains_ref,
    shifts_ref,
    counts_ref,
    send_ref,
    node_ref,
    up_ref,
    wide_in_ref,
    wide_out_ref,
    weight_ref,
    weight_t_ref,
    column_ref,
    out_t_ref,
    turned_edge_ref,
    vector_ref,
    share_ref,
    table_ref,
    wide_bias_ref,
    own_node_ref,
    own_up_ref,
    block_ref,
    *,
    count,
):
    row = lambda ref: ref[...].astype(F32).reshape(1, -1)
    core = perm_ref[count + 1]
    half = wide_out_ref.shape[0] // 2
    start = pl.multiple_of(core * half, half)
    block_ref[0:half, :] = wide_in_ref[:, pl.ds(start, half)].T
    block_ref[half : 2 * half, :] = wide_out_ref[pl.ds(start, half), :]
    wide = row(wide_ref)
    line = jnp.where(core == 0, wide[:, 0:half], wide[:, half:])
    block_ref[2 * half :, 0:half] = jnp.broadcast_to(line, (16, half)).astype(BF16)
    block_ref[2 * half :, half:] = jnp.zeros((16, block_ref.shape[1] - half), BF16)
    part = edge_ref.shape[1] // count
    for spot in range(count):
        span = slice(spot * part, (spot + 1) * part)
        block = edge_ref[:, pl.ds(pl.multiple_of(perm_ref[spot] * part, part), part)]
        weight_ref[:, span] = block
        weight_t_ref[span, :] = block.T
    tall = lambda row: jnp.broadcast_to(row, (8, row.shape[1])).T[:, 0:1]
    channels = edge_ref.shape[0]
    lane = lax.broadcasted_iota(jnp.int32, (channels, 128), 1)
    column_ref[...] = jnp.where(
        lane == 0,
        tall(row(hidden_bias_ref)),
        jnp.where(lane == 1, tall(row(gain_ref)), tall(row(shift_ref))),
    )
    hidden = out_ref.shape[0]
    extra = out_t_ref.shape[1] - hidden
    lane = lax.broadcasted_iota(jnp.int32, (channels, extra), 1)
    last = jnp.where(lane == 0, tall(row(branch_ref)), 0.0).astype(BF16)
    out_t_ref[...] = jnp.concatenate([out_ref[...].T, last], axis=1)
    turned_edge_ref[...] = turned_ref[:, turned_ref.shape[1] - channels :].T
    vector_ref[0:2, :] = biases_ref[...].astype(F32)
    vector_ref[2:4, :] = gains_ref[...].astype(F32)
    vector_ref[4:6, :] = shifts_ref[...].astype(F32)
    vector_ref[6:8, :] = jnp.zeros((2, vector_ref.shape[1]), F32)
    me = perm_ref[0]
    pick = lambda value: jnp.sum(
        jnp.where(lax.broadcasted_iota(jnp.int32, value.shape, 0) == me, value, 0.0), axis=0, keepdims=True
    )
    counts = pick(counts_ref[...].astype(F32))
    share = counts * (1.0 / jnp.maximum(counts, 1.0))
    share_ref[...] = jnp.broadcast_to(tall(share), share_ref.shape)
    rows = tall(pick(send_ref[...].astype(F32)))
    lane = lax.broadcasted_iota(jnp.int32, table_ref.shape, 1).astype(F32)
    table_ref[...] = jnp.where(lane == rows, 1.0, 0.0).astype(BF16)
    wide_bias_ref[...] = jnp.broadcast_to(wide, wide_bias_ref.shape).astype(BF16)
    own_node_ref[...] = node_ref[...]
    own_up_ref[...] = up_ref[...]


def fill_weights(perm_ref, mine, other, target, count):
    core = perm_ref[count + 1]
    half = mine[0].shape[0]
    for spot in range(count):
        for place, value in ((core, mine[spot][...]), (1 - core, other[spot][...])):
            start = pl.multiple_of((2 * spot + place) * half, half)
            target[pl.ds(start, half), :] = value


def forward_body(*refs, count):
    parts = refs[:count]
    node_ref, share_ref, vector_ref, send_ref, turned_ref = refs[count : count + 5]
    blocks = list(refs[count + 5 : 2 * count + 5])
    blocks = blocks + [refs[2 * count + 5].at[spot] for spot in range(count)]
    one_ref, two_ref, first_ref, second_ref, leave_ref, term_ref, slope_ref = refs[2 * count + 6 :]
    total = parts[0][...].astype(F32)
    for spot in range(1, count):
        total = total + parts[spot][...].astype(F32)
    value = node_ref[0].astype(F32) + total + share_ref[:, 0:1] * vector_ref[0:1, :]
    one_ref[...] = value
    first_norm, _, _ = norm_forward(value, vector_ref[2:3, :], vector_ref[4:5, :])
    first_low = first_norm.astype(BF16)
    first_ref[...] = first_low
    value = first_norm + vector_ref[1:2, :]
    for spot in range(2 * count):
        block = blocks[spot]
        half = (block.shape[0] - 16) // 2
        pre = dot_nt(first_low, block[0:half, :]) + block[2 * half : 2 * half + 1, 0:half].astype(F32)
        out, slope = gelu_pair(pre)
        slope_ref[:, spot * half : (spot + 1) * half] = slope.astype(BF16)
        value = value + dot(out.astype(BF16), block[half : 2 * half, :])
    two_ref[...] = value
    second_norm, _, _ = norm_forward(value, vector_ref[3:4, :], vector_ref[5:6, :])
    second = second_norm.astype(BF16)
    second_ref[...] = second
    leave_ref[...] = dot(send_ref[...], second).astype(BF16)
    lanes, width = second.shape
    term_ref[:, 0:lanes] = dot_nt(turned_ref[:, 0:width], second).astype(BF16)
    term_ref[:, lanes:] = dot_nt(turned_ref[:, width : 2 * width], second).astype(BF16)


def update_body(perm_ref, *refs, count, calls, first_call, joint):
    edge_ref, slot_ref, up_ref = refs[:3]
    terms = refs[3 : 3 + calls]
    if joint:
        refs = refs[: 3 + calls] + refs[3:]
        hidden = refs[3 + 2 * calls].shape[0]
        remotes = [ref.at[hidden:, :] for ref in terms]
        terms = [ref.at[0:hidden, :] for ref in terms]
    else:
        remotes = refs[3 + calls : 3 + 2 * calls]
    turned_ref, column_ref, out_t_ref, out_ref, weight_ref = refs[3 + 2 * calls : 8 + 2 * calls]
    refs = refs[8 + 2 * calls :]
    if not first_call:
        start_ref = refs[0]
        refs = refs[2:]
    result_ref, part_ref = refs[:2]
    sums = refs[2 : 2 + calls]
    total_ref = refs[2 + calls]
    table_ref, self_ref, table_grad_ref, self_grad_ref = refs[3 + calls : 7 + calls]
    gain_grad_ref, shift_grad_ref, edge_grad_ref, out_grad_ref = refs[7 + calls : 11 + calls]
    gain_ref, shift_ref, operand_ref, out_low_ref, mixed_ref, grad_ref, product_ref, value_ref, slope_ref = refs[
        11 + calls :
    ]
    group = operand_ref.shape[1] // edge_ref.shape[3]
    number = pl.program_id(0)
    dead = perm_ref[count]
    steps, channels, lanes = edge_ref.shape[1:]
    hidden = turned_ref.shape[0]
    width = remotes[0].shape[1]
    pool = lanes + remotes[0].shape[0]
    extra = out_t_ref.shape[1] - hidden
    grads = (edge_grad_ref, out_grad_ref, gain_grad_ref, shift_grad_ref)
    bases = (0, 256, 512, 640)

    @pl.when(number == 0)
    def _():
        for ref, base in zip(grads, bases):
            if first_call:
                ref[...] = jnp.zeros_like(ref)
            else:
                ref[...] = start_ref[:, base : base + ref.shape[1]]
        gain_ref[...] = jnp.broadcast_to(column_ref[:, 1:2], gain_ref.shape)
        shift_ref[...] = jnp.broadcast_to(column_ref[:, 2:3], shift_ref.shape)

    for spot in range(calls):

        @pl.when(number == spot)
        def _(spot=spot):
            remote = dot_nt(turned_ref[:, width : 2 * width], remotes[spot][...])
            term = jnp.concatenate([terms[spot][:, lanes:].astype(F32), remote], axis=1)
            table_ref[...] = masked_table(turned_ref[:, 2 * width :], term, dead)
            self_ref[...] = terms[spot][:, 0:lanes].astype(F32) + column_ref[:, 0:1]

    table_grad_ref[...] = jnp.zeros_like(table_grad_ref)
    self_grad_ref[...] = jnp.zeros_like(self_grad_ref)
    share = 1.0 / channels
    first = lax.broadcasted_iota(jnp.int32, (extra, lanes), 0) == 0
    spans = [slice(spot * lanes, (spot + 1) * lanes) for spot in range(group)]
    total = lambda value: jnp.sum(value, axis=0, keepdims=True)

    def some(index, carry):
        spots = [index * group + spot for spot in range(group)]
        for spot, span in zip(spots, spans):
            slot_row = slot_ref[0, pl.ds(spot, 1), :]
            operand_ref[0:channels, span] = edge_ref[0, spot]
            operand_ref[channels:, span] = selector(slot_row, pool)
            live = jnp.where(first & (slot_row != dead), 1.0, 0.0)
            out_low_ref[hidden:, span] = live.astype(BF16)
        for span in spans:
            value_ref[:, span] = dot(table_ref[...], operand_ref[:, span])
        for span in spans:
            out, slope = gelu_pair_low(value_ref[:, span] + self_ref[...])
            out_low_ref[0:hidden, span] = out
            slope_ref[:, span] = slope
        for span in spans:
            value_ref[:, span] = dot(out_t_ref[...], out_low_ref[:, span])
        for spot, span in zip(spots, spans):
            value = edge_ref[0, spot].astype(F32) + value_ref[:, span]
            centred = value - total(value) * share
            inverse = lax.rsqrt(total(centred * centred) * share + EPSILON)
            normed = centred * inverse
            gain = gain_ref[...]
            result_ref[0, spot] = (normed * gain + shift_ref[...]).astype(BF16)
            scaled = up_ref[0, spot].astype(F32) * gain
            product = scaled * normed
            product_ref[:, span] = product.astype(BF16)
            mixed = inverse * (scaled - total(scaled) * share - normed * (total(product) * share))
            mixed_ref[:, span] = mixed.astype(BF16)
        for span in spans:
            value_ref[:, span] = dot(out_ref[...], mixed_ref[:, span])
        for span in spans:
            grad = slope_ref[:, span].astype(F32) * value_ref[:, span]
            self_grad_ref[...] += grad
            grad_ref[:, span] = grad.astype(BF16)
        out_grad_ref[...] += dot_nt(mixed_ref[...], out_low_ref[...])
        for spot, span in zip(spots, spans):
            edge = dot(weight_ref[...], grad_ref[:, span])
            part_ref[0, spot] = (mixed_ref[:, span].astype(F32) + edge).astype(BF16)
        table_grad_ref[...] += dot_nt(grad_ref[...], operand_ref[...])
        gain_grad_ref[...] += dot_nt(product_ref[...], jnp.ones((8, group * lanes), BF16))
        for spot in spots:
            shift_grad_ref[...] += dot_nt(up_ref[0, spot], jnp.ones((8, lanes), BF16))
        return carry

    lax.fori_loop(0, steps // group, some, 0)
    edge_grad_ref[...] += table_grad_ref[:, 0:channels]
    for spot in range(calls):

        @pl.when(number == spot)
        def _(spot=spot):
            sums[spot][:, 0:lanes] = self_grad_ref[...].astype(BF16)
            sums[spot][:, lanes:] = table_grad_ref[:, channels:].astype(BF16)

    @pl.when(number == calls - 1)
    def _():
        for ref, base in zip(grads, bases):
            total_ref[:, base : base + ref.shape[1]] = ref[...]


def return_body(perm_ref, *refs, count):
    sums = refs[:count]
    turned_ref, up_ref, low_ref, arrive_ref, grad_ref, column_ref = refs[count : count + 6]
    second_ref, leave_ref, mine_ref, other_ref, whole_ref = refs[count + 6 :]
    total = sums[0][...].astype(F32)
    for spot in range(1, count):
        total = total + sums[spot][...].astype(F32)
    low = total.astype(BF16)
    lanes, width = second_ref.shape
    back = dot_tn(low[:, lanes:], turned_ref[:, width : 2 * width])
    leave_ref[...] = back[lanes:].astype(BF16)
    second_ref[...] = (
        up_ref[0].astype(F32) + dot_tn(low[:, 0:lanes], turned_ref[:, 0:width]) + back[0:lanes]
    )
    channels = grad_ref.shape[0]
    hidden = low.shape[0]
    rows = jnp.concatenate([low_ref[...], arrive_ref[...]], axis=0)
    lane = lax.broadcasted_iota(jnp.int32, (channels, 128), 1)
    vectors = jnp.where(
        lane == 0,
        jnp.sum(total[:, 0:lanes], axis=1, keepdims=True),
        jnp.where(
            lane == 1,
            grad_ref[:, 512:513] / column_ref[:, 1:2],
            jnp.where(lane == 2, grad_ref[:, 640:641], grad_ref[:, 256 + hidden : 257 + hidden]),
        ),
    )
    whole_ref[...] = jnp.concatenate(
        [
            dot(low[:, 0:lanes], low_ref[...]),
            dot(low[:, lanes:], rows),
            grad_ref[:, 0:channels],
            grad_ref[:, 256 : 256 + hidden],
            vectors,
        ],
        axis=1,
    )
    core = perm_ref[count + 1]
    half = mine_ref.shape[0]
    mine_ref[...] = whole_ref[pl.ds(pl.multiple_of(core * half, 8), half), :]
    other_ref[...] = whole_ref[pl.ds(pl.multiple_of((1 - core) * half, 8), half), :].astype(BF16)


def backward_body(*refs, count):
    second_ref, return_ref, send_ref, one_ref, two_ref, share_ref, vector_ref, slope_ref = refs[:8]
    blocks = list(refs[8 : 8 + count])
    blocks = blocks + [refs[8 + count].at[spot] for spot in range(count)]
    aggregate_ref, forward_ref, sum_ref, grad_ref = refs[9 + count :]
    lanes = one_ref.shape[0]
    second_grad = second_ref[...] + dot_tn(send_ref[...], return_ref[...])
    _, first_normed, first_inverse = norm_forward(
        one_ref[...], vector_ref[2:3, :], vector_ref[4:5, :]
    )
    _, second_normed, second_inverse = norm_forward(
        two_ref[...], vector_ref[3:4, :], vector_ref[5:6, :]
    )
    total = lambda value: jnp.sum(value, axis=0, keepdims=True)
    grad_ref[3:4, :] = total(second_grad * second_normed)
    grad_ref[5:6, :] = total(second_grad)
    sum_two = norm_backward(second_grad, second_normed, second_inverse, vector_ref[3:4, :])
    low = sum_two.astype(BF16)
    forward_ref[0:lanes, :] = low
    grad_ref[1:2, :] = total(low.astype(F32))
    first_grad = sum_two
    for spot in range(2 * count):
        block = blocks[spot]
        half = (block.shape[0] - 16) // 2
        slope = slope_ref[:, spot * half : (spot + 1) * half].astype(F32)
        grad = (slope * dot_nt(low, block[half : 2 * half, :])).astype(BF16)
        first_grad = first_grad + dot(grad, block[0:half, :])
    grad_ref[2:3, :] = total(first_grad * first_normed)
    grad_ref[4:5, :] = total(first_grad)
    sum_one = norm_backward(first_grad, first_normed, first_inverse, vector_ref[2:3, :])
    sum_ref[...] = sum_one
    aggregate = sum_one.astype(BF16)
    aggregate_ref[...] = aggregate
    grad_ref[0:1, :] = total(share_ref[:, 0:1] * aggregate.astype(F32))
    grad_ref[6:16, :] = jnp.zeros((10, grad_ref.shape[1]), F32)
    forward_ref[lanes:, :] = grad_ref[...].astype(BF16)


def message_backward_body(perm_ref, *refs, count, calls, first_call):
    edge_ref, slot_ref, slope_ref, part_ref, edge_weight_ref, scale_ref = refs[:6]
    weights = refs[6 : 6 + count]
    others = refs[6 + count : 6 + 2 * count]
    ups = refs[6 + 2 * count : 6 + 2 * count + calls]
    refs = refs[6 + 2 * count + calls :]
    if not first_call:
        node_ref, arrive_ref, own_node_ref, own_arrive_ref, mean_ref, own_mean_ref = refs[:6]
        own_up_ref, own_low_ref, own_edge_ref = refs[6:9]
        refs = refs[10:]
    grad_ref = refs[0]
    backs = refs[1 : 1 + calls]
    low_out_ref, edge_out_ref = refs[1 + calls : 3 + calls]
    weight_ref, up_ref, table_grad_ref, self_grad_ref = refs[3 + calls : 7 + calls]
    operand_ref, grad_low_ref = refs[7 + calls : 9 + calls]
    if not first_call:
        mine_ref, other_ref = low_out_ref, edge_out_ref
        low_ref, row_ref, mean_all_ref, up_all_ref = refs[9 + calls : 13 + calls]
        edge_total_ref, bias_ref, total_ref, out_total_ref = refs[13 + calls :]
    group = operand_ref.shape[1] // edge_ref.shape[3]
    number = pl.program_id(0)
    steps, channels, lanes = edge_ref.shape[1:]
    part = 2 * weights[0].shape[0]
    hidden = part * count
    width = backs[0].shape[1]
    pool = backs[0].shape[0]

    @pl.when(number == 0)
    def _():
        fill_weights(perm_ref, weights, others, weight_ref, count)
        if not first_call:
            low_ref[:, 0:pool] = own_low_ref[...]
            row_ref[0:lanes, :] = own_node_ref[0]
            row_ref[lanes:pool, :] = own_arrive_ref[...].reshape(-1, width)
            mean_all_ref[:, 0:lanes] = own_mean_ref[0]
            up_all_ref[0:lanes, :] = own_up_ref[...]
            edge_total_ref[...] = own_edge_ref[...]

    for spot in range(calls):

        @pl.when(number == spot)
        def _(spot=spot):
            value = dot_nt(weight_ref[:, 2 * width : 3 * width], ups[spot][...])
            up_ref[...] = (value * scale_ref[0]).astype(BF16)
            if not first_call:
                at = (spot + 1) * pool
                row_ref[at : at + lanes, :] = node_ref[0]
                row_ref[at + lanes : at + pool, :] = arrive_ref[...].reshape(-1, width)
                at = (spot + 1) * lanes
                mean_all_ref[:, at : at + lanes] = mean_ref[0]
                up_all_ref[at : at + lanes, :] = ups[spot][...]

    table_grad_ref[...] = jnp.zeros_like(table_grad_ref)
    self_grad_ref[...] = jnp.zeros_like(self_grad_ref)
    spans = [slice(spot * lanes, (spot + 1) * lanes) for spot in range(group)]

    def some(index, carry):
        spots = [index * group + spot for spot in range(group)]
        for spot, span in zip(spots, spans):
            operand_ref[0:channels, span] = edge_ref[0, spot]
            operand_ref[channels:, span] = selector(slot_ref[0, pl.ds(spot, 1), :], pool)
        total = self_grad_ref[...]
        for spot, span in zip(spots, spans):
            grad = slope_ref[0, spot] * up_ref[...]
            grad_low_ref[:, span] = grad
            total = total + grad.astype(F32)
        self_grad_ref[...] = total
        for spot, span in zip(spots, spans):
            edge = dot(edge_weight_ref[...], grad_low_ref[:, span])
            grad_ref[0, spot] = (part_ref[0, spot].astype(F32) + edge).astype(BF16)
        table_grad_ref[...] += dot_nt(grad_low_ref[...], operand_ref[...])
        return carry

    lax.fori_loop(0, steps // group, some, 0)
    self_low = self_grad_ref[...].astype(BF16)
    pool_low = table_grad_ref[:, channels:].astype(BF16)
    self_back = dot_tn(self_low, weight_ref[:, 0:width])
    pool_back = dot_tn(pool_low, weight_ref[:, width : 2 * width])
    low_both = jnp.concatenate(
        [
            jnp.concatenate([self_low, jnp.zeros((hidden, pool - lanes), BF16)], axis=1),
            pool_low,
        ],
        axis=0,
    )
    for spot in range(calls):

        @pl.when(number == spot)
        def _(spot=spot):
            backs[spot][0:lanes, :] = (self_back + pool_back[0:lanes]).astype(BF16)
            backs[spot][lanes:, :] = pool_back[lanes:].astype(BF16)
            if not first_call:
                low_ref[:, (spot + 1) * pool : (spot + 2) * pool] = low_both

    if first_call:
        low_out_ref[...] = low_both
        edge_out_ref[...] = table_grad_ref[:, 0:channels]
        return
    edge_total_ref[...] += table_grad_ref[:, 0:channels]

    @pl.when(number == calls - 1)
    def _():
        total_ref[...] = dot(low_ref[...], row_ref[...])
        out_total_ref[...] = dot(mean_all_ref[...], up_all_ref[...])
        ones = jnp.ones((row_ref.shape[0], 128), BF16)
        bias_ref[...] = dot(low_ref[0:hidden, :], ones)
        core = perm_ref[count + 1]
        half = part // 2
        for spot in range(count):
            for place, ref in ((core, mine_ref), (1 - core, other_ref)):
                first = pl.multiple_of(spot * part + place * half, half)
                kind = ref.dtype
                ref[spot, :, 0:width] = total_ref[pl.ds(first, half), :].astype(kind)
                ref[spot, :, width : 2 * width] = total_ref[pl.ds(hidden + first, half), :].astype(kind)
                ref[spot, :, 2 * width : 3 * width] = out_total_ref[pl.ds(first, half), :].astype(kind)
                both = jnp.concatenate(
                    [
                        edge_total_ref[pl.ds(first, half), :],
                        bias_ref[pl.ds(first, half), 0 : ref.shape[2] - 3 * width - channels],
                    ],
                    axis=1,
                )
                ref[spot, :, 3 * width :] = both.astype(kind)


def wide_body(
    perm_ref, low_ref, forward_ref, weight_ref, bias_ref, output_ref, mine_ref, other_ref, all_ref, *, count
):
    width = low_ref.shape[1]
    wide = weight_ref.shape[1]
    step = forward_ref.shape[0] // count
    lanes = step - 16
    low = low_ref[...]
    forward = jnp.concatenate(
        [forward_ref[spot * step : spot * step + lanes, :] for spot in range(count)], axis=0
    )
    lines = None
    for spot in range(count):
        line = forward_ref[spot * step + lanes : (spot + 1) * step, :].astype(F32)
        lines = line if spot == 0 else lines + line
    pre = dot(low, weight_ref[...]) + bias_ref[0:1, :].astype(F32)
    out, slope = gelu_pair(pre)
    grad = slope * dot_nt(forward, output_ref[...])
    all_ref[0:width, :] = dot_tn(low, grad.astype(BF16))
    all_ref[width : width + wide, :] = dot_tn(out.astype(BF16), forward)
    at = width + wide
    total = jnp.broadcast_to(jnp.sum(grad, axis=0, keepdims=True), (8, wide))
    all_ref[at : at + 8, :] = total
    all_ref[at + 8 : at + 16, :] = lines[0:8]
    all_ref[at + 16 :, :] = jnp.zeros((all_ref.shape[0] - at - 16, width), F32)
    half = mine_ref.shape[0]
    core = perm_ref[count + 1]
    mine_ref[...] = all_ref[pl.ds(pl.multiple_of(core * half, 8), half), :]
    other_ref[...] = all_ref[pl.ds(pl.multiple_of((1 - core) * half, 8), half), :].astype(BF16)


def wide_finish_body(
    perm_ref, mine_ref, other_ref, in_ref, out_ref, bias_ref, one_ref, two_ref, three_ref, all_ref, *, count
):
    core = perm_ref[count + 1]
    half = mine_ref.shape[0]
    all_ref[pl.ds(pl.multiple_of(core * half, 8), half), :] = mine_ref[...].astype(F32)
    all_ref[pl.ds(pl.multiple_of((1 - core) * half, 8), half), :] = other_ref[...].astype(F32)
    width = in_ref.shape[0]
    wide = out_ref.shape[0]
    in_ref[...] = all_ref[0:width, :]
    out_ref[...] = all_ref[width : width + wide, :]
    at = width + wide
    bias_ref[...] = all_ref[at : at + 1, :]
    one_ref[...] = all_ref[at + 8 : at + 10, :]
    two_ref[...] = all_ref[at + 10 : at + 12, :]
    three_ref[...] = all_ref[at + 12 : at + 14, :]


def late_finish_body(
    perm_ref,
    mine_ref,
    other_ref,
    mine_parts_ref,
    other_parts_ref,
    nodes_ref,
    output_ref,
    bias_ref,
    turned_ref,
    update_ref,
    hidden_bias_ref,
    gain_ref,
    shift_ref,
    branch_ref,
    edge_ref,
    own_ref,
    whole_ref,
    edges_ref,
    *,
    count,
):
    core = perm_ref[count + 1]
    part = own_ref.shape[0]
    half = part // 2
    width = output_ref.shape[1]
    rows = whole_ref.shape[0] // count // 2
    channels = edges_ref.shape[1]
    for place, ref, parts in ((core, mine_ref, mine_parts_ref), (1 - core, other_ref, other_parts_ref)):
        own_ref[pl.ds(pl.multiple_of(place * half, 8), half), :] = ref[...].astype(F32)
        for spot in range(count):
            value = parts[spot].astype(F32)
            start = pl.multiple_of((place * count + perm_ref[spot]) * rows, 8)
            whole_ref[pl.ds(start, rows), :] = value[0:rows, :]
            first = perm_ref[spot] * part + place * half
            for turn in range(half // 8):
                start = pl.multiple_of(first + 8 * turn, 8)
                edges_ref[pl.ds(start, 8), :] = value[rows:, turn * channels : (turn + 1) * channels]
    nodes_ref[0] = own_ref[:, 0:width].T
    nodes_ref[1] = own_ref[:, width : 2 * width].T
    output_ref[...] = own_ref[:, 2 * width : 3 * width]
    last = own_ref.shape[1]
    bias_ref[...] = own_ref[:, last - 128 :].T[127:128, :]
    end = turned_ref.shape[1]
    hidden = update_ref.shape[0]
    turned_ref[...] = whole_ref[:, 0:end]
    update_ref[...] = whole_ref[:, end : end + hidden].T
    vectors = whole_ref[:, end + hidden :].T
    hidden_bias_ref[...] = vectors[0:1, :]
    gain_ref[...] = vectors[1:2, :]
    shift_ref[...] = vectors[2:3, :]
    branch_ref[...] = vectors[3:4, :]
    edge_ref[...] = edges_ref[...].T


def place_body(perm_ref, *refs, count):
    for spot in range(count):

        @pl.when(pl.program_id(0) == spot)
        def _(spot=spot):
            refs[count][0] = refs[spot][...]


def group_of(total):
    for size in (5, 4, 3, 2, 1):
        if total % size == 0:
            return size


def call(body, grid, ins, outs, scratch, flops, moved, name, perm=None, limit=56, aliases=()):
    whole = lambda block: (block, lambda *_: (0,) * len(block))
    in_specs = [
        pl.BlockSpec(memory_space=pl.ANY)
        if len(entry) == 2
        else pl.BlockSpec(*(entry[1:] if len(entry) == 3 else whole(entry[0].shape)))
        for entry in ins
    ]
    out_specs = [
        pl.BlockSpec(*(entry[2:] if len(entry) == 4 else whole(entry[0]))) for entry in outs
    ]
    spec = pltpu.PrefetchScalarGridSpec(
        num_scalar_prefetch=0 if perm is None else 1,
        grid=grid,
        in_specs=in_specs,
        out_specs=out_specs,
        scratch_shapes=scratch,
    )
    operands = [entry[0] for entry in ins]
    return pl.pallas_call(
        body,
        grid_spec=spec,
        out_shape=[(pltpu.HBM if name in PINNED else jax.ShapeDtypeStruct)(entry[0], entry[1]) for entry in outs],
        input_output_aliases={source + 1: target for source, target in aliases},
        compiler_params=pltpu.CompilerParams(
            dimension_semantics=("arbitrary",) * len(grid), vmem_limit_bytes=limit * 2**20
        ),
        cost_estimate=pl.CostEstimate(flops=flops, bytes_accessed=moved, transcendentals=0),
        name=name,
    )(*([] if perm is None else [perm]), *operands)


def build(prot_size, res_size, mp_size):
    def across(value, offset):
        pairs = [(spot, spot ^ offset) for spot in range(mp_size)]
        return lax.ppermute(value, "mp", pairs)

    def gather(value):
        return [value] + [across(value, offset) for offset in range(1, mp_size)]

    def scatter(parts):
        return [parts[0]] + [across(parts[offset], offset) for offset in range(1, mp_size)]

    def exchange(value):
        return lax.all_to_all(value, "res", split_axis=0, concat_axis=0, tiled=True)

    def block_parts(value):
        place = lax.axis_index("res")
        piece = value.shape[0] // res_size
        parts = [lax.dynamic_slice_in_dim(value, place * piece, piece, 0)]
        low = value.astype(BF16)
        for hop in range(1, res_size):
            target = lax.rem(place + hop, res_size)
            part = lax.dynamic_slice_in_dim(low, target * piece, piece, 0)
            pairs = [(spot, (spot + hop) % res_size) for spot in range(res_size)]
            parts.append(lax.ppermute(part, "res", pairs))
        return parts

    def block_gather(own):
        parts = [own]
        for hop in range(1, res_size):
            pairs = [(spot, (spot - hop) % res_size) for spot in range(res_size)]
            parts.append(lax.ppermute(own, "res", pairs))
        return parts

    def block_order(parts):
        place = lax.axis_index("res")
        piece = parts[0].shape[0]
        both = jnp.concatenate(parts + parts, axis=0)
        return lax.dynamic_slice_in_dim(both, (res_size - place) * piece, res_size * piece, 0)

    def swap(value):
        return lax.ppermute(value, "prot", [(0, 1), (1, 0)])

    def per_device(
        node_states,
        edge_states,
        neighbour_slots,
        send_rows,
        live_counts,
        message_nodes,
        message_edges,
        message_bias,
        message_output,
        feedforward_weight,
        feedforward_bias,
        feedforward_output,
        output_biases,
        norm_gains,
        norm_shifts,
        update_weight,
        update_bias,
        update_output,
        branch_bias,
        edge_gain,
        edge_shift,
        node_cotangent,
        edge_cotangent,
    ):
        proteins, lanes, width = node_states.shape
        own_k, channels = edge_states.shape[2:]
        slots = send_rows.shape[3]
        remote = res_size * slots
        pool = lanes + remote
        part = message_nodes.shape[2]
        hidden = part * mp_size
        update_hidden = update_output.shape[0]
        wide = feedforward_weight.shape[1]
        assert proteins == mp_size and prot_size == 2
        me = lax.axis_index("mp")
        core = lax.axis_index("prot")
        place = lax.axis_index("res")
        dead = lanes + place * slots
        order = [me ^ offset for offset in range(mp_size)]
        perm = jnp.stack(order + [dead, core]).astype(jnp.int32)

        def reorder(value, axis=0):
            size = value.shape[axis] // mp_size
            return jnp.concatenate(
                [lax.dynamic_slice_in_dim(value, spot * size, size, axis) for spot in order], axis=axis
            )

        send_flat = send_rows.reshape(proteins, -1)
        message_pack, leaving = call(
            functools.partial(pack_body, count=mp_size),
            (1,),
            [
                (message_nodes,),
                (message_output,),
                (message_bias,),
                (send_flat,),
                (node_states,),
            ],
            [
                ((part // 2, 3 * width + 128), BF16),
                ((res_size, proteins, slots, width), BF16),
            ],
            [pltpu.VMEM((part, 3 * width + 128), BF16)],
            0,
            0,
            "pack",
            perm,
        )
        arriving = exchange(leaving)
        weights = gather(message_pack)
        other_weights = [swap(value) for value in weights]
        own_slots = lax.dynamic_slice_in_dim(neighbour_slots, me * own_k, own_k, 2)
        alive = lax.broadcasted_iota(jnp.int32, own_slots.shape, 2) + me * own_k < live_counts[..., None]
        own_slots = jnp.transpose(jnp.where(alive, own_slots, dead), (0, 2, 1))
        counts = live_counts.astype(F32)
        scale = (1.0 / jnp.maximum(counts, 1.0))[:, None, :]
        edges = jnp.transpose(edge_states, (0, 2, 3, 1))
        edge_up = jnp.transpose(edge_cotangent, (0, 2, 3, 1))
        turned = update_weight.T
        small = call(
            functools.partial(prepare_body, count=mp_size),
            (1,),
            [
                (message_edges,),
                (turned,),
                (update_output,),
                (update_bias,),
                (edge_gain,),
                (edge_shift,),
                (branch_bias,),
                (feedforward_bias,),
                (output_biases,),
                (norm_gains,),
                (norm_shifts,),
                (live_counts,),
                (send_flat,),
                (node_states, (1, lanes, width), lambda p, perm: (perm[0], 0, 0)),
                (node_cotangent, (1, lanes, width), lambda p, perm: (perm[0], 0, 0)),
                (feedforward_weight,),
                (feedforward_output,),
            ],
            [
                ((channels, hidden), BF16),
                ((hidden, channels), BF16),
                ((channels, 128), F32),
                ((channels, update_hidden + 16), BF16),
                ((channels, update_hidden), BF16),
                ((8, width), F32),
                ((lanes, 128), F32),
                ((remote, lanes), BF16),
                ((16, wide), BF16),
                ((1, lanes, width), BF16),
                ((1, lanes, width), BF16),
                ((wide + 16, width), BF16),
            ],
            [],
            0,
            0,
            "prepare",
            perm,
        )
        weights, other_weights, arriving, own_slots, scale, small = lax.optimization_barrier(
            (weights, other_weights, arriving, own_slots, scale, small)
        )
        (
            edge_weight,
            edge_weight_t,
            columns,
            out_t,
            turned_edge,
            vectors,
            share,
            own_table,
            wide_bias,
            own_node,
            own_up,
            block,
        ) = small
        blocks = gather(block)

        depth = channels + pool
        group = group_of(own_k)
        count = proteins * own_k * lanes
        by_step4 = lambda p, perm: (p, 0, 0, 0)
        by_step3 = lambda p, perm: (p, 0, 0)
        others = proteins - 1

        def shifted(start):
            return (
                lambda p, perm: (perm[p + start], 0, 0, 0),
                lambda p, perm: (perm[p + start], 0, 0),
                lambda p, perm: (0, perm[p + start], 0, 0),
            )

        edge_block = (1, own_k, channels, lanes)
        edge_shape = (proteins, own_k, channels, lanes)
        slope_shape = (proteins, own_k, hidden, lanes)
        slope_block = (1, own_k, hidden, lanes)

        def edge_ins(start):
            by_perm4, by_perm3, _ = shifted(start)
            return [(edges, edge_block, by_perm4), (own_slots, (1, own_k, lanes), by_perm3)]

        def row_ins(start):
            _, by_perm3, by_arrive = shifted(start)
            return [
                (node_states, (1, lanes, width), by_perm3),
                (arriving, (res_size, 1, slots, width), by_arrive),
            ]

        def scale_in(start):
            return (scale, (1, 1, lanes), shifted(start)[1])

        def message_forward(start, calls, after):
            slots_after, _ = lax.optimization_barrier((own_slots, after))
            found = call(
                functools.partial(message_forward_body, count=proteins, calls=calls),
                (calls,),
                [edge_ins(start)[0], (slots_after,) + edge_ins(start)[1][1:]]
                + row_ins(start)
                + [(edge_weight_t,), scale_in(start)]
                + [(value,) for value in weights + other_weights],
                [
                    ((calls, own_k, hidden, lanes), BF16, slope_block, by_step4),
                    ((calls, hidden, lanes), BF16, (1, hidden, lanes), by_step3),
                ]
                + [((lanes, width), BF16)] * calls,
                [
                    pltpu.VMEM((hidden, weights[0].shape[1]), BF16),
                    pltpu.VMEM((hidden, depth), BF16),
                    pltpu.VMEM((hidden, lanes), F32),
                    pltpu.VMEM((hidden, lanes), F32),
                    pltpu.VMEM((group, depth, lanes), BF16),
                    pltpu.VMEM((group, hidden, lanes), F32),
                ],
                2 * calls * own_k * lanes * depth * hidden,
                calls * own_k * lanes * (channels + hidden) * 2,
                "message_forward",
                perm,
            )
            return found[0], found[1], list(found[2:])

        slope_others, mean_others, part_others = message_forward(1, others, own_slots)
        slope_own, mean_own, part_own = message_forward(0, 1, part_others[0])
        parts = scatter(part_own + part_others)
        blocks, _ = lax.optimization_barrier((blocks, part_others[0]))
        other_blocks = swap(jnp.stack(blocks))
        one, two, first_low, second_low, leaving, own_term, wide_slope = call(
            functools.partial(forward_body, count=proteins),
            (),
            [(value,) for value in parts]
            + [(own_node,), (share,), (vectors,), (own_table,), (turned,)]
            + [(value,) for value in blocks]
            + [(other_blocks,)],
            [
                ((lanes, width), F32),
                ((lanes, width), F32),
                ((lanes, width), BF16),
                ((lanes, width), BF16),
                ((remote, width), BF16),
                ((update_hidden, 2 * lanes), BF16),
                ((lanes, wide * mp_size), BF16),
            ],
            [],
            4 * lanes * width * wide * mp_size,
            4 * width * wide * mp_size,
            "feed_forward",
            limit=56,
        )

        arrived = exchange(leaving.reshape(res_size, slots, width)).reshape(remote, width)
        joint = own_term.shape[1] == width
        if joint:
            terms = gather(jnp.concatenate([own_term, arrived], axis=0))
            pool_remotes = []
        else:
            terms = gather(own_term)
            pool_remotes = gather(arrived)
        all_low = lax.all_gather(first_low, "mp", axis=0, tiled=True)
        node_result = lax.all_gather(second_low[None], "mp", axis=0, tiled=True)
        turned_width = 2 * width + channels

        def edge_update(start, calls, earlier):
            by_perm4 = shifted(start)[0]
            ins = (
                edge_ins(start)
                + [(edge_up, edge_block, by_perm4)]
                + [(value,) for value in terms[start : start + calls]]
                + [(value,) for value in pool_remotes[start : start + calls]]
                + [(turned,), (columns,), (out_t,), (update_output,), (turned_edge,)]
            )
            aliases = ()
            if earlier is not None:
                ins = ins + [(earlier[1],), (earlier[0], None)]
                aliases = ((len(ins) - 1, 0),)
            found = call(
                functools.partial(
                    update_body,
                    count=proteins,
                    calls=calls,
                    first_call=earlier is None,
                    joint=joint,
                ),
                (calls,),
                ins,
                [
                    (edge_shape, BF16, edge_block, by_perm4),
                    ((calls, own_k, channels, lanes), BF16, edge_block, by_step4),
                ]
                + [((update_hidden, lanes + pool), BF16)] * calls
                + [((update_hidden, 768), F32)],
                [
                    pltpu.VMEM((update_hidden, depth), BF16),
                    pltpu.VMEM((update_hidden, lanes), F32),
                    pltpu.VMEM((update_hidden, depth), F32),
                    pltpu.VMEM((update_hidden, lanes), F32),
                    pltpu.VMEM((channels, 8), F32),
                    pltpu.VMEM((channels, 8), F32),
                    pltpu.VMEM((update_hidden, channels), F32),
                    pltpu.VMEM((channels, update_hidden + 16), F32),
                    pltpu.VMEM((channels, lanes), F32),
                    pltpu.VMEM((channels, lanes), F32),
                    pltpu.VMEM((depth, group * lanes), BF16),
                    pltpu.VMEM((update_hidden + 16, group * lanes), BF16),
                    pltpu.VMEM((channels, group * lanes), BF16),
                    pltpu.VMEM((update_hidden, group * lanes), BF16),
                    pltpu.VMEM((channels, group * lanes), BF16),
                    pltpu.VMEM((update_hidden, group * lanes), F32),
                    pltpu.VMEM((update_hidden, group * lanes), BF16),
                ],
                2 * calls * own_k * lanes * (2 * depth + 4 * channels) * update_hidden,
                calls * own_k * lanes * channels * 8,
                "edge_update",
                perm,
                aliases=aliases,
            )
            return found[0], found[-1], found[1], found[2:-1]

        edge_result, grads, edge_part_own, sums_own = edge_update(0, 1, None)
        edge_result, grads, edge_part_others, sums_others = edge_update(1, others, (edge_result, grads))
        sums_own, sums_others, all_low = lax.optimization_barrier((sums_own, sums_others, all_low))
        sums = scatter(list(sums_own) + list(sums_others))
        whole_width = turned_width + update_hidden + 128
        second_part, leaving, whole_mine, whole_other = call(
            functools.partial(return_body, count=proteins),
            (1,),
            [(value,) for value in sums]
            + [(turned,), (own_up,), (second_low,), (arrived,), (grads,), (columns,)],
            [
                ((lanes, width), F32),
                ((remote, width), BF16),
                ((update_hidden // 2, whole_width), F32),
                ((update_hidden // 2, whole_width), BF16),
            ],
            [pltpu.VMEM((update_hidden, whole_width), F32)],
            2 * (lanes + pool) * width * update_hidden,
            (lanes + pool) * width * 2,
            "update_return",
            perm,
        )
        whole_swapped = swap(whole_other)
        returned = exchange(leaving.reshape(res_size, slots, width)).reshape(remote, width)
        whole = (whole_mine + whole_swapped.astype(F32)).astype(BF16)
        whole, returned = lax.optimization_barrier((whole, returned))
        whole = lax.psum_scatter(whole, "mp", scatter_dimension=0, tiled=True)
        aggregate_grad, forward_grad, sum_one, _ = call(
            functools.partial(backward_body, count=proteins),
            (),
            [(second_part,), (returned,), (own_table,), (one,), (two,), (share,), (vectors,), (wide_slope,)]
            + [(value,) for value in blocks]
            + [(other_blocks,)],
            [
                ((lanes, width), BF16),
                ((lanes + 16, width), BF16),
                ((lanes, width), F32),
                ((16, width), F32),
            ],
            [],
            6 * lanes * width * wide * mp_size,
            4 * width * wide * mp_size,
            "feed_backward",
            limit=56,
        )
        ups = gather(aggregate_grad)
        all_forward = lax.all_gather(forward_grad, "mp", axis=0, tiled=True)
        total_width = 3 * width + -(-(channels + 1) // 128) * 128
        late_shape = (proteins, part // 2, total_width)

        def message_backward(start, calls, earlier):
            by_perm4 = shifted(start)[0]
            ins = (
                edge_ins(start)
                + [
                    (slope_own if earlier is None else slope_others, slope_block, by_step4),
                    (edge_part_own if earlier is None else edge_part_others, edge_block, by_step4),
                    (edge_weight,),
                    scale_in(start),
                ]
                + [(value,) for value in weights + other_weights + ups[start : start + calls]]
            )
            aliases = ()
            scratch = [
                pltpu.VMEM((hidden, weights[0].shape[1]), BF16),
                pltpu.VMEM((hidden, lanes), BF16),
                pltpu.VMEM((hidden, depth), F32),
                pltpu.VMEM((hidden, lanes), F32),
                pltpu.VMEM((depth, group * lanes), BF16),
                pltpu.VMEM((hidden, group * lanes), BF16),
            ]
            if earlier is None:
                last = [((2 * hidden, pool), BF16), ((hidden, channels), F32)]
            else:
                mean_block = (1, hidden, lanes)
                ins = ins + row_ins(start)
                ins = ins + [
                    (node_states, (1, lanes, width), lambda p, perm: (perm[0], 0, 0)),
                    (arriving, (res_size, 1, slots, width), lambda p, perm: (0, perm[0], 0, 0)),
                    (mean_others, mean_block, by_step3),
                    (mean_own,),
                    (ups[0],),
                    (earlier[1],),
                    (earlier[2],),
                    (earlier[0], None),
                ]
                aliases = ((len(ins) - 1, 0),)
                last = [(late_shape, F32), (late_shape, BF16)]
                scratch = scratch + [
                    pltpu.VMEM((2 * hidden, proteins * pool), BF16),
                    pltpu.VMEM((proteins * pool, width), BF16),
                    pltpu.VMEM((hidden, proteins * lanes), BF16),
                    pltpu.VMEM((proteins * lanes, width), BF16),
                    pltpu.VMEM((hidden, channels), F32),
                    pltpu.VMEM((hidden, 128), F32),
                    pltpu.VMEM((2 * hidden, width), F32),
                    pltpu.VMEM((hidden, width), F32),
                ]
            found = call(
                functools.partial(
                    message_backward_body, count=proteins, calls=calls, first_call=earlier is None
                ),
                (calls,),
                ins,
                [(edge_shape, BF16, edge_block, by_perm4)] + [((pool, width), BF16)] * calls + last,
                scratch,
                2 * calls * own_k * lanes * (depth + channels) * hidden,
                calls * own_k * lanes * (3 * channels + hidden) * 2,
                "message_backward",
                perm,
                aliases=aliases,
            )
            return found[0], found[-2], found[-1], found[1 : 1 + calls]

        edge_grad, own_low, own_edge, back_own = message_backward(0, 1, None)
        edge_grad, late_mine, late_other, back_others = message_backward(
            1, others, (edge_grad, own_low, own_edge)
        )
        found = list(back_own) + list(back_others)
        late_swapped = swap(late_other)
        backs, late_mine, all_forward, node_result, whole = lax.optimization_barrier(
            (found, late_mine, all_forward, node_result, whole)
        )
        back = scatter(backs)
        late = late_mine + late_swapped.astype(F32)
        late_own = late[0]
        late_low = [late[offset].astype(BF16) for offset in range(1, mp_size)]
        all_forward, late_own, late_low = lax.optimization_barrier((all_forward, late_own, late_low))
        late_parts = scatter([late_own] + late_low)
        unit = prot_size * res_size * 8
        wide_rows = -(-(width + wide + 16) // unit) * unit
        early_mine, early_other = call(
            functools.partial(wide_body, count=proteins),
            (1,),
            [
                (all_low,),
                (all_forward,),
                (feedforward_weight,),
                (wide_bias,),
                (feedforward_output,),
            ],
            [((wide_rows // 2, width), F32), ((wide_rows // 2, width), BF16)],
            [pltpu.VMEM((wide_rows, width), F32)],
            10 * proteins * lanes * width * wide,
            8 * proteins * lanes * width,
            "feed_weights",
            perm,
        )
        back, early_other, early_mine = lax.optimization_barrier((back, early_other, early_mine))
        early_swapped = swap(early_other)
        total = sum(value.astype(F32) for value in back)
        leaving = total[lanes:].astype(BF16).reshape(res_size, slots, width)
        leaving, early_swapped = lax.optimization_barrier((leaving, early_swapped))
        early = (early_mine + early_swapped.astype(F32)).astype(BF16)
        early, leaving = lax.optimization_barrier((early, leaving))
        early, whole = lax.psum((early, whole), "res")
        returned = exchange(leaving)
        node_grad = (
            sum_one
            + total[:lanes]
            + jnp.einsum(
                "sr,sd->rd", own_table, returned.reshape(remote, width), preferred_element_type=F32
            )
        ).astype(BF16)
        node_grad, late_parts = lax.optimization_barrier((node_grad, late_parts))
        late = sum(value.astype(F32) for value in late_parts)
        late_parts = block_parts(late)
        node_parts = gather(node_grad)
        late = sum(value.astype(F32) for value in late_parts).astype(BF16)
        late, node_parts = lax.optimization_barrier((late, node_parts))
        late_parts = block_gather(late)
        (node_grad,) = call(
            functools.partial(place_body, count=proteins),
            (proteins,),
            [(value,) for value in node_parts],
            [((proteins, lanes, width), BF16, (1, lanes, width), shifted(0)[1])],
            [],
            0,
            4 * proteins * lanes * width,
            "place_rows",
            perm,
        )
        early, whole, node_grad, late_parts = lax.optimization_barrier(
            (early, whole, node_grad, late_parts)
        )
        late = block_order(late_parts)
        early_swapped = swap(early)
        late_swapped = swap(late)
        fold = late[:, 3 * width : 3 * width + channels].reshape(-1, 8, channels)
        fold = jnp.transpose(fold, (1, 0, 2)).reshape(8, -1)
        shared_parts = gather(jnp.concatenate([whole, fold], axis=0))
        weight_in_grad, weight_out_grad, wide_bias_grad, biases_grad, gains_grad, shifts_grad = call(
            functools.partial(wide_finish_body, count=proteins),
            (1,),
            [(early,), (early_swapped,)],
            [
                ((width, wide), F32),
                ((wide, width), F32),
                ((1, wide), F32),
                ((2, width), F32),
                ((2, width), F32),
                ((2, width), F32),
            ],
            [pltpu.VMEM((wide_rows, width), F32)],
            0,
            8 * wide_rows * width,
            "feed_weights_out",
            perm,
        )
        weight_in_grad, shared_parts, late_swapped = lax.optimization_barrier(
            (weight_in_grad, shared_parts, late_swapped)
        )
        shared = jnp.stack(shared_parts)
        found = call(
            functools.partial(late_finish_body, count=proteins),
            (1,),
            [(late,), (late_swapped,), (shared,), (swap(shared),)],
            [
                ((2, width, part), F32),
                ((part, width), F32),
                ((1, part), F32),
                ((update_hidden, turned_width), F32),
                ((update_hidden, channels), F32),
                ((1, update_hidden), F32),
                ((1, channels), F32),
                ((1, channels), F32),
                ((1, channels), F32),
                ((channels, hidden), F32),
            ],
            [
                pltpu.VMEM((part, total_width), F32),
                pltpu.VMEM((update_hidden, turned_width + update_hidden + 128), F32),
                pltpu.VMEM((hidden, channels), F32),
            ],
            0,
            8 * hidden * total_width,
            "message_weights_out",
            perm,
            16,
        )
        turn = lambda value: jnp.transpose(value, (0, 3, 1, 2))
        return (
            node_result,
            turn(edge_result),
            node_grad,
            turn(edge_grad),
            found[0],
            found[9],
            found[2].reshape(part),
            found[1],
            weight_in_grad,
            wide_bias_grad.reshape(wide),
            weight_out_grad,
            biases_grad,
            gains_grad,
            shifts_grad,
            found[3].T,
            found[5].reshape(update_hidden),
            found[4],
            found[8].reshape(channels),
            found[6].reshape(channels),
            found[7].reshape(channels),
        )

    return per_device


def solution(mesh):
    return jax.shard_map(
        build(mesh.shape["prot"], mesh.shape["res"], mesh.shape["mp"]),
        mesh=mesh,
        in_specs=(
            P("prot", "res", None),
            P("prot", "res", "mp", None),
            P("prot", "res", None),
            P("prot", "res", None, None),
            P("prot", "res"),
            P(None, None, "mp"),
            P(),
            P("mp"),
            P("mp", None),
            P(None, "mp"),
            P("mp"),
            P("mp", None),
            P(),
            P(),
            P(),
            P(),
            P(),
            P(),
            P(),
            P(),
            P(),
            P("prot", "res", None),
            P("prot", "res", "mp", None),
        ),
        out_specs=(
            P("prot", "res", None),
            P("prot", "res", "mp", None),
            P("prot", "res", None),
            P("prot", "res", "mp", None),
            P(None, None, "mp"),
            P(),
            P("mp"),
            P("mp", None),
            P(None, "mp"),
            P("mp"),
            P("mp", None),
            P(),
            P(),
            P(),
            P(),
            P(),
            P(),
            P(),
            P(),
            P(),
        ),
        check_vma=False,
    )
```

```python
import functools

import jax
import jax.numpy as jnp
from jax import lax
from jax.experimental import pallas as pl
from jax.experimental.pallas import tpu as pltpu
from jax.sharding import PartitionSpec as P

EPSILON = 1e-05
F32 = jnp.float32
PINNED = ("prepare",)
BF16 = jnp.bfloat16
DEAD = -30000.0
CUBIC = 0.044715
ROOT = 0.7978845608028654


def dot(left, right):
    return jnp.dot(left, right, preferred_element_type=F32)


def dot_nt(left, right):
    return lax.dot_general(left, right, (((1,), (1,)), ((), ())), preferred_element_type=F32)


def gelu_pair(value):
    square = value * value
    gate = 0.5 + 0.5 * jnp.tanh(value * (ROOT + (ROOT * CUBIC) * square))
    out = value * gate
    slope = gate + (out - out * gate) * (2.0 * ROOT + (6.0 * ROOT * CUBIC) * square)
    return out, slope


def low(value):
    return jnp.asarray(value, BF16)


def gelu_pair_low(value):
    value = value.astype(BF16)
    square = value * value
    inner = value * (low(-2.0 * ROOT) + low(-2.0 * ROOT * CUBIC) * square)
    power = jnp.exp(jnp.minimum(inner, low(80.0)))
    gate = pl.reciprocal(low(1.0) + power, approx=True)
    out = value * gate
    slope = gate + (out * (power * gate)) * (low(2.0 * ROOT) + low(6.0 * ROOT * CUBIC) * square)
    return out, slope


def activation(value):
    return jax.nn.gelu(value, approximate=True)


def activation_grad(value, upstream):
    return jax.vjp(activation, value)[1](upstream)[0]


def norm_forward(value, gain, shift):
    centred = value - jnp.mean(value, axis=-1, keepdims=True)
    inverse = lax.rsqrt(jnp.mean(centred * centred, axis=-1, keepdims=True) + EPSILON)
    normed = centred * inverse
    return (normed * gain + shift, normed, inverse)


def norm_backward(upstream, normed, inverse, gain):
    scaled = upstream * gain
    inner = (
        scaled
        - jnp.mean(scaled, axis=-1, keepdims=True)
        - normed * jnp.mean(scaled * normed, axis=-1, keepdims=True)
    )
    return inverse * inner


def chosen_row(value, row):
    rows = lax.broadcasted_iota(jnp.int32, value.shape, 0)
    return jnp.sum(jnp.where(rows == row, value.astype(F32), 0.0), axis=0, keepdims=True)


def selector(slot_row, rows):
    positions = lax.broadcasted_iota(jnp.int16, (rows, slot_row.shape[1]), 0)
    return jnp.where(positions == slot_row.astype(jnp.int16), low(1.0), low(0.0))


def dot_tn(left, right):
    return lax.dot_general(left, right, (((0,), (0,)), ((), ())), preferred_element_type=F32)


def masked_table(fixed, term, dead):
    positions = lax.broadcasted_iota(jnp.int32, term.shape, 1)
    term = jnp.where(positions == dead, DEAD, term).astype(BF16)
    return jnp.concatenate([fixed, term], axis=1)


def message_forward_body(perm_ref, *refs, count, calls, start):
    edge_ref, slot_ref, node_ref, arrive_ref, fixed_ref, count_ref = refs[:6]
    weights = refs[6 : 6 + count]
    others = refs[6 + count : 6 + 2 * count]
    refs = refs[6 + 2 * count :]
    slope_ref, mean_ref = refs[:2]
    parts = refs[2 : 2 + calls]
    weight_ref, table_ref, self_ref, sum_ref, operand_ref, value_ref = refs[2 + calls :]
    number = pl.program_id(0)
    group = operand_ref.shape[0]
    dead = perm_ref[count]
    steps, channels, lanes = edge_ref.shape[1:]
    width = node_ref.shape[2]

    @pl.when(number == 0)
    def _():
        fill_weights(perm_ref, weights, others, weight_ref, count)

    nodes = node_ref[0]
    arrive = arrive_ref[...].reshape(-1, width)
    pool = lanes + arrive.shape[0]
    rows = jnp.concatenate([nodes, arrive], axis=0)
    term = dot_nt(weight_ref[:, width : 2 * width], rows)
    table_ref[...] = masked_table(fixed_ref[...], term, dead)
    bias = weight_ref[:, 3 * width : 3 * width + 1].astype(F32)
    self_ref[...] = dot_nt(weight_ref[:, 0:width], nodes) + bias
    sum_ref[...] = jnp.zeros_like(sum_ref)

    def some(index, carry):
        spots = [index * group + spot for spot in range(group)]
        for spot in range(group):
            operand_ref[spot, 0:channels] = edge_ref[0, spots[spot]]
            operand_ref[spot, channels:] = selector(slot_ref[0, pl.ds(spots[spot], 1), :], pool)
        for spot in range(group):
            value_ref[spot] = dot(table_ref[...], operand_ref[spot])
        total = sum_ref[...]
        for spot in range(group):
            out, slope = gelu_pair_low(value_ref[spot] + self_ref[...])
            slope_ref[0, spots[spot]] = slope
            total = total + out.astype(F32)
        sum_ref[...] = total
        return carry

    lax.fori_loop(0, steps // group, some, 0)
    scale = 1.0 / jnp.maximum(chosen_row(count_ref[...], perm_ref[number + start]), 1.0)
    mean = (sum_ref[...] * scale).astype(BF16)
    mean_ref[0] = mean
    total = dot_tn(mean, weight_ref[:, 2 * width : 3 * width]).astype(BF16)
    for spot in range(calls):

        @pl.when(number == spot)
        def _(spot=spot):
            parts[spot][...] = total


def send_selector(rows, lanes):
    peers, slots = rows.shape
    lane = lax.broadcasted_iota(jnp.int32, (slots, lanes), 1).astype(F32)
    parts = []
    for peer in range(peers):
        column = jnp.broadcast_to(rows[peer : peer + 1, :].astype(F32), (8, slots)).T[:, 0:1]
        parts.append(jnp.where(lane == column, 1.0, 0.0).astype(BF16))
    return jnp.concatenate(parts, axis=0)


def pack_body(perm_ref, nodes_ref, output_ref, bias_ref, send_ref, node_ref, pack_ref, leave_ref, all_ref, *, count):
    width = output_ref.shape[1]
    part = output_ref.shape[0]
    all_ref[:, 0:width] = nodes_ref[0].T
    all_ref[:, width : 2 * width] = nodes_ref[1].T
    all_ref[:, 2 * width : 3 * width] = output_ref[...]
    tall = lambda row: jnp.broadcast_to(row, (8, row.shape[1])).T[:, 0:1]
    bias = tall(bias_ref[...].astype(F32).reshape(1, -1)).astype(BF16)
    all_ref[:, 3 * width :] = jnp.broadcast_to(bias, (part, all_ref.shape[1] - 3 * width))
    half = part // 2
    start = pl.multiple_of(perm_ref[count + 1] * half, half)
    pack_ref[...] = all_ref[pl.ds(start, half), :]
    proteins, lanes, _ = node_ref.shape
    for spot in range(proteins):
        table = send_selector(send_ref[spot, 0], lanes)
        leave_ref[:, spot] = dot(table, node_ref[spot]).astype(BF16).reshape(leave_ref[:, spot].shape)


def prepare_body(
    perm_ref,
    edge_ref,
    turned_ref,
    out_ref,
    hidden_bias_ref,
    gain_ref,
    shift_ref,
    branch_ref,
    wide_ref,
    biases_ref,
    gains_ref,
    shifts_ref,
    counts_ref,
    send_ref,
    node_ref,
    up_ref,
    wide_in_ref,
    wide_out_ref,
    weight_ref,
    weight_t_ref,
    column_ref,
    out_t_ref,
    turned_edge_ref,
    vector_ref,
    share_ref,
    table_ref,
    wide_bias_ref,
    own_node_ref,
    own_up_ref,
    block_ref,
    *,
    count,
):
    row = lambda ref: ref[...].astype(F32).reshape(1, -1)
    core = perm_ref[count + 1]
    half = wide_out_ref.shape[0] // 2
    start = pl.multiple_of(core * half, half)
    block_ref[0:half, :] = wide_in_ref[:, pl.ds(start, half)].T
    block_ref[half : 2 * half, :] = wide_out_ref[pl.ds(start, half), :]
    wide = row(wide_ref)
    line = jnp.where(core == 0, wide[:, 0:half], wide[:, half:])
    block_ref[2 * half :, 0:half] = jnp.broadcast_to(line, (16, half)).astype(BF16)
    block_ref[2 * half :, half:] = jnp.zeros((16, block_ref.shape[1] - half), BF16)
    part = edge_ref.shape[1] // count
    for spot in range(count):
        span = slice(spot * part, (spot + 1) * part)
        block = edge_ref[:, pl.ds(pl.multiple_of(perm_ref[spot] * part, part), part)]
        weight_ref[:, span] = block
        weight_t_ref[span, :] = block.T
    tall = lambda row: jnp.broadcast_to(row, (8, row.shape[1])).T[:, 0:1]
    channels = edge_ref.shape[0]
    lane = lax.broadcasted_iota(jnp.int32, (channels, 128), 1)
    column_ref[...] = jnp.where(
        lane == 0,
        tall(row(hidden_bias_ref)),
        jnp.where(lane == 1, tall(row(gain_ref)), tall(row(shift_ref))),
    )
    hidden = out_ref.shape[0]
    extra = out_t_ref.shape[1] - hidden
    lane = lax.broadcasted_iota(jnp.int32, (channels, extra), 1)
    last = jnp.where(lane == 0, tall(row(branch_ref)), 0.0).astype(BF16)
    out_t_ref[...] = jnp.concatenate([out_ref[...].T, last], axis=1)
    turned_edge_ref[...] = turned_ref[:, turned_ref.shape[1] - channels :].T
    vector_ref[0:2, :] = biases_ref[...].astype(F32)
    vector_ref[2:4, :] = gains_ref[...].astype(F32)
    vector_ref[4:6, :] = shifts_ref[...].astype(F32)
    vector_ref[6:8, :] = jnp.zeros((2, vector_ref.shape[1]), F32)
    me = perm_ref[0]
    counts = chosen_row(counts_ref[...], me)
    share = counts * (1.0 / jnp.maximum(counts, 1.0))
    share_ref[...] = jnp.broadcast_to(tall(share), share_ref.shape)
    table_ref[...] = send_selector(send_ref[me, 0], table_ref.shape[1])
    wide_bias_ref[...] = jnp.broadcast_to(wide, wide_bias_ref.shape).astype(BF16)
    own_node_ref[...] = node_ref[...]
    own_up_ref[...] = up_ref[...]


def fill_weights(perm_ref, mine, other, target, count):
    core = perm_ref[count + 1]
    half = mine[0].shape[0]
    for spot in range(count):
        for place, value in ((core, mine[spot][...]), (1 - core, other[spot][...])):
            start = pl.multiple_of((2 * spot + place) * half, half)
            target[pl.ds(start, half), :] = value


def forward_body(*refs, count):
    parts = refs[:count]
    node_ref, share_ref, vector_ref, send_ref, turned_ref = refs[count : count + 5]
    blocks = list(refs[count + 5 : 2 * count + 5])
    blocks = blocks + [refs[2 * count + 5].at[spot] for spot in range(count)]
    one_ref, two_ref, first_ref, second_ref, leave_ref, term_ref, slope_ref = refs[2 * count + 6 :]
    total = parts[0][...].astype(F32)
    for spot in range(1, count):
        total = total + parts[spot][...].astype(F32)
    value = node_ref[0].astype(F32) + total + share_ref[:, 0:1] * vector_ref[0:1, :]
    one_ref[...] = value
    first_norm, _, _ = norm_forward(value, vector_ref[2:3, :], vector_ref[4:5, :])
    first_low = first_norm.astype(BF16)
    first_ref[...] = first_low
    value = first_norm + vector_ref[1:2, :]
    for spot in range(2 * count):
        block = blocks[spot]
        half = (block.shape[0] - 16) // 2
        pre = dot_nt(first_low, block[0:half, :]) + block[2 * half : 2 * half + 1, 0:half].astype(F32)
        out, slope = gelu_pair(pre)
        slope_ref[:, spot * half : (spot + 1) * half] = slope.astype(BF16)
        value = value + dot(out.astype(BF16), block[half : 2 * half, :])
    two_ref[...] = value
    second_norm, _, _ = norm_forward(value, vector_ref[3:4, :], vector_ref[5:6, :])
    second = second_norm.astype(BF16)
    second_ref[...] = second
    leave_ref[...] = dot(send_ref[...], second).astype(BF16)
    lanes, width = second.shape
    term_ref[:, 0:lanes] = dot_nt(turned_ref[:, 0:width], second).astype(BF16)
    term_ref[:, lanes:] = dot_nt(turned_ref[:, width : 2 * width], second).astype(BF16)


def update_body(perm_ref, *refs, count, calls, first_call, joint):
    edge_ref, slot_ref, up_ref = refs[:3]
    terms = refs[3 : 3 + calls]
    if joint:
        refs = refs[: 3 + calls] + refs[3:]
        hidden = refs[3 + 2 * calls].shape[0]
        remotes = [ref.at[hidden:, :] for ref in terms]
        terms = [ref.at[0:hidden, :] for ref in terms]
    else:
        remotes = refs[3 + calls : 3 + 2 * calls]
    turned_ref, column_ref, out_t_ref, out_ref, weight_ref = refs[3 + 2 * calls : 8 + 2 * calls]
    refs = refs[8 + 2 * calls :]
    if not first_call:
        start_ref = refs[0]
        refs = refs[2:]
    result_ref, part_ref = refs[:2]
    sums = refs[2 : 2 + calls]
    total_ref = refs[2 + calls]
    table_ref, self_ref, table_grad_ref, self_grad_ref = refs[3 + calls : 7 + calls]
    gain_grad_ref, shift_grad_ref, edge_grad_ref, out_grad_ref = refs[7 + calls : 11 + calls]
    gain_ref, shift_ref, operand_ref, out_low_ref, mixed_ref, grad_ref, product_ref, value_ref, slope_ref = refs[
        11 + calls :
    ]
    group = operand_ref.shape[1] // edge_ref.shape[3]
    number = pl.program_id(0)
    dead = perm_ref[count]
    steps, channels, lanes = edge_ref.shape[1:]
    hidden = turned_ref.shape[0]
    width = remotes[0].shape[1]
    pool = lanes + remotes[0].shape[0]
    extra = out_t_ref.shape[1] - hidden
    grads = (edge_grad_ref, out_grad_ref, gain_grad_ref, shift_grad_ref)
    bases = (0, 256, 512, 640)

    @pl.when(number == 0)
    def _():
        for ref, base in zip(grads, bases):
            if first_call:
                ref[...] = jnp.zeros_like(ref)
            else:
                ref[...] = start_ref[:, base : base + ref.shape[1]]
        gain_ref[...] = jnp.broadcast_to(column_ref[:, 1:2], gain_ref.shape)
        shift_ref[...] = jnp.broadcast_to(column_ref[:, 2:3], shift_ref.shape)

    for spot in range(calls):

        @pl.when(number == spot)
        def _(spot=spot):
            remote = dot_nt(turned_ref[:, width : 2 * width], remotes[spot][...])
            term = jnp.concatenate([terms[spot][:, lanes:].astype(F32), remote], axis=1)
            table_ref[...] = masked_table(turned_ref[:, 2 * width :], term, dead)
            self_ref[...] = terms[spot][:, 0:lanes].astype(F32) + column_ref[:, 0:1]

    table_grad_ref[...] = jnp.zeros_like(table_grad_ref)
    self_grad_ref[...] = jnp.zeros_like(self_grad_ref)
    share = 1.0 / channels
    first = lax.broadcasted_iota(jnp.int32, (extra, lanes), 0) == 0
    spans = [slice(spot * lanes, (spot + 1) * lanes) for spot in range(group)]
    total = lambda value: jnp.sum(value, axis=0, keepdims=True)

    def some(index, carry):
        spots = [index * group + spot for spot in range(group)]
        for spot, span in zip(spots, spans):
            slot_row = slot_ref[0, pl.ds(spot, 1), :]
            operand_ref[0:channels, span] = edge_ref[0, spot]
            operand_ref[channels:, span] = selector(slot_row, pool)
            live = jnp.where(first & (slot_row != dead), 1.0, 0.0)
            out_low_ref[hidden:, span] = live.astype(BF16)
        for span in spans:
            value_ref[:, span] = dot(table_ref[...], operand_ref[:, span])
        for span in spans:
            out, slope = gelu_pair_low(value_ref[:, span] + self_ref[...])
            out_low_ref[0:hidden, span] = out
            slope_ref[:, span] = slope
        for span in spans:
            value_ref[:, span] = dot(out_t_ref[...], out_low_ref[:, span])
        for spot, span in zip(spots, spans):
            value = edge_ref[0, spot].astype(F32) + value_ref[:, span]
            centred = value - total(value) * share
            inverse = lax.rsqrt(total(centred * centred) * share + EPSILON)
            normed = centred * inverse
            gain = gain_ref[...]
            result_ref[0, spot] = (normed * gain + shift_ref[...]).astype(BF16)
            scaled = up_ref[0, spot].astype(F32) * gain
            product = scaled * normed
            product_ref[:, span] = product.astype(BF16)
            mixed = inverse * (scaled - total(scaled) * share - normed * (total(product) * share))
            mixed_ref[:, span] = mixed.astype(BF16)
        for span in spans:
            value_ref[:, span] = dot(out_ref[...], mixed_ref[:, span])
        for span in spans:
            grad = slope_ref[:, span].astype(F32) * value_ref[:, span]
            self_grad_ref[...] += grad
            grad_ref[:, span] = grad.astype(BF16)
        out_grad_ref[...] += dot_nt(mixed_ref[...], out_low_ref[...])
        for spot, span in zip(spots, spans):
            edge = dot(weight_ref[...], grad_ref[:, span])
            part_ref[0, spot] = (mixed_ref[:, span].astype(F32) + edge).astype(BF16)
        table_grad_ref[...] += dot_nt(grad_ref[...], operand_ref[...])
        gain_grad_ref[...] += dot_nt(product_ref[...], jnp.ones((8, group * lanes), BF16))
        for spot in spots:
            shift_grad_ref[...] += dot_nt(up_ref[0, spot], jnp.ones((8, lanes), BF16))
        return carry

    lax.fori_loop(0, steps // group, some, 0)
    edge_grad_ref[...] += table_grad_ref[:, 0:channels]
    for spot in range(calls):

        @pl.when(number == spot)
        def _(spot=spot):
            sums[spot][:, 0:lanes] = self_grad_ref[...].astype(BF16)
            sums[spot][:, lanes:] = table_grad_ref[:, channels:].astype(BF16)

    @pl.when(number == calls - 1)
    def _():
        for ref, base in zip(grads, bases):
            total_ref[:, base : base + ref.shape[1]] = ref[...]


def return_body(perm_ref, *refs, count):
    sums = refs[:count]
    turned_ref, up_ref = refs[count : count + 2]
    second_ref, leave_ref, sum_ref = refs[count + 2 :]
    total = sums[0][...].astype(F32)
    for spot in range(1, count):
        total = total + sums[spot][...].astype(F32)
    low = total.astype(BF16)
    lanes, width = second_ref.shape
    back = dot_tn(low[:, lanes:], turned_ref[:, width : 2 * width])
    leave_ref[...] = back[lanes:].astype(BF16)
    second_ref[...] = (
        up_ref[0].astype(F32) + dot_tn(low[:, 0:lanes], turned_ref[:, 0:width]) + back[0:lanes]
    )
    sum_ref[...] = total


def update_weights_body(perm_ref, sum_ref, low_ref, arrive_ref, grad_ref, column_ref, whole_ref):
    total = sum_ref[...]
    low = total.astype(BF16)
    lanes = low_ref.shape[0]
    channels = grad_ref.shape[0]
    hidden = low.shape[0]
    rows = jnp.concatenate([low_ref[...], arrive_ref[...]], axis=0)
    lane = lax.broadcasted_iota(jnp.int32, (channels, 128), 1)
    vectors = jnp.where(
        lane == 0,
        jnp.sum(total[:, 0:lanes], axis=1, keepdims=True),
        jnp.where(
            lane == 1,
            grad_ref[:, 512:513] / column_ref[:, 1:2],
            jnp.where(lane == 2, grad_ref[:, 640:641], grad_ref[:, 256 + hidden : 257 + hidden]),
        ),
    )
    whole_ref[...] = jnp.concatenate(
        [
            dot(low[:, 0:lanes], low_ref[...]),
            dot(low[:, lanes:], rows),
            grad_ref[:, 0:channels],
            grad_ref[:, 256 : 256 + hidden],
            vectors,
        ],
        axis=1,
    )


def backward_body(*refs, count):
    second_ref, return_ref, send_ref, one_ref, two_ref, share_ref, vector_ref, slope_ref = refs[:8]
    blocks = list(refs[8 : 8 + count])
    blocks = blocks + [refs[8 + count].at[spot] for spot in range(count)]
    aggregate_ref, forward_ref, sum_ref, grad_ref = refs[9 + count :]
    lanes = one_ref.shape[0]
    second_grad = second_ref[...] + dot_tn(send_ref[...], return_ref[...])
    _, first_normed, first_inverse = norm_forward(
        one_ref[...], vector_ref[2:3, :], vector_ref[4:5, :]
    )
    _, second_normed, second_inverse = norm_forward(
        two_ref[...], vector_ref[3:4, :], vector_ref[5:6, :]
    )
    total = lambda value: jnp.sum(value, axis=0, keepdims=True)
    grad_ref[3:4, :] = total(second_grad * second_normed)
    grad_ref[5:6, :] = total(second_grad)
    sum_two = norm_backward(second_grad, second_normed, second_inverse, vector_ref[3:4, :])
    low = sum_two.astype(BF16)
    forward_ref[0:lanes, :] = low
    grad_ref[1:2, :] = total(low.astype(F32))
    first_grad = sum_two
    for spot in range(2 * count):
        block = blocks[spot]
        half = (block.shape[0] - 16) // 2
        slope = slope_ref[:, spot * half : (spot + 1) * half].astype(F32)
        grad = (slope * dot_nt(low, block[half : 2 * half, :])).astype(BF16)
        first_grad = first_grad + dot(grad, block[0:half, :])
    grad_ref[2:3, :] = total(first_grad * first_normed)
    grad_ref[4:5, :] = total(first_grad)
    sum_one = norm_backward(first_grad, first_normed, first_inverse, vector_ref[2:3, :])
    sum_ref[...] = sum_one
    aggregate = sum_one.astype(BF16)
    aggregate_ref[...] = aggregate
    grad_ref[0:1, :] = total(share_ref[:, 0:1] * aggregate.astype(F32))
    grad_ref[6:16, :] = jnp.zeros((10, grad_ref.shape[1]), F32)
    forward_ref[lanes:, :] = grad_ref[...].astype(BF16)


def message_backward_body(perm_ref, *refs, count, calls, first_call):
    edge_ref, slot_ref, slope_ref, part_ref, edge_weight_ref, count_ref = refs[:6]
    weights = refs[6 : 6 + count]
    others = refs[6 + count : 6 + 2 * count]
    ups = refs[6 + 2 * count : 6 + 2 * count + calls]
    refs = refs[6 + 2 * count + calls :]
    if not first_call:
        node_ref, arrive_ref, own_node_ref, own_arrive_ref, mean_ref, own_mean_ref = refs[:6]
        own_up_ref, own_low_ref, own_edge_ref, whole_ref = refs[6:10]
        refs = refs[11:]
    grad_ref = refs[0]
    backs = refs[1 : 1 + calls]
    low_out_ref, edge_out_ref = refs[1 + calls : 3 + calls]
    weight_ref, up_ref, table_grad_ref, self_grad_ref = refs[3 + calls : 7 + calls]
    operand_ref, grad_low_ref = refs[7 + calls : 9 + calls]
    if not first_call:
        mine_ref, other_ref = low_out_ref, edge_out_ref
        low_ref, row_ref, mean_all_ref, up_all_ref = refs[9 + calls : 13 + calls]
        edge_total_ref, bias_ref, total_ref, out_total_ref = refs[13 + calls :]
    group = operand_ref.shape[1] // edge_ref.shape[3]
    number = pl.program_id(0)
    steps, channels, lanes = edge_ref.shape[1:]
    part = 2 * weights[0].shape[0]
    hidden = part * count
    width = backs[0].shape[1]
    pool = backs[0].shape[0]

    @pl.when(number == 0)
    def _():
        fill_weights(perm_ref, weights, others, weight_ref, count)
        if not first_call:
            low_ref[:, 0:pool] = own_low_ref[...]
            row_ref[0:lanes, :] = own_node_ref[0]
            row_ref[lanes:pool, :] = own_arrive_ref[...].reshape(-1, width)
            mean_all_ref[:, 0:lanes] = own_mean_ref[0]
            up_all_ref[0:lanes, :] = own_up_ref[...]
            edge_total_ref[...] = own_edge_ref[...]

    for spot in range(calls):

        @pl.when(number == spot)
        def _(spot=spot):
            value = dot_nt(weight_ref[:, 2 * width : 3 * width], ups[spot][...])
            number_of = perm_ref[spot if first_call else spot + 1]
            scale = 1.0 / jnp.maximum(chosen_row(count_ref[...], number_of), 1.0)
            up_ref[...] = (value * scale).astype(BF16)
            if not first_call:
                at = (spot + 1) * pool
                row_ref[at : at + lanes, :] = node_ref[0]
                row_ref[at + lanes : at + pool, :] = arrive_ref[...].reshape(-1, width)
                at = (spot + 1) * lanes
                mean_all_ref[:, at : at + lanes] = mean_ref[0]
                up_all_ref[at : at + lanes, :] = ups[spot][...]

    table_grad_ref[...] = jnp.zeros_like(table_grad_ref)
    self_grad_ref[...] = jnp.zeros_like(self_grad_ref)
    spans = [slice(spot * lanes, (spot + 1) * lanes) for spot in range(group)]

    def some(index, carry):
        spots = [index * group + spot for spot in range(group)]
        for spot, span in zip(spots, spans):
            operand_ref[0:channels, span] = edge_ref[0, spot]
            operand_ref[channels:, span] = selector(slot_ref[0, pl.ds(spot, 1), :], pool)
        total = self_grad_ref[...]
        for spot, span in zip(spots, spans):
            grad = slope_ref[0, spot] * up_ref[...]
            grad_low_ref[:, span] = grad
            total = total + grad.astype(F32)
        self_grad_ref[...] = total
        for spot, span in zip(spots, spans):
            edge = dot(edge_weight_ref[...], grad_low_ref[:, span])
            grad_ref[0, spot] = (part_ref[0, spot].astype(F32) + edge).astype(BF16)
        table_grad_ref[...] += dot_nt(grad_low_ref[...], operand_ref[...])
        return carry

    lax.fori_loop(0, steps // group, some, 0)
    self_low = self_grad_ref[...].astype(BF16)
    pool_low = table_grad_ref[:, channels:].astype(BF16)
    self_back = dot_tn(self_low, weight_ref[:, 0:width])
    pool_back = dot_tn(pool_low, weight_ref[:, width : 2 * width])
    low_both = jnp.concatenate(
        [
            jnp.concatenate([self_low, jnp.zeros((hidden, pool - lanes), BF16)], axis=1),
            pool_low,
        ],
        axis=0,
    )
    for spot in range(calls):

        @pl.when(number == spot)
        def _(spot=spot):
            backs[spot][0:lanes, :] = (self_back + pool_back[0:lanes]).astype(BF16)
            backs[spot][lanes:, :] = pool_back[lanes:].astype(BF16)
            if not first_call:
                low_ref[:, (spot + 1) * pool : (spot + 2) * pool] = low_both

    if first_call:
        low_out_ref[...] = low_both
        edge_out_ref[...] = table_grad_ref[:, 0:channels]
        return
    edge_total_ref[...] += table_grad_ref[:, 0:channels]

    @pl.when(number == calls - 1)
    def _():
        total_ref[...] = dot(low_ref[...], row_ref[...])
        out_total_ref[...] = dot(mean_all_ref[...], up_all_ref[...])
        ones = jnp.ones((row_ref.shape[0], 128), BF16)
        bias_ref[...] = dot(low_ref[0:hidden, :], ones)
        core = perm_ref[count + 1]
        half = part // 2
        rows = whole_ref.shape[0] // count // 2
        for spot in range(count):
            for place, ref in ((core, mine_ref), (1 - core, other_ref)):
                first = pl.multiple_of(spot * part + place * half, half)
                kind = ref.dtype
                ref[spot, 0:half, 0:width] = total_ref[pl.ds(first, half), :].astype(kind)
                ref[spot, 0:half, width : 2 * width] = total_ref[pl.ds(hidden + first, half), :].astype(kind)
                ref[spot, 0:half, 2 * width : 3 * width] = out_total_ref[pl.ds(first, half), :].astype(kind)
                start = pl.multiple_of((place * count + perm_ref[spot]) * rows, 8)
                wide = whole_ref.shape[1]
                below = jnp.concatenate(
                    [
                        whole_ref[pl.ds(start, rows), :],
                        jnp.zeros((ref.shape[1] - half - rows, wide), F32),
                    ],
                    axis=0,
                )
                ref[spot, half:, 0:wide] = below.astype(kind)
                ref[spot, half:, wide:] = jnp.zeros((below.shape[0], ref.shape[2] - wide), kind)
                both = jnp.concatenate(
                    [
                        edge_total_ref[pl.ds(first, half), :],
                        bias_ref[pl.ds(first, half), 0 : ref.shape[2] - 3 * width - channels],
                    ],
                    axis=1,
                )
                ref[spot, 0:half, 3 * width :] = both.astype(kind)


def wide_body(
    perm_ref, low_ref, forward_ref, weight_ref, bias_ref, output_ref, mine_ref, other_ref, all_ref, *, count
):
    width = low_ref.shape[1]
    wide = weight_ref.shape[1]
    step = forward_ref.shape[0] // count
    lanes = step - 16
    low = low_ref[...]
    forward = jnp.concatenate(
        [forward_ref[spot * step : spot * step + lanes, :] for spot in range(count)], axis=0
    )
    lines = None
    for spot in range(count):
        line = forward_ref[spot * step + lanes : (spot + 1) * step, :].astype(F32)
        lines = line if spot == 0 else lines + line
    pre = dot(low, weight_ref[...]) + bias_ref[0:1, :].astype(F32)
    out, slope = gelu_pair_low(pre)
    grad = slope.astype(F32) * dot_nt(forward, output_ref[...])
    all_ref[0:width, :] = dot_tn(low, grad.astype(BF16))
    all_ref[width : width + wide, :] = dot_tn(out, forward)
    at = width + wide
    total = jnp.broadcast_to(jnp.sum(grad, axis=0, keepdims=True), (8, wide))
    all_ref[at : at + 8, :] = total
    all_ref[at + 8 : at + 16, :] = lines[0:8]
    all_ref[at + 16 :, :] = jnp.zeros((all_ref.shape[0] - at - 16, width), F32)
    half = mine_ref.shape[0]
    core = perm_ref[count + 1]
    mine_ref[...] = all_ref[pl.ds(pl.multiple_of(core * half, 8), half), :]
    other_ref[...] = all_ref[pl.ds(pl.multiple_of((1 - core) * half, 8), half), :].astype(BF16)


def wide_finish_body(
    perm_ref, mine_ref, other_ref, in_ref, out_ref, bias_ref, one_ref, two_ref, three_ref, all_ref, *, count
):
    core = perm_ref[count + 1]
    half = mine_ref.shape[0]
    all_ref[pl.ds(pl.multiple_of(core * half, 8), half), :] = mine_ref[...].astype(F32)
    all_ref[pl.ds(pl.multiple_of((1 - core) * half, 8), half), :] = other_ref[...].astype(F32)
    width = in_ref.shape[0]
    wide = out_ref.shape[0]
    in_ref[...] = all_ref[0:width, :]
    out_ref[...] = all_ref[width : width + wide, :]
    at = width + wide
    bias_ref[...] = all_ref[at : at + 1, :]
    one_ref[...] = all_ref[at + 8 : at + 10, :]
    two_ref[...] = all_ref[at + 10 : at + 12, :]
    three_ref[...] = all_ref[at + 12 : at + 14, :]


def late_finish_body(
    perm_ref,
    mine_ref,
    other_ref,
    mine_parts_ref,
    other_parts_ref,
    nodes_ref,
    output_ref,
    bias_ref,
    turned_ref,
    update_ref,
    hidden_bias_ref,
    gain_ref,
    shift_ref,
    branch_ref,
    edge_ref,
    own_ref,
    whole_ref,
    edges_ref,
    *,
    count,
):
    core = perm_ref[count + 1]
    part = own_ref.shape[0]
    half = part // 2
    width = output_ref.shape[1]
    rows = whole_ref.shape[0] // count // 2
    channels = edges_ref.shape[1]
    for place, ref, parts in ((core, mine_ref, mine_parts_ref), (1 - core, other_ref, other_parts_ref)):
        own_ref[pl.ds(pl.multiple_of(place * half, 8), half), :] = ref[...].astype(F32)
        for spot in range(count):
            value = parts[spot].astype(F32)
            start = pl.multiple_of((place * count + perm_ref[spot]) * rows, 8)
            whole_ref[pl.ds(start, rows), :] = value[0:rows, :]
            first = perm_ref[spot] * part + place * half
            for turn in range(half // 8):
                start = pl.multiple_of(first + 8 * turn, 8)
                edges_ref[pl.ds(start, 8), :] = value[rows:, turn * channels : (turn + 1) * channels]
    nodes_ref[0] = own_ref[:, 0:width].T
    nodes_ref[1] = own_ref[:, width : 2 * width].T
    output_ref[...] = own_ref[:, 2 * width : 3 * width]
    last = own_ref.shape[1]
    bias_ref[...] = own_ref[:, last - 128 :].T[127:128, :]
    end = turned_ref.shape[1]
    hidden = update_ref.shape[0]
    turned_ref[...] = whole_ref[:, 0:end]
    update_ref[...] = whole_ref[:, end : end + hidden].T
    vectors = whole_ref[:, end + hidden :].T
    hidden_bias_ref[...] = vectors[0:1, :]
    gain_ref[...] = vectors[1:2, :]
    shift_ref[...] = vectors[2:3, :]
    branch_ref[...] = vectors[3:4, :]
    edge_ref[...] = edges_ref[...].T


def place_body(perm_ref, *refs, count):
    for spot in range(count):

        @pl.when(pl.program_id(0) == spot)
        def _(spot=spot):
            refs[count][0] = refs[spot][...]


def held(value):
    return pltpu.with_memory_space_constraint(value, pltpu.HBM)


def group_of(total):
    for size in (15, 5, 4, 3, 2, 1):
        if total % size == 0:
            return size


def call(body, grid, ins, outs, scratch, flops, moved, name, perm=None, limit=56, aliases=()):
    whole = lambda block: (block, lambda *_: (0,) * len(block))
    in_specs = [
        pl.BlockSpec(memory_space=pl.ANY)
        if len(entry) == 2
        else pl.BlockSpec(*(entry[1:] if len(entry) == 3 else whole(entry[0].shape)))
        for entry in ins
    ]
    out_specs = [
        pl.BlockSpec(*(entry[2:] if len(entry) == 4 else whole(entry[0]))) for entry in outs
    ]
    spec = pltpu.PrefetchScalarGridSpec(
        num_scalar_prefetch=0 if perm is None else 1,
        grid=grid,
        in_specs=in_specs,
        out_specs=out_specs,
        scratch_shapes=scratch,
    )
    operands = [entry[0] for entry in ins]
    return pl.pallas_call(
        body,
        grid_spec=spec,
        out_shape=[(pltpu.HBM if name in PINNED else jax.ShapeDtypeStruct)(entry[0], entry[1]) for entry in outs],
        input_output_aliases={source + 1: target for source, target in aliases},
        compiler_params=pltpu.CompilerParams(
            dimension_semantics=("arbitrary",) * len(grid), vmem_limit_bytes=limit * 2**20
        ),
        cost_estimate=pl.CostEstimate(flops=flops, bytes_accessed=moved, transcendentals=0),
        name=name,
    )(*([] if perm is None else [perm]), *operands)


def build(prot_size, res_size, mp_size):
    def across(value, offset):
        pairs = [(spot, spot ^ offset) for spot in range(mp_size)]
        return lax.ppermute(value, "mp", pairs)

    def gather(value):
        return [value] + [across(value, offset) for offset in range(1, mp_size)]

    def scatter(parts):
        return [parts[0]] + [across(parts[offset], offset) for offset in range(1, mp_size)]

    def exchange(value):
        return lax.all_to_all(value, "res", split_axis=0, concat_axis=0, tiled=True)

    def block_parts(value):
        place = lax.axis_index("res")
        piece = value.shape[0] // res_size
        parts = [lax.dynamic_slice_in_dim(value, place * piece, piece, 0)]
        low = value.astype(BF16)
        for hop in range(1, res_size):
            target = lax.rem(place + hop, res_size)
            part = lax.dynamic_slice_in_dim(low, target * piece, piece, 0)
            pairs = [(spot, (spot + hop) % res_size) for spot in range(res_size)]
            parts.append(lax.ppermute(part, "res", pairs))
        return parts

    def block_gather(own):
        parts = [own]
        for hop in range(1, res_size):
            pairs = [(spot, (spot - hop) % res_size) for spot in range(res_size)]
            parts.append(lax.ppermute(own, "res", pairs))
        return parts

    def block_order(parts):
        place = lax.axis_index("res")
        piece = parts[0].shape[0]
        both = jnp.concatenate(parts + parts, axis=0)
        return lax.dynamic_slice_in_dim(both, (res_size - place) * piece, res_size * piece, 0)

    def swap(value):
        return lax.ppermute(value, "prot", [(0, 1), (1, 0)])

    def per_device(
        node_states,
        edge_states,
        neighbour_slots,
        send_rows,
        live_counts,
        message_nodes,
        message_edges,
        message_bias,
        message_output,
        feedforward_weight,
        feedforward_bias,
        feedforward_output,
        output_biases,
        norm_gains,
        norm_shifts,
        update_weight,
        update_bias,
        update_output,
        branch_bias,
        edge_gain,
        edge_shift,
        node_cotangent,
        edge_cotangent,
    ):
        proteins, lanes, width = node_states.shape
        own_k, channels = edge_states.shape[2:]
        slots = send_rows.shape[3]
        remote = res_size * slots
        pool = lanes + remote
        part = message_nodes.shape[2]
        hidden = part * mp_size
        update_hidden = update_output.shape[0]
        wide = feedforward_weight.shape[1]
        assert proteins == mp_size and prot_size == 2
        me = lax.axis_index("mp")
        core = lax.axis_index("prot")
        place = lax.axis_index("res")
        dead = lanes + place * slots
        order = [me ^ offset for offset in range(mp_size)]
        perm = jnp.stack(order + [dead, core]).astype(jnp.int32)

        def reorder(value, axis=0):
            size = value.shape[axis] // mp_size
            return jnp.concatenate(
                [lax.dynamic_slice_in_dim(value, spot * size, size, axis) for spot in order], axis=axis
            )

        message_pack, leaving = call(
            functools.partial(pack_body, count=mp_size),
            (1,),
            [
                (message_nodes,),
                (message_output,),
                (message_bias,),
                (send_rows,),
                (node_states,),
            ],
            [
                ((part // 2, 3 * width + 128), BF16),
                ((res_size, proteins, slots, width), BF16),
            ],
            [pltpu.VMEM((part, 3 * width + 128), BF16)],
            0,
            0,
            "pack",
            perm,
        )
        arriving = exchange(leaving)
        weights = gather(message_pack)
        other_weights = [swap(value) for value in weights]
        own_slots = lax.dynamic_slice_in_dim(neighbour_slots, me * own_k, own_k, 2)
        alive = lax.broadcasted_iota(jnp.int32, own_slots.shape, 2) + me * own_k < live_counts[..., None]
        own_slots = jnp.transpose(jnp.where(alive, own_slots, dead), (0, 2, 1))
        edges = jnp.transpose(edge_states, (0, 2, 3, 1))
        edge_up = jnp.transpose(edge_cotangent, (0, 2, 3, 1))
        turned = update_weight.T
        small = call(
            functools.partial(prepare_body, count=mp_size),
            (1,),
            [
                (message_edges,),
                (turned,),
                (update_output,),
                (update_bias,),
                (edge_gain,),
                (edge_shift,),
                (branch_bias,),
                (feedforward_bias,),
                (output_biases,),
                (norm_gains,),
                (norm_shifts,),
                (live_counts,),
                (send_rows,),
                (node_states, (1, lanes, width), lambda p, perm: (perm[0], 0, 0)),
                (node_cotangent, (1, lanes, width), lambda p, perm: (perm[0], 0, 0)),
                (feedforward_weight,),
                (feedforward_output,),
            ],
            [
                ((channels, hidden), BF16),
                ((hidden, channels), BF16),
                ((channels, 128), F32),
                ((channels, update_hidden + 16), BF16),
                ((channels, update_hidden), BF16),
                ((8, width), F32),
                ((lanes, 128), F32),
                ((remote, lanes), BF16),
                ((16, wide), BF16),
                ((1, lanes, width), BF16),
                ((1, lanes, width), BF16),
                ((wide + 16, width), BF16),
            ],
            [],
            0,
            0,
            "prepare",
            perm,
        )
        weights, other_weights, arriving, own_slots, small = lax.optimization_barrier(
            (weights, other_weights, arriving, own_slots, small)
        )
        (
            edge_weight,
            edge_weight_t,
            columns,
            out_t,
            turned_edge,
            vectors,
            share,
            own_table,
            wide_bias,
            own_node,
            own_up,
            block,
        ) = small
        blocks = gather(block)

        depth = channels + pool
        group = group_of(own_k)
        count = proteins * own_k * lanes
        by_step4 = lambda p, perm: (p, 0, 0, 0)
        by_step3 = lambda p, perm: (p, 0, 0)
        others = proteins - 1

        def shifted(start):
            return (
                lambda p, perm: (perm[p + start], 0, 0, 0),
                lambda p, perm: (perm[p + start], 0, 0),
                lambda p, perm: (0, perm[p + start], 0, 0),
            )

        edge_block = (1, own_k, channels, lanes)
        edge_shape = (proteins, own_k, channels, lanes)
        slope_shape = (proteins, own_k, hidden, lanes)
        slope_block = (1, own_k, hidden, lanes)

        def edge_ins(start):
            by_perm4, by_perm3, _ = shifted(start)
            return [(edges, edge_block, by_perm4), (own_slots, (1, own_k, lanes), by_perm3)]

        def row_ins(start):
            _, by_perm3, by_arrive = shifted(start)
            return [
                (node_states, (1, lanes, width), by_perm3),
                (arriving, (res_size, 1, slots, width), by_arrive),
            ]

        def message_forward(start, calls, after):
            slots_after, _ = lax.optimization_barrier((own_slots, after))
            found = call(
                functools.partial(message_forward_body, count=proteins, calls=calls, start=start),
                (calls,),
                [edge_ins(start)[0], (slots_after,) + edge_ins(start)[1][1:]]
                + row_ins(start)
                + [(edge_weight_t,), (live_counts,)]
                + [(value,) for value in weights + other_weights],
                [
                    ((calls, own_k, hidden, lanes), BF16, slope_block, by_step4),
                    ((calls, hidden, lanes), BF16, (1, hidden, lanes), by_step3),
                ]
                + [((lanes, width), BF16)] * calls,
                [
                    pltpu.VMEM((hidden, weights[0].shape[1]), BF16),
                    pltpu.VMEM((hidden, depth), BF16),
                    pltpu.VMEM((hidden, lanes), F32),
                    pltpu.VMEM((hidden, lanes), F32),
                    pltpu.VMEM((group, depth, lanes), BF16),
                    pltpu.VMEM((group, hidden, lanes), F32),
                ],
                2 * calls * own_k * lanes * depth * hidden,
                calls * own_k * lanes * (channels + hidden) * 2,
                "message_forward",
                perm,
            )
            return found[0], found[1], list(found[2:])

        slope_others, mean_others, part_others = message_forward(1, others, own_slots)
        slope_own, mean_own, part_own = message_forward(0, 1, part_others[0])
        parts = scatter(part_own + part_others)
        blocks, _ = lax.optimization_barrier((blocks, part_others[0]))
        other_blocks = swap(jnp.stack(blocks))
        one, two, first_low, second_low, leaving, own_term, wide_slope = call(
            functools.partial(forward_body, count=proteins),
            (),
            [(value,) for value in parts]
            + [(own_node,), (share,), (vectors,), (own_table,), (turned,)]
            + [(held(value),) for value in blocks]
            + [(held(other_blocks),)],
            [
                ((lanes, width), F32),
                ((lanes, width), F32),
                ((lanes, width), BF16),
                ((lanes, width), BF16),
                ((remote, width), BF16),
                ((update_hidden, 2 * lanes), BF16),
                ((lanes, wide * mp_size), BF16),
            ],
            [],
            4 * lanes * width * wide * mp_size,
            4 * width * wide * mp_size,
            "feed_forward",
            limit=24,
        )

        arrived = exchange(leaving.reshape(res_size, slots, width)).reshape(remote, width)
        joint = own_term.shape[1] == width
        if joint:
            terms = gather(jnp.concatenate([own_term, arrived], axis=0))
            pool_remotes = []
        else:
            terms = gather(own_term)
            pool_remotes = gather(arrived)
        all_low = lax.all_gather(first_low, "mp", axis=0, tiled=True)
        node_result = lax.all_gather(second_low[None], "mp", axis=0, tiled=True)
        turned_width = 2 * width + channels

        def edge_update(start, calls, earlier):
            by_perm4 = shifted(start)[0]
            ins = (
                edge_ins(start)
                + [(edge_up, edge_block, by_perm4)]
                + [(value,) for value in terms[start : start + calls]]
                + [(value,) for value in pool_remotes[start : start + calls]]
                + [(turned,), (columns,), (out_t,), (update_output,), (turned_edge,)]
            )
            aliases = ()
            if earlier is not None:
                ins = ins + [(earlier[1],), (earlier[0], None)]
                aliases = ((len(ins) - 1, 0),)
            found = call(
                functools.partial(
                    update_body,
                    count=proteins,
                    calls=calls,
                    first_call=earlier is None,
                    joint=joint,
                ),
                (calls,),
                ins,
                [
                    (edge_shape, BF16, edge_block, by_perm4),
                    ((calls, own_k, channels, lanes), BF16, edge_block, by_step4),
                ]
                + [((update_hidden, lanes + pool), BF16)] * calls
                + [((update_hidden, 768), F32)],
                [
                    pltpu.VMEM((update_hidden, depth), BF16),
                    pltpu.VMEM((update_hidden, lanes), F32),
                    pltpu.VMEM((update_hidden, depth), F32),
                    pltpu.VMEM((update_hidden, lanes), F32),
                    pltpu.VMEM((channels, 8), F32),
                    pltpu.VMEM((channels, 8), F32),
                    pltpu.VMEM((update_hidden, channels), F32),
                    pltpu.VMEM((channels, update_hidden + 16), F32),
                    pltpu.VMEM((channels, lanes), F32),
                    pltpu.VMEM((channels, lanes), F32),
                    pltpu.VMEM((depth, group * lanes), BF16),
                    pltpu.VMEM((update_hidden + 16, group * lanes), BF16),
                    pltpu.VMEM((channels, group * lanes), BF16),
                    pltpu.VMEM((update_hidden, group * lanes), BF16),
                    pltpu.VMEM((channels, group * lanes), BF16),
                    pltpu.VMEM((update_hidden, group * lanes), F32),
                    pltpu.VMEM((update_hidden, group * lanes), BF16),
                ],
                2 * calls * own_k * lanes * (2 * depth + 4 * channels) * update_hidden,
                calls * own_k * lanes * channels * 8,
                "edge_update",
                perm,
                aliases=aliases,
            )
            return found[0], found[-1], found[1], found[2:-1]

        edge_result, grads, edge_part_own, sums_own = edge_update(0, 1, None)
        edge_result, grads, edge_part_others, sums_others = edge_update(1, others, (edge_result, grads))
        sums_own, sums_others, all_low = lax.optimization_barrier((sums_own, sums_others, all_low))
        sums = scatter(list(sums_own) + list(sums_others))
        whole_width = turned_width + update_hidden + 128
        second_part, leaving, update_sums = call(
            functools.partial(return_body, count=proteins),
            (1,),
            [(value,) for value in sums]
            + [(turned,), (own_up,)],
            [
                ((lanes, width), F32),
                ((remote, width), BF16),
                ((update_hidden, lanes + pool), F32),
            ],
            [],
            2 * (lanes + pool) * width * update_hidden,
            (lanes + pool) * width * 2,
            "update_return",
            perm,
        )
        returned = exchange(leaving.reshape(res_size, slots, width)).reshape(remote, width)
        (whole,) = call(
            update_weights_body,
            (1,),
            [(update_sums,), (second_low,), (arrived,), (grads,), (columns,)],
            [((update_hidden, whole_width), F32)],
            [],
            2 * (lanes + pool) * width * update_hidden,
            (lanes + pool) * width * 2,
            "update_weights",
            perm,
        )
        whole, returned = lax.optimization_barrier((whole, returned))
        aggregate_grad, forward_grad, sum_one, _ = call(
            functools.partial(backward_body, count=proteins),
            (),
            [(second_part,), (returned,), (own_table,), (one,), (two,), (share,), (vectors,), (wide_slope,)]
            + [(held(value),) for value in blocks]
            + [(held(other_blocks),)],
            [
                ((lanes, width), BF16),
                ((lanes + 16, width), BF16),
                ((lanes, width), F32),
                ((16, width), F32),
            ],
            [],
            6 * lanes * width * wide * mp_size,
            4 * width * wide * mp_size,
            "feed_backward",
            limit=24,
        )
        ups = gather(aggregate_grad)
        all_forward = lax.all_gather(forward_grad, "mp", axis=0, tiled=True)
        total_width = 3 * width + -(-(channels + 1) // 128) * 128
        whole_rows = update_hidden // 2 // mp_size
        late_rows = -(-(part // 2 + whole_rows) // (8 * res_size)) * 8 * res_size
        late_shape = (proteins, late_rows, total_width)

        def message_backward(start, calls, earlier):
            by_perm4 = shifted(start)[0]
            ins = (
                edge_ins(start)
                + [
                    (slope_own if earlier is None else slope_others, slope_block, by_step4),
                    (edge_part_own if earlier is None else edge_part_others, edge_block, by_step4),
                    (edge_weight,),
                    (live_counts,),
                ]
                + [(value,) for value in weights + other_weights + ups[start : start + calls]]
            )
            aliases = ()
            scratch = [
                pltpu.VMEM((hidden, weights[0].shape[1]), BF16),
                pltpu.VMEM((hidden, lanes), BF16),
                pltpu.VMEM((hidden, depth), F32),
                pltpu.VMEM((hidden, lanes), F32),
                pltpu.VMEM((depth, group * lanes), BF16),
                pltpu.VMEM((hidden, group * lanes), BF16),
            ]
            if earlier is None:
                last = [((2 * hidden, pool), BF16), ((hidden, channels), F32)]
            else:
                mean_block = (1, hidden, lanes)
                ins = ins + row_ins(start)
                ins = ins + [
                    (node_states, (1, lanes, width), lambda p, perm: (perm[0], 0, 0)),
                    (arriving, (res_size, 1, slots, width), lambda p, perm: (0, perm[0], 0, 0)),
                    (mean_others, mean_block, by_step3),
                    (mean_own,),
                    (ups[0],),
                    (earlier[1],),
                    (earlier[2],),
                    (whole,),
                    (earlier[0], None),
                ]
                aliases = ((len(ins) - 1, 0),)
                last = [(late_shape, F32), (late_shape, BF16)]
                scratch = scratch + [
                    pltpu.VMEM((2 * hidden, proteins * pool), BF16),
                    pltpu.VMEM((proteins * pool, width), BF16),
                    pltpu.VMEM((hidden, proteins * lanes), BF16),
                    pltpu.VMEM((proteins * lanes, width), BF16),
                    pltpu.VMEM((hidden, channels), F32),
                    pltpu.VMEM((hidden, 128), F32),
                    pltpu.VMEM((2 * hidden, width), F32),
                    pltpu.VMEM((hidden, width), F32),
                ]
            found = call(
                functools.partial(
                    message_backward_body, count=proteins, calls=calls, first_call=earlier is None
                ),
                (calls,),
                ins,
                [(edge_shape, BF16, edge_block, by_perm4)] + [((pool, width), BF16)] * calls + last,
                scratch,
                2 * calls * own_k * lanes * (depth + channels) * hidden,
                calls * own_k * lanes * (3 * channels + hidden) * 2,
                "message_backward",
                perm,
                aliases=aliases,
            )
            return found[0], found[-2], found[-1], found[1 : 1 + calls]

        edge_grad, own_low, own_edge, back_own = message_backward(0, 1, None)
        edge_grad, late_mine, late_other, back_others = message_backward(
            1, others, (edge_grad, own_low, own_edge)
        )
        found = list(back_own) + list(back_others)
        late_swapped = swap(late_other)
        backs, late_mine, all_forward, node_result = lax.optimization_barrier(
            (found, late_mine, all_forward, node_result)
        )
        back = scatter(backs)
        late = late_mine + late_swapped.astype(F32)
        late_own = late[0]
        late_low = [late[offset].astype(BF16) for offset in range(1, mp_size)]
        all_forward, late_own, late_low = lax.optimization_barrier((all_forward, late_own, late_low))
        late_parts = scatter([late_own] + late_low)
        unit = prot_size * res_size * 8
        wide_rows = -(-(width + wide + 16) // unit) * unit
        early_mine, early_other = call(
            functools.partial(wide_body, count=proteins),
            (1,),
            [
                (all_low,),
                (all_forward,),
                (feedforward_weight,),
                (wide_bias,),
                (feedforward_output,),
            ],
            [((wide_rows // 2, width), F32), ((wide_rows // 2, width), BF16)],
            [pltpu.VMEM((wide_rows, width), F32)],
            10 * proteins * lanes * width * wide,
            8 * proteins * lanes * width,
            "feed_weights",
            perm,
        )
        back, early_other, early_mine = lax.optimization_barrier((back, early_other, early_mine))
        early_swapped = swap(early_other)
        total = sum(value.astype(F32) for value in back)
        leaving = total[lanes:].astype(BF16).reshape(res_size, slots, width)
        leaving, early_swapped = lax.optimization_barrier((leaving, early_swapped))
        early = (early_mine + early_swapped.astype(F32)).astype(BF16)
        early, leaving = lax.optimization_barrier((early, leaving))
        cut = early.shape[0] // 2
        early = jnp.concatenate(lax.psum((early[:cut], early[cut:]), "res"), axis=0)
        returned = exchange(leaving)
        node_grad = (
            sum_one
            + total[:lanes]
            + jnp.einsum(
                "sr,sd->rd", own_table, returned.reshape(remote, width), preferred_element_type=F32
            )
        ).astype(BF16)
        node_grad, late_parts = lax.optimization_barrier((node_grad, late_parts))
        late = sum(value.astype(F32) for value in late_parts)
        late_parts = block_parts(late)
        node_parts = gather(node_grad)
        late = sum(value.astype(F32) for value in late_parts).astype(BF16)
        late, node_parts = lax.optimization_barrier((late, node_parts))
        late_parts = block_gather(late)
        (node_grad,) = call(
            functools.partial(place_body, count=proteins),
            (proteins,),
            [(value,) for value in node_parts],
            [((proteins, lanes, width), BF16, (1, lanes, width), shifted(0)[1])],
            [],
            0,
            0,
            "place_rows",
            perm,
        )
        early, node_grad, late_parts = lax.optimization_barrier((early, node_grad, late_parts))
        late = block_order(late_parts)
        whole = late[part // 2 : part // 2 + whole_rows, :whole_width]
        late = late[: part // 2]
        early_swapped = swap(early)
        late_swapped = swap(late)
        fold = late[:, 3 * width : 3 * width + channels].reshape(-1, 8, channels)
        fold = jnp.transpose(fold, (1, 0, 2)).reshape(8, -1)
        shared_parts = gather(jnp.concatenate([whole, fold], axis=0))
        weight_in_grad, weight_out_grad, wide_bias_grad, biases_grad, gains_grad, shifts_grad = call(
            functools.partial(wide_finish_body, count=proteins),
            (1,),
            [(early,), (early_swapped,)],
            [
                ((width, wide), F32),
                ((wide, width), F32),
                ((1, wide), F32),
                ((2, width), F32),
                ((2, width), F32),
                ((2, width), F32),
            ],
            [pltpu.VMEM((wide_rows, width), F32)],
            0,
            8 * wide_rows * width,
            "feed_weights_out",
            perm,
        )
        weight_in_grad, shared_parts, late_swapped = lax.optimization_barrier(
            (weight_in_grad, shared_parts, late_swapped)
        )
        shared = jnp.stack(shared_parts)
        found = call(
            functools.partial(late_finish_body, count=proteins),
            (1,),
            [(late,), (late_swapped,), (shared,), (swap(shared),)],
            [
                ((2, width, part), F32),
                ((part, width), F32),
                ((1, part), F32),
                ((update_hidden, turned_width), F32),
                ((update_hidden, channels), F32),
                ((1, update_hidden), F32),
                ((1, channels), F32),
                ((1, channels), F32),
                ((1, channels), F32),
                ((channels, hidden), F32),
            ],
            [
                pltpu.VMEM((part, total_width), F32),
                pltpu.VMEM((update_hidden, turned_width + update_hidden + 128), F32),
                pltpu.VMEM((hidden, channels), F32),
            ],
            0,
            8 * hidden * total_width,
            "message_weights_out",
            perm,
            16,
        )
        turn = lambda value: jnp.transpose(value, (0, 3, 1, 2))
        return (
            node_result,
            turn(edge_result),
            node_grad,
            turn(edge_grad),
            found[0],
            found[9],
            found[2].reshape(part),
            found[1],
            weight_in_grad,
            wide_bias_grad.reshape(wide),
            weight_out_grad,
            biases_grad,
            gains_grad,
            shifts_grad,
            found[3].T,
            found[5].reshape(update_hidden),
            found[4],
            found[8].reshape(channels),
            found[6].reshape(channels),
            found[7].reshape(channels),
        )

    return per_device


def solution(mesh):
    return jax.shard_map(
        build(mesh.shape["prot"], mesh.shape["res"], mesh.shape["mp"]),
        mesh=mesh,
        in_specs=(
            P("prot", "res", None),
            P("prot", "res", "mp", None),
            P("prot", "res", None),
            P("prot", "res", None, None),
            P("prot", "res"),
            P(None, None, "mp"),
            P(),
            P("mp"),
            P("mp", None),
            P(None, "mp"),
            P("mp"),
            P("mp", None),
            P(),
            P(),
            P(),
            P(),
            P(),
            P(),
            P(),
            P(),
            P(),
            P("prot", "res", None),
            P("prot", "res", "mp", None),
        ),
        out_specs=(
            P("prot", "res", None),
            P("prot", "res", "mp", None),
            P("prot", "res", None),
            P("prot", "res", "mp", None),
            P(None, None, "mp"),
            P(),
            P("mp"),
            P("mp", None),
            P(None, "mp"),
            P("mp"),
            P("mp", None),
            P(),
            P(),
            P(),
            P(),
            P(),
            P(),
            P(),
            P(),
            P(),
        ),
        check_vma=False,
    )
```

```python
import functools

import jax
import jax.numpy as jnp
from jax import lax
from jax.experimental import pallas as pl
from jax.experimental.pallas import tpu as pltpu
from jax.sharding import PartitionSpec as P

EPSILON = 1e-05
F32 = jnp.float32
PINNED = ("prepare",)
BF16 = jnp.bfloat16
DEAD = -30000.0
CUBIC = 0.044715
ROOT = 0.7978845608028654


def dot(left, right):
    return jnp.dot(left, right, preferred_element_type=F32)


def dot_nt(left, right):
    return lax.dot_general(left, right, (((1,), (1,)), ((), ())), preferred_element_type=F32)


def gelu_pair(value):
    square = value * value
    gate = 0.5 + 0.5 * jnp.tanh(value * (ROOT + (ROOT * CUBIC) * square))
    out = value * gate
    slope = gate + (out - out * gate) * (2.0 * ROOT + (6.0 * ROOT * CUBIC) * square)
    return out, slope


def low(value):
    return jnp.asarray(value, BF16)


def gelu_pair_low(value):
    value = value.astype(BF16)
    square = value * value
    inner = value * (low(-2.0 * ROOT) + low(-2.0 * ROOT * CUBIC) * square)
    power = jnp.exp(jnp.minimum(inner, low(80.0)))
    gate = pl.reciprocal(low(1.0) + power, approx=True)
    out = value * gate
    slope = gate + (out * (power * gate)) * (low(2.0 * ROOT) + low(6.0 * ROOT * CUBIC) * square)
    return out, slope


def activation(value):
    return jax.nn.gelu(value, approximate=True)


def activation_grad(value, upstream):
    return jax.vjp(activation, value)[1](upstream)[0]


def norm_forward(value, gain, shift):
    centred = value - jnp.mean(value, axis=-1, keepdims=True)
    inverse = lax.rsqrt(jnp.mean(centred * centred, axis=-1, keepdims=True) + EPSILON)
    normed = centred * inverse
    return (normed * gain + shift, normed, inverse)


def norm_backward(upstream, normed, inverse, gain):
    scaled = upstream * gain
    inner = (
        scaled
        - jnp.mean(scaled, axis=-1, keepdims=True)
        - normed * jnp.mean(scaled * normed, axis=-1, keepdims=True)
    )
    return inverse * inner


def chosen_row(value, row):
    rows = lax.broadcasted_iota(jnp.int32, value.shape, 0)
    return jnp.sum(jnp.where(rows == row, value.astype(F32), 0.0), axis=0, keepdims=True)


def selector(slot_row, rows):
    positions = lax.broadcasted_iota(jnp.int16, (rows, slot_row.shape[1]), 0)
    return jnp.where(positions == slot_row.astype(jnp.int16), low(1.0), low(0.0))


def dot_tn(left, right):
    return lax.dot_general(left, right, (((0,), (0,)), ((), ())), preferred_element_type=F32)


def masked_table(fixed, term, dead):
    positions = lax.broadcasted_iota(jnp.int32, term.shape, 1)
    term = jnp.where(positions == dead, DEAD, term).astype(BF16)
    return jnp.concatenate([fixed, term], axis=1)


def message_forward_body(perm_ref, *refs, count, calls, start):
    edge_ref, slot_ref, node_ref, arrive_ref, fixed_ref, count_ref = refs[:6]
    weights = refs[6 : 6 + count]
    others = refs[6 + count : 6 + 2 * count]
    refs = refs[6 + 2 * count :]
    slope_ref, mean_ref = refs[:2]
    parts = refs[2 : 2 + calls]
    weight_ref, table_ref, self_ref, sum_ref, operand_ref, value_ref = refs[2 + calls :]
    number = pl.program_id(0)
    group = operand_ref.shape[0]
    dead = perm_ref[count]
    steps, channels, lanes = edge_ref.shape[1:]
    width = node_ref.shape[2]

    @pl.when(number == 0)
    def _():
        fill_weights(perm_ref, weights, others, weight_ref, count)

    nodes = node_ref[0]
    arrive = arrive_ref[...].reshape(-1, width)
    pool = lanes + arrive.shape[0]
    rows = jnp.concatenate([nodes, arrive], axis=0)
    term = dot_nt(weight_ref[:, width : 2 * width], rows)
    table_ref[...] = masked_table(fixed_ref[...], term, dead)
    bias = weight_ref[:, 3 * width : 3 * width + 1].astype(F32)
    self_ref[...] = dot_nt(weight_ref[:, 0:width], nodes) + bias
    sum_ref[...] = jnp.zeros_like(sum_ref)

    def some(index, carry):
        spots = [index * group + spot for spot in range(group)]
        for spot in range(group):
            operand_ref[spot, 0:channels] = edge_ref[0, spots[spot]]
            operand_ref[spot, channels:] = selector(slot_ref[0, pl.ds(spots[spot], 1), :], pool)
        for spot in range(group):
            value_ref[spot] = dot(table_ref[...], operand_ref[spot])
        total = sum_ref[...]
        for spot in range(group):
            out, slope = gelu_pair_low(value_ref[spot] + self_ref[...])
            slope_ref[0, spots[spot]] = slope
            total = total + out.astype(F32)
        sum_ref[...] = total
        return carry

    lax.fori_loop(0, steps // group, some, 0)
    scale = 1.0 / jnp.maximum(chosen_row(count_ref[...], perm_ref[number + start]), 1.0)
    mean = (sum_ref[...] * scale).astype(BF16)
    mean_ref[0] = mean
    total = dot_tn(mean, weight_ref[:, 2 * width : 3 * width]).astype(BF16)
    for spot in range(calls):

        @pl.when(number == spot)
        def _(spot=spot):
            parts[spot][...] = total


def send_selector(rows, lanes):
    peers, slots = rows.shape
    lane = lax.broadcasted_iota(jnp.int32, (slots, lanes), 1).astype(F32)
    parts = []
    for peer in range(peers):
        column = jnp.broadcast_to(rows[peer : peer + 1, :].astype(F32), (8, slots)).T[:, 0:1]
        parts.append(jnp.where(lane == column, 1.0, 0.0).astype(BF16))
    return jnp.concatenate(parts, axis=0)


def pack_body(perm_ref, nodes_ref, output_ref, bias_ref, send_ref, node_ref, pack_ref, leave_ref, all_ref, *, count):
    width = output_ref.shape[1]
    part = output_ref.shape[0]
    all_ref[:, 0:width] = nodes_ref[0].T
    all_ref[:, width : 2 * width] = nodes_ref[1].T
    all_ref[:, 2 * width : 3 * width] = output_ref[...]
    tall = lambda row: jnp.broadcast_to(row, (8, row.shape[1])).T[:, 0:1]
    bias = tall(bias_ref[...].astype(F32).reshape(1, -1)).astype(BF16)
    all_ref[:, 3 * width :] = jnp.broadcast_to(bias, (part, all_ref.shape[1] - 3 * width))
    half = part // 2
    start = pl.multiple_of(perm_ref[count + 1] * half, half)
    pack_ref[...] = all_ref[pl.ds(start, half), :]
    proteins, lanes, _ = node_ref.shape
    for spot in range(proteins):
        table = send_selector(send_ref[spot, 0], lanes)
        leave_ref[:, spot] = dot(table, node_ref[spot]).astype(BF16).reshape(leave_ref[:, spot].shape)


def prepare_body(
    perm_ref,
    edge_ref,
    turned_ref,
    out_ref,
    hidden_bias_ref,
    gain_ref,
    shift_ref,
    branch_ref,
    wide_ref,
    biases_ref,
    gains_ref,
    shifts_ref,
    counts_ref,
    send_ref,
    node_ref,
    up_ref,
    wide_in_ref,
    wide_out_ref,
    weight_ref,
    weight_t_ref,
    column_ref,
    out_t_ref,
    turned_edge_ref,
    vector_ref,
    share_ref,
    table_ref,
    wide_bias_ref,
    own_node_ref,
    own_up_ref,
    block_ref,
    *,
    count,
):
    row = lambda ref: ref[...].astype(F32).reshape(1, -1)
    core = perm_ref[count + 1]
    half = wide_out_ref.shape[0] // 2
    start = pl.multiple_of(core * half, half)
    block_ref[0:half, :] = wide_in_ref[:, pl.ds(start, half)].T
    block_ref[half : 2 * half, :] = wide_out_ref[pl.ds(start, half), :]
    wide = row(wide_ref)
    line = jnp.where(core == 0, wide[:, 0:half], wide[:, half:])
    block_ref[2 * half :, 0:half] = jnp.broadcast_to(line, (16, half)).astype(BF16)
    block_ref[2 * half :, half:] = jnp.zeros((16, block_ref.shape[1] - half), BF16)
    part = edge_ref.shape[1] // count
    for spot in range(count):
        span = slice(spot * part, (spot + 1) * part)
        block = edge_ref[:, pl.ds(pl.multiple_of(perm_ref[spot] * part, part), part)]
        weight_ref[:, span] = block
        weight_t_ref[span, :] = block.T
    tall = lambda row: jnp.broadcast_to(row, (8, row.shape[1])).T[:, 0:1]
    channels = edge_ref.shape[0]
    lane = lax.broadcasted_iota(jnp.int32, (channels, 128), 1)
    column_ref[...] = jnp.where(
        lane == 0,
        tall(row(hidden_bias_ref)),
        jnp.where(lane == 1, tall(row(gain_ref)), tall(row(shift_ref))),
    )
    hidden = out_ref.shape[0]
    extra = out_t_ref.shape[1] - hidden
    lane = lax.broadcasted_iota(jnp.int32, (channels, extra), 1)
    last = jnp.where(lane == 0, tall(row(branch_ref)), 0.0).astype(BF16)
    out_t_ref[...] = jnp.concatenate([out_ref[...].T, last], axis=1)
    turned_edge_ref[...] = turned_ref[:, turned_ref.shape[1] - channels :].T
    vector_ref[0:2, :] = biases_ref[...].astype(F32)
    vector_ref[2:4, :] = gains_ref[...].astype(F32)
    vector_ref[4:6, :] = shifts_ref[...].astype(F32)
    vector_ref[6:8, :] = jnp.zeros((2, vector_ref.shape[1]), F32)
    me = perm_ref[0]
    counts = chosen_row(counts_ref[...], me)
    share = counts * (1.0 / jnp.maximum(counts, 1.0))
    share_ref[...] = jnp.broadcast_to(tall(share), share_ref.shape)
    table_ref[...] = send_selector(send_ref[me, 0], table_ref.shape[1])
    wide_bias_ref[...] = jnp.broadcast_to(wide, wide_bias_ref.shape).astype(BF16)
    own_node_ref[...] = node_ref[...]
    own_up_ref[...] = up_ref[...]


def fill_weights(perm_ref, mine, other, target, count):
    core = perm_ref[count + 1]
    half = mine[0].shape[0]
    for spot in range(count):
        for place, value in ((core, mine[spot][...]), (1 - core, other[spot][...])):
            start = pl.multiple_of((2 * spot + place) * half, half)
            target[pl.ds(start, half), :] = value


def forward_body(*refs, count):
    parts = refs[:count]
    node_ref, share_ref, vector_ref, send_ref, turned_ref = refs[count : count + 5]
    blocks = list(refs[count + 5 : 2 * count + 5])
    blocks = blocks + [refs[2 * count + 5].at[spot] for spot in range(count)]
    one_ref, two_ref, first_ref, second_ref, leave_ref, term_ref, slope_ref = refs[2 * count + 6 :]
    total = parts[0][...].astype(F32)
    for spot in range(1, count):
        total = total + parts[spot][...].astype(F32)
    value = node_ref[0].astype(F32) + total + share_ref[:, 0:1] * vector_ref[0:1, :]
    one_ref[...] = value
    first_norm, _, _ = norm_forward(value, vector_ref[2:3, :], vector_ref[4:5, :])
    first_low = first_norm.astype(BF16)
    first_ref[...] = first_low
    value = first_norm + vector_ref[1:2, :]
    for spot in range(2 * count):
        block = blocks[spot]
        half = (block.shape[0] - 16) // 2
        pre = dot_nt(first_low, block[0:half, :]) + block[2 * half : 2 * half + 1, 0:half].astype(F32)
        out, slope = gelu_pair(pre)
        slope_ref[:, spot * half : (spot + 1) * half] = slope.astype(BF16)
        value = value + dot(out.astype(BF16), block[half : 2 * half, :])
    two_ref[...] = value
    second_norm, _, _ = norm_forward(value, vector_ref[3:4, :], vector_ref[5:6, :])
    second = second_norm.astype(BF16)
    second_ref[...] = second
    leave_ref[...] = dot(send_ref[...], second).astype(BF16)
    lanes, width = second.shape
    term_ref[:, 0:lanes] = dot_nt(turned_ref[:, 0:width], second).astype(BF16)
    term_ref[:, lanes:] = dot_nt(turned_ref[:, width : 2 * width], second).astype(BF16)


def update_body(perm_ref, *refs, count, calls, first_call, joint):
    edge_ref, slot_ref, up_ref = refs[:3]
    terms = refs[3 : 3 + calls]
    if joint:
        refs = refs[: 3 + calls] + refs[3:]
        hidden = refs[3 + 2 * calls].shape[0]
        remotes = [ref.at[hidden:, :] for ref in terms]
        terms = [ref.at[0:hidden, :] for ref in terms]
    else:
        remotes = refs[3 + calls : 3 + 2 * calls]
    turned_ref, column_ref, out_t_ref, out_ref, weight_ref = refs[3 + 2 * calls : 8 + 2 * calls]
    refs = refs[8 + 2 * calls :]
    if not first_call:
        start_ref = refs[0]
        refs = refs[2:]
    result_ref, part_ref = refs[:2]
    sums = refs[2 : 2 + calls]
    total_ref = refs[2 + calls]
    table_ref, self_ref, table_grad_ref, self_grad_ref = refs[3 + calls : 7 + calls]
    gain_grad_ref, shift_grad_ref, edge_grad_ref, out_grad_ref = refs[7 + calls : 11 + calls]
    gain_ref, shift_ref, operand_ref, out_low_ref, mixed_ref, grad_ref, product_ref, value_ref, slope_ref = refs[
        11 + calls :
    ]
    group = operand_ref.shape[1] // edge_ref.shape[3]
    number = pl.program_id(0)
    dead = perm_ref[count]
    steps, channels, lanes = edge_ref.shape[1:]
    hidden = turned_ref.shape[0]
    width = remotes[0].shape[1]
    pool = lanes + remotes[0].shape[0]
    extra = out_t_ref.shape[1] - hidden
    grads = (edge_grad_ref, out_grad_ref)
    bases = (0, 256)
    sum_refs = (gain_grad_ref, shift_grad_ref)
    sum_bases = (512, 640)

    @pl.when(number == 0)
    def _():
        for ref, base in zip(grads, bases):
            if first_call:
                ref[...] = jnp.zeros_like(ref)
            else:
                ref[...] = start_ref[:, base : base + ref.shape[1]]
        for ref, base in zip(sum_refs, sum_bases):
            if first_call:
                ref[...] = jnp.zeros_like(ref)
            else:
                lane = lax.broadcasted_iota(jnp.int32, ref.shape, 1)
                ref[...] = jnp.where(lane == 0, start_ref[:, base : base + 1], 0.0)
        gain_ref[...] = jnp.broadcast_to(column_ref[:, 1:2], gain_ref.shape)
        shift_ref[...] = jnp.broadcast_to(column_ref[:, 2:3], shift_ref.shape)

    for spot in range(calls):

        @pl.when(number == spot)
        def _(spot=spot):
            remote = dot_nt(turned_ref[:, width : 2 * width], remotes[spot][...])
            term = jnp.concatenate([terms[spot][:, lanes:].astype(F32), remote], axis=1)
            table_ref[...] = masked_table(turned_ref[:, 2 * width :], term, dead)
            self_ref[...] = terms[spot][:, 0:lanes].astype(F32) + column_ref[:, 0:1]

    table_grad_ref[...] = jnp.zeros_like(table_grad_ref)
    self_grad_ref[...] = jnp.zeros_like(self_grad_ref)
    share = 1.0 / channels
    first = lax.broadcasted_iota(jnp.int32, (extra, lanes), 0) == 0
    spans = [slice(spot * lanes, (spot + 1) * lanes) for spot in range(group)]
    total = lambda value: jnp.sum(value, axis=0, keepdims=True)

    def some(index, carry):
        spots = [index * group + spot for spot in range(group)]
        for spot, span in zip(spots, spans):
            slot_row = slot_ref[0, pl.ds(spot, 1), :]
            operand_ref[0:channels, span] = edge_ref[0, spot]
            operand_ref[channels:, span] = selector(slot_row, pool)
            live = jnp.where(first & (slot_row != dead), 1.0, 0.0)
            out_low_ref[hidden:, span] = live.astype(BF16)
        for span in spans:
            value_ref[:, span] = dot(table_ref[...], operand_ref[:, span])
        for span in spans:
            out, slope = gelu_pair_low(value_ref[:, span] + self_ref[...])
            out_low_ref[0:hidden, span] = out
            slope_ref[:, span] = slope
        for span in spans:
            value_ref[:, span] = dot(out_t_ref[...], out_low_ref[:, span])
        for spot, span in zip(spots, spans):
            value = edge_ref[0, spot].astype(F32) + value_ref[:, span]
            centred = value - total(value) * share
            inverse = lax.rsqrt(total(centred * centred) * share + EPSILON)
            normed = centred * inverse
            gain = gain_ref[...]
            result_ref[0, spot] = (normed * gain + shift_ref[...]).astype(BF16)
            scaled = up_ref[0, spot].astype(F32) * gain
            product = scaled * normed
            product_ref[:, span] = product.astype(BF16)
            mixed = inverse * (scaled - total(scaled) * share - normed * (total(product) * share))
            mixed_ref[:, span] = mixed.astype(BF16)
        for span in spans:
            value_ref[:, span] = dot(out_ref[...], mixed_ref[:, span])
        for span in spans:
            grad = slope_ref[:, span].astype(F32) * value_ref[:, span]
            self_grad_ref[...] += grad
            grad_ref[:, span] = grad.astype(BF16)
        out_grad_ref[...] += dot_nt(mixed_ref[...], out_low_ref[...])
        for spot, span in zip(spots, spans):
            edge = dot(weight_ref[...], grad_ref[:, span])
            part_ref[0, spot] = (mixed_ref[:, span].astype(F32) + edge).astype(BF16)
        table_grad_ref[...] += dot_nt(grad_ref[...], operand_ref[...])
        sums_of = gain_grad_ref[...]
        for span in spans:
            sums_of = sums_of + product_ref[:, span].astype(F32)
        gain_grad_ref[...] = sums_of
        sums_of = shift_grad_ref[...]
        for spot in spots:
            sums_of = sums_of + up_ref[0, spot].astype(F32)
        shift_grad_ref[...] = sums_of
        return carry

    lax.fori_loop(0, steps // group, some, 0)
    edge_grad_ref[...] += table_grad_ref[:, 0:channels]
    for spot in range(calls):

        @pl.when(number == spot)
        def _(spot=spot):
            sums[spot][:, 0:lanes] = self_grad_ref[...].astype(BF16)
            sums[spot][:, lanes:] = table_grad_ref[:, channels:].astype(BF16)

    @pl.when(number == calls - 1)
    def _():
        for ref, base in zip(grads, bases):
            total_ref[:, base : base + ref.shape[1]] = ref[...]
        for ref, base in zip(sum_refs, sum_bases):
            flat = jnp.sum(ref[...], axis=1, keepdims=True)
            total_ref[:, base : base + 128] = jnp.broadcast_to(flat, (channels, 128))


def return_body(perm_ref, *refs, count):
    sums = refs[:count]
    turned_ref, up_ref = refs[count : count + 2]
    second_ref, leave_ref, sum_ref = refs[count + 2 :]
    total = sums[0][...].astype(F32)
    for spot in range(1, count):
        total = total + sums[spot][...].astype(F32)
    low = total.astype(BF16)
    lanes, width = second_ref.shape
    back = dot_tn(low[:, lanes:], turned_ref[:, width : 2 * width])
    leave_ref[...] = back[lanes:].astype(BF16)
    second_ref[...] = (
        up_ref[0].astype(F32) + dot_tn(low[:, 0:lanes], turned_ref[:, 0:width]) + back[0:lanes]
    )
    sum_ref[...] = total


def update_weights_body(perm_ref, sum_ref, low_ref, arrive_ref, grad_ref, column_ref, whole_ref):
    total = sum_ref[...]
    low = total.astype(BF16)
    lanes = low_ref.shape[0]
    channels = grad_ref.shape[0]
    hidden = low.shape[0]
    rows = jnp.concatenate([low_ref[...], arrive_ref[...]], axis=0)
    lane = lax.broadcasted_iota(jnp.int32, (channels, 128), 1)
    vectors = jnp.where(
        lane == 0,
        jnp.sum(total[:, 0:lanes], axis=1, keepdims=True),
        jnp.where(
            lane == 1,
            grad_ref[:, 512:513] / column_ref[:, 1:2],
            jnp.where(lane == 2, grad_ref[:, 640:641], grad_ref[:, 256 + hidden : 257 + hidden]),
        ),
    )
    whole_ref[...] = jnp.concatenate(
        [
            dot(low[:, 0:lanes], low_ref[...]),
            dot(low[:, lanes:], rows),
            grad_ref[:, 0:channels],
            grad_ref[:, 256 : 256 + hidden],
            vectors,
        ],
        axis=1,
    )


def backward_body(*refs, count):
    second_ref, return_ref, send_ref, one_ref, two_ref, share_ref, vector_ref, slope_ref = refs[:8]
    blocks = list(refs[8 : 8 + count])
    blocks = blocks + [refs[8 + count].at[spot] for spot in range(count)]
    aggregate_ref, forward_ref, sum_ref, grad_ref = refs[9 + count :]
    lanes = one_ref.shape[0]
    second_grad = second_ref[...] + dot_tn(send_ref[...], return_ref[...])
    _, first_normed, first_inverse = norm_forward(
        one_ref[...], vector_ref[2:3, :], vector_ref[4:5, :]
    )
    _, second_normed, second_inverse = norm_forward(
        two_ref[...], vector_ref[3:4, :], vector_ref[5:6, :]
    )
    total = lambda value: jnp.sum(value, axis=0, keepdims=True)
    grad_ref[3:4, :] = total(second_grad * second_normed)
    grad_ref[5:6, :] = total(second_grad)
    sum_two = norm_backward(second_grad, second_normed, second_inverse, vector_ref[3:4, :])
    low = sum_two.astype(BF16)
    forward_ref[0:lanes, :] = low
    grad_ref[1:2, :] = total(low.astype(F32))
    first_grad = sum_two
    for spot in range(2 * count):
        block = blocks[spot]
        half = (block.shape[0] - 16) // 2
        slope = slope_ref[:, spot * half : (spot + 1) * half].astype(F32)
        grad = (slope * dot_nt(low, block[half : 2 * half, :])).astype(BF16)
        first_grad = first_grad + dot(grad, block[0:half, :])
    grad_ref[2:3, :] = total(first_grad * first_normed)
    grad_ref[4:5, :] = total(first_grad)
    sum_one = norm_backward(first_grad, first_normed, first_inverse, vector_ref[2:3, :])
    sum_ref[...] = sum_one
    aggregate = sum_one.astype(BF16)
    aggregate_ref[...] = aggregate
    grad_ref[0:1, :] = total(share_ref[:, 0:1] * aggregate.astype(F32))
    grad_ref[6:16, :] = jnp.zeros((10, grad_ref.shape[1]), F32)
    forward_ref[lanes:, :] = grad_ref[...].astype(BF16)


def message_backward_body(perm_ref, *refs, count, calls, first_call):
    edge_ref, slot_ref, slope_ref, part_ref, edge_weight_ref, count_ref = refs[:6]
    weights = refs[6 : 6 + count]
    others = refs[6 + count : 6 + 2 * count]
    ups = refs[6 + 2 * count : 6 + 2 * count + calls]
    refs = refs[6 + 2 * count + calls :]
    if not first_call:
        node_ref, arrive_ref, own_node_ref, own_arrive_ref, mean_ref, own_mean_ref = refs[:6]
        own_up_ref, own_low_ref, own_edge_ref, whole_ref = refs[6:10]
        refs = refs[11:]
    grad_ref = refs[0]
    backs = refs[1 : 1 + calls]
    low_out_ref, edge_out_ref = refs[1 + calls : 3 + calls]
    weight_ref, up_ref, table_grad_ref, self_grad_ref = refs[3 + calls : 7 + calls]
    operand_ref, grad_low_ref = refs[7 + calls : 9 + calls]
    if not first_call:
        mine_ref, other_ref = low_out_ref, edge_out_ref
        low_ref, row_ref, mean_all_ref, up_all_ref = refs[9 + calls : 13 + calls]
        edge_total_ref, bias_ref, total_ref, out_total_ref = refs[13 + calls :]
    group = operand_ref.shape[1] // edge_ref.shape[3]
    number = pl.program_id(0)
    steps, channels, lanes = edge_ref.shape[1:]
    part = 2 * weights[0].shape[0]
    hidden = part * count
    width = backs[0].shape[1]
    pool = backs[0].shape[0]

    @pl.when(number == 0)
    def _():
        fill_weights(perm_ref, weights, others, weight_ref, count)
        if not first_call:
            low_ref[:, 0:pool] = own_low_ref[...]
            row_ref[0:lanes, :] = own_node_ref[0]
            row_ref[lanes:pool, :] = own_arrive_ref[...].reshape(-1, width)
            mean_all_ref[:, 0:lanes] = own_mean_ref[0]
            up_all_ref[0:lanes, :] = own_up_ref[...]
            edge_total_ref[...] = own_edge_ref[...]

    for spot in range(calls):

        @pl.when(number == spot)
        def _(spot=spot):
            value = dot_nt(weight_ref[:, 2 * width : 3 * width], ups[spot][...])
            number_of = perm_ref[spot if first_call else spot + 1]
            scale = 1.0 / jnp.maximum(chosen_row(count_ref[...], number_of), 1.0)
            up_ref[...] = (value * scale).astype(BF16)
            if not first_call:
                at = (spot + 1) * pool
                row_ref[at : at + lanes, :] = node_ref[0]
                row_ref[at + lanes : at + pool, :] = arrive_ref[...].reshape(-1, width)
                at = (spot + 1) * lanes
                mean_all_ref[:, at : at + lanes] = mean_ref[0]
                up_all_ref[at : at + lanes, :] = ups[spot][...]

    table_grad_ref[...] = jnp.zeros_like(table_grad_ref)
    self_grad_ref[...] = jnp.zeros_like(self_grad_ref)
    spans = [slice(spot * lanes, (spot + 1) * lanes) for spot in range(group)]

    def some(index, carry):
        spots = [index * group + spot for spot in range(group)]
        for spot, span in zip(spots, spans):
            operand_ref[0:channels, span] = edge_ref[0, spot]
            operand_ref[channels:, span] = selector(slot_ref[0, pl.ds(spot, 1), :], pool)
        total = self_grad_ref[...]
        for spot, span in zip(spots, spans):
            grad = slope_ref[0, spot] * up_ref[...]
            grad_low_ref[:, span] = grad
            total = total + grad.astype(F32)
        self_grad_ref[...] = total
        for spot, span in zip(spots, spans):
            edge = dot(edge_weight_ref[...], grad_low_ref[:, span])
            grad_ref[0, spot] = (part_ref[0, spot].astype(F32) + edge).astype(BF16)
        table_grad_ref[...] += dot_nt(grad_low_ref[...], operand_ref[...])
        return carry

    lax.fori_loop(0, steps // group, some, 0)
    self_low = self_grad_ref[...].astype(BF16)
    pool_low = table_grad_ref[:, channels:].astype(BF16)
    self_back = dot_tn(self_low, weight_ref[:, 0:width])
    pool_back = dot_tn(pool_low, weight_ref[:, width : 2 * width])
    low_both = jnp.concatenate(
        [
            jnp.concatenate([self_low, jnp.zeros((hidden, pool - lanes), BF16)], axis=1),
            pool_low,
        ],
        axis=0,
    )
    for spot in range(calls):

        @pl.when(number == spot)
        def _(spot=spot):
            backs[spot][0:lanes, :] = (self_back + pool_back[0:lanes]).astype(BF16)
            backs[spot][lanes:, :] = pool_back[lanes:].astype(BF16)
            if not first_call:
                low_ref[:, (spot + 1) * pool : (spot + 2) * pool] = low_both

    if first_call:
        low_out_ref[...] = low_both
        edge_out_ref[...] = table_grad_ref[:, 0:channels]
        return
    edge_total_ref[...] += table_grad_ref[:, 0:channels]

    @pl.when(number == calls - 1)
    def _():
        total_ref[...] = dot(low_ref[...], row_ref[...])
        out_total_ref[...] = dot(mean_all_ref[...], up_all_ref[...])
        ones = jnp.ones((row_ref.shape[0], 128), BF16)
        bias_ref[...] = dot(low_ref[0:hidden, :], ones)
        core = perm_ref[count + 1]
        half = part // 2
        rows = whole_ref.shape[0] // count // 2
        for spot in range(count):
            for place, ref in ((core, mine_ref), (1 - core, other_ref)):
                first = pl.multiple_of(spot * part + place * half, half)
                kind = ref.dtype
                ref[spot, 0:half, 0:width] = total_ref[pl.ds(first, half), :].astype(kind)
                ref[spot, 0:half, width : 2 * width] = total_ref[pl.ds(hidden + first, half), :].astype(kind)
                ref[spot, 0:half, 2 * width : 3 * width] = out_total_ref[pl.ds(first, half), :].astype(kind)
                start = pl.multiple_of((place * count + perm_ref[spot]) * rows, 8)
                wide = whole_ref.shape[1]
                below = jnp.concatenate(
                    [
                        whole_ref[pl.ds(start, rows), :],
                        jnp.zeros((ref.shape[1] - half - rows, wide), F32),
                    ],
                    axis=0,
                )
                ref[spot, half:, 0:wide] = below.astype(kind)
                ref[spot, half:, wide:] = jnp.zeros((below.shape[0], ref.shape[2] - wide), kind)
                both = jnp.concatenate(
                    [
                        edge_total_ref[pl.ds(first, half), :],
                        bias_ref[pl.ds(first, half), 0 : ref.shape[2] - 3 * width - channels],
                    ],
                    axis=1,
                )
                ref[spot, 0:half, 3 * width :] = both.astype(kind)


def wide_body(
    perm_ref, low_ref, forward_ref, weight_ref, bias_ref, output_ref, mine_ref, other_ref, all_ref, *, count
):
    width = low_ref.shape[1]
    wide = weight_ref.shape[1]
    step = forward_ref.shape[0] // count
    lanes = step - 16
    low = low_ref[...]
    forward = jnp.concatenate(
        [forward_ref[spot * step : spot * step + lanes, :] for spot in range(count)], axis=0
    )
    lines = None
    for spot in range(count):
        line = forward_ref[spot * step + lanes : (spot + 1) * step, :].astype(F32)
        lines = line if spot == 0 else lines + line
    pre = dot(low, weight_ref[...]) + bias_ref[0:1, :].astype(F32)
    out, slope = gelu_pair_low(pre)
    grad = slope.astype(F32) * dot_nt(forward, output_ref[...])
    all_ref[0:width, :] = dot_tn(low, grad.astype(BF16))
    all_ref[width : width + wide, :] = dot_tn(out, forward)
    at = width + wide
    total = jnp.broadcast_to(jnp.sum(grad, axis=0, keepdims=True), (8, wide))
    all_ref[at : at + 8, :] = total
    all_ref[at + 8 : at + 16, :] = lines[0:8]
    all_ref[at + 16 :, :] = jnp.zeros((all_ref.shape[0] - at - 16, width), F32)
    half = mine_ref.shape[0]
    core = perm_ref[count + 1]
    mine_ref[...] = all_ref[pl.ds(pl.multiple_of(core * half, 8), half), :]
    other_ref[...] = all_ref[pl.ds(pl.multiple_of((1 - core) * half, 8), half), :].astype(BF16)


def wide_finish_body(
    perm_ref, mine_ref, other_ref, in_ref, out_ref, bias_ref, one_ref, two_ref, three_ref, all_ref, *, count
):
    core = perm_ref[count + 1]
    half = mine_ref.shape[0]
    all_ref[pl.ds(pl.multiple_of(core * half, 8), half), :] = mine_ref[...].astype(F32)
    all_ref[pl.ds(pl.multiple_of((1 - core) * half, 8), half), :] = other_ref[...].astype(F32)
    width = in_ref.shape[0]
    wide = out_ref.shape[0]
    in_ref[...] = all_ref[0:width, :]
    out_ref[...] = all_ref[width : width + wide, :]
    at = width + wide
    bias_ref[...] = all_ref[at : at + 1, :]
    one_ref[...] = all_ref[at + 8 : at + 10, :]
    two_ref[...] = all_ref[at + 10 : at + 12, :]
    three_ref[...] = all_ref[at + 12 : at + 14, :]


def late_finish_body(
    perm_ref,
    mine_ref,
    other_ref,
    mine_parts_ref,
    other_parts_ref,
    nodes_ref,
    output_ref,
    bias_ref,
    turned_ref,
    update_ref,
    hidden_bias_ref,
    gain_ref,
    shift_ref,
    branch_ref,
    edge_ref,
    own_ref,
    whole_ref,
    edges_ref,
    *,
    count,
):
    core = perm_ref[count + 1]
    part = own_ref.shape[0]
    half = part // 2
    width = output_ref.shape[1]
    rows = whole_ref.shape[0] // count // 2
    channels = edges_ref.shape[1]
    for place, ref, parts in ((core, mine_ref, mine_parts_ref), (1 - core, other_ref, other_parts_ref)):
        own_ref[pl.ds(pl.multiple_of(place * half, 8), half), :] = ref[...].astype(F32)
        for spot in range(count):
            value = parts[spot].astype(F32)
            start = pl.multiple_of((place * count + perm_ref[spot]) * rows, 8)
            whole_ref[pl.ds(start, rows), :] = value[0:rows, :]
            first = perm_ref[spot] * part + place * half
            for turn in range(half // 8):
                start = pl.multiple_of(first + 8 * turn, 8)
                edges_ref[pl.ds(start, 8), :] = value[rows:, turn * channels : (turn + 1) * channels]
    nodes_ref[0] = own_ref[:, 0:width].T
    nodes_ref[1] = own_ref[:, width : 2 * width].T
    output_ref[...] = own_ref[:, 2 * width : 3 * width]
    last = own_ref.shape[1]
    bias_ref[...] = own_ref[:, last - 128 :].T[127:128, :]
    end = turned_ref.shape[1]
    hidden = update_ref.shape[0]
    turned_ref[...] = whole_ref[:, 0:end]
    update_ref[...] = whole_ref[:, end : end + hidden].T
    vectors = whole_ref[:, end + hidden :].T
    hidden_bias_ref[...] = vectors[0:1, :]
    gain_ref[...] = vectors[1:2, :]
    shift_ref[...] = vectors[2:3, :]
    branch_ref[...] = vectors[3:4, :]
    edge_ref[...] = edges_ref[...].T


def place_body(perm_ref, *refs, count):
    for spot in range(count):

        @pl.when(pl.program_id(0) == spot)
        def _(spot=spot):
            refs[count][0] = refs[spot][...]


def held(value):
    return pltpu.with_memory_space_constraint(value, pltpu.HBM)


def group_of(total):
    for size in (15, 5, 4, 3, 2, 1):
        if total % size == 0:
            return size


def call(body, grid, ins, outs, scratch, flops, moved, name, perm=None, limit=56, aliases=()):
    whole = lambda block: (block, lambda *_: (0,) * len(block))
    in_specs = [
        pl.BlockSpec(memory_space=pl.ANY)
        if len(entry) == 2
        else pl.BlockSpec(*(entry[1:] if len(entry) == 3 else whole(entry[0].shape)))
        for entry in ins
    ]
    out_specs = [
        pl.BlockSpec(*(entry[2:] if len(entry) == 4 else whole(entry[0]))) for entry in outs
    ]
    spec = pltpu.PrefetchScalarGridSpec(
        num_scalar_prefetch=0 if perm is None else 1,
        grid=grid,
        in_specs=in_specs,
        out_specs=out_specs,
        scratch_shapes=scratch,
    )
    operands = [entry[0] for entry in ins]
    return pl.pallas_call(
        body,
        grid_spec=spec,
        out_shape=[(pltpu.HBM if name in PINNED else jax.ShapeDtypeStruct)(entry[0], entry[1]) for entry in outs],
        input_output_aliases={source + 1: target for source, target in aliases},
        compiler_params=pltpu.CompilerParams(
            dimension_semantics=("arbitrary",) * len(grid), vmem_limit_bytes=limit * 2**20
        ),
        cost_estimate=pl.CostEstimate(flops=flops, bytes_accessed=moved, transcendentals=0),
        name=name,
    )(*([] if perm is None else [perm]), *operands)


def build(prot_size, res_size, mp_size):
    def across(value, offset):
        pairs = [(spot, spot ^ offset) for spot in range(mp_size)]
        return lax.ppermute(value, "mp", pairs)

    def gather(value):
        return [value] + [across(value, offset) for offset in range(1, mp_size)]

    def scatter(parts):
        return [parts[0]] + [across(parts[offset], offset) for offset in range(1, mp_size)]

    def exchange(value):
        return lax.all_to_all(value, "res", split_axis=0, concat_axis=0, tiled=True)

    def block_parts(value):
        place = lax.axis_index("res")
        piece = value.shape[0] // res_size
        parts = [lax.dynamic_slice_in_dim(value, place * piece, piece, 0)]
        low = value.astype(BF16)
        for hop in range(1, res_size):
            target = lax.rem(place + hop, res_size)
            part = lax.dynamic_slice_in_dim(low, target * piece, piece, 0)
            pairs = [(spot, (spot + hop) % res_size) for spot in range(res_size)]
            parts.append(lax.ppermute(part, "res", pairs))
        return parts

    def block_gather(own):
        parts = [own]
        for hop in range(1, res_size):
            pairs = [(spot, (spot - hop) % res_size) for spot in range(res_size)]
            parts.append(lax.ppermute(own, "res", pairs))
        return parts

    def block_order(parts):
        place = lax.axis_index("res")
        piece = parts[0].shape[0]
        both = jnp.concatenate(parts + parts, axis=0)
        return lax.dynamic_slice_in_dim(both, (res_size - place) * piece, res_size * piece, 0)

    def swap(value):
        return lax.ppermute(value, "prot", [(0, 1), (1, 0)])

    def per_device(
        node_states,
        edge_states,
        neighbour_slots,
        send_rows,
        live_counts,
        message_nodes,
        message_edges,
        message_bias,
        message_output,
        feedforward_weight,
        feedforward_bias,
        feedforward_output,
        output_biases,
        norm_gains,
        norm_shifts,
        update_weight,
        update_bias,
        update_output,
        branch_bias,
        edge_gain,
        edge_shift,
        node_cotangent,
        edge_cotangent,
    ):
        proteins, lanes, width = node_states.shape
        own_k, channels = edge_states.shape[2:]
        slots = send_rows.shape[3]
        remote = res_size * slots
        pool = lanes + remote
        part = message_nodes.shape[2]
        hidden = part * mp_size
        update_hidden = update_output.shape[0]
        wide = feedforward_weight.shape[1]
        assert proteins == mp_size and prot_size == 2
        me = lax.axis_index("mp")
        core = lax.axis_index("prot")
        place = lax.axis_index("res")
        dead = lanes + place * slots
        order = [me ^ offset for offset in range(mp_size)]
        perm = jnp.stack(order + [dead, core]).astype(jnp.int32)

        def reorder(value, axis=0):
            size = value.shape[axis] // mp_size
            return jnp.concatenate(
                [lax.dynamic_slice_in_dim(value, spot * size, size, axis) for spot in order], axis=axis
            )

        message_pack, leaving = call(
            functools.partial(pack_body, count=mp_size),
            (1,),
            [
                (message_nodes,),
                (message_output,),
                (message_bias,),
                (send_rows,),
                (node_states,),
            ],
            [
                ((part // 2, 3 * width + 128), BF16),
                ((res_size, proteins, slots, width), BF16),
            ],
            [pltpu.VMEM((part, 3 * width + 128), BF16)],
            0,
            0,
            "pack",
            perm,
        )
        arriving = exchange(leaving)
        weights = gather(message_pack)
        other_weights = [swap(value) for value in weights]
        own_slots = lax.dynamic_slice_in_dim(neighbour_slots, me * own_k, own_k, 2)
        alive = lax.broadcasted_iota(jnp.int32, own_slots.shape, 2) + me * own_k < live_counts[..., None]
        own_slots = jnp.transpose(jnp.where(alive, own_slots, dead), (0, 2, 1))
        edges = jnp.transpose(edge_states, (0, 2, 3, 1))
        edge_up = jnp.transpose(edge_cotangent, (0, 2, 3, 1))
        turned = update_weight.T
        small = call(
            functools.partial(prepare_body, count=mp_size),
            (1,),
            [
                (message_edges,),
                (turned,),
                (update_output,),
                (update_bias,),
                (edge_gain,),
                (edge_shift,),
                (branch_bias,),
                (feedforward_bias,),
                (output_biases,),
                (norm_gains,),
                (norm_shifts,),
                (live_counts,),
                (send_rows,),
                (node_states, (1, lanes, width), lambda p, perm: (perm[0], 0, 0)),
                (node_cotangent, (1, lanes, width), lambda p, perm: (perm[0], 0, 0)),
                (feedforward_weight,),
                (feedforward_output,),
            ],
            [
                ((channels, hidden), BF16),
                ((hidden, channels), BF16),
                ((channels, 128), F32),
                ((channels, update_hidden + 16), BF16),
                ((channels, update_hidden), BF16),
                ((8, width), F32),
                ((lanes, 128), F32),
                ((remote, lanes), BF16),
                ((16, wide), BF16),
                ((1, lanes, width), BF16),
                ((1, lanes, width), BF16),
                ((wide + 16, width), BF16),
            ],
            [],
            0,
            0,
            "prepare",
            perm,
        )
        *small, block = small
        blocks = gather(block)
        weights, other_weights, arriving, own_slots, small = lax.optimization_barrier(
            (weights, other_weights, arriving, own_slots, small)
        )
        (
            edge_weight,
            edge_weight_t,
            columns,
            out_t,
            turned_edge,
            vectors,
            share,
            own_table,
            wide_bias,
            own_node,
            own_up,
        ) = small

        depth = channels + pool
        group = group_of(own_k)
        count = proteins * own_k * lanes
        by_step4 = lambda p, perm: (p, 0, 0, 0)
        by_step3 = lambda p, perm: (p, 0, 0)
        others = proteins - 1

        def shifted(start):
            return (
                lambda p, perm: (perm[p + start], 0, 0, 0),
                lambda p, perm: (perm[p + start], 0, 0),
                lambda p, perm: (0, perm[p + start], 0, 0),
            )

        edge_block = (1, own_k, channels, lanes)
        edge_shape = (proteins, own_k, channels, lanes)
        slope_shape = (proteins, own_k, hidden, lanes)
        slope_block = (1, own_k, hidden, lanes)

        def edge_ins(start):
            by_perm4, by_perm3, _ = shifted(start)
            return [(edges, edge_block, by_perm4), (own_slots, (1, own_k, lanes), by_perm3)]

        def row_ins(start):
            _, by_perm3, by_arrive = shifted(start)
            return [
                (node_states, (1, lanes, width), by_perm3),
                (arriving, (res_size, 1, slots, width), by_arrive),
            ]

        def message_forward(start, calls, after):
            slots_after, _ = lax.optimization_barrier((own_slots, after))
            found = call(
                functools.partial(message_forward_body, count=proteins, calls=calls, start=start),
                (calls,),
                [edge_ins(start)[0], (slots_after,) + edge_ins(start)[1][1:]]
                + row_ins(start)
                + [(edge_weight_t,), (live_counts,)]
                + [(value,) for value in weights + other_weights],
                [
                    ((calls, own_k, hidden, lanes), BF16, slope_block, by_step4),
                    ((calls, hidden, lanes), BF16, (1, hidden, lanes), by_step3),
                ]
                + [((lanes, width), BF16)] * calls,
                [
                    pltpu.VMEM((hidden, weights[0].shape[1]), BF16),
                    pltpu.VMEM((hidden, depth), BF16),
                    pltpu.VMEM((hidden, lanes), F32),
                    pltpu.VMEM((hidden, lanes), F32),
                    pltpu.VMEM((group, depth, lanes), BF16),
                    pltpu.VMEM((group, hidden, lanes), F32),
                ],
                2 * calls * own_k * lanes * depth * hidden,
                calls * own_k * lanes * (channels + hidden) * 2,
                "message_forward",
                perm,
            )
            return found[0], found[1], list(found[2:])

        slope_others, mean_others, part_others = message_forward(1, others, own_slots)
        slope_own, mean_own, part_own = message_forward(0, 1, part_others[0])
        parts = scatter(part_own + part_others)
        blocks, _ = lax.optimization_barrier((blocks, part_others[0]))
        other_blocks = swap(jnp.stack(blocks))
        one, two, first_low, second_low, leaving, own_term, wide_slope = call(
            functools.partial(forward_body, count=proteins),
            (),
            [(value,) for value in parts]
            + [(own_node,), (share,), (vectors,), (own_table,), (turned,)]
            + [(held(value),) for value in blocks]
            + [(held(other_blocks),)],
            [
                ((lanes, width), F32),
                ((lanes, width), F32),
                ((lanes, width), BF16),
                ((lanes, width), BF16),
                ((remote, width), BF16),
                ((update_hidden, 2 * lanes), BF16),
                ((lanes, wide * mp_size), BF16),
            ],
            [],
            4 * lanes * width * wide * mp_size,
            4 * width * wide * mp_size,
            "feed_forward",
            limit=24,
        )

        arrived = exchange(leaving.reshape(res_size, slots, width)).reshape(remote, width)
        joint = own_term.shape[1] == width
        if joint:
            terms = gather(jnp.concatenate([own_term, arrived], axis=0))
            pool_remotes = []
        else:
            terms = gather(own_term)
            pool_remotes = gather(arrived)
        all_low = lax.all_gather(first_low, "mp", axis=0, tiled=True)
        node_result = lax.all_gather(second_low[None], "mp", axis=0, tiled=True)
        turned_width = 2 * width + channels

        def edge_update(start, calls, earlier):
            by_perm4 = shifted(start)[0]
            ins = (
                edge_ins(start)
                + [(edge_up, edge_block, by_perm4)]
                + [(value,) for value in terms[start : start + calls]]
                + [(value,) for value in pool_remotes[start : start + calls]]
                + [(turned,), (columns,), (out_t,), (update_output,), (turned_edge,)]
            )
            aliases = ()
            if earlier is not None:
                ins = ins + [(earlier[1],), (earlier[0], None)]
                aliases = ((len(ins) - 1, 0),)
            found = call(
                functools.partial(
                    update_body,
                    count=proteins,
                    calls=calls,
                    first_call=earlier is None,
                    joint=joint,
                ),
                (calls,),
                ins,
                [
                    (edge_shape, BF16, edge_block, by_perm4),
                    ((calls, own_k, channels, lanes), BF16, edge_block, by_step4),
                ]
                + [((update_hidden, lanes + pool), BF16)] * calls
                + [((update_hidden, 768), F32)],
                [
                    pltpu.VMEM((update_hidden, depth), BF16),
                    pltpu.VMEM((update_hidden, lanes), F32),
                    pltpu.VMEM((update_hidden, depth), F32),
                    pltpu.VMEM((update_hidden, lanes), F32),
                    pltpu.VMEM((channels, lanes), F32),
                    pltpu.VMEM((channels, lanes), F32),
                    pltpu.VMEM((update_hidden, channels), F32),
                    pltpu.VMEM((channels, update_hidden + 16), F32),
                    pltpu.VMEM((channels, lanes), F32),
                    pltpu.VMEM((channels, lanes), F32),
                    pltpu.VMEM((depth, group * lanes), BF16),
                    pltpu.VMEM((update_hidden + 16, group * lanes), BF16),
                    pltpu.VMEM((channels, group * lanes), BF16),
                    pltpu.VMEM((update_hidden, group * lanes), BF16),
                    pltpu.VMEM((channels, group * lanes), BF16),
                    pltpu.VMEM((update_hidden, group * lanes), F32),
                    pltpu.VMEM((update_hidden, group * lanes), BF16),
                ],
                2 * calls * own_k * lanes * (2 * depth + 4 * channels) * update_hidden,
                calls * own_k * lanes * channels * 8,
                "edge_update",
                perm,
                aliases=aliases,
            )
            return found[0], found[-1], found[1], found[2:-1]

        edge_result, grads, edge_part_own, sums_own = edge_update(0, 1, None)
        edge_result, grads, edge_part_others, sums_others = edge_update(1, others, (edge_result, grads))
        sums_own, sums_others, all_low = lax.optimization_barrier((sums_own, sums_others, all_low))
        sums = scatter(list(sums_own) + list(sums_others))
        whole_width = turned_width + update_hidden + 128
        second_part, leaving, update_sums = call(
            functools.partial(return_body, count=proteins),
            (1,),
            [(value,) for value in sums]
            + [(turned,), (own_up,)],
            [
                ((lanes, width), F32),
                ((remote, width), BF16),
                ((update_hidden, lanes + pool), F32),
            ],
            [],
            2 * (lanes + pool) * width * update_hidden,
            (lanes + pool) * width * 2,
            "update_return",
            perm,
        )
        returned = exchange(leaving.reshape(res_size, slots, width)).reshape(remote, width)
        (whole,) = call(
            update_weights_body,
            (1,),
            [(update_sums,), (second_low,), (arrived,), (grads,), (columns,)],
            [((update_hidden, whole_width), F32)],
            [],
            2 * (lanes + pool) * width * update_hidden,
            (lanes + pool) * width * 2,
            "update_weights",
            perm,
        )
        whole, returned = lax.optimization_barrier((whole, returned))
        aggregate_grad, forward_grad, sum_one, _ = call(
            functools.partial(backward_body, count=proteins),
            (),
            [(second_part,), (returned,), (own_table,), (one,), (two,), (share,), (vectors,), (wide_slope,)]
            + [(held(value),) for value in blocks]
            + [(held(other_blocks),)],
            [
                ((lanes, width), BF16),
                ((lanes + 16, width), BF16),
                ((lanes, width), F32),
                ((16, width), F32),
            ],
            [],
            6 * lanes * width * wide * mp_size,
            4 * width * wide * mp_size,
            "feed_backward",
            limit=24,
        )
        ups = gather(aggregate_grad)
        all_forward = lax.all_gather(forward_grad, "mp", axis=0, tiled=True)
        total_width = 3 * width + -(-(channels + 1) // 128) * 128
        whole_rows = update_hidden // 2 // mp_size
        late_rows = -(-(part // 2 + whole_rows) // (8 * res_size)) * 8 * res_size
        late_shape = (proteins, late_rows, total_width)

        def message_backward(start, calls, earlier):
            by_perm4 = shifted(start)[0]
            ins = (
                edge_ins(start)
                + [
                    (slope_own if earlier is None else slope_others, slope_block, by_step4),
                    (edge_part_own if earlier is None else edge_part_others, edge_block, by_step4),
                    (edge_weight,),
                    (live_counts,),
                ]
                + [(value,) for value in weights + other_weights + ups[start : start + calls]]
            )
            aliases = ()
            scratch = [
                pltpu.VMEM((hidden, weights[0].shape[1]), BF16),
                pltpu.VMEM((hidden, lanes), BF16),
                pltpu.VMEM((hidden, depth), F32),
                pltpu.VMEM((hidden, lanes), F32),
                pltpu.VMEM((depth, group * lanes), BF16),
                pltpu.VMEM((hidden, group * lanes), BF16),
            ]
            if earlier is None:
                last = [((2 * hidden, pool), BF16), ((hidden, channels), F32)]
            else:
                mean_block = (1, hidden, lanes)
                ins = ins + row_ins(start)
                ins = ins + [
                    (node_states, (1, lanes, width), lambda p, perm: (perm[0], 0, 0)),
                    (arriving, (res_size, 1, slots, width), lambda p, perm: (0, perm[0], 0, 0)),
                    (mean_others, mean_block, by_step3),
                    (mean_own,),
                    (ups[0],),
                    (earlier[1],),
                    (earlier[2],),
                    (whole,),
                    (earlier[0], None),
                ]
                aliases = ((len(ins) - 1, 0),)
                last = [(late_shape, F32), (late_shape, BF16)]
                scratch = scratch + [
                    pltpu.VMEM((2 * hidden, proteins * pool), BF16),
                    pltpu.VMEM((proteins * pool, width), BF16),
                    pltpu.VMEM((hidden, proteins * lanes), BF16),
                    pltpu.VMEM((proteins * lanes, width), BF16),
                    pltpu.VMEM((hidden, channels), F32),
                    pltpu.VMEM((hidden, 128), F32),
                    pltpu.VMEM((2 * hidden, width), F32),
                    pltpu.VMEM((hidden, width), F32),
                ]
            found = call(
                functools.partial(
                    message_backward_body, count=proteins, calls=calls, first_call=earlier is None
                ),
                (calls,),
                ins,
                [(edge_shape, BF16, edge_block, by_perm4)] + [((pool, width), BF16)] * calls + last,
                scratch,
                2 * calls * own_k * lanes * (depth + channels) * hidden,
                calls * own_k * lanes * (3 * channels + hidden) * 2,
                "message_backward",
                perm,
                aliases=aliases,
            )
            return found[0], found[-2], found[-1], found[1 : 1 + calls]

        edge_grad, own_low, own_edge, back_own = message_backward(0, 1, None)
        edge_grad, late_mine, late_other, back_others = message_backward(
            1, others, (edge_grad, own_low, own_edge)
        )
        found = list(back_own) + list(back_others)
        late_swapped = swap(late_other)
        backs, late_mine, all_forward, node_result = lax.optimization_barrier(
            (found, late_mine, all_forward, node_result)
        )
        back = scatter(backs)
        late = late_mine + late_swapped.astype(F32)
        late_own = late[0]
        late_low = [late[offset].astype(BF16) for offset in range(1, mp_size)]
        all_forward, late_own, late_low = lax.optimization_barrier((all_forward, late_own, late_low))
        late_parts = scatter([late_own] + late_low)
        unit = prot_size * res_size * 8
        wide_rows = -(-(width + wide + 16) // unit) * unit
        early_mine, early_other = call(
            functools.partial(wide_body, count=proteins),
            (1,),
            [
                (all_low,),
                (all_forward,),
                (feedforward_weight,),
                (wide_bias,),
                (feedforward_output,),
            ],
            [((wide_rows // 2, width), F32), ((wide_rows // 2, width), BF16)],
            [pltpu.VMEM((wide_rows, width), F32)],
            10 * proteins * lanes * width * wide,
            8 * proteins * lanes * width,
            "feed_weights",
            perm,
        )
        back, early_other, early_mine = lax.optimization_barrier((back, early_other, early_mine))
        early_swapped = swap(early_other)
        total = sum(value.astype(F32) for value in back)
        leaving = total[lanes:].astype(BF16).reshape(res_size, slots, width)
        leaving, early_swapped = lax.optimization_barrier((leaving, early_swapped))
        cut = early_mine.shape[0] // 2
        early = [
            (early_mine[spot : spot + cut] + early_swapped[spot : spot + cut].astype(F32)).astype(BF16)
            for spot in (0, cut)
        ]
        early, leaving = lax.optimization_barrier((early, leaving))
        early = jnp.concatenate(lax.psum(tuple(early), "res"), axis=0)
        returned = exchange(leaving)
        node_grad = (
            sum_one
            + total[:lanes]
            + jnp.einsum(
                "sr,sd->rd", own_table, returned.reshape(remote, width), preferred_element_type=F32
            )
        ).astype(BF16)
        node_grad, late_parts = lax.optimization_barrier((node_grad, late_parts))
        late = sum(value.astype(F32) for value in late_parts)
        late_parts = block_parts(late)
        node_parts = gather(node_grad)
        late = sum(value.astype(F32) for value in late_parts).astype(BF16)
        late, node_parts = lax.optimization_barrier((late, node_parts))
        late_parts = block_gather(late)
        (node_grad,) = call(
            functools.partial(place_body, count=proteins),
            (proteins,),
            [(value,) for value in node_parts],
            [((proteins, lanes, width), BF16, (1, lanes, width), shifted(0)[1])],
            [],
            0,
            0,
            "place_rows",
            perm,
        )
        early, node_grad, late_parts = lax.optimization_barrier((early, node_grad, late_parts))
        late = block_order(late_parts)
        whole = late[part // 2 : part // 2 + whole_rows, :whole_width]
        late = late[: part // 2]
        early_swapped = swap(early)
        late_swapped = swap(late)
        fold = late[:, 3 * width : 3 * width + channels].reshape(-1, 8, channels)
        fold = jnp.transpose(fold, (1, 0, 2)).reshape(8, -1)
        shared_parts = gather(jnp.concatenate([whole, fold], axis=0))
        weight_in_grad, weight_out_grad, wide_bias_grad, biases_grad, gains_grad, shifts_grad = call(
            functools.partial(wide_finish_body, count=proteins),
            (1,),
            [(early,), (early_swapped,)],
            [
                ((width, wide), F32),
                ((wide, width), F32),
                ((1, wide), F32),
                ((2, width), F32),
                ((2, width), F32),
                ((2, width), F32),
            ],
            [pltpu.VMEM((wide_rows, width), F32)],
            0,
            8 * wide_rows * width,
            "feed_weights_out",
            perm,
        )
        weight_in_grad, shared_parts, late_swapped = lax.optimization_barrier(
            (weight_in_grad, shared_parts, late_swapped)
        )
        shared = jnp.stack(shared_parts)
        found = call(
            functools.partial(late_finish_body, count=proteins),
            (1,),
            [(late,), (late_swapped,), (shared,), (swap(shared),)],
            [
                ((2, width, part), F32),
                ((part, width), F32),
                ((1, part), F32),
                ((update_hidden, turned_width), F32),
                ((update_hidden, channels), F32),
                ((1, update_hidden), F32),
                ((1, channels), F32),
                ((1, channels), F32),
                ((1, channels), F32),
                ((channels, hidden), F32),
            ],
            [
                pltpu.VMEM((part, total_width), F32),
                pltpu.VMEM((update_hidden, turned_width + update_hidden + 128), F32),
                pltpu.VMEM((hidden, channels), F32),
            ],
            0,
            8 * hidden * total_width,
            "message_weights_out",
            perm,
            16,
        )
        turn = lambda value: jnp.transpose(value, (0, 3, 1, 2))
        return (
            node_result,
            turn(edge_result),
            node_grad,
            turn(edge_grad),
            found[0],
            found[9],
            found[2].reshape(part),
            found[1],
            weight_in_grad,
            wide_bias_grad.reshape(wide),
            weight_out_grad,
            biases_grad,
            gains_grad,
            shifts_grad,
            found[3].T,
            found[5].reshape(update_hidden),
            found[4],
            found[8].reshape(channels),
            found[6].reshape(channels),
            found[7].reshape(channels),
        )

    return per_device


def solution(mesh):
    return jax.shard_map(
        build(mesh.shape["prot"], mesh.shape["res"], mesh.shape["mp"]),
        mesh=mesh,
        in_specs=(
            P("prot", "res", None),
            P("prot", "res", "mp", None),
            P("prot", "res", None),
            P("prot", "res", None, None),
            P("prot", "res"),
            P(None, None, "mp"),
            P(),
            P("mp"),
            P("mp", None),
            P(None, "mp"),
            P("mp"),
            P("mp", None),
            P(),
            P(),
            P(),
            P(),
            P(),
            P(),
            P(),
            P(),
            P(),
            P("prot", "res", None),
            P("prot", "res", "mp", None),
        ),
        out_specs=(
            P("prot", "res", None),
            P("prot", "res", "mp", None),
            P("prot", "res", None),
            P("prot", "res", "mp", None),
            P(None, None, "mp"),
            P(),
            P("mp"),
            P("mp", None),
            P(None, "mp"),
            P("mp"),
            P("mp", None),
            P(),
            P(),
            P(),
            P(),
            P(),
            P(),
            P(),
            P(),
            P(),
        ),
        check_vma=False,
    )
```

```python
import functools

import jax
import jax.numpy as jnp
from jax import lax
from jax.experimental import pallas as pl
from jax.experimental.pallas import tpu as pltpu
from jax.sharding import PartitionSpec as P

EPSILON = 1e-05
F32 = jnp.float32
PINNED = ("prepare",)
BF16 = jnp.bfloat16
DEAD = -30000.0
CUBIC = 0.044715
ROOT = 0.7978845608028654


def dot(left, right):
    return jnp.dot(left, right, preferred_element_type=F32)


def dot_nt(left, right):
    return lax.dot_general(left, right, (((1,), (1,)), ((), ())), preferred_element_type=F32)


def gelu_pair(value):
    square = value * value
    gate = 0.5 + 0.5 * jnp.tanh(value * (ROOT + (ROOT * CUBIC) * square))
    out = value * gate
    slope = gate + (out - out * gate) * (2.0 * ROOT + (6.0 * ROOT * CUBIC) * square)
    return out, slope


def low(value):
    return jnp.asarray(value, BF16)


def gelu_pair_low(value):
    value = value.astype(BF16)
    square = value * value
    inner = value * (low(-2.0 * ROOT) + low(-2.0 * ROOT * CUBIC) * square)
    power = jnp.exp(jnp.minimum(inner, low(80.0)))
    gate = pl.reciprocal(low(1.0) + power, approx=True)
    out = value * gate
    slope = gate + (out * (power * gate)) * (low(2.0 * ROOT) + low(6.0 * ROOT * CUBIC) * square)
    return out, slope


def activation(value):
    return jax.nn.gelu(value, approximate=True)


def activation_grad(value, upstream):
    return jax.vjp(activation, value)[1](upstream)[0]


def norm_forward(value, gain, shift):
    centred = value - jnp.mean(value, axis=-1, keepdims=True)
    inverse = lax.rsqrt(jnp.mean(centred * centred, axis=-1, keepdims=True) + EPSILON)
    normed = centred * inverse
    return (normed * gain + shift, normed, inverse)


def norm_backward(upstream, normed, inverse, gain):
    scaled = upstream * gain
    inner = (
        scaled
        - jnp.mean(scaled, axis=-1, keepdims=True)
        - normed * jnp.mean(scaled * normed, axis=-1, keepdims=True)
    )
    return inverse * inner


def chosen_row(value, row):
    rows = lax.broadcasted_iota(jnp.int32, value.shape, 0)
    return jnp.sum(jnp.where(rows == row, value.astype(F32), 0.0), axis=0, keepdims=True)


def selector(slot_row, rows):
    positions = lax.broadcasted_iota(jnp.int16, (rows, slot_row.shape[1]), 0)
    return jnp.where(positions == slot_row.astype(jnp.int16), low(1.0), low(0.0))


def dot_tn(left, right):
    return lax.dot_general(left, right, (((0,), (0,)), ((), ())), preferred_element_type=F32)


def masked_table(fixed, term, dead):
    positions = lax.broadcasted_iota(jnp.int32, term.shape, 1)
    term = jnp.where(positions == dead, DEAD, term).astype(BF16)
    return jnp.concatenate([fixed, term], axis=1)


def message_forward_body(perm_ref, *refs, count, calls, start):
    edge_ref, slot_ref, node_ref, arrive_ref, fixed_ref, count_ref = refs[:6]
    weights = refs[6 : 6 + count]
    others = refs[6 + count : 6 + 2 * count]
    refs = refs[6 + 2 * count :]
    slope_ref, mean_ref = refs[:2]
    parts = refs[2 : 2 + calls]
    weight_ref, table_ref, self_ref, sum_ref, operand_ref, value_ref = refs[2 + calls :]
    number = pl.program_id(0)
    group = operand_ref.shape[0]
    dead = perm_ref[count]
    steps, channels, lanes = edge_ref.shape[1:]
    width = node_ref.shape[2]

    @pl.when(number == 0)
    def _():
        fill_weights(perm_ref, weights, others, weight_ref, count)

    nodes = node_ref[0]
    arrive = arrive_ref[...].reshape(-1, width)
    pool = lanes + arrive.shape[0]
    rows = jnp.concatenate([nodes, arrive], axis=0)
    term = dot_nt(weight_ref[:, width : 2 * width], rows)
    table_ref[...] = masked_table(fixed_ref[...], term, dead)
    bias = weight_ref[:, 3 * width : 3 * width + 1].astype(F32)
    self_ref[...] = dot_nt(weight_ref[:, 0:width], nodes) + bias
    sum_ref[...] = jnp.zeros_like(sum_ref)

    def some(index, carry):
        spots = [index * group + spot for spot in range(group)]
        for spot in range(group):
            operand_ref[spot, 0:channels] = edge_ref[0, spots[spot]]
            operand_ref[spot, channels:] = selector(slot_ref[0, pl.ds(spots[spot], 1), :], pool)
        for spot in range(group):
            value_ref[spot] = dot(table_ref[...], operand_ref[spot])
        total = sum_ref[...]
        for spot in range(group):
            out, slope = gelu_pair_low(value_ref[spot] + self_ref[...])
            slope_ref[0, spots[spot]] = slope
            total = total + out.astype(F32)
        sum_ref[...] = total
        return carry

    lax.fori_loop(0, steps // group, some, 0)
    scale = 1.0 / jnp.maximum(chosen_row(count_ref[...], perm_ref[number + start]), 1.0)
    mean = (sum_ref[...] * scale).astype(BF16)
    mean_ref[0] = mean
    total = dot_tn(mean, weight_ref[:, 2 * width : 3 * width]).astype(BF16)
    for spot in range(calls):

        @pl.when(number == spot)
        def _(spot=spot):
            parts[spot][...] = total


def send_selector(rows, lanes):
    peers, slots = rows.shape
    lane = lax.broadcasted_iota(jnp.int32, (slots, lanes), 1).astype(F32)
    parts = []
    for peer in range(peers):
        column = jnp.broadcast_to(rows[peer : peer + 1, :].astype(F32), (8, slots)).T[:, 0:1]
        parts.append(jnp.where(lane == column, 1.0, 0.0).astype(BF16))
    return jnp.concatenate(parts, axis=0)


def pack_body(perm_ref, nodes_ref, output_ref, bias_ref, send_ref, node_ref, pack_ref, leave_ref, all_ref, *, count):
    width = output_ref.shape[1]
    part = output_ref.shape[0]
    all_ref[:, 0:width] = nodes_ref[0].T
    all_ref[:, width : 2 * width] = nodes_ref[1].T
    all_ref[:, 2 * width : 3 * width] = output_ref[...]
    tall = lambda row: jnp.broadcast_to(row, (8, row.shape[1])).T[:, 0:1]
    bias = tall(bias_ref[...].astype(F32).reshape(1, -1)).astype(BF16)
    all_ref[:, 3 * width :] = jnp.broadcast_to(bias, (part, all_ref.shape[1] - 3 * width))
    half = part // 2
    start = pl.multiple_of(perm_ref[count + 1] * half, half)
    pack_ref[...] = all_ref[pl.ds(start, half), :]
    proteins, lanes, _ = node_ref.shape
    for spot in range(proteins):
        table = send_selector(send_ref[spot, 0], lanes)
        leave_ref[:, spot] = dot(table, node_ref[spot]).astype(BF16).reshape(leave_ref[:, spot].shape)


def prepare_body(
    perm_ref,
    edge_ref,
    turned_ref,
    out_ref,
    hidden_bias_ref,
    gain_ref,
    shift_ref,
    branch_ref,
    wide_ref,
    biases_ref,
    gains_ref,
    shifts_ref,
    counts_ref,
    send_ref,
    node_ref,
    up_ref,
    wide_in_ref,
    wide_out_ref,
    weight_ref,
    weight_t_ref,
    column_ref,
    out_t_ref,
    turned_edge_ref,
    vector_ref,
    share_ref,
    table_ref,
    wide_bias_ref,
    own_node_ref,
    own_up_ref,
    block_ref,
    *,
    count,
):
    row = lambda ref: ref[...].astype(F32).reshape(1, -1)
    core = perm_ref[count + 1]
    half = wide_out_ref.shape[0] // 2
    start = pl.multiple_of(core * half, half)
    block_ref[0:half, :] = wide_in_ref[:, pl.ds(start, half)].T
    block_ref[half : 2 * half, :] = wide_out_ref[pl.ds(start, half), :]
    wide = row(wide_ref)
    line = jnp.where(core == 0, wide[:, 0:half], wide[:, half:])
    block_ref[2 * half :, 0:half] = jnp.broadcast_to(line, (16, half)).astype(BF16)
    block_ref[2 * half :, half:] = jnp.zeros((16, block_ref.shape[1] - half), BF16)
    part = edge_ref.shape[1] // count
    for spot in range(count):
        span = slice(spot * part, (spot + 1) * part)
        block = edge_ref[:, pl.ds(pl.multiple_of(perm_ref[spot] * part, part), part)]
        weight_ref[:, span] = block
        weight_t_ref[span, :] = block.T
    tall = lambda row: jnp.broadcast_to(row, (8, row.shape[1])).T[:, 0:1]
    channels = edge_ref.shape[0]
    lane = lax.broadcasted_iota(jnp.int32, (channels, 128), 1)
    column_ref[...] = jnp.where(
        lane == 0,
        tall(row(hidden_bias_ref)),
        jnp.where(lane == 1, tall(row(gain_ref)), tall(row(shift_ref))),
    )
    hidden = out_ref.shape[0]
    extra = out_t_ref.shape[1] - hidden
    lane = lax.broadcasted_iota(jnp.int32, (channels, extra), 1)
    last = jnp.where(lane == 0, tall(row(branch_ref)), 0.0).astype(BF16)
    out_t_ref[...] = jnp.concatenate([out_ref[...].T, last], axis=1)
    turned_edge_ref[...] = turned_ref[:, turned_ref.shape[1] - channels :].T
    vector_ref[0:2, :] = biases_ref[...].astype(F32)
    vector_ref[2:4, :] = gains_ref[...].astype(F32)
    vector_ref[4:6, :] = shifts_ref[...].astype(F32)
    vector_ref[6:8, :] = jnp.zeros((2, vector_ref.shape[1]), F32)
    me = perm_ref[0]
    counts = chosen_row(counts_ref[...], me)
    share = counts * (1.0 / jnp.maximum(counts, 1.0))
    share_ref[...] = jnp.broadcast_to(tall(share), share_ref.shape)
    table_ref[...] = send_selector(send_ref[me, 0], table_ref.shape[1])
    wide_bias_ref[...] = jnp.broadcast_to(wide, wide_bias_ref.shape).astype(BF16)
    own_node_ref[...] = node_ref[...]
    own_up_ref[...] = up_ref[...]


def fill_weights(perm_ref, mine, other, target, count):
    core = perm_ref[count + 1]
    half = mine[0].shape[0]
    for spot in range(count):
        for place, value in ((core, mine[spot][...]), (1 - core, other[spot][...])):
            start = pl.multiple_of((2 * spot + place) * half, half)
            target[pl.ds(start, half), :] = value


def forward_body(*refs, count):
    parts = refs[:count]
    node_ref, share_ref, vector_ref, send_ref, turned_ref = refs[count : count + 5]
    blocks = list(refs[count + 5 : 2 * count + 5])
    blocks = blocks + [refs[2 * count + 5].at[spot] for spot in range(count)]
    one_ref, two_ref, first_ref, second_ref, leave_ref, term_ref, slope_ref = refs[2 * count + 6 :]
    total = parts[0][...].astype(F32)
    for spot in range(1, count):
        total = total + parts[spot][...].astype(F32)
    value = node_ref[0].astype(F32) + total + share_ref[:, 0:1] * vector_ref[0:1, :]
    one_ref[...] = value
    first_norm, _, _ = norm_forward(value, vector_ref[2:3, :], vector_ref[4:5, :])
    first_low = first_norm.astype(BF16)
    first_ref[...] = first_low
    value = first_norm + vector_ref[1:2, :]
    for spot in range(2 * count):
        block = blocks[spot]
        half = (block.shape[0] - 16) // 2
        pre = dot_nt(first_low, block[0:half, :]) + block[2 * half : 2 * half + 1, 0:half].astype(F32)
        out, slope = gelu_pair(pre)
        slope_ref[:, spot * half : (spot + 1) * half] = slope.astype(BF16)
        value = value + dot(out.astype(BF16), block[half : 2 * half, :])
    two_ref[...] = value
    second_norm, _, _ = norm_forward(value, vector_ref[3:4, :], vector_ref[5:6, :])
    second = second_norm.astype(BF16)
    second_ref[...] = second
    leave_ref[...] = dot(send_ref[...], second).astype(BF16)
    lanes, width = second.shape
    term_ref[:, 0:lanes] = dot_nt(turned_ref[:, 0:width], second).astype(BF16)
    term_ref[:, lanes:] = dot_nt(turned_ref[:, width : 2 * width], second).astype(BF16)


def update_body(perm_ref, *refs, count, calls, first_call, joint):
    edge_ref, slot_ref, up_ref = refs[:3]
    terms = refs[3 : 3 + calls]
    if joint:
        refs = refs[: 3 + calls] + refs[3:]
        hidden = refs[3 + 2 * calls].shape[0]
        remotes = [ref.at[hidden:, :] for ref in terms]
        terms = [ref.at[0:hidden, :] for ref in terms]
    else:
        remotes = refs[3 + calls : 3 + 2 * calls]
    turned_ref, column_ref, out_t_ref, out_ref, weight_ref = refs[3 + 2 * calls : 8 + 2 * calls]
    refs = refs[8 + 2 * calls :]
    if not first_call:
        start_ref = refs[0]
        refs = refs[2:]
    result_ref, part_ref = refs[:2]
    sums = refs[2 : 2 + calls]
    total_ref = refs[2 + calls]
    table_ref, self_ref, table_grad_ref, self_grad_ref = refs[3 + calls : 7 + calls]
    gain_grad_ref, shift_grad_ref, edge_grad_ref, out_grad_ref = refs[7 + calls : 11 + calls]
    gain_ref, shift_ref, operand_ref, out_low_ref, mixed_ref, grad_ref, product_ref, value_ref, slope_ref = refs[
        11 + calls :
    ]
    group = operand_ref.shape[1] // edge_ref.shape[3]
    number = pl.program_id(0)
    dead = perm_ref[count]
    steps, channels, lanes = edge_ref.shape[1:]
    hidden = turned_ref.shape[0]
    width = remotes[0].shape[1]
    pool = lanes + remotes[0].shape[0]
    extra = out_t_ref.shape[1] - hidden
    grads = (edge_grad_ref, out_grad_ref)
    bases = (0, 256)
    sum_refs = (gain_grad_ref, shift_grad_ref)
    sum_bases = (512, 640)

    @pl.when(number == 0)
    def _():
        for ref, base in zip(grads, bases):
            if first_call:
                ref[...] = jnp.zeros_like(ref)
            else:
                ref[...] = start_ref[:, base : base + ref.shape[1]]
        for ref, base in zip(sum_refs, sum_bases):
            if first_call:
                ref[...] = jnp.zeros_like(ref)
            else:
                lane = lax.broadcasted_iota(jnp.int32, ref.shape, 1)
                ref[...] = jnp.where(lane == 0, start_ref[:, base : base + 1], 0.0)
        gain_ref[...] = jnp.broadcast_to(column_ref[:, 1:2], gain_ref.shape)
        shift_ref[...] = jnp.broadcast_to(column_ref[:, 2:3], shift_ref.shape)

    for spot in range(calls):

        @pl.when(number == spot)
        def _(spot=spot):
            remote = dot_nt(turned_ref[:, width : 2 * width], remotes[spot][...])
            term = jnp.concatenate([terms[spot][:, lanes:].astype(F32), remote], axis=1)
            table_ref[...] = masked_table(turned_ref[:, 2 * width :], term, dead)
            self_ref[...] = terms[spot][:, 0:lanes].astype(F32) + column_ref[:, 0:1]

    table_grad_ref[...] = jnp.zeros_like(table_grad_ref)
    self_grad_ref[...] = jnp.zeros_like(self_grad_ref)
    share = 1.0 / channels
    first = lax.broadcasted_iota(jnp.int32, (extra, lanes), 0) == 0
    spans = [slice(spot * lanes, (spot + 1) * lanes) for spot in range(group)]
    total = lambda value: jnp.sum(value, axis=0, keepdims=True)

    def some(index, carry):
        spots = [index * group + spot for spot in range(group)]
        for spot, span in zip(spots, spans):
            slot_row = slot_ref[0, pl.ds(spot, 1), :]
            operand_ref[0:channels, span] = edge_ref[0, spot]
            operand_ref[channels:, span] = selector(slot_row, pool)
            live = jnp.where(first & (slot_row != dead), 1.0, 0.0)
            out_low_ref[hidden:, span] = live.astype(BF16)
        for span in spans:
            value_ref[:, span] = dot(table_ref[...], operand_ref[:, span])
        for span in spans:
            out, slope = gelu_pair_low(value_ref[:, span] + self_ref[...])
            out_low_ref[0:hidden, span] = out
            slope_ref[:, span] = slope
        for span in spans:
            value_ref[:, span] = dot(out_t_ref[...], out_low_ref[:, span])
        for spot, span in zip(spots, spans):
            value = edge_ref[0, spot].astype(F32) + value_ref[:, span]
            centred = value - total(value) * share
            inverse = lax.rsqrt(total(centred * centred) * share + EPSILON)
            normed = centred * inverse
            gain = gain_ref[...]
            result_ref[0, spot] = (normed * gain + shift_ref[...]).astype(BF16)
            scaled = up_ref[0, spot].astype(F32) * gain
            product = scaled * normed
            product_ref[:, span] = product.astype(BF16)
            mixed = inverse * (scaled - total(scaled) * share - normed * (total(product) * share))
            mixed_ref[:, span] = mixed.astype(BF16)
        for span in spans:
            value_ref[:, span] = dot(out_ref[...], mixed_ref[:, span])
        for span in spans:
            grad = slope_ref[:, span].astype(F32) * value_ref[:, span]
            self_grad_ref[...] += grad
            grad_ref[:, span] = grad.astype(BF16)
        out_grad_ref[...] += dot_nt(mixed_ref[...], out_low_ref[...])
        for spot, span in zip(spots, spans):
            edge = dot(weight_ref[...], grad_ref[:, span])
            part_ref[0, spot] = (mixed_ref[:, span].astype(F32) + edge).astype(BF16)
        table_grad_ref[...] += dot_nt(grad_ref[...], operand_ref[...])
        sums_of = gain_grad_ref[...]
        for span in spans:
            sums_of = sums_of + product_ref[:, span].astype(F32)
        gain_grad_ref[...] = sums_of
        sums_of = shift_grad_ref[...]
        for spot in spots:
            sums_of = sums_of + up_ref[0, spot].astype(F32)
        shift_grad_ref[...] = sums_of
        return carry

    lax.fori_loop(0, steps // group, some, 0)
    edge_grad_ref[...] += table_grad_ref[:, 0:channels]
    for spot in range(calls):

        @pl.when(number == spot)
        def _(spot=spot):
            sums[spot][:, 0:lanes] = self_grad_ref[...].astype(BF16)
            sums[spot][:, lanes:] = table_grad_ref[:, channels:].astype(BF16)

    @pl.when(number == calls - 1)
    def _():
        for ref, base in zip(grads, bases):
            total_ref[:, base : base + ref.shape[1]] = ref[...]
        for ref, base in zip(sum_refs, sum_bases):
            flat = jnp.sum(ref[...], axis=1, keepdims=True)
            total_ref[:, base : base + 128] = jnp.broadcast_to(flat, (channels, 128))


def return_body(perm_ref, *refs, count):
    sums = refs[:count]
    turned_ref, up_ref = refs[count : count + 2]
    second_ref, leave_ref, sum_ref = refs[count + 2 :]
    total = sums[0][...].astype(F32)
    for spot in range(1, count):
        total = total + sums[spot][...].astype(F32)
    low = total.astype(BF16)
    lanes, width = second_ref.shape
    back = dot_tn(low[:, lanes:], turned_ref[:, width : 2 * width])
    leave_ref[...] = back[lanes:].astype(BF16)
    second_ref[...] = (
        up_ref[0].astype(F32) + dot_tn(low[:, 0:lanes], turned_ref[:, 0:width]) + back[0:lanes]
    )
    sum_ref[...] = total


def update_weights_body(perm_ref, sum_ref, low_ref, arrive_ref, grad_ref, column_ref, whole_ref):
    total = sum_ref[...]
    low = total.astype(BF16)
    lanes = low_ref.shape[0]
    channels = grad_ref.shape[0]
    hidden = low.shape[0]
    rows = jnp.concatenate([low_ref[...], arrive_ref[...]], axis=0)
    lane = lax.broadcasted_iota(jnp.int32, (channels, 128), 1)
    vectors = jnp.where(
        lane == 0,
        jnp.sum(total[:, 0:lanes], axis=1, keepdims=True),
        jnp.where(
            lane == 1,
            grad_ref[:, 512:513] / column_ref[:, 1:2],
            jnp.where(lane == 2, grad_ref[:, 640:641], grad_ref[:, 256 + hidden : 257 + hidden]),
        ),
    )
    whole_ref[...] = jnp.concatenate(
        [
            dot(low[:, 0:lanes], low_ref[...]),
            dot(low[:, lanes:], rows),
            grad_ref[:, 0:channels],
            grad_ref[:, 256 : 256 + hidden],
            vectors,
        ],
        axis=1,
    )


def backward_body(*refs, count):
    second_ref, return_ref, send_ref, one_ref, two_ref, share_ref, vector_ref, slope_ref = refs[:8]
    blocks = list(refs[8 : 8 + count])
    blocks = blocks + [refs[8 + count].at[spot] for spot in range(count)]
    aggregate_ref, forward_ref, sum_ref, grad_ref = refs[9 + count :]
    lanes = one_ref.shape[0]
    second_grad = second_ref[...] + dot_tn(send_ref[...], return_ref[...])
    _, first_normed, first_inverse = norm_forward(
        one_ref[...], vector_ref[2:3, :], vector_ref[4:5, :]
    )
    _, second_normed, second_inverse = norm_forward(
        two_ref[...], vector_ref[3:4, :], vector_ref[5:6, :]
    )
    total = lambda value: jnp.sum(value, axis=0, keepdims=True)
    grad_ref[3:4, :] = total(second_grad * second_normed)
    grad_ref[5:6, :] = total(second_grad)
    sum_two = norm_backward(second_grad, second_normed, second_inverse, vector_ref[3:4, :])
    low = sum_two.astype(BF16)
    forward_ref[0:lanes, :] = low
    grad_ref[1:2, :] = total(low.astype(F32))
    first_grad = sum_two
    for spot in range(2 * count):
        block = blocks[spot]
        half = (block.shape[0] - 16) // 2
        slope = slope_ref[:, spot * half : (spot + 1) * half].astype(F32)
        grad = (slope * dot_nt(low, block[half : 2 * half, :])).astype(BF16)
        first_grad = first_grad + dot(grad, block[0:half, :])
    grad_ref[2:3, :] = total(first_grad * first_normed)
    grad_ref[4:5, :] = total(first_grad)
    sum_one = norm_backward(first_grad, first_normed, first_inverse, vector_ref[2:3, :])
    sum_ref[...] = sum_one
    aggregate = sum_one.astype(BF16)
    aggregate_ref[...] = aggregate
    grad_ref[0:1, :] = total(share_ref[:, 0:1] * aggregate.astype(F32))
    grad_ref[6:16, :] = jnp.zeros((10, grad_ref.shape[1]), F32)
    forward_ref[lanes:, :] = grad_ref[...].astype(BF16)


def message_backward_body(perm_ref, *refs, count, calls, first_call):
    edge_ref, slot_ref, slope_ref, part_ref, edge_weight_ref, count_ref = refs[:6]
    weights = refs[6 : 6 + count]
    others = refs[6 + count : 6 + 2 * count]
    ups = refs[6 + 2 * count : 6 + 2 * count + calls]
    refs = refs[6 + 2 * count + calls :]
    if not first_call:
        node_ref, arrive_ref, own_node_ref, own_arrive_ref, mean_ref, own_mean_ref = refs[:6]
        own_up_ref, own_low_ref, own_edge_ref, whole_ref = refs[6:10]
        refs = refs[11:]
    grad_ref = refs[0]
    backs = refs[1 : 1 + calls]
    low_out_ref, edge_out_ref = refs[1 + calls : 3 + calls]
    weight_ref, up_ref, table_grad_ref, self_grad_ref = refs[3 + calls : 7 + calls]
    operand_ref, grad_low_ref = refs[7 + calls : 9 + calls]
    if not first_call:
        mine_ref, other_ref = low_out_ref, edge_out_ref
        low_ref, row_ref, mean_all_ref, up_all_ref = refs[9 + calls : 13 + calls]
        edge_total_ref, bias_ref, total_ref, out_total_ref = refs[13 + calls :]
    group = operand_ref.shape[1] // edge_ref.shape[3]
    number = pl.program_id(0)
    steps, channels, lanes = edge_ref.shape[1:]
    part = 2 * weights[0].shape[0]
    hidden = part * count
    width = backs[0].shape[1]
    pool = backs[0].shape[0]

    @pl.when(number == 0)
    def _():
        fill_weights(perm_ref, weights, others, weight_ref, count)
        if not first_call:
            low_ref[:, 0:pool] = own_low_ref[...]
            row_ref[0:lanes, :] = own_node_ref[0]
            row_ref[lanes:pool, :] = own_arrive_ref[...].reshape(-1, width)
            mean_all_ref[:, 0:lanes] = own_mean_ref[0]
            up_all_ref[0:lanes, :] = own_up_ref[...]
            edge_total_ref[...] = own_edge_ref[...]

    for spot in range(calls):

        @pl.when(number == spot)
        def _(spot=spot):
            value = dot_nt(weight_ref[:, 2 * width : 3 * width], ups[spot][...])
            number_of = perm_ref[spot if first_call else spot + 1]
            scale = 1.0 / jnp.maximum(chosen_row(count_ref[...], number_of), 1.0)
            up_ref[...] = (value * scale).astype(BF16)
            if not first_call:
                at = (spot + 1) * pool
                row_ref[at : at + lanes, :] = node_ref[0]
                row_ref[at + lanes : at + pool, :] = arrive_ref[...].reshape(-1, width)
                at = (spot + 1) * lanes
                mean_all_ref[:, at : at + lanes] = mean_ref[0]
                up_all_ref[at : at + lanes, :] = ups[spot][...]

    table_grad_ref[...] = jnp.zeros_like(table_grad_ref)
    self_grad_ref[...] = jnp.zeros_like(self_grad_ref)
    spans = [slice(spot * lanes, (spot + 1) * lanes) for spot in range(group)]

    def some(index, carry):
        spots = [index * group + spot for spot in range(group)]
        for spot, span in zip(spots, spans):
            operand_ref[0:channels, span] = edge_ref[0, spot]
            operand_ref[channels:, span] = selector(slot_ref[0, pl.ds(spot, 1), :], pool)
        total = self_grad_ref[...]
        for spot, span in zip(spots, spans):
            grad = slope_ref[0, spot] * up_ref[...]
            grad_low_ref[:, span] = grad
            total = total + grad.astype(F32)
        self_grad_ref[...] = total
        for spot, span in zip(spots, spans):
            edge = dot(edge_weight_ref[...], grad_low_ref[:, span])
            grad_ref[0, spot] = (part_ref[0, spot].astype(F32) + edge).astype(BF16)
        table_grad_ref[...] += dot_nt(grad_low_ref[...], operand_ref[...])
        return carry

    lax.fori_loop(0, steps // group, some, 0)
    self_low = self_grad_ref[...].astype(BF16)
    pool_low = table_grad_ref[:, channels:].astype(BF16)
    self_back = dot_tn(self_low, weight_ref[:, 0:width])
    pool_back = dot_tn(pool_low, weight_ref[:, width : 2 * width])
    low_both = jnp.concatenate(
        [
            jnp.concatenate([self_low, jnp.zeros((hidden, pool - lanes), BF16)], axis=1),
            pool_low,
        ],
        axis=0,
    )
    for spot in range(calls):

        @pl.when(number == spot)
        def _(spot=spot):
            backs[spot][0:lanes, :] = (self_back + pool_back[0:lanes]).astype(BF16)
            backs[spot][lanes:, :] = pool_back[lanes:].astype(BF16)
            if not first_call:
                low_ref[:, (spot + 1) * pool : (spot + 2) * pool] = low_both

    if first_call:
        low_out_ref[...] = low_both
        edge_out_ref[...] = table_grad_ref[:, 0:channels]
        return
    edge_total_ref[...] += table_grad_ref[:, 0:channels]

    @pl.when(number == calls - 1)
    def _():
        total_ref[...] = dot(low_ref[...], row_ref[...])
        out_total_ref[...] = dot(mean_all_ref[...], up_all_ref[...])
        ones = jnp.ones((row_ref.shape[0], 128), BF16)
        bias_ref[...] = dot(low_ref[0:hidden, :], ones)
        core = perm_ref[count + 1]
        half = part // 2
        rows = whole_ref.shape[0] // count // 2
        for spot in range(count):
            for place, ref in ((core, mine_ref), (1 - core, other_ref)):
                first = pl.multiple_of(spot * part + place * half, half)
                kind = ref.dtype
                ref[spot, 0:half, 0:width] = total_ref[pl.ds(first, half), :].astype(kind)
                ref[spot, 0:half, width : 2 * width] = total_ref[pl.ds(hidden + first, half), :].astype(kind)
                ref[spot, 0:half, 2 * width : 3 * width] = out_total_ref[pl.ds(first, half), :].astype(kind)
                start = pl.multiple_of((place * count + perm_ref[spot]) * rows, 8)
                wide = whole_ref.shape[1]
                below = jnp.concatenate(
                    [
                        whole_ref[pl.ds(start, rows), :],
                        jnp.zeros((ref.shape[1] - half - rows, wide), F32),
                    ],
                    axis=0,
                )
                ref[spot, half:, 0:wide] = below.astype(kind)
                ref[spot, half:, wide:] = jnp.zeros((below.shape[0], ref.shape[2] - wide), kind)
                both = jnp.concatenate(
                    [
                        edge_total_ref[pl.ds(first, half), :],
                        bias_ref[pl.ds(first, half), 0 : ref.shape[2] - 3 * width - channels],
                    ],
                    axis=1,
                )
                ref[spot, 0:half, 3 * width :] = both.astype(kind)


def wide_body(
    perm_ref, low_ref, forward_ref, weight_ref, bias_ref, output_ref, mine_ref, other_ref, all_ref, *, count
):
    width = low_ref.shape[1]
    wide = weight_ref.shape[1]
    step = forward_ref.shape[0] // count
    lanes = step - 16
    low = low_ref[...]
    forward = jnp.concatenate(
        [forward_ref[spot * step : spot * step + lanes, :] for spot in range(count)], axis=0
    )
    lines = None
    for spot in range(count):
        line = forward_ref[spot * step + lanes : (spot + 1) * step, :].astype(F32)
        lines = line if spot == 0 else lines + line
    pre = dot(low, weight_ref[...]) + bias_ref[0:1, :].astype(F32)
    out, slope = gelu_pair_low(pre)
    grad = slope.astype(F32) * dot_nt(forward, output_ref[...])
    all_ref[0:width, :] = dot_tn(low, grad.astype(BF16))
    all_ref[width : width + wide, :] = dot_tn(out, forward)
    at = width + wide
    total = jnp.broadcast_to(jnp.sum(grad, axis=0, keepdims=True), (8, wide))
    all_ref[at : at + 8, :] = total
    all_ref[at + 8 : at + 16, :] = lines[0:8]
    all_ref[at + 16 :, :] = jnp.zeros((all_ref.shape[0] - at - 16, width), F32)
    half = mine_ref.shape[0]
    core = perm_ref[count + 1]
    mine_ref[...] = all_ref[pl.ds(pl.multiple_of(core * half, 8), half), :]
    other_ref[...] = all_ref[pl.ds(pl.multiple_of((1 - core) * half, 8), half), :].astype(BF16)


def wide_finish_body(
    perm_ref, mine_ref, other_ref, in_ref, out_ref, bias_ref, one_ref, two_ref, three_ref, all_ref, *, count
):
    core = perm_ref[count + 1]
    half = mine_ref.shape[0]
    all_ref[pl.ds(pl.multiple_of(core * half, 8), half), :] = mine_ref[...].astype(F32)
    all_ref[pl.ds(pl.multiple_of((1 - core) * half, 8), half), :] = other_ref[...].astype(F32)
    width = in_ref.shape[0]
    wide = out_ref.shape[0]
    in_ref[...] = all_ref[0:width, :]
    out_ref[...] = all_ref[width : width + wide, :]
    at = width + wide
    bias_ref[...] = all_ref[at : at + 1, :]
    one_ref[...] = all_ref[at + 8 : at + 10, :]
    two_ref[...] = all_ref[at + 10 : at + 12, :]
    three_ref[...] = all_ref[at + 12 : at + 14, :]


def late_finish_body(
    perm_ref,
    mine_ref,
    other_ref,
    mine_parts_ref,
    other_parts_ref,
    nodes_ref,
    output_ref,
    bias_ref,
    turned_ref,
    update_ref,
    hidden_bias_ref,
    gain_ref,
    shift_ref,
    branch_ref,
    edge_ref,
    own_ref,
    whole_ref,
    edges_ref,
    *,
    count,
):
    core = perm_ref[count + 1]
    part = own_ref.shape[0]
    half = part // 2
    width = output_ref.shape[1]
    rows = whole_ref.shape[0] // count // 2
    channels = edges_ref.shape[1]
    for place, ref, parts in ((core, mine_ref, mine_parts_ref), (1 - core, other_ref, other_parts_ref)):
        own_ref[pl.ds(pl.multiple_of(place * half, 8), half), :] = ref[...].astype(F32)
        for spot in range(count):
            value = parts[spot].astype(F32)
            start = pl.multiple_of((place * count + perm_ref[spot]) * rows, 8)
            whole_ref[pl.ds(start, rows), :] = value[0:rows, :]
            first = perm_ref[spot] * part + place * half
            for turn in range(half // 8):
                start = pl.multiple_of(first + 8 * turn, 8)
                edges_ref[pl.ds(start, 8), :] = value[rows:, turn * channels : (turn + 1) * channels]
    nodes_ref[0] = own_ref[:, 0:width].T
    nodes_ref[1] = own_ref[:, width : 2 * width].T
    output_ref[...] = own_ref[:, 2 * width : 3 * width]
    last = own_ref.shape[1]
    bias_ref[...] = own_ref[:, last - 128 :].T[127:128, :]
    end = turned_ref.shape[1]
    hidden = update_ref.shape[0]
    turned_ref[...] = whole_ref[:, 0:end]
    update_ref[...] = whole_ref[:, end : end + hidden].T
    vectors = whole_ref[:, end + hidden :].T
    hidden_bias_ref[...] = vectors[0:1, :]
    gain_ref[...] = vectors[1:2, :]
    shift_ref[...] = vectors[2:3, :]
    branch_ref[...] = vectors[3:4, :]
    edge_ref[...] = edges_ref[...].T


def place_body(perm_ref, *refs, count):
    for spot in range(count):

        @pl.when(pl.program_id(0) == spot)
        def _(spot=spot):
            refs[count][0] = refs[spot][...]


def held(value):
    return pltpu.with_memory_space_constraint(value, pltpu.HBM)


def group_of(total, most=15):
    for size in (15, 5, 4, 3, 2, 1):
        if size <= most and total % size == 0:
            return size


def call(body, grid, ins, outs, scratch, flops, moved, name, perm=None, limit=56, aliases=()):
    whole = lambda block: (block, lambda *_: (0,) * len(block))
    in_specs = [
        pl.BlockSpec(memory_space=pl.ANY)
        if len(entry) == 2
        else pl.BlockSpec(*(entry[1:] if len(entry) == 3 else whole(entry[0].shape)))
        for entry in ins
    ]
    out_specs = [
        pl.BlockSpec(*(entry[2:] if len(entry) == 4 else whole(entry[0]))) for entry in outs
    ]
    spec = pltpu.PrefetchScalarGridSpec(
        num_scalar_prefetch=0 if perm is None else 1,
        grid=grid,
        in_specs=in_specs,
        out_specs=out_specs,
        scratch_shapes=scratch,
    )
    operands = [entry[0] for entry in ins]
    return pl.pallas_call(
        body,
        grid_spec=spec,
        out_shape=[(pltpu.HBM if name in PINNED else jax.ShapeDtypeStruct)(entry[0], entry[1]) for entry in outs],
        input_output_aliases={source + 1: target for source, target in aliases},
        compiler_params=pltpu.CompilerParams(
            dimension_semantics=("arbitrary",) * len(grid), vmem_limit_bytes=limit * 2**20
        ),
        cost_estimate=pl.CostEstimate(flops=flops, bytes_accessed=moved, transcendentals=0),
        name=name,
    )(*([] if perm is None else [perm]), *operands)


def build(prot_size, res_size, mp_size):
    def across(value, offset):
        pairs = [(spot, spot ^ offset) for spot in range(mp_size)]
        return lax.ppermute(value, "mp", pairs)

    def gather(value):
        return [value] + [across(value, offset) for offset in range(1, mp_size)]

    def scatter(parts):
        return [parts[0]] + [across(parts[offset], offset) for offset in range(1, mp_size)]

    def exchange(value):
        return lax.all_to_all(value, "res", split_axis=0, concat_axis=0, tiled=True)

    def block_parts(value):
        place = lax.axis_index("res")
        piece = value.shape[0] // res_size
        parts = [lax.dynamic_slice_in_dim(value, place * piece, piece, 0)]
        low = value.astype(BF16)
        for hop in range(1, res_size):
            target = lax.rem(place + hop, res_size)
            part = lax.dynamic_slice_in_dim(low, target * piece, piece, 0)
            pairs = [(spot, (spot + hop) % res_size) for spot in range(res_size)]
            parts.append(lax.ppermute(part, "res", pairs))
        return parts

    def block_gather(own):
        parts = [own]
        for hop in range(1, res_size):
            pairs = [(spot, (spot - hop) % res_size) for spot in range(res_size)]
            parts.append(lax.ppermute(own, "res", pairs))
        return parts

    def block_order(parts):
        place = lax.axis_index("res")
        piece = parts[0].shape[0]
        both = jnp.concatenate(parts + parts, axis=0)
        return lax.dynamic_slice_in_dim(both, (res_size - place) * piece, res_size * piece, 0)

    def swap(value):
        return lax.ppermute(value, "prot", [(0, 1), (1, 0)])

    def per_device(
        node_states,
        edge_states,
        neighbour_slots,
        send_rows,
        live_counts,
        message_nodes,
        message_edges,
        message_bias,
        message_output,
        feedforward_weight,
        feedforward_bias,
        feedforward_output,
        output_biases,
        norm_gains,
        norm_shifts,
        update_weight,
        update_bias,
        update_output,
        branch_bias,
        edge_gain,
        edge_shift,
        node_cotangent,
        edge_cotangent,
    ):
        proteins, lanes, width = node_states.shape
        own_k, channels = edge_states.shape[2:]
        slots = send_rows.shape[3]
        remote = res_size * slots
        pool = lanes + remote
        part = message_nodes.shape[2]
        hidden = part * mp_size
        update_hidden = update_output.shape[0]
        wide = feedforward_weight.shape[1]
        assert proteins == mp_size and prot_size == 2
        me = lax.axis_index("mp")
        core = lax.axis_index("prot")
        place = lax.axis_index("res")
        dead = lanes + place * slots
        order = [me ^ offset for offset in range(mp_size)]
        perm = jnp.stack(order + [dead, core]).astype(jnp.int32)

        def reorder(value, axis=0):
            size = value.shape[axis] // mp_size
            return jnp.concatenate(
                [lax.dynamic_slice_in_dim(value, spot * size, size, axis) for spot in order], axis=axis
            )

        message_pack, leaving = call(
            functools.partial(pack_body, count=mp_size),
            (1,),
            [
                (message_nodes,),
                (message_output,),
                (message_bias,),
                (send_rows,),
                (node_states,),
            ],
            [
                ((part // 2, 3 * width + 128), BF16),
                ((res_size, proteins, slots, width), BF16),
            ],
            [pltpu.VMEM((part, 3 * width + 128), BF16)],
            0,
            0,
            "pack",
            perm,
        )
        arriving = exchange(leaving)
        weights = gather(message_pack)
        other_weights = [swap(value) for value in weights]
        own_slots = lax.dynamic_slice_in_dim(neighbour_slots, me * own_k, own_k, 2)
        alive = lax.broadcasted_iota(jnp.int32, own_slots.shape, 2) + me * own_k < live_counts[..., None]
        own_slots = jnp.transpose(jnp.where(alive, own_slots, dead), (0, 2, 1))
        edges = jnp.transpose(edge_states, (0, 2, 3, 1))
        edge_up = jnp.transpose(edge_cotangent, (0, 2, 3, 1))
        turned = update_weight.T
        small = call(
            functools.partial(prepare_body, count=mp_size),
            (1,),
            [
                (message_edges,),
                (turned,),
                (update_output,),
                (update_bias,),
                (edge_gain,),
                (edge_shift,),
                (branch_bias,),
                (feedforward_bias,),
                (output_biases,),
                (norm_gains,),
                (norm_shifts,),
                (live_counts,),
                (send_rows,),
                (node_states, (1, lanes, width), lambda p, perm: (perm[0], 0, 0)),
                (node_cotangent, (1, lanes, width), lambda p, perm: (perm[0], 0, 0)),
                (feedforward_weight,),
                (feedforward_output,),
            ],
            [
                ((channels, hidden), BF16),
                ((hidden, channels), BF16),
                ((channels, 128), F32),
                ((channels, update_hidden + 16), BF16),
                ((channels, update_hidden), BF16),
                ((8, width), F32),
                ((lanes, 128), F32),
                ((remote, lanes), BF16),
                ((16, wide), BF16),
                ((1, lanes, width), BF16),
                ((1, lanes, width), BF16),
                ((wide + 16, width), BF16),
            ],
            [],
            0,
            0,
            "prepare",
            perm,
        )
        *small, block = small
        blocks = gather(block)
        weights, other_weights, arriving, own_slots, small = lax.optimization_barrier(
            (weights, other_weights, arriving, own_slots, small)
        )
        (
            edge_weight,
            edge_weight_t,
            columns,
            out_t,
            turned_edge,
            vectors,
            share,
            own_table,
            wide_bias,
            own_node,
            own_up,
        ) = small

        depth = channels + pool
        group = group_of(own_k, 5)
        group_update = group_of(own_k, 5)
        group_back = group_of(own_k, 5)
        count = proteins * own_k * lanes
        by_step4 = lambda p, perm: (p, 0, 0, 0)
        by_step3 = lambda p, perm: (p, 0, 0)
        others = proteins - 1

        def shifted(start):
            return (
                lambda p, perm: (perm[p + start], 0, 0, 0),
                lambda p, perm: (perm[p + start], 0, 0),
                lambda p, perm: (0, perm[p + start], 0, 0),
            )

        edge_block = (1, own_k, channels, lanes)
        edge_shape = (proteins, own_k, channels, lanes)
        slope_shape = (proteins, own_k, hidden, lanes)
        slope_block = (1, own_k, hidden, lanes)

        def edge_ins(start):
            by_perm4, by_perm3, _ = shifted(start)
            return [(edges, edge_block, by_perm4), (own_slots, (1, own_k, lanes), by_perm3)]

        def row_ins(start):
            _, by_perm3, by_arrive = shifted(start)
            return [
                (node_states, (1, lanes, width), by_perm3),
                (arriving, (res_size, 1, slots, width), by_arrive),
            ]

        def message_forward(start, calls, after):
            slots_after, _ = lax.optimization_barrier((own_slots, after))
            found = call(
                functools.partial(message_forward_body, count=proteins, calls=calls, start=start),
                (calls,),
                [edge_ins(start)[0], (slots_after,) + edge_ins(start)[1][1:]]
                + row_ins(start)
                + [(edge_weight_t,), (live_counts,)]
                + [(value,) for value in weights + other_weights],
                [
                    ((calls, own_k, hidden, lanes), BF16, slope_block, by_step4),
                    ((calls, hidden, lanes), BF16, (1, hidden, lanes), by_step3),
                ]
                + [((lanes, width), BF16)] * calls,
                [
                    pltpu.VMEM((hidden, weights[0].shape[1]), BF16),
                    pltpu.VMEM((hidden, depth), BF16),
                    pltpu.VMEM((hidden, lanes), F32),
                    pltpu.VMEM((hidden, lanes), F32),
                    pltpu.VMEM((group, depth, lanes), BF16),
                    pltpu.VMEM((group, hidden, lanes), F32),
                ],
                2 * calls * own_k * lanes * depth * hidden,
                calls * own_k * lanes * (channels + hidden) * 2,
                "message_forward",
                perm,
            )
            return found[0], found[1], list(found[2:])

        slope_others, mean_others, part_others = message_forward(1, others, own_slots)
        slope_own, mean_own, part_own = message_forward(0, 1, part_others[0])
        parts = scatter(part_own + part_others)
        blocks, _ = lax.optimization_barrier((blocks, part_others[0]))
        other_blocks = swap(jnp.stack(blocks))
        one, two, first_low, second_low, leaving, own_term, wide_slope = call(
            functools.partial(forward_body, count=proteins),
            (),
            [(value,) for value in parts]
            + [(own_node,), (share,), (vectors,), (own_table,), (turned,)]
            + [(held(value),) for value in blocks]
            + [(held(other_blocks),)],
            [
                ((lanes, width), F32),
                ((lanes, width), F32),
                ((lanes, width), BF16),
                ((lanes, width), BF16),
                ((remote, width), BF16),
                ((update_hidden, 2 * lanes), BF16),
                ((lanes, wide * mp_size), BF16),
            ],
            [],
            4 * lanes * width * wide * mp_size,
            4 * width * wide * mp_size,
            "feed_forward",
            limit=24,
        )

        arrived = exchange(leaving.reshape(res_size, slots, width)).reshape(remote, width)
        joint = own_term.shape[1] == width
        if joint:
            terms = gather(jnp.concatenate([own_term, arrived], axis=0))
            pool_remotes = []
        else:
            terms = gather(own_term)
            pool_remotes = gather(arrived)
        all_low = lax.all_gather(first_low, "mp", axis=0, tiled=True)
        node_result = lax.all_gather(second_low[None], "mp", axis=0, tiled=True)
        turned_width = 2 * width + channels

        def edge_update(start, calls, earlier):
            by_perm4 = shifted(start)[0]
            ins = (
                edge_ins(start)
                + [(edge_up, edge_block, by_perm4)]
                + [(value,) for value in terms[start : start + calls]]
                + [(value,) for value in pool_remotes[start : start + calls]]
                + [(turned,), (columns,), (out_t,), (update_output,), (turned_edge,)]
            )
            aliases = ()
            if earlier is not None:
                ins = ins + [(earlier[1],), (earlier[0], None)]
                aliases = ((len(ins) - 1, 0),)
            found = call(
                functools.partial(
                    update_body,
                    count=proteins,
                    calls=calls,
                    first_call=earlier is None,
                    joint=joint,
                ),
                (calls,),
                ins,
                [
                    (edge_shape, BF16, edge_block, by_perm4),
                    ((calls, own_k, channels, lanes), BF16, edge_block, by_step4),
                ]
                + [((update_hidden, lanes + pool), BF16)] * calls
                + [((update_hidden, 768), F32)],
                [
                    pltpu.VMEM((update_hidden, depth), BF16),
                    pltpu.VMEM((update_hidden, lanes), F32),
                    pltpu.VMEM((update_hidden, depth), F32),
                    pltpu.VMEM((update_hidden, lanes), F32),
                    pltpu.VMEM((channels, lanes), F32),
                    pltpu.VMEM((channels, lanes), F32),
                    pltpu.VMEM((update_hidden, channels), F32),
                    pltpu.VMEM((channels, update_hidden + 16), F32),
                    pltpu.VMEM((channels, lanes), F32),
                    pltpu.VMEM((channels, lanes), F32),
                    pltpu.VMEM((depth, group_update * lanes), BF16),
                    pltpu.VMEM((update_hidden + 16, group_update * lanes), BF16),
                    pltpu.VMEM((channels, group_update * lanes), BF16),
                    pltpu.VMEM((update_hidden, group_update * lanes), BF16),
                    pltpu.VMEM((channels, group_update * lanes), BF16),
                    pltpu.VMEM((update_hidden, group_update * lanes), F32),
                    pltpu.VMEM((update_hidden, group_update * lanes), BF16),
                ],
                2 * calls * own_k * lanes * (2 * depth + 4 * channels) * update_hidden,
                calls * own_k * lanes * channels * 8,
                "edge_update",
                perm,
                aliases=aliases,
            )
            return found[0], found[-1], found[1], found[2:-1]

        edge_result, grads, edge_part_own, sums_own = edge_update(0, 1, None)
        edge_result, grads, edge_part_others, sums_others = edge_update(1, others, (edge_result, grads))
        sums_own, sums_others, all_low = lax.optimization_barrier((sums_own, sums_others, all_low))
        sums = scatter(list(sums_own) + list(sums_others))
        whole_width = turned_width + update_hidden + 128
        second_part, leaving, update_sums = call(
            functools.partial(return_body, count=proteins),
            (1,),
            [(value,) for value in sums]
            + [(turned,), (own_up,)],
            [
                ((lanes, width), F32),
                ((remote, width), BF16),
                ((update_hidden, lanes + pool), F32),
            ],
            [],
            2 * (lanes + pool) * width * update_hidden,
            (lanes + pool) * width * 2,
            "update_return",
            perm,
        )
        returned = exchange(leaving.reshape(res_size, slots, width)).reshape(remote, width)
        (whole,) = call(
            update_weights_body,
            (1,),
            [(update_sums,), (second_low,), (arrived,), (grads,), (columns,)],
            [((update_hidden, whole_width), F32)],
            [],
            2 * (lanes + pool) * width * update_hidden,
            (lanes + pool) * width * 2,
            "update_weights",
            perm,
        )
        whole, returned = lax.optimization_barrier((whole, returned))
        aggregate_grad, forward_grad, sum_one, _ = call(
            functools.partial(backward_body, count=proteins),
            (),
            [(second_part,), (returned,), (own_table,), (one,), (two,), (share,), (vectors,), (wide_slope,)]
            + [(held(value),) for value in blocks]
            + [(held(other_blocks),)],
            [
                ((lanes, width), BF16),
                ((lanes + 16, width), BF16),
                ((lanes, width), F32),
                ((16, width), F32),
            ],
            [],
            6 * lanes * width * wide * mp_size,
            4 * width * wide * mp_size,
            "feed_backward",
            limit=24,
        )
        ups = gather(aggregate_grad)
        all_forward = lax.all_gather(forward_grad, "mp", axis=0, tiled=True)
        total_width = 3 * width + -(-(channels + 1) // 128) * 128
        whole_rows = update_hidden // 2 // mp_size
        late_rows = -(-(part // 2 + whole_rows) // (8 * res_size)) * 8 * res_size
        late_shape = (proteins, late_rows, total_width)

        def message_backward(start, calls, earlier):
            by_perm4 = shifted(start)[0]
            ins = (
                edge_ins(start)
                + [
                    (slope_own if earlier is None else slope_others, slope_block, by_step4),
                    (edge_part_own if earlier is None else edge_part_others, edge_block, by_step4),
                    (edge_weight,),
                    (live_counts,),
                ]
                + [(value,) for value in weights + other_weights + ups[start : start + calls]]
            )
            aliases = ()
            scratch = [
                pltpu.VMEM((hidden, weights[0].shape[1]), BF16),
                pltpu.VMEM((hidden, lanes), BF16),
                pltpu.VMEM((hidden, depth), F32),
                pltpu.VMEM((hidden, lanes), F32),
                pltpu.VMEM((depth, group_back * lanes), BF16),
                pltpu.VMEM((hidden, group_back * lanes), BF16),
            ]
            if earlier is None:
                last = [((2 * hidden, pool), BF16), ((hidden, channels), F32)]
            else:
                mean_block = (1, hidden, lanes)
                ins = ins + row_ins(start)
                ins = ins + [
                    (node_states, (1, lanes, width), lambda p, perm: (perm[0], 0, 0)),
                    (arriving, (res_size, 1, slots, width), lambda p, perm: (0, perm[0], 0, 0)),
                    (mean_others, mean_block, by_step3),
                    (mean_own,),
                    (ups[0],),
                    (earlier[1],),
                    (earlier[2],),
                    (whole,),
                    (earlier[0], None),
                ]
                aliases = ((len(ins) - 1, 0),)
                last = [(late_shape, F32), (late_shape, BF16)]
                scratch = scratch + [
                    pltpu.VMEM((2 * hidden, proteins * pool), BF16),
                    pltpu.VMEM((proteins * pool, width), BF16),
                    pltpu.VMEM((hidden, proteins * lanes), BF16),
                    pltpu.VMEM((proteins * lanes, width), BF16),
                    pltpu.VMEM((hidden, channels), F32),
                    pltpu.VMEM((hidden, 128), F32),
                    pltpu.VMEM((2 * hidden, width), F32),
                    pltpu.VMEM((hidden, width), F32),
                ]
            found = call(
                functools.partial(
                    message_backward_body, count=proteins, calls=calls, first_call=earlier is None
                ),
                (calls,),
                ins,
                [(edge_shape, BF16, edge_block, by_perm4)] + [((pool, width), BF16)] * calls + last,
                scratch,
                2 * calls * own_k * lanes * (depth + channels) * hidden,
                calls * own_k * lanes * (3 * channels + hidden) * 2,
                "message_backward",
                perm,
                aliases=aliases,
            )
            return found[0], found[-2], found[-1], found[1 : 1 + calls]

        edge_grad, own_low, own_edge, back_own = message_backward(0, 1, None)
        edge_grad, late_mine, late_other, back_others = message_backward(
            1, others, (edge_grad, own_low, own_edge)
        )
        found = list(back_own) + list(back_others)
        late_swapped = swap(late_other)
        backs, late_mine, all_forward, node_result = lax.optimization_barrier(
            (found, late_mine, all_forward, node_result)
        )
        back = scatter(backs)
        late = late_mine + late_swapped.astype(F32)
        late_own = late[0]
        late_low = [late[offset].astype(BF16) for offset in range(1, mp_size)]
        all_forward, late_own, late_low = lax.optimization_barrier((all_forward, late_own, late_low))
        late_parts = scatter([late_own] + late_low)
        unit = prot_size * res_size * 8
        wide_rows = -(-(width + wide + 16) // unit) * unit
        early_mine, early_other = call(
            functools.partial(wide_body, count=proteins),
            (1,),
            [
                (all_low,),
                (all_forward,),
                (feedforward_weight,),
                (wide_bias,),
                (feedforward_output,),
            ],
            [((wide_rows // 2, width), F32), ((wide_rows // 2, width), BF16)],
            [pltpu.VMEM((wide_rows, width), F32)],
            10 * proteins * lanes * width * wide,
            8 * proteins * lanes * width,
            "feed_weights",
            perm,
        )
        back, early_other, early_mine = lax.optimization_barrier((back, early_other, early_mine))
        early_swapped = swap(early_other)
        total = sum(value.astype(F32) for value in back)
        leaving = total[lanes:].astype(BF16).reshape(res_size, slots, width)
        leaving, early_swapped = lax.optimization_barrier((leaving, early_swapped))
        cut = early_mine.shape[0] // 2
        early = [
            (early_mine[spot : spot + cut] + early_swapped[spot : spot + cut].astype(F32)).astype(BF16)
            for spot in (0, cut)
        ]
        early, leaving = lax.optimization_barrier((early, leaving))
        early = jnp.concatenate(lax.psum(tuple(early), "res"), axis=0)
        returned = exchange(leaving)
        node_grad = (
            sum_one
            + total[:lanes]
            + jnp.einsum(
                "sr,sd->rd", own_table, returned.reshape(remote, width), preferred_element_type=F32
            )
        ).astype(BF16)
        node_grad, late_parts = lax.optimization_barrier((node_grad, late_parts))
        late = sum(value.astype(F32) for value in late_parts)
        late_parts = block_parts(late)
        node_parts = gather(node_grad)
        late = sum(value.astype(F32) for value in late_parts).astype(BF16)
        late, node_parts = lax.optimization_barrier((late, node_parts))
        late_parts = block_gather(late)
        (node_grad,) = call(
            functools.partial(place_body, count=proteins),
            (proteins,),
            [(value,) for value in node_parts],
            [((proteins, lanes, width), BF16, (1, lanes, width), shifted(0)[1])],
            [],
            0,
            0,
            "place_rows",
            perm,
        )
        early, node_grad, late_parts = lax.optimization_barrier((early, node_grad, late_parts))
        late = block_order(late_parts)
        whole = late[part // 2 : part // 2 + whole_rows, :whole_width]
        late = late[: part // 2]
        early_swapped = swap(early)
        late_swapped = swap(late)
        fold = late[:, 3 * width : 3 * width + channels].reshape(-1, 8, channels)
        fold = jnp.transpose(fold, (1, 0, 2)).reshape(8, -1)
        shared_parts = gather(jnp.concatenate([whole, fold], axis=0))
        weight_in_grad, weight_out_grad, wide_bias_grad, biases_grad, gains_grad, shifts_grad = call(
            functools.partial(wide_finish_body, count=proteins),
            (1,),
            [(early,), (early_swapped,)],
            [
                ((width, wide), F32),
                ((wide, width), F32),
                ((1, wide), F32),
                ((2, width), F32),
                ((2, width), F32),
                ((2, width), F32),
            ],
            [pltpu.VMEM((wide_rows, width), F32)],
            0,
            8 * wide_rows * width,
            "feed_weights_out",
            perm,
        )
        weight_in_grad, shared_parts, late_swapped = lax.optimization_barrier(
            (weight_in_grad, shared_parts, late_swapped)
        )
        shared = jnp.stack(shared_parts)
        found = call(
            functools.partial(late_finish_body, count=proteins),
            (1,),
            [(late,), (late_swapped,), (shared,), (swap(shared),)],
            [
                ((2, width, part), F32),
                ((part, width), F32),
                ((1, part), F32),
                ((update_hidden, turned_width), F32),
                ((update_hidden, channels), F32),
                ((1, update_hidden), F32),
                ((1, channels), F32),
                ((1, channels), F32),
                ((1, channels), F32),
                ((channels, hidden), F32),
            ],
            [
                pltpu.VMEM((part, total_width), F32),
                pltpu.VMEM((update_hidden, turned_width + update_hidden + 128), F32),
                pltpu.VMEM((hidden, channels), F32),
            ],
            0,
            8 * hidden * total_width,
            "message_weights_out",
            perm,
            16,
        )
        turn = lambda value: jnp.transpose(value, (0, 3, 1, 2))
        return (
            node_result,
            turn(edge_result),
            node_grad,
            turn(edge_grad),
            found[0],
            found[9],
            found[2].reshape(part),
            found[1],
            weight_in_grad,
            wide_bias_grad.reshape(wide),
            weight_out_grad,
            biases_grad,
            gains_grad,
            shifts_grad,
            found[3].T,
            found[5].reshape(update_hidden),
            found[4],
            found[8].reshape(channels),
            found[6].reshape(channels),
            found[7].reshape(channels),
        )

    return per_device


def solution(mesh):
    return jax.shard_map(
        build(mesh.shape["prot"], mesh.shape["res"], mesh.shape["mp"]),
        mesh=mesh,
        in_specs=(
            P("prot", "res", None),
            P("prot", "res", "mp", None),
            P("prot", "res", None),
            P("prot", "res", None, None),
            P("prot", "res"),
            P(None, None, "mp"),
            P(),
            P("mp"),
            P("mp", None),
            P(None, "mp"),
            P("mp"),
            P("mp", None),
            P(),
            P(),
            P(),
            P(),
            P(),
            P(),
            P(),
            P(),
            P(),
            P("prot", "res", None),
            P("prot", "res", "mp", None),
        ),
        out_specs=(
            P("prot", "res", None),
            P("prot", "res", "mp", None),
            P("prot", "res", None),
            P("prot", "res", "mp", None),
            P(None, None, "mp"),
            P(),
            P("mp"),
            P("mp", None),
            P(None, "mp"),
            P("mp"),
            P("mp", None),
            P(),
            P(),
            P(),
            P(),
            P(),
            P(),
            P(),
            P(),
            P(),
        ),
        check_vma=False,
    )
```

```python
import functools

import jax
import jax.numpy as jnp
from jax import lax
from jax.experimental import pallas as pl
from jax.experimental.pallas import tpu as pltpu
from jax.sharding import PartitionSpec as P

EPSILON = 1e-05
F32 = jnp.float32
PINNED = ("prepare",)
BF16 = jnp.bfloat16
DEAD = -30000.0
CUBIC = 0.044715
ROOT = 0.7978845608028654


def dot(left, right):
    return jnp.dot(left, right, preferred_element_type=F32)


def dot_nt(left, right):
    return lax.dot_general(left, right, (((1,), (1,)), ((), ())), preferred_element_type=F32)


def gelu_pair(value):
    square = value * value
    gate = 0.5 + 0.5 * jnp.tanh(value * (ROOT + (ROOT * CUBIC) * square))
    out = value * gate
    slope = gate + (out - out * gate) * (2.0 * ROOT + (6.0 * ROOT * CUBIC) * square)
    return out, slope


def low(value):
    return jnp.asarray(value, BF16)


def gelu_pair_low(value):
    value = value.astype(BF16)
    square = value * value
    inner = value * (low(-2.0 * ROOT) + low(-2.0 * ROOT * CUBIC) * square)
    power = jnp.exp(jnp.minimum(inner, low(80.0)))
    gate = pl.reciprocal(low(1.0) + power, approx=True)
    out = value * gate
    slope = gate + (out * (power * gate)) * (low(2.0 * ROOT) + low(6.0 * ROOT * CUBIC) * square)
    return out, slope


def activation(value):
    return jax.nn.gelu(value, approximate=True)


def activation_grad(value, upstream):
    return jax.vjp(activation, value)[1](upstream)[0]


def norm_forward(value, gain, shift):
    centred = value - jnp.mean(value, axis=-1, keepdims=True)
    inverse = lax.rsqrt(jnp.mean(centred * centred, axis=-1, keepdims=True) + EPSILON)
    normed = centred * inverse
    return (normed * gain + shift, normed, inverse)


def norm_backward(upstream, normed, inverse, gain):
    scaled = upstream * gain
    inner = (
        scaled
        - jnp.mean(scaled, axis=-1, keepdims=True)
        - normed * jnp.mean(scaled * normed, axis=-1, keepdims=True)
    )
    return inverse * inner


def chosen_row(value, row):
    rows = lax.broadcasted_iota(jnp.int32, value.shape, 0)
    return jnp.sum(jnp.where(rows == row, value.astype(F32), 0.0), axis=0, keepdims=True)


def selector(slot_row, rows):
    positions = lax.broadcasted_iota(jnp.int16, (rows, slot_row.shape[1]), 0)
    return jnp.where(positions == slot_row.astype(jnp.int16), low(1.0), low(0.0))


def dot_tn(left, right):
    return lax.dot_general(left, right, (((0,), (0,)), ((), ())), preferred_element_type=F32)


def masked_table(fixed, term, dead):
    positions = lax.broadcasted_iota(jnp.int32, term.shape, 1)
    term = jnp.where(positions == dead, DEAD, term).astype(BF16)
    return jnp.concatenate([fixed, term], axis=1)


def message_forward_body(perm_ref, *refs, count, calls, start):
    edge_ref, slot_ref, node_ref, arrive_ref, fixed_ref, count_ref = refs[:6]
    weights = refs[6 : 6 + count]
    others = refs[6 + count : 6 + 2 * count]
    refs = refs[6 + 2 * count :]
    slope_ref, mean_ref = refs[:2]
    parts = refs[2 : 2 + calls]
    weight_ref, table_ref, self_ref, sum_ref, operand_ref, value_ref = refs[2 + calls :]
    number = pl.program_id(0)
    group = operand_ref.shape[0]
    dead = perm_ref[count]
    steps, channels, lanes = edge_ref.shape[1:]
    width = node_ref.shape[2]

    @pl.when(number == 0)
    def _():
        fill_weights(perm_ref, weights, others, weight_ref, count)

    nodes = node_ref[0]
    arrive = arrive_ref[...].reshape(-1, width)
    pool = lanes + arrive.shape[0]
    rows = jnp.concatenate([nodes, arrive], axis=0)
    term = dot_nt(weight_ref[:, width : 2 * width], rows)
    table_ref[...] = masked_table(fixed_ref[...], term, dead)
    bias = weight_ref[:, 3 * width : 3 * width + 1].astype(F32)
    self_ref[...] = dot_nt(weight_ref[:, 0:width], nodes) + bias
    sum_ref[...] = jnp.zeros_like(sum_ref)

    def some(index, carry):
        spots = [index * group + spot for spot in range(group)]
        for spot in range(group):
            operand_ref[spot, 0:channels] = edge_ref[0, spots[spot]]
            operand_ref[spot, channels:] = selector(slot_ref[0, pl.ds(spots[spot], 1), :], pool)
        for spot in range(group):
            value_ref[spot] = dot(table_ref[...], operand_ref[spot])
        total = sum_ref[...]
        for spot in range(group):
            out, slope = gelu_pair_low(value_ref[spot] + self_ref[...])
            slope_ref[0, spots[spot]] = slope
            total = total + out.astype(F32)
        sum_ref[...] = total
        return carry

    lax.fori_loop(0, steps // group, some, 0)
    scale = 1.0 / jnp.maximum(chosen_row(count_ref[...], perm_ref[number + start]), 1.0)
    mean = (sum_ref[...] * scale).astype(BF16)
    mean_ref[0] = mean
    total = dot_tn(mean, weight_ref[:, 2 * width : 3 * width]).astype(BF16)
    for spot in range(calls):

        @pl.when(number == spot)
        def _(spot=spot):
            parts[spot][...] = total


def send_selector(rows, lanes):
    peers, slots = rows.shape
    lane = lax.broadcasted_iota(jnp.int32, (slots, lanes), 1).astype(F32)
    parts = []
    for peer in range(peers):
        column = jnp.broadcast_to(rows[peer : peer + 1, :].astype(F32), (8, slots)).T[:, 0:1]
        parts.append(jnp.where(lane == column, 1.0, 0.0).astype(BF16))
    return jnp.concatenate(parts, axis=0)


def pack_body(perm_ref, nodes_ref, output_ref, bias_ref, send_ref, node_ref, pack_ref, leave_ref, all_ref, *, count):
    width = output_ref.shape[1]
    part = output_ref.shape[0]
    all_ref[:, 0:width] = nodes_ref[0].T
    all_ref[:, width : 2 * width] = nodes_ref[1].T
    all_ref[:, 2 * width : 3 * width] = output_ref[...]
    tall = lambda row: jnp.broadcast_to(row, (8, row.shape[1])).T[:, 0:1]
    bias = tall(bias_ref[...].astype(F32).reshape(1, -1)).astype(BF16)
    all_ref[:, 3 * width :] = jnp.broadcast_to(bias, (part, all_ref.shape[1] - 3 * width))
    half = part // 2
    start = pl.multiple_of(perm_ref[count + 1] * half, half)
    pack_ref[...] = all_ref[pl.ds(start, half), :]
    proteins, lanes, _ = node_ref.shape
    for spot in range(proteins):
        table = send_selector(send_ref[spot, 0], lanes)
        leave_ref[:, spot] = dot(table, node_ref[spot]).astype(BF16).reshape(leave_ref[:, spot].shape)


def prepare_body(
    perm_ref,
    edge_ref,
    turned_ref,
    out_ref,
    hidden_bias_ref,
    gain_ref,
    shift_ref,
    branch_ref,
    wide_ref,
    biases_ref,
    gains_ref,
    shifts_ref,
    counts_ref,
    send_ref,
    node_ref,
    up_ref,
    wide_in_ref,
    wide_out_ref,
    weight_ref,
    weight_t_ref,
    column_ref,
    out_t_ref,
    turned_edge_ref,
    vector_ref,
    share_ref,
    table_ref,
    wide_bias_ref,
    own_node_ref,
    own_up_ref,
    block_ref,
    *,
    count,
):
    row = lambda ref: ref[...].astype(F32).reshape(1, -1)
    core = perm_ref[count + 1]
    half = wide_out_ref.shape[0] // 2
    start = pl.multiple_of(core * half, half)
    block_ref[0:half, :] = wide_in_ref[:, pl.ds(start, half)].T
    block_ref[half : 2 * half, :] = wide_out_ref[pl.ds(start, half), :]
    wide = row(wide_ref)
    line = jnp.where(core == 0, wide[:, 0:half], wide[:, half:])
    block_ref[2 * half :, 0:half] = jnp.broadcast_to(line, (16, half)).astype(BF16)
    block_ref[2 * half :, half:] = jnp.zeros((16, block_ref.shape[1] - half), BF16)
    part = edge_ref.shape[1] // count
    for spot in range(count):
        span = slice(spot * part, (spot + 1) * part)
        block = edge_ref[:, pl.ds(pl.multiple_of(perm_ref[spot] * part, part), part)]
        weight_ref[:, span] = block
        weight_t_ref[span, :] = block.T
    tall = lambda row: jnp.broadcast_to(row, (8, row.shape[1])).T[:, 0:1]
    channels = edge_ref.shape[0]
    lane = lax.broadcasted_iota(jnp.int32, (channels, 128), 1)
    column_ref[...] = jnp.where(
        lane == 0,
        tall(row(hidden_bias_ref)),
        jnp.where(lane == 1, tall(row(gain_ref)), tall(row(shift_ref))),
    )
    hidden = out_ref.shape[0]
    extra = out_t_ref.shape[1] - hidden
    lane = lax.broadcasted_iota(jnp.int32, (channels, extra), 1)
    last = jnp.where(lane == 0, tall(row(branch_ref)), 0.0).astype(BF16)
    out_t_ref[...] = jnp.concatenate([out_ref[...].T, last], axis=1)
    turned_edge_ref[...] = turned_ref[:, turned_ref.shape[1] - channels :].T
    vector_ref[0:2, :] = biases_ref[...].astype(F32)
    vector_ref[2:4, :] = gains_ref[...].astype(F32)
    vector_ref[4:6, :] = shifts_ref[...].astype(F32)
    vector_ref[6:8, :] = jnp.zeros((2, vector_ref.shape[1]), F32)
    me = perm_ref[0]
    counts = chosen_row(counts_ref[...], me)
    share = counts * (1.0 / jnp.maximum(counts, 1.0))
    share_ref[...] = jnp.broadcast_to(tall(share), share_ref.shape)
    table_ref[...] = send_selector(send_ref[me, 0], table_ref.shape[1])
    wide_bias_ref[...] = jnp.broadcast_to(wide, wide_bias_ref.shape).astype(BF16)
    own_node_ref[...] = node_ref[...]
    own_up_ref[...] = up_ref[...]


def fill_weights(perm_ref, mine, other, target, count):
    core = perm_ref[count + 1]
    half = mine[0].shape[0]
    for spot in range(count):
        for place, value in ((core, mine[spot][...]), (1 - core, other[spot][...])):
            start = pl.multiple_of((2 * spot + place) * half, half)
            target[pl.ds(start, half), :] = value


def forward_body(*refs, count):
    parts = refs[:count]
    node_ref, share_ref, vector_ref, send_ref, turned_ref = refs[count : count + 5]
    blocks = list(refs[count + 5 : 2 * count + 5])
    blocks = blocks + [refs[2 * count + 5].at[spot] for spot in range(count)]
    one_ref, two_ref, first_ref, second_ref, leave_ref, term_ref, slope_ref = refs[2 * count + 6 :]
    total = parts[0][...].astype(F32)
    for spot in range(1, count):
        total = total + parts[spot][...].astype(F32)
    value = node_ref[0].astype(F32) + total + share_ref[:, 0:1] * vector_ref[0:1, :]
    one_ref[...] = value
    first_norm, _, _ = norm_forward(value, vector_ref[2:3, :], vector_ref[4:5, :])
    first_low = first_norm.astype(BF16)
    first_ref[...] = first_low
    value = first_norm + vector_ref[1:2, :]
    for spot in range(2 * count):
        block = blocks[spot]
        half = (block.shape[0] - 16) // 2
        pre = dot_nt(first_low, block[0:half, :]) + block[2 * half : 2 * half + 1, 0:half].astype(F32)
        out, slope = gelu_pair(pre)
        slope_ref[:, spot * half : (spot + 1) * half] = slope.astype(BF16)
        value = value + dot(out.astype(BF16), block[half : 2 * half, :])
    two_ref[...] = value
    second_norm, _, _ = norm_forward(value, vector_ref[3:4, :], vector_ref[5:6, :])
    second = second_norm.astype(BF16)
    second_ref[...] = second
    leave_ref[...] = dot(send_ref[...], second).astype(BF16)
    lanes, width = second.shape
    term_ref[:, 0:lanes] = dot_nt(turned_ref[:, 0:width], second).astype(BF16)
    term_ref[:, lanes:] = dot_nt(turned_ref[:, width : 2 * width], second).astype(BF16)


def update_body(perm_ref, *refs, count, calls, first_call, joint):
    edge_ref, slot_ref, up_ref = refs[:3]
    terms = refs[3 : 3 + calls]
    if joint:
        refs = refs[: 3 + calls] + refs[3:]
        hidden = refs[3 + 2 * calls].shape[0]
        remotes = [ref.at[hidden:, :] for ref in terms]
        terms = [ref.at[0:hidden, :] for ref in terms]
    else:
        remotes = refs[3 + calls : 3 + 2 * calls]
    turned_ref, column_ref, out_t_ref, out_ref, weight_ref = refs[3 + 2 * calls : 8 + 2 * calls]
    refs = refs[8 + 2 * calls :]
    if not first_call:
        start_ref = refs[0]
        refs = refs[2:]
    result_ref, part_ref = refs[:2]
    sums = refs[2 : 2 + calls]
    total_ref = refs[2 + calls]
    table_ref, self_ref, table_grad_ref, self_grad_ref = refs[3 + calls : 7 + calls]
    gain_grad_ref, shift_grad_ref, edge_grad_ref, out_grad_ref = refs[7 + calls : 11 + calls]
    gain_ref, shift_ref, operand_ref, out_low_ref, mixed_ref, grad_ref = refs[11 + calls : 17 + calls]
    product_ref, value_ref, slope_ref, term_ref, remote_ref = refs[17 + calls :]
    group = operand_ref.shape[1] // edge_ref.shape[3]
    number = pl.program_id(0)
    dead = perm_ref[count]
    steps, channels, lanes = edge_ref.shape[1:]
    hidden = turned_ref.shape[0]
    width = remotes[0].shape[1]
    pool = lanes + remotes[0].shape[0]
    extra = out_t_ref.shape[1] - hidden
    grads = (edge_grad_ref, out_grad_ref)
    bases = (0, 256)
    sum_refs = (gain_grad_ref, shift_grad_ref)
    sum_bases = (512, 640)

    @pl.when(number == 0)
    def _():
        for ref, base in zip(grads, bases):
            if first_call:
                ref[...] = jnp.zeros_like(ref)
            else:
                ref[...] = start_ref[:, base : base + ref.shape[1]]
        for ref, base in zip(sum_refs, sum_bases):
            if first_call:
                ref[...] = jnp.zeros_like(ref)
            else:
                lane = lax.broadcasted_iota(jnp.int32, ref.shape, 1)
                ref[...] = jnp.where(lane == 0, start_ref[:, base : base + 1], 0.0)
        gain_ref[...] = jnp.broadcast_to(column_ref[:, 1:2], gain_ref.shape)
        shift_ref[...] = jnp.broadcast_to(column_ref[:, 2:3], shift_ref.shape)

    for spot in range(calls):

        @pl.when(number == spot)
        def _(spot=spot):
            term_ref[...] = terms[spot][...]
            remote_ref[...] = remotes[spot][...]

    remote = dot_nt(turned_ref[:, width : 2 * width], remote_ref[...])
    term = jnp.concatenate([term_ref[:, lanes:].astype(F32), remote], axis=1)
    table_ref[...] = masked_table(turned_ref[:, 2 * width :], term, dead)
    self_ref[...] = term_ref[:, 0:lanes].astype(F32) + column_ref[:, 0:1]
    table_grad_ref[...] = jnp.zeros_like(table_grad_ref)
    self_grad_ref[...] = jnp.zeros_like(self_grad_ref)
    share = 1.0 / channels
    first = lax.broadcasted_iota(jnp.int32, (extra, lanes), 0) == 0
    spans = [slice(spot * lanes, (spot + 1) * lanes) for spot in range(group)]
    total = lambda value: jnp.sum(value, axis=0, keepdims=True)

    def some(index, carry):
        spots = [index * group + spot for spot in range(group)]
        for spot, span in zip(spots, spans):
            slot_row = slot_ref[0, pl.ds(spot, 1), :]
            operand_ref[0:channels, span] = edge_ref[0, spot]
            operand_ref[channels:, span] = selector(slot_row, pool)
            live = jnp.where(first & (slot_row != dead), 1.0, 0.0)
            out_low_ref[hidden:, span] = live.astype(BF16)
        for span in spans:
            value_ref[:, span] = dot(table_ref[...], operand_ref[:, span])
        for span in spans:
            out, slope = gelu_pair_low(value_ref[:, span] + self_ref[...])
            out_low_ref[0:hidden, span] = out
            slope_ref[:, span] = slope
        for span in spans:
            value_ref[:, span] = dot(out_t_ref[...], out_low_ref[:, span])
        for spot, span in zip(spots, spans):
            value = edge_ref[0, spot].astype(F32) + value_ref[:, span]
            centred = value - total(value) * share
            inverse = lax.rsqrt(total(centred * centred) * share + EPSILON)
            normed = centred * inverse
            gain = gain_ref[...]
            result_ref[0, spot] = (normed * gain + shift_ref[...]).astype(BF16)
            scaled = up_ref[0, spot].astype(F32) * gain
            product = scaled * normed
            product_ref[:, span] = product.astype(BF16)
            mixed = inverse * (scaled - total(scaled) * share - normed * (total(product) * share))
            mixed_ref[:, span] = mixed.astype(BF16)
        for span in spans:
            value_ref[:, span] = dot(out_ref[...], mixed_ref[:, span])
        for span in spans:
            grad = slope_ref[:, span].astype(F32) * value_ref[:, span]
            self_grad_ref[...] += grad
            grad_ref[:, span] = grad.astype(BF16)
        out_grad_ref[...] += dot_nt(mixed_ref[...], out_low_ref[...])
        for spot, span in zip(spots, spans):
            edge = dot(weight_ref[...], grad_ref[:, span])
            part_ref[0, spot] = (mixed_ref[:, span].astype(F32) + edge).astype(BF16)
        table_grad_ref[...] += dot_nt(grad_ref[...], operand_ref[...])
        sums_of = gain_grad_ref[...]
        for span in spans:
            sums_of = sums_of + product_ref[:, span].astype(F32)
        gain_grad_ref[...] = sums_of
        sums_of = shift_grad_ref[...]
        for spot in spots:
            sums_of = sums_of + up_ref[0, spot].astype(F32)
        shift_grad_ref[...] = sums_of
        return carry

    lax.fori_loop(0, steps // group, some, 0)
    edge_grad_ref[...] += table_grad_ref[:, 0:channels]
    for spot in range(calls):

        @pl.when(number == spot)
        def _(spot=spot):
            sums[spot][:, 0:lanes] = self_grad_ref[...].astype(BF16)
            sums[spot][:, lanes:] = table_grad_ref[:, channels:].astype(BF16)

    @pl.when(number == calls - 1)
    def _():
        for ref, base in zip(grads, bases):
            total_ref[:, base : base + ref.shape[1]] = ref[...]
        for ref, base in zip(sum_refs, sum_bases):
            flat = jnp.sum(ref[...], axis=1, keepdims=True)
            total_ref[:, base : base + 128] = jnp.broadcast_to(flat, (channels, 128))


def return_body(perm_ref, *refs, count):
    sums = refs[:count]
    turned_ref, up_ref = refs[count : count + 2]
    second_ref, leave_ref, sum_ref = refs[count + 2 :]
    total = sums[0][...].astype(F32)
    for spot in range(1, count):
        total = total + sums[spot][...].astype(F32)
    low = total.astype(BF16)
    lanes, width = second_ref.shape
    back = dot_tn(low[:, lanes:], turned_ref[:, width : 2 * width])
    leave_ref[...] = back[lanes:].astype(BF16)
    second_ref[...] = (
        up_ref[0].astype(F32) + dot_tn(low[:, 0:lanes], turned_ref[:, 0:width]) + back[0:lanes]
    )
    sum_ref[...] = total


def update_weights_body(perm_ref, sum_ref, low_ref, arrive_ref, grad_ref, column_ref, whole_ref):
    total = sum_ref[...]
    low = total.astype(BF16)
    lanes = low_ref.shape[0]
    channels = grad_ref.shape[0]
    hidden = low.shape[0]
    rows = jnp.concatenate([low_ref[...], arrive_ref[...]], axis=0)
    lane = lax.broadcasted_iota(jnp.int32, (channels, 128), 1)
    vectors = jnp.where(
        lane == 0,
        jnp.sum(total[:, 0:lanes], axis=1, keepdims=True),
        jnp.where(
            lane == 1,
            grad_ref[:, 512:513] / column_ref[:, 1:2],
            jnp.where(lane == 2, grad_ref[:, 640:641], grad_ref[:, 256 + hidden : 257 + hidden]),
        ),
    )
    whole_ref[...] = jnp.concatenate(
        [
            dot(low[:, 0:lanes], low_ref[...]),
            dot(low[:, lanes:], rows),
            grad_ref[:, 0:channels],
            grad_ref[:, 256 : 256 + hidden],
            vectors,
        ],
        axis=1,
    )


def backward_body(*refs, count):
    second_ref, return_ref, send_ref, one_ref, two_ref, share_ref, vector_ref, slope_ref = refs[:8]
    blocks = list(refs[8 : 8 + count])
    blocks = blocks + [refs[8 + count].at[spot] for spot in range(count)]
    aggregate_ref, forward_ref, sum_ref, grad_ref = refs[9 + count :]
    lanes = one_ref.shape[0]
    second_grad = second_ref[...] + dot_tn(send_ref[...], return_ref[...])
    _, first_normed, first_inverse = norm_forward(
        one_ref[...], vector_ref[2:3, :], vector_ref[4:5, :]
    )
    _, second_normed, second_inverse = norm_forward(
        two_ref[...], vector_ref[3:4, :], vector_ref[5:6, :]
    )
    total = lambda value: jnp.sum(value, axis=0, keepdims=True)
    grad_ref[3:4, :] = total(second_grad * second_normed)
    grad_ref[5:6, :] = total(second_grad)
    sum_two = norm_backward(second_grad, second_normed, second_inverse, vector_ref[3:4, :])
    low = sum_two.astype(BF16)
    forward_ref[0:lanes, :] = low
    grad_ref[1:2, :] = total(low.astype(F32))
    first_grad = sum_two
    for spot in range(2 * count):
        block = blocks[spot]
        half = (block.shape[0] - 16) // 2
        slope = slope_ref[:, spot * half : (spot + 1) * half].astype(F32)
        grad = (slope * dot_nt(low, block[half : 2 * half, :])).astype(BF16)
        first_grad = first_grad + dot(grad, block[0:half, :])
    grad_ref[2:3, :] = total(first_grad * first_normed)
    grad_ref[4:5, :] = total(first_grad)
    sum_one = norm_backward(first_grad, first_normed, first_inverse, vector_ref[2:3, :])
    sum_ref[...] = sum_one
    aggregate = sum_one.astype(BF16)
    aggregate_ref[...] = aggregate
    grad_ref[0:1, :] = total(share_ref[:, 0:1] * aggregate.astype(F32))
    grad_ref[6:16, :] = jnp.zeros((10, grad_ref.shape[1]), F32)
    forward_ref[lanes:, :] = grad_ref[...].astype(BF16)


def message_backward_body(perm_ref, *refs, count, calls, first_call):
    edge_ref, slot_ref, slope_ref, part_ref, edge_weight_ref, count_ref = refs[:6]
    weights = refs[6 : 6 + count]
    others = refs[6 + count : 6 + 2 * count]
    ups = refs[6 + 2 * count : 6 + 2 * count + calls]
    refs = refs[6 + 2 * count + calls :]
    if not first_call:
        node_ref, arrive_ref, own_node_ref, own_arrive_ref, mean_ref, own_mean_ref = refs[:6]
        own_up_ref, own_low_ref, own_edge_ref, whole_ref = refs[6:10]
        refs = refs[11:]
    grad_ref = refs[0]
    backs = refs[1 : 1 + calls]
    low_out_ref, edge_out_ref = refs[1 + calls : 3 + calls]
    weight_ref, up_ref, table_grad_ref, self_grad_ref = refs[3 + calls : 7 + calls]
    operand_ref, grad_low_ref, up_in_ref = refs[7 + calls : 10 + calls]
    if not first_call:
        mine_ref, other_ref = low_out_ref, edge_out_ref
        low_ref, row_ref, mean_all_ref, up_all_ref = refs[10 + calls : 14 + calls]
        edge_total_ref, bias_ref, total_ref, out_total_ref = refs[14 + calls :]
    group = operand_ref.shape[1] // edge_ref.shape[3]
    number = pl.program_id(0)
    steps, channels, lanes = edge_ref.shape[1:]
    part = 2 * weights[0].shape[0]
    hidden = part * count
    width = backs[0].shape[1]
    pool = backs[0].shape[0]

    @pl.when(number == 0)
    def _():
        fill_weights(perm_ref, weights, others, weight_ref, count)
        if not first_call:
            low_ref[:, 0:pool] = own_low_ref[...]
            row_ref[0:lanes, :] = own_node_ref[0]
            row_ref[lanes:pool, :] = own_arrive_ref[...].reshape(-1, width)
            mean_all_ref[:, 0:lanes] = own_mean_ref[0]
            up_all_ref[0:lanes, :] = own_up_ref[...]
            edge_total_ref[...] = own_edge_ref[...]

    for spot in range(calls):

        @pl.when(number == spot)
        def _(spot=spot):
            up_in_ref[...] = ups[spot][...]
            if not first_call:
                at = (spot + 1) * pool
                row_ref[at : at + lanes, :] = node_ref[0]
                row_ref[at + lanes : at + pool, :] = arrive_ref[...].reshape(-1, width)
                at = (spot + 1) * lanes
                mean_all_ref[:, at : at + lanes] = mean_ref[0]
                up_all_ref[at : at + lanes, :] = ups[spot][...]

    value = dot_nt(weight_ref[:, 2 * width : 3 * width], up_in_ref[...])
    number_of = perm_ref[number if first_call else number + 1]
    scale = 1.0 / jnp.maximum(chosen_row(count_ref[...], number_of), 1.0)
    up_ref[...] = (value * scale).astype(BF16)
    table_grad_ref[...] = jnp.zeros_like(table_grad_ref)
    self_grad_ref[...] = jnp.zeros_like(self_grad_ref)
    spans = [slice(spot * lanes, (spot + 1) * lanes) for spot in range(group)]

    def some(index, carry):
        spots = [index * group + spot for spot in range(group)]
        for spot, span in zip(spots, spans):
            operand_ref[0:channels, span] = edge_ref[0, spot]
            operand_ref[channels:, span] = selector(slot_ref[0, pl.ds(spot, 1), :], pool)
        total = self_grad_ref[...]
        for spot, span in zip(spots, spans):
            grad = slope_ref[0, spot] * up_ref[...]
            grad_low_ref[:, span] = grad
            total = total + grad.astype(F32)
        self_grad_ref[...] = total
        for spot, span in zip(spots, spans):
            edge = dot(edge_weight_ref[...], grad_low_ref[:, span])
            grad_ref[0, spot] = (part_ref[0, spot].astype(F32) + edge).astype(BF16)
        table_grad_ref[...] += dot_nt(grad_low_ref[...], operand_ref[...])
        return carry

    lax.fori_loop(0, steps // group, some, 0)
    self_low = self_grad_ref[...].astype(BF16)
    pool_low = table_grad_ref[:, channels:].astype(BF16)
    self_back = dot_tn(self_low, weight_ref[:, 0:width])
    pool_back = dot_tn(pool_low, weight_ref[:, width : 2 * width])
    low_both = jnp.concatenate(
        [
            jnp.concatenate([self_low, jnp.zeros((hidden, pool - lanes), BF16)], axis=1),
            pool_low,
        ],
        axis=0,
    )
    for spot in range(calls):

        @pl.when(number == spot)
        def _(spot=spot):
            backs[spot][0:lanes, :] = (self_back + pool_back[0:lanes]).astype(BF16)
            backs[spot][lanes:, :] = pool_back[lanes:].astype(BF16)
            if not first_call:
                low_ref[:, (spot + 1) * pool : (spot + 2) * pool] = low_both

    if first_call:
        low_out_ref[...] = low_both
        edge_out_ref[...] = table_grad_ref[:, 0:channels]
        return
    edge_total_ref[...] += table_grad_ref[:, 0:channels]

    @pl.when(number == calls - 1)
    def _():
        total_ref[...] = dot(low_ref[...], row_ref[...])
        out_total_ref[...] = dot(mean_all_ref[...], up_all_ref[...])
        ones = jnp.ones((row_ref.shape[0], 128), BF16)
        bias_ref[...] = dot(low_ref[0:hidden, :], ones)
        core = perm_ref[count + 1]
        half = part // 2
        rows = whole_ref.shape[0] // count // 2
        for spot in range(count):
            for place, ref in ((core, mine_ref), (1 - core, other_ref)):
                first = pl.multiple_of(spot * part + place * half, half)
                kind = ref.dtype
                ref[spot, 0:half, 0:width] = total_ref[pl.ds(first, half), :].astype(kind)
                ref[spot, 0:half, width : 2 * width] = total_ref[pl.ds(hidden + first, half), :].astype(kind)
                ref[spot, 0:half, 2 * width : 3 * width] = out_total_ref[pl.ds(first, half), :].astype(kind)
                start = pl.multiple_of((place * count + perm_ref[spot]) * rows, 8)
                wide = whole_ref.shape[1]
                below = jnp.concatenate(
                    [
                        whole_ref[pl.ds(start, rows), :],
                        jnp.zeros((ref.shape[1] - half - rows, wide), F32),
                    ],
                    axis=0,
                )
                ref[spot, half:, 0:wide] = below.astype(kind)
                ref[spot, half:, wide:] = jnp.zeros((below.shape[0], ref.shape[2] - wide), kind)
                both = jnp.concatenate(
                    [
                        edge_total_ref[pl.ds(first, half), :],
                        bias_ref[pl.ds(first, half), 0 : ref.shape[2] - 3 * width - channels],
                    ],
                    axis=1,
                )
                ref[spot, 0:half, 3 * width :] = both.astype(kind)


def wide_body(
    perm_ref, low_ref, forward_ref, weight_ref, bias_ref, output_ref, mine_ref, other_ref, all_ref, *, count
):
    width = low_ref.shape[1]
    wide = weight_ref.shape[1]
    step = forward_ref.shape[0] // count
    lanes = step - 16
    low = low_ref[...]
    forward = jnp.concatenate(
        [forward_ref[spot * step : spot * step + lanes, :] for spot in range(count)], axis=0
    )
    lines = None
    for spot in range(count):
        line = forward_ref[spot * step + lanes : (spot + 1) * step, :].astype(F32)
        lines = line if spot == 0 else lines + line
    pre = dot(low, weight_ref[...]) + bias_ref[0:1, :].astype(F32)
    out, slope = gelu_pair_low(pre)
    grad = slope.astype(F32) * dot_nt(forward, output_ref[...])
    all_ref[0:width, :] = dot_tn(low, grad.astype(BF16))
    all_ref[width : width + wide, :] = dot_tn(out, forward)
    at = width + wide
    total = jnp.broadcast_to(jnp.sum(grad, axis=0, keepdims=True), (8, wide))
    all_ref[at : at + 8, :] = total
    all_ref[at + 8 : at + 16, :] = lines[0:8]
    all_ref[at + 16 :, :] = jnp.zeros((all_ref.shape[0] - at - 16, width), F32)
    half = mine_ref.shape[0]
    core = perm_ref[count + 1]
    mine_ref[...] = all_ref[pl.ds(pl.multiple_of(core * half, 8), half), :]
    other_ref[...] = all_ref[pl.ds(pl.multiple_of((1 - core) * half, 8), half), :].astype(BF16)


def wide_finish_body(
    perm_ref, mine_ref, other_ref, in_ref, out_ref, bias_ref, one_ref, two_ref, three_ref, all_ref, *, count
):
    core = perm_ref[count + 1]
    half = mine_ref.shape[0]
    all_ref[pl.ds(pl.multiple_of(core * half, 8), half), :] = mine_ref[...].astype(F32)
    all_ref[pl.ds(pl.multiple_of((1 - core) * half, 8), half), :] = other_ref[...].astype(F32)
    width = in_ref.shape[0]
    wide = out_ref.shape[0]
    in_ref[...] = all_ref[0:width, :]
    out_ref[...] = all_ref[width : width + wide, :]
    at = width + wide
    bias_ref[...] = all_ref[at : at + 1, :]
    one_ref[...] = all_ref[at + 8 : at + 10, :]
    two_ref[...] = all_ref[at + 10 : at + 12, :]
    three_ref[...] = all_ref[at + 12 : at + 14, :]


def late_finish_body(
    perm_ref,
    mine_ref,
    other_ref,
    mine_parts_ref,
    other_parts_ref,
    nodes_ref,
    output_ref,
    bias_ref,
    turned_ref,
    update_ref,
    hidden_bias_ref,
    gain_ref,
    shift_ref,
    branch_ref,
    edge_ref,
    own_ref,
    whole_ref,
    edges_ref,
    *,
    count,
):
    core = perm_ref[count + 1]
    part = own_ref.shape[0]
    half = part // 2
    width = output_ref.shape[1]
    rows = whole_ref.shape[0] // count // 2
    channels = edges_ref.shape[1]
    for place, ref, parts in ((core, mine_ref, mine_parts_ref), (1 - core, other_ref, other_parts_ref)):
        own_ref[pl.ds(pl.multiple_of(place * half, 8), half), :] = ref[...].astype(F32)
        for spot in range(count):
            value = parts[spot].astype(F32)
            start = pl.multiple_of((place * count + perm_ref[spot]) * rows, 8)
            whole_ref[pl.ds(start, rows), :] = value[0:rows, :]
            first = perm_ref[spot] * part + place * half
            for turn in range(half // 8):
                start = pl.multiple_of(first + 8 * turn, 8)
                edges_ref[pl.ds(start, 8), :] = value[rows:, turn * channels : (turn + 1) * channels]
    nodes_ref[0] = own_ref[:, 0:width].T
    nodes_ref[1] = own_ref[:, width : 2 * width].T
    output_ref[...] = own_ref[:, 2 * width : 3 * width]
    last = own_ref.shape[1]
    bias_ref[...] = own_ref[:, last - 128 :].T[127:128, :]
    end = turned_ref.shape[1]
    hidden = update_ref.shape[0]
    turned_ref[...] = whole_ref[:, 0:end]
    update_ref[...] = whole_ref[:, end : end + hidden].T
    vectors = whole_ref[:, end + hidden :].T
    hidden_bias_ref[...] = vectors[0:1, :]
    gain_ref[...] = vectors[1:2, :]
    shift_ref[...] = vectors[2:3, :]
    branch_ref[...] = vectors[3:4, :]
    edge_ref[...] = edges_ref[...].T


def place_body(perm_ref, *refs, count):
    for spot in range(count):

        @pl.when(pl.program_id(0) == spot)
        def _(spot=spot):
            refs[count][0] = refs[spot][...]


def held(value):
    return pltpu.with_memory_space_constraint(value, pltpu.HBM)


def group_of(total, most=15):
    for size in (15, 5, 4, 3, 2, 1):
        if size <= most and total % size == 0:
            return size


def call(body, grid, ins, outs, scratch, flops, moved, name, perm=None, limit=56, aliases=()):
    whole = lambda block: (block, lambda *_: (0,) * len(block))
    in_specs = [
        pl.BlockSpec(memory_space=pl.ANY)
        if len(entry) == 2
        else pl.BlockSpec(*(entry[1:] if len(entry) == 3 else whole(entry[0].shape)))
        for entry in ins
    ]
    out_specs = [
        pl.BlockSpec(*(entry[2:] if len(entry) == 4 else whole(entry[0]))) for entry in outs
    ]
    spec = pltpu.PrefetchScalarGridSpec(
        num_scalar_prefetch=0 if perm is None else 1,
        grid=grid,
        in_specs=in_specs,
        out_specs=out_specs,
        scratch_shapes=scratch,
    )
    operands = [entry[0] for entry in ins]
    return pl.pallas_call(
        body,
        grid_spec=spec,
        out_shape=[(pltpu.HBM if name in PINNED else jax.ShapeDtypeStruct)(entry[0], entry[1]) for entry in outs],
        input_output_aliases={source + 1: target for source, target in aliases},
        compiler_params=pltpu.CompilerParams(
            dimension_semantics=("arbitrary",) * len(grid), vmem_limit_bytes=limit * 2**20
        ),
        cost_estimate=pl.CostEstimate(flops=flops, bytes_accessed=moved, transcendentals=0),
        name=name,
    )(*([] if perm is None else [perm]), *operands)


def build(prot_size, res_size, mp_size):
    def across(value, offset):
        pairs = [(spot, spot ^ offset) for spot in range(mp_size)]
        return lax.ppermute(value, "mp", pairs)

    def gather(value):
        return [value] + [across(value, offset) for offset in range(1, mp_size)]

    def scatter(parts):
        return [parts[0]] + [across(parts[offset], offset) for offset in range(1, mp_size)]

    def exchange(value):
        return lax.all_to_all(value, "res", split_axis=0, concat_axis=0, tiled=True)

    def block_parts(value):
        place = lax.axis_index("res")
        piece = value.shape[0] // res_size
        parts = [lax.dynamic_slice_in_dim(value, place * piece, piece, 0)]
        low = value.astype(BF16)
        for hop in range(1, res_size):
            target = lax.rem(place + hop, res_size)
            part = lax.dynamic_slice_in_dim(low, target * piece, piece, 0)
            pairs = [(spot, (spot + hop) % res_size) for spot in range(res_size)]
            parts.append(lax.ppermute(part, "res", pairs))
        return parts

    def block_gather(own):
        parts = [own]
        for hop in range(1, res_size):
            pairs = [(spot, (spot - hop) % res_size) for spot in range(res_size)]
            parts.append(lax.ppermute(own, "res", pairs))
        return parts

    def block_order(parts):
        place = lax.axis_index("res")
        piece = parts[0].shape[0]
        both = jnp.concatenate(parts + parts, axis=0)
        return lax.dynamic_slice_in_dim(both, (res_size - place) * piece, res_size * piece, 0)

    def swap(value):
        return lax.ppermute(value, "prot", [(0, 1), (1, 0)])

    def per_device(
        node_states,
        edge_states,
        neighbour_slots,
        send_rows,
        live_counts,
        message_nodes,
        message_edges,
        message_bias,
        message_output,
        feedforward_weight,
        feedforward_bias,
        feedforward_output,
        output_biases,
        norm_gains,
        norm_shifts,
        update_weight,
        update_bias,
        update_output,
        branch_bias,
        edge_gain,
        edge_shift,
        node_cotangent,
        edge_cotangent,
    ):
        proteins, lanes, width = node_states.shape
        own_k, channels = edge_states.shape[2:]
        slots = send_rows.shape[3]
        remote = res_size * slots
        pool = lanes + remote
        part = message_nodes.shape[2]
        hidden = part * mp_size
        update_hidden = update_output.shape[0]
        wide = feedforward_weight.shape[1]
        assert proteins == mp_size and prot_size == 2
        me = lax.axis_index("mp")
        core = lax.axis_index("prot")
        place = lax.axis_index("res")
        dead = lanes + place * slots
        order = [me ^ offset for offset in range(mp_size)]
        perm = jnp.stack(order + [dead, core]).astype(jnp.int32)

        def reorder(value, axis=0):
            size = value.shape[axis] // mp_size
            return jnp.concatenate(
                [lax.dynamic_slice_in_dim(value, spot * size, size, axis) for spot in order], axis=axis
            )

        message_pack, leaving = call(
            functools.partial(pack_body, count=mp_size),
            (1,),
            [
                (message_nodes,),
                (message_output,),
                (message_bias,),
                (send_rows,),
                (node_states,),
            ],
            [
                ((part // 2, 3 * width + 128), BF16),
                ((res_size, proteins, slots, width), BF16),
            ],
            [pltpu.VMEM((part, 3 * width + 128), BF16)],
            0,
            0,
            "pack",
            perm,
        )
        arriving = exchange(leaving)
        weights = gather(message_pack)
        other_weights = [swap(value) for value in weights]
        own_slots = lax.dynamic_slice_in_dim(neighbour_slots, me * own_k, own_k, 2)
        alive = lax.broadcasted_iota(jnp.int32, own_slots.shape, 2) + me * own_k < live_counts[..., None]
        own_slots = jnp.transpose(jnp.where(alive, own_slots, dead), (0, 2, 1))
        edges = jnp.transpose(edge_states, (0, 2, 3, 1))
        edge_up = jnp.transpose(edge_cotangent, (0, 2, 3, 1))
        turned = update_weight.T
        small = call(
            functools.partial(prepare_body, count=mp_size),
            (1,),
            [
                (message_edges,),
                (turned,),
                (update_output,),
                (update_bias,),
                (edge_gain,),
                (edge_shift,),
                (branch_bias,),
                (feedforward_bias,),
                (output_biases,),
                (norm_gains,),
                (norm_shifts,),
                (live_counts,),
                (send_rows,),
                (node_states, (1, lanes, width), lambda p, perm: (perm[0], 0, 0)),
                (node_cotangent, (1, lanes, width), lambda p, perm: (perm[0], 0, 0)),
                (feedforward_weight,),
                (feedforward_output,),
            ],
            [
                ((channels, hidden), BF16),
                ((hidden, channels), BF16),
                ((channels, 128), F32),
                ((channels, update_hidden + 16), BF16),
                ((channels, update_hidden), BF16),
                ((8, width), F32),
                ((lanes, 128), F32),
                ((remote, lanes), BF16),
                ((16, wide), BF16),
                ((1, lanes, width), BF16),
                ((1, lanes, width), BF16),
                ((wide + 16, width), BF16),
            ],
            [],
            0,
            0,
            "prepare",
            perm,
        )
        *small, block = small
        blocks = gather(block)
        weights, other_weights, arriving, own_slots, small = lax.optimization_barrier(
            (weights, other_weights, arriving, own_slots, small)
        )
        (
            edge_weight,
            edge_weight_t,
            columns,
            out_t,
            turned_edge,
            vectors,
            share,
            own_table,
            wide_bias,
            own_node,
            own_up,
        ) = small

        depth = channels + pool
        group = group_of(own_k, 5)
        group_update = group_of(own_k, 5)
        group_back = group_of(own_k, 5)
        count = proteins * own_k * lanes
        by_step4 = lambda p, perm: (p, 0, 0, 0)
        by_step3 = lambda p, perm: (p, 0, 0)
        others = proteins - 1

        def shifted(start):
            return (
                lambda p, perm: (perm[p + start], 0, 0, 0),
                lambda p, perm: (perm[p + start], 0, 0),
                lambda p, perm: (0, perm[p + start], 0, 0),
            )

        edge_block = (1, own_k, channels, lanes)
        edge_shape = (proteins, own_k, channels, lanes)
        slope_shape = (proteins, own_k, hidden, lanes)
        slope_block = (1, own_k, hidden, lanes)

        def edge_ins(start):
            by_perm4, by_perm3, _ = shifted(start)
            return [(edges, edge_block, by_perm4), (own_slots, (1, own_k, lanes), by_perm3)]

        def row_ins(start):
            _, by_perm3, by_arrive = shifted(start)
            return [
                (node_states, (1, lanes, width), by_perm3),
                (arriving, (res_size, 1, slots, width), by_arrive),
            ]

        def message_forward(start, calls, after):
            slots_after, _ = lax.optimization_barrier((own_slots, after))
            found = call(
                functools.partial(message_forward_body, count=proteins, calls=calls, start=start),
                (calls,),
                [edge_ins(start)[0], (slots_after,) + edge_ins(start)[1][1:]]
                + row_ins(start)
                + [(edge_weight_t,), (live_counts,)]
                + [(value,) for value in weights + other_weights],
                [
                    ((calls, own_k, hidden, lanes), BF16, slope_block, by_step4),
                    ((calls, hidden, lanes), BF16, (1, hidden, lanes), by_step3),
                ]
                + [((lanes, width), BF16)] * calls,
                [
                    pltpu.VMEM((hidden, weights[0].shape[1]), BF16),
                    pltpu.VMEM((hidden, depth), BF16),
                    pltpu.VMEM((hidden, lanes), F32),
                    pltpu.VMEM((hidden, lanes), F32),
                    pltpu.VMEM((group, depth, lanes), BF16),
                    pltpu.VMEM((group, hidden, lanes), F32),
                ],
                2 * calls * own_k * lanes * depth * hidden,
                calls * own_k * lanes * (channels + hidden) * 2,
                "message_forward",
                perm,
            )
            return found[0], found[1], list(found[2:])

        slope_others, mean_others, part_others = message_forward(1, others, own_slots)
        slope_own, mean_own, part_own = message_forward(0, 1, part_others[0])
        parts = scatter(part_own + part_others)
        blocks, _ = lax.optimization_barrier((blocks, part_others[0]))
        other_blocks = swap(jnp.stack(blocks))
        one, two, first_low, second_low, leaving, own_term, wide_slope = call(
            functools.partial(forward_body, count=proteins),
            (),
            [(value,) for value in parts]
            + [(own_node,), (share,), (vectors,), (own_table,), (turned,)]
            + [(held(value),) for value in blocks]
            + [(held(other_blocks),)],
            [
                ((lanes, width), F32),
                ((lanes, width), F32),
                ((lanes, width), BF16),
                ((lanes, width), BF16),
                ((remote, width), BF16),
                ((update_hidden, 2 * lanes), BF16),
                ((lanes, wide * mp_size), BF16),
            ],
            [],
            4 * lanes * width * wide * mp_size,
            4 * width * wide * mp_size,
            "feed_forward",
            limit=24,
        )

        arrived = exchange(leaving.reshape(res_size, slots, width)).reshape(remote, width)
        joint = own_term.shape[1] == width
        if joint:
            terms = gather(jnp.concatenate([own_term, arrived], axis=0))
            pool_remotes = []
        else:
            terms = gather(own_term)
            pool_remotes = gather(arrived)
        all_low = lax.all_gather(first_low, "mp", axis=0, tiled=True)
        node_result = lax.all_gather(second_low[None], "mp", axis=0, tiled=True)
        turned_width = 2 * width + channels

        def edge_update(start, calls, earlier):
            by_perm4 = shifted(start)[0]
            ins = (
                edge_ins(start)
                + [(edge_up, edge_block, by_perm4)]
                + [(value,) for value in terms[start : start + calls]]
                + [(value,) for value in pool_remotes[start : start + calls]]
                + [(turned,), (columns,), (out_t,), (update_output,), (turned_edge,)]
            )
            aliases = ()
            if earlier is not None:
                ins = ins + [(earlier[1],), (earlier[0], None)]
                aliases = ((len(ins) - 1, 0),)
            found = call(
                functools.partial(
                    update_body,
                    count=proteins,
                    calls=calls,
                    first_call=earlier is None,
                    joint=joint,
                ),
                (calls,),
                ins,
                [
                    (edge_shape, BF16, edge_block, by_perm4),
                    ((calls, own_k, channels, lanes), BF16, edge_block, by_step4),
                ]
                + [((update_hidden, lanes + pool), BF16)] * calls
                + [((update_hidden, 768), F32)],
                [
                    pltpu.VMEM((update_hidden, depth), BF16),
                    pltpu.VMEM((update_hidden, lanes), F32),
                    pltpu.VMEM((update_hidden, depth), F32),
                    pltpu.VMEM((update_hidden, lanes), F32),
                    pltpu.VMEM((channels, lanes), F32),
                    pltpu.VMEM((channels, lanes), F32),
                    pltpu.VMEM((update_hidden, channels), F32),
                    pltpu.VMEM((channels, update_hidden + 16), F32),
                    pltpu.VMEM((channels, lanes), F32),
                    pltpu.VMEM((channels, lanes), F32),
                    pltpu.VMEM((depth, group_update * lanes), BF16),
                    pltpu.VMEM((update_hidden + 16, group_update * lanes), BF16),
                    pltpu.VMEM((channels, group_update * lanes), BF16),
                    pltpu.VMEM((update_hidden, group_update * lanes), BF16),
                    pltpu.VMEM((channels, group_update * lanes), BF16),
                    pltpu.VMEM((update_hidden, group_update * lanes), F32),
                    pltpu.VMEM((update_hidden, group_update * lanes), BF16),
                    pltpu.VMEM((update_hidden, 2 * lanes), BF16),
                    pltpu.VMEM((remote, width), BF16),
                ],
                2 * calls * own_k * lanes * (2 * depth + 4 * channels) * update_hidden,
                calls * own_k * lanes * channels * 8,
                "edge_update",
                perm,
                aliases=aliases,
            )
            return found[0], found[-1], found[1], found[2:-1]

        edge_result, grads, edge_part_own, sums_own = edge_update(0, 1, None)
        edge_result, grads, edge_part_others, sums_others = edge_update(1, others, (edge_result, grads))
        sums_own, sums_others, all_low = lax.optimization_barrier((sums_own, sums_others, all_low))
        sums = scatter(list(sums_own) + list(sums_others))
        whole_width = turned_width + update_hidden + 128
        second_part, leaving, update_sums = call(
            functools.partial(return_body, count=proteins),
            (1,),
            [(value,) for value in sums]
            + [(turned,), (own_up,)],
            [
                ((lanes, width), F32),
                ((remote, width), BF16),
                ((update_hidden, lanes + pool), F32),
            ],
            [],
            2 * (lanes + pool) * width * update_hidden,
            (lanes + pool) * width * 2,
            "update_return",
            perm,
        )
        returned = exchange(leaving.reshape(res_size, slots, width)).reshape(remote, width)
        (whole,) = call(
            update_weights_body,
            (1,),
            [(update_sums,), (second_low,), (arrived,), (grads,), (columns,)],
            [((update_hidden, whole_width), F32)],
            [],
            2 * (lanes + pool) * width * update_hidden,
            (lanes + pool) * width * 2,
            "update_weights",
            perm,
        )
        whole, returned = lax.optimization_barrier((whole, returned))
        aggregate_grad, forward_grad, sum_one, _ = call(
            functools.partial(backward_body, count=proteins),
            (),
            [(second_part,), (returned,), (own_table,), (one,), (two,), (share,), (vectors,), (wide_slope,)]
            + [(held(value),) for value in blocks]
            + [(held(other_blocks),)],
            [
                ((lanes, width), BF16),
                ((lanes + 16, width), BF16),
                ((lanes, width), F32),
                ((16, width), F32),
            ],
            [],
            6 * lanes * width * wide * mp_size,
            4 * width * wide * mp_size,
            "feed_backward",
            limit=24,
        )
        ups = gather(aggregate_grad)
        all_forward = lax.all_gather(forward_grad, "mp", axis=0, tiled=True)
        total_width = 3 * width + -(-(channels + 1) // 128) * 128
        whole_rows = update_hidden // 2 // mp_size
        late_rows = -(-(part // 2 + whole_rows) // (8 * res_size)) * 8 * res_size
        late_shape = (proteins, late_rows, total_width)

        def message_backward(start, calls, earlier):
            by_perm4 = shifted(start)[0]
            ins = (
                edge_ins(start)
                + [
                    (slope_own if earlier is None else slope_others, slope_block, by_step4),
                    (edge_part_own if earlier is None else edge_part_others, edge_block, by_step4),
                    (edge_weight,),
                    (live_counts,),
                ]
                + [(value,) for value in weights + other_weights + ups[start : start + calls]]
            )
            aliases = ()
            scratch = [
                pltpu.VMEM((hidden, weights[0].shape[1]), BF16),
                pltpu.VMEM((hidden, lanes), BF16),
                pltpu.VMEM((hidden, depth), F32),
                pltpu.VMEM((hidden, lanes), F32),
                pltpu.VMEM((depth, group_back * lanes), BF16),
                pltpu.VMEM((hidden, group_back * lanes), BF16),
                pltpu.VMEM((lanes, width), BF16),
            ]
            if earlier is None:
                last = [((2 * hidden, pool), BF16), ((hidden, channels), F32)]
            else:
                mean_block = (1, hidden, lanes)
                ins = ins + row_ins(start)
                ins = ins + [
                    (node_states, (1, lanes, width), lambda p, perm: (perm[0], 0, 0)),
                    (arriving, (res_size, 1, slots, width), lambda p, perm: (0, perm[0], 0, 0)),
                    (mean_others, mean_block, by_step3),
                    (mean_own,),
                    (ups[0],),
                    (earlier[1],),
                    (earlier[2],),
                    (whole,),
                    (earlier[0], None),
                ]
                aliases = ((len(ins) - 1, 0),)
                last = [(late_shape, F32), (late_shape, BF16)]
                scratch = scratch + [
                    pltpu.VMEM((2 * hidden, proteins * pool), BF16),
                    pltpu.VMEM((proteins * pool, width), BF16),
                    pltpu.VMEM((hidden, proteins * lanes), BF16),
                    pltpu.VMEM((proteins * lanes, width), BF16),
                    pltpu.VMEM((hidden, channels), F32),
                    pltpu.VMEM((hidden, 128), F32),
                    pltpu.VMEM((2 * hidden, width), F32),
                    pltpu.VMEM((hidden, width), F32),
                ]
            found = call(
                functools.partial(
                    message_backward_body, count=proteins, calls=calls, first_call=earlier is None
                ),
                (calls,),
                ins,
                [(edge_shape, BF16, edge_block, by_perm4)] + [((pool, width), BF16)] * calls + last,
                scratch,
                2 * calls * own_k * lanes * (depth + channels) * hidden,
                calls * own_k * lanes * (3 * channels + hidden) * 2,
                "message_backward",
                perm,
                aliases=aliases,
            )
            return found[0], found[-2], found[-1], found[1 : 1 + calls]

        edge_grad, own_low, own_edge, back_own = message_backward(0, 1, None)
        edge_grad, late_mine, late_other, back_others = message_backward(
            1, others, (edge_grad, own_low, own_edge)
        )
        found = list(back_own) + list(back_others)
        late_swapped = swap(late_other)
        backs, late_mine, all_forward, node_result = lax.optimization_barrier(
            (found, late_mine, all_forward, node_result)
        )
        back = scatter(backs)
        late = late_mine + late_swapped.astype(F32)
        late_own = late[0]
        late_low = [late[offset].astype(BF16) for offset in range(1, mp_size)]
        all_forward, late_own, late_low = lax.optimization_barrier((all_forward, late_own, late_low))
        late_parts = scatter([late_own] + late_low)
        unit = prot_size * res_size * 8
        wide_rows = -(-(width + wide + 16) // unit) * unit
        early_mine, early_other = call(
            functools.partial(wide_body, count=proteins),
            (1,),
            [
                (all_low,),
                (all_forward,),
                (feedforward_weight,),
                (wide_bias,),
                (feedforward_output,),
            ],
            [((wide_rows // 2, width), F32), ((wide_rows // 2, width), BF16)],
            [pltpu.VMEM((wide_rows, width), F32)],
            10 * proteins * lanes * width * wide,
            8 * proteins * lanes * width,
            "feed_weights",
            perm,
            limit=24,
        )
        back, early_other, early_mine = lax.optimization_barrier((back, early_other, early_mine))
        early_swapped = swap(early_other)
        total = sum(value.astype(F32) for value in back)
        leaving = total[lanes:].astype(BF16).reshape(res_size, slots, width)
        leaving, early_swapped = lax.optimization_barrier((leaving, early_swapped))
        cut = early_mine.shape[0] // 2
        early = [
            (early_mine[spot : spot + cut] + early_swapped[spot : spot + cut].astype(F32)).astype(BF16)
            for spot in (0, cut)
        ]
        early, leaving = lax.optimization_barrier((early, leaving))
        early = jnp.concatenate(lax.psum(tuple(early), "res"), axis=0)
        returned = exchange(leaving)
        node_grad = (
            sum_one
            + total[:lanes]
            + jnp.einsum(
                "sr,sd->rd", own_table, returned.reshape(remote, width), preferred_element_type=F32
            )
        ).astype(BF16)
        node_grad, late_parts = lax.optimization_barrier((node_grad, late_parts))
        late = sum(value.astype(F32) for value in late_parts)
        late_parts = block_parts(late)
        node_parts = gather(node_grad)
        late = sum(value.astype(F32) for value in late_parts).astype(BF16)
        late, node_parts = lax.optimization_barrier((late, node_parts))
        late_parts = block_gather(late)
        (node_grad,) = call(
            functools.partial(place_body, count=proteins),
            (proteins,),
            [(value,) for value in node_parts],
            [((proteins, lanes, width), BF16, (1, lanes, width), shifted(0)[1])],
            [],
            0,
            0,
            "place_rows",
            perm,
        )
        early, node_grad, late_parts = lax.optimization_barrier((early, node_grad, late_parts))
        late = block_order(late_parts)
        whole = late[part // 2 : part // 2 + whole_rows, :whole_width]
        late = late[: part // 2]
        early_swapped = swap(early)
        late_swapped = swap(late)
        fold = late[:, 3 * width : 3 * width + channels].reshape(-1, 8, channels)
        fold = jnp.transpose(fold, (1, 0, 2)).reshape(8, -1)
        shared_parts = gather(jnp.concatenate([whole, fold], axis=0))
        weight_in_grad, weight_out_grad, wide_bias_grad, biases_grad, gains_grad, shifts_grad = call(
            functools.partial(wide_finish_body, count=proteins),
            (1,),
            [(early,), (early_swapped,)],
            [
                ((width, wide), F32),
                ((wide, width), F32),
                ((1, wide), F32),
                ((2, width), F32),
                ((2, width), F32),
                ((2, width), F32),
            ],
            [pltpu.VMEM((wide_rows, width), F32)],
            0,
            8 * wide_rows * width,
            "feed_weights_out",
            perm,
        )
        weight_in_grad, shared_parts, late_swapped = lax.optimization_barrier(
            (weight_in_grad, shared_parts, late_swapped)
        )
        shared = jnp.stack(shared_parts)
        found = call(
            functools.partial(late_finish_body, count=proteins),
            (1,),
            [(late,), (late_swapped,), (shared,), (swap(shared),)],
            [
                ((2, width, part), F32),
                ((part, width), F32),
                ((1, part), F32),
                ((update_hidden, turned_width), F32),
                ((update_hidden, channels), F32),
                ((1, update_hidden), F32),
                ((1, channels), F32),
                ((1, channels), F32),
                ((1, channels), F32),
                ((channels, hidden), F32),
            ],
            [
                pltpu.VMEM((part, total_width), F32),
                pltpu.VMEM((update_hidden, turned_width + update_hidden + 128), F32),
                pltpu.VMEM((hidden, channels), F32),
            ],
            0,
            8 * hidden * total_width,
            "message_weights_out",
            perm,
            16,
        )
        turn = lambda value: jnp.transpose(value, (0, 3, 1, 2))
        return (
            node_result,
            turn(edge_result),
            node_grad,
            turn(edge_grad),
            found[0],
            found[9],
            found[2].reshape(part),
            found[1],
            weight_in_grad,
            wide_bias_grad.reshape(wide),
            weight_out_grad,
            biases_grad,
            gains_grad,
            shifts_grad,
            found[3].T,
            found[5].reshape(update_hidden),
            found[4],
            found[8].reshape(channels),
            found[6].reshape(channels),
            found[7].reshape(channels),
        )

    return per_device


def solution(mesh):
    return jax.shard_map(
        build(mesh.shape["prot"], mesh.shape["res"], mesh.shape["mp"]),
        mesh=mesh,
        in_specs=(
            P("prot", "res", None),
            P("prot", "res", "mp", None),
            P("prot", "res", None),
            P("prot", "res", None, None),
            P("prot", "res"),
            P(None, None, "mp"),
            P(),
            P("mp"),
            P("mp", None),
            P(None, "mp"),
            P("mp"),
            P("mp", None),
            P(),
            P(),
            P(),
            P(),
            P(),
            P(),
            P(),
            P(),
            P(),
            P("prot", "res", None),
            P("prot", "res", "mp", None),
        ),
        out_specs=(
            P("prot", "res", None),
            P("prot", "res", "mp", None),
            P("prot", "res", None),
            P("prot", "res", "mp", None),
            P(None, None, "mp"),
            P(),
            P("mp"),
            P("mp", None),
            P(None, "mp"),
            P("mp"),
            P("mp", None),
            P(),
            P(),
            P(),
            P(),
            P(),
            P(),
            P(),
            P(),
            P(),
        ),
        check_vma=False,
    )
```
